32 devices in a mesh: dp: 8 (over z, x), mp: 4 (over y, core).
Axes of the slice: x: 2, y: 2, z: 4, core: 2. Of those that a mesh axis runs over, the one named last changes fastest.
Arguments:
- words: bfloat16 [16, 512, 768], P('dp'), may hold values from -6 to 6
- word_extra: int32 [16], P('dp'), may hold values from 1 to 448, 4096 in all
- span_pos: int32 [16, 128], P('dp'), may hold values from 0 to 511
- span_len: int32 [16, 128], P('dp'), may hold values from 1 to 4
- entity_shard: int32 [16, 128, 1], P('dp'), may hold values from 0 to 7; in each aligned block of 256 rows (0 to 255, 256 to 511, ..., all dimensions but the last counted through in order) at most 64 rows name the same one
- entity_row: int32 [16, 128], P('dp'), may hold values from 0 to 7999
- targets: int32 [16, 16], replicated, may hold values from 0 to 63999, as said below
- table: bfloat16 [64000, 256], P('dp', 'mp'), may hold values from -1.125 to 1.125
- ent_proj: bfloat16 [256, 768], P('mp'), may hold values from -2 to 2
- query_weight: bfloat16 [4, 768, 768], P(None, None, 'mp'), may hold values from -0.21875 to 0.21875
- w_key: bfloat16 [768, 768], P(None, 'mp'), may hold values from -0.21875 to 0.21875
- w_value: bfloat16 [768, 768], P(None, 'mp'), may hold values from -0.21875 to 0.21875
- w_out: bfloat16 [768, 768], P('mp'), may hold values from -1.25 to 1.25
- gain_attn: float32 [768], replicated, may hold values from 0.5 to 1.5
- bias_attn: float32 [768], replicated, may hold values from -3 to 3
- w_up: bfloat16 [768, 3072], P(None, 'mp'), may hold values from -0.21875 to 0.21875
- w_down: bfloat16 [3072, 768], P('mp'), may hold values from -0.109375 to 0.109375
- gain_ffn: float32 [768], replicated, may hold values from 0.5 to 1.5
- bias_ffn: float32 [768], replicated, may hold values from -3 to 3
- w_head: bfloat16 [768, 256], replicated, may hold values from -0.21875 to 0.21875
- gain_head: float32 [256], replicated, may hold values from 0.5 to 1.5
- cot_words: bfloat16 [16, 512, 768], P('dp'), may hold values from -6 to 6
- cot_ents: bfloat16 [16, 128, 768], P('dp'), may hold values from -6 to 6
Outputs:
- out_words: bfloat16 [16, 512, 768], P('dp')
- out_ents: bfloat16 [16, 128, 768], P('dp')
- loss: float32 [256], replicated
- grad_words: float32 [16, 512, 768], P('dp')
- grad_table: float32 [64000, 256], P('dp', 'mp')
- grad_ent_proj: float32 [256, 768], P('mp')
- grad_query: float32 [4, 768, 768], P(None, None, 'mp')
- grad_key: float32 [768, 768], P(None, 'mp')
- grad_value: float32 [768, 768], P(None, 'mp')
- grad_out: float32 [768, 768], P('mp')
- grad_gain_attn: float32 [768], replicated
- grad_bias_attn: float32 [768], replicated
- grad_up: float32 [768, 3072], P(None, 'mp')
- grad_down: float32 [3072, 768], P('mp')
- grad_gain_ffn: float32 [768], replicated
- grad_bias_ffn: float32 [768], replicated
- grad_head: float32 [768, 256], replicated
- grad_gain_head: float32 [256], replicated
The draws below stay inside these ranges and needn't reach their ends.
Inputs may be any that keep to these rules, and one draw needn't show every extreme that they name: `entity_shard`: among the entity slots of one index of dp, at most 64 name the same table shard; in some of those blocks one shard is named exactly 64 times. `word_extra`: some sequence holds all 512 words. Each table shard of 8000 rows holds the targets of exactly 32 scored slots.
All inputs are finite; a program needn't handle non-finite values. No bound on the sum of `word_extra` on one device may be relied on, other than what follows from the above.
Results may differ from the reference program's by a relative error of at most 0.017.
Values may be sent and summed in bfloat16 or wider, within the bound.
A program may use at most 192 MiB of HBM per device.

```python
import math
import jax
import jax.numpy as jnp
import numpy as np
from jax import lax

D = 768
H = 12
DH = 64
FF = 3072
EDIM = 256
ROWS_DEV = 8000
L = 512
E = 128
MSEQ = 16
SPANW = 4
SEQ_DEV = 2
SEQS = 16
TABLE_ROWS = 64000
MASKED = 256
CAP = 64
N_DP = 8


def draw_targets(key, part):
    key = jax.random.fold_in(key, 7)
    shard_count = TABLE_ROWS // ROWS_DEV
    per_dev = SEQ_DEV * MSEQ
    offsets = jax.random.randint(jax.random.fold_in(key, 11), (per_dev,), 0, shard_count).astype(jnp.int32)
    forced = jnp.array([1, shard_count // 2, shard_count - 1], jnp.int32)[:min(3, per_dev)]
    places = jax.random.permutation(jax.random.fold_in(key, 13), per_dev)[:forced.shape[0]]
    offsets = offsets.at[places].set(forced)
    device_of = (jnp.arange(SEQS * MSEQ, dtype=jnp.int32) // per_dev).astype(jnp.int32)
    shard_of = ((device_of + jnp.tile(offsets, SEQS // SEQ_DEV)) % shard_count).astype(jnp.int32)
    row_of = jax.random.randint(jax.random.fold_in(key, 12), (SEQS * MSEQ,), 0, ROWS_DEV).astype(jnp.int32)
    return (shard_of * ROWS_DEV + row_of).reshape(SEQS, MSEQ).astype(jnp.int32)


def set_ends(entries, rng, smallest, top_value):
    spot = [jax.random.randint(jax.random.fold_in(rng, axis), (), 0, length) for axis, length in enumerate(entries.shape)]
    widest = entries.shape.index(max(entries.shape))
    next_to = spot[:widest] + [(spot[widest] + 1) % entries.shape[widest]] + spot[widest + 1:]
    return entries.at[tuple(spot)].set(smallest).at[tuple(next_to)].set(top_value)


def shard_levels(rng, extent, split, low, largest):
    def one(axis_at, blocks):
        heights = jax.random.uniform(jax.random.fold_in(jax.random.fold_in(rng, 6), axis_at), (blocks,), jnp.float32, low / len(split), largest / len(split))
        return jnp.repeat(jnp.exp(heights), extent[axis_at] // blocks).reshape((-1,) + (1,) * (len(extent) - axis_at - 1))

    loudness = one(*split[0])
    for cut in split[1:]:
        loudness = loudness * one(*cut)
    return loudness


def split_up(number_of, total, bound, skew):
    loads = [(1 << 20) // math.isqrt(rank ** skew) + 1 for rank in range(2, number_of + 1)]
    surplus, holding = total - bound - (number_of - 1), [1] * (number_of - 1)
    while surplus > 0:
        free = [i for i in range(number_of - 1) if holding[i] < bound]
        mass, left = sum([loads[i] for i in free]), surplus
        for i in free:
            more = min(bound - holding[i], max(1, left * loads[i] // mass), surplus)
            holding[i] = holding[i] + more
            surplus = surplus - more
    return np.array([bound] + holding)


def ragged(stream_key, count, total, limit, skew):
    if count == 2:
        one = jax.random.randint(stream_key, (), max(1, total - limit), min(limit, total - 1) + 1)
        return jnp.stack([one, total - one])
    sizes = jnp.asarray(split_up(count, total, limit, skew), jnp.int32)
    twos = (count - 1) // 2
    giver, taker = sizes[1:1 + 2 * twos:2], sizes[2:2 + 2 * twos:2]
    slack = jnp.minimum(giver - 1, limit - taker)
    passed = jax.random.randint(jax.random.fold_in(stream_key, 1), (twos,), 0, 1 << 20) % (slack + 1)
    sizes = sizes.at[1:1 + 2 * twos:2].set(giver - passed).at[2:2 + 2 * twos:2].set(taker + passed)
    return sizes[jax.random.permutation(jax.random.fold_in(stream_key, 2), count)]


def assign_block(key, own, number, rows, count, top, bound, slope):
    order = jax.random.permutation(key, count)
    crowded, ordinary = portions_of(count, rows * top, bound, slope, True), portions_of(count, rows * top, bound, slope, False)
    places = jnp.arange(count)

    def named(tallies, rotation):
        used = int((tallies > 0).sum())
        fixed = max(1, used // 4)
        passed = fixed + (places - fixed + rotation * (used - fixed)) % max(1, count - fixed)
        return jnp.zeros((count,), jnp.int32).at[order[jnp.where(places < fixed, places, passed)]].set(jnp.asarray(tallies, jnp.int32))

    tallies = jnp.where(number % 4 == 0, named(crowded, number // 4), named(ordinary, number - number // 4 - 1))
    mixed = jax.random.permutation(jax.random.fold_in(own, 3), count)
    source_of, taker = mixed[0:count // 2 * 2:2], mixed[1:count // 2 * 2:2]
    margin = jnp.minimum(tallies[source_of] - 1, bound - tallies[taker]) // 2
    margin = jnp.where((source_of == order[0]) | (taker == order[0]) | (tallies[taker] == 0), 0, jnp.maximum(margin, 0))
    passed = jax.random.randint(jax.random.fold_in(own, 4), (count // 2,), 0, 1 << 20) % (margin + 1)
    tallies = tallies.at[source_of].add(-passed).at[taker].add(passed)
    items = jnp.searchsorted(jnp.cumsum(tallies), jnp.arange(rows * top), side="right").astype(jnp.int32)
    listing = items.reshape(top, rows).T
    listing = listing[jax.random.permutation(jax.random.fold_in(own, 1), rows)]
    rotation = jax.random.randint(jax.random.fold_in(own, 2), (rows, 1), 0, top)
    return jnp.take_along_axis(listing, (jnp.arange(top)[None, :] + rotation) % top, axis=1)


def portions_of(amount, total, limit, lean, full):
    portions = [(1 << 20) // math.isqrt(grade ** lean) + 1 for grade in range(1, amount + 1)]
    largest = limit if full else min(limit, max(-(-total // amount), total * portions[0] // sum(portions)))
    least = 1 if total - largest >= amount - 1 else 0
    counts, rest = [largest] + [least] * (amount - 1), total - largest - least * (amount - 1)
    while rest > 0:
        movable = [i for i in range(1, amount) if counts[i] < largest] or [i for i in range(1, amount) if counts[i] < limit]
        mass, left = sum([portions[i] for i in movable]), rest
        for i in movable:
            more = min(limit - counts[i], max(1, left * portions[i] // mass), rest)
            counts[i] = counts[i] + more
            rest = rest - more
    return np.array(counts)


def scatter_about(stream_key, dims, scale, reach, cuts=(), held_as=jnp.bfloat16):
    values = jax.random.normal(stream_key, dims, jnp.float32) * scale
    if len(cuts) > 0:
        values = shard_levels(stream_key, dims, cuts, -0.22, 0.18) * values
    return jnp.clip(values, min=-reach, max=reach).astype(held_as)


def setup_inputs(seed: int = 0) -> dict:
    key_list = jax.random.split(jax.random.key(seed), 24)
    words = scatter_about(key_list[0], (SEQS, L, D), 1.0, 6.0, ((0, 8),))
    word_extra = ragged(key_list[1], SEQS, SEQS * (L // 2), L - L // 8, 2).astype(jnp.int32)
    span_pos = set_ends(jax.random.randint(key_list[2], (SEQS, E), 0, L), jax.random.fold_in(key_list[2], 1), 0, L - 1).astype(jnp.int32)
    span_len = set_ends(jax.random.randint(key_list[3], (SEQS, E), 1, SPANW + 1), jax.random.fold_in(key_list[3], 1), 1, SPANW).astype(jnp.int32)
    entity_shard_keys = jax.random.split(jax.random.fold_in(key_list[4], 1), SEQS * E // (SEQ_DEV * E))
    entity_shard_turns = jax.random.permutation(jax.random.fold_in(key_list[4], 3), SEQS * E // (SEQ_DEV * E))
    entity_shard = jax.vmap(lambda own, number: assign_block(jax.random.fold_in(key_list[4], 2), own, number, SEQ_DEV * E, N_DP, 1, CAP, 2))(entity_shard_keys, entity_shard_turns).reshape((SEQS, E, 1))
    entity_row = set_ends(jax.random.randint(key_list[5], (SEQS, E), 0, ROWS_DEV), jax.random.fold_in(key_list[5], 1), 0, ROWS_DEV - 1).astype(jnp.int32)
    targets = draw_targets(jax.random.fold_in(key_list[23], 71), 0)
    table = scatter_about(key_list[7], (TABLE_ROWS, EDIM), 0.1875, 1.125, ((0, 8), (1, 4)))
    ent_proj = scatter_about(key_list[8], (EDIM, D), (max(1, EDIM // 28)) ** -0.5, 2.0, ((0, 4),))
    query_weight = scatter_about(key_list[9], (4, D, D), D ** -0.5, 0.21875, ((2, 4),))
    w_key = scatter_about(key_list[10], (D, D), D ** -0.5, 0.21875, ((1, 4),))
    w_value = scatter_about(key_list[11], (D, D), D ** -0.5, 0.21875, ((1, 4),))
    w_out = scatter_about(key_list[12], (D, D), (D // 32) ** -0.5, 1.25, ((0, 4),))
    gain_attn = jnp.clip(1.0 + 0.1 * jax.random.normal(key_list[13], (D,), jnp.float32), 0.5, 1.5)
    bias_attn = scatter_about(key_list[14], (D,), 0.5, 3.0, (), jnp.float32)
    w_up = scatter_about(key_list[15], (D, FF), D ** -0.5, 0.21875, ((1, 4),))
    w_down = scatter_about(key_list[16], (FF, D), FF ** -0.5, 0.109375, ((0, 4),))
    gain_ffn = jnp.clip(1.0 + 0.1 * jax.random.normal(key_list[17], (D,), jnp.float32), 0.5, 1.5)
    bias_ffn = scatter_about(key_list[18], (D,), 0.5, 3.0, (), jnp.float32)
    w_head = scatter_about(key_list[19], (D, EDIM), D ** -0.5, 0.21875)
    gain_head = jnp.clip(1.0 + 0.1 * jax.random.normal(key_list[20], (EDIM,), jnp.float32), 0.5, 1.5)
    cot_words = scatter_about(key_list[21], (SEQS, L, D), 1.0, 6.0, ((0, 8),))
    cot_ents = scatter_about(key_list[22], (SEQS, E, D), 1.0, 6.0, ((0, 8),))
    return dict(words=words, word_extra=word_extra, span_pos=span_pos, span_len=span_len, entity_shard=entity_shard, entity_row=entity_row, targets=targets, table=table, ent_proj=ent_proj, query_weight=query_weight, w_key=w_key, w_value=w_value, w_out=w_out, gain_attn=gain_attn, bias_attn=bias_attn, w_up=w_up, w_down=w_down, gain_ffn=gain_ffn, bias_ffn=bias_ffn, w_head=w_head, gain_head=gain_head, cot_words=cot_words, cot_ents=cot_ents)


EPSILON = 1e-05
MASKED_SCORE = -1000000000.0
HIGHEST_PRECISION = lax.Precision.HIGHEST

@jax.custom_vjp
def low(v):
    return lax.optimization_barrier(v.astype(jnp.bfloat16)).astype(jnp.float32)

@jax.custom_vjp
def low_back(v):
    return v

def low_keep(v):
    return (low(v), None)

def low_pass(kept, grad):
    return (grad,)

def back_keep(v):
    return (v, None)

def back_low(kept, grad):
    return (low(grad),)
low.defvjp(low_keep, low_pass)
low_back.defvjp(back_keep, back_low)

def matmul(first_op, second_op):
    return jnp.dot(first_op, second_op, precision=HIGHEST_PRECISION)

def contract_product(form, first_op, second_op):
    return jnp.einsum(form, first_op, second_op, precision=HIGHEST_PRECISION)

def layer_norm(source, gain_vec, shift_vec):
    center = source - lax.optimization_barrier(jnp.mean(source, axis=-1, keepdims=True))
    inv_scale = lax.rsqrt(lax.optimization_barrier(jnp.mean(center * center, axis=-1, keepdims=True)) + EPSILON)
    return center * inv_scale * gain_vec + shift_vec

def split_heads(source):
    return source.reshape(L + E, H, DH)

def reference(words, word_extra, span_pos, span_len, entity_shard, entity_row, targets, table, ent_proj, query_weight, w_key, w_value, w_out, gain_attn, bias_attn, w_up, w_down, gain_ffn, bias_ffn, w_head, gain_head, cot_words, cot_ents):
    word_count = L // 8 + word_extra
    span_start = span_pos * (word_count[:, None] - SPANW) // L
    positions = jnp.arange(L, dtype=jnp.int32)
    inside = ((positions[None, None, :] >= span_start[..., None]) & (positions[None, None, :] < (span_start + span_len)[..., None])).astype(jnp.float32)
    span_width = span_len.astype(jnp.float32)[..., None]
    key_valid = jnp.concatenate([positions[None, :] < word_count[:, None], jnp.ones((SEQS, E), dtype=bool)], axis=1)
    ent_ids = (entity_shard[..., 0] * ROWS_DEV + entity_row).astype(jnp.int32)
    flat_targets = targets.reshape(-1).astype(jnp.int32)
    params = tuple((item.astype(jnp.float32) for item in (words, table, ent_proj, query_weight, w_key, w_value, w_out, gain_attn, bias_attn, w_up, w_down, gain_ffn, bias_ffn, w_head, gain_head)))

    def forward(words32, table32, proj32, query32, key32, value32, out32, gain_one, bias_one, up32, down32, gain_two, bias_two, head32, head_gain):
        vectors = low_back(table32[ent_ids])

        def one_sequence(inputs):
            word_s, vec_s, inside_s, width_s, valid_s = inputs
            ent_rows = low(low_back(matmul(vec_s, proj32) + matmul(inside_s, word_s) / width_s))
            stream = jnp.concatenate([word_s, ent_rows], axis=0)

            def project(source, weight):
                return low(low_back(matmul(source, weight)))
            to_words = jnp.concatenate([project(word_s, query32[0]), project(ent_rows, query32[2])], axis=0)
            to_ents = jnp.concatenate([project(word_s, query32[1]), project(ent_rows, query32[3])], axis=0)
            key_rows = split_heads(project(stream, key32))
            value_rows = split_heads(project(stream, value32))
            word_part = contract_product('qhc,khc->hqk', split_heads(to_words), key_rows[:L])
            ent_part = contract_product('qhc,khc->hqk', split_heads(to_ents), key_rows[L:])
            scores = jnp.concatenate([word_part, ent_part], axis=-1) * 0.125
            scores = low_back(jnp.where(valid_s[None, None, :], scores, MASKED_SCORE))
            prob_rows = low(jax.nn.softmax(scores, axis=-1))
            context = contract_product('hqk,khc->qhc', prob_rows, value_rows).reshape(L + E, D)
            context = low(low_back(context))
            attn_term = low_back(matmul(context, out32))
            first_norm = layer_norm(stream + attn_term, gain_one, bias_one)
            pre_act = low_back(matmul(low(first_norm), up32))
            hidden = low(jax.nn.gelu(pre_act, approximate=False))
            ffn_term = low_back(matmul(hidden, down32))
            return layer_norm(first_norm + ffn_term, gain_two, bias_two)
        outputs = lax.map(jax.checkpoint(one_sequence), (words32, vectors, inside, span_width, key_valid))
        head_in = low(outputs[:, L:L + MSEQ].reshape(MASKED, D))
        head_pre = low_back(matmul(head_in, head32))
        head_vec = low(layer_norm(jax.nn.gelu(head_pre, approximate=False), head_gain, 0.0))
        target_logit = lax.optimization_barrier(jnp.sum(head_vec * table32[flat_targets], axis=-1))

        def table_step(running, table_block):
            run_top, run_total = running
            logits = low_back(contract_product('md,rd->mr', head_vec, table_block))
            new_top = jnp.maximum(run_top, lax.optimization_barrier(jnp.max(logits, axis=1)))
            run_total = run_total * jnp.exp(run_top - new_top) + lax.optimization_barrier(jnp.sum(jnp.exp(logits - new_top[:, None]), axis=1))
            return ((new_top, run_total), None)
        start_state = (jnp.full((MASKED,), -1e+30, jnp.float32), jnp.zeros((MASKED,), jnp.float32))
        (run_top, run_total), _ = lax.scan(jax.checkpoint(table_step), start_state, table32.reshape(N_DP, ROWS_DEV, EDIM))
        entropy = run_top + jnp.log(run_total) - target_logit
        return (outputs, entropy)
    (outputs, entropy), backward_fn = jax.vjp(forward, *params)
    cotangent = jnp.concatenate([cot_words, cot_ents], axis=1).astype(jnp.float32)
    gradients = backward_fn((cotangent, jnp.ones((MASKED,), jnp.float32)))
    out_low = outputs.astype(jnp.bfloat16)
    return (out_low[:, :L], out_low[:, L:], entropy, gradients[0], gradients[1], gradients[2], gradients[3], gradients[4], gradients[5], gradients[6], gradients[7], gradients[8], gradients[9], gradients[10], gradients[11], gradients[12], gradients[13], gradients[14])
```

```python
import functools
import math

import jax
import jax.numpy as jnp
from jax import lax
from jax.experimental import pallas as pl
from jax.experimental.pallas import tpu as pltpu
from jax.sharding import PartitionSpec as P

DH = 64
SPANW = 4
EPSILON = 1e-05
MASKED_SCORE = -1000000000.0
LANES = 128
BF = jnp.bfloat16
F32 = jnp.float32
MESH = pl.DeviceIdType.MESH
VM = pl.BlockSpec(memory_space=pltpu.VMEM)


def matmul(first_op, second_op):
    return jnp.dot(first_op, second_op, preferred_element_type=F32)


def contract_product(form, first_op, second_op):
    return jnp.einsum(form, first_op, second_op, preferred_element_type=F32)


def normalize(source, gain_vec, shift_vec):
    center = source - jnp.mean(source, axis=-1, keepdims=True)
    inv_scale = lax.rsqrt(jnp.mean(center * center, axis=-1, keepdims=True) + EPSILON)
    return center * inv_scale * gain_vec + shift_vec


def gelu_exact(source):
    return jax.nn.gelu(source, approximate=False)


def head_map(head_pre, gain_vec):
    return normalize(gelu_exact(head_pre), gain_vec, 0.0)


def remote(src, dst, send, recv, axis, peer):
    return pltpu.make_async_remote_copy(
        src_ref=src, dst_ref=dst, send_sem=send, recv_sem=recv,
        device_id={axis: peer}, device_id_type=MESH,
    )


def exchange_kernel(axis, n, kinds, *refs):
    k = len(kinds)
    ins, outs, (send_sems, recv_sems, own_sems) = refs[:k], refs[k:2 * k], refs[2 * k:]
    me = lax.axis_index(axis)
    barrier = pltpu.get_barrier_semaphore()

    def greet(step, carry):
        pl.semaphore_signal(
            barrier, inc=1, device_id={axis: lax.rem(me + step, n)}, device_id_type=MESH
        )
        return carry

    lax.fori_loop(1, n, greet, 0)
    own = []
    for i, kind in enumerate(kinds):
        src = ins[i].at[me] if kind == "a2a" else ins[i]
        own.append(pltpu.make_async_copy(src, outs[i].at[me], own_sems.at[i]))
        own[-1].start()
    pl.semaphore_wait(barrier, n - 1)

    def copies(step):
        peer = lax.rem(me + step, n)
        return [
            remote(
                ins[i].at[peer] if kind == "a2a" else ins[i], outs[i].at[me],
                send_sems.at[i, step - 1], recv_sems.at[i, step - 1], axis, peer,
            )
            for i, kind in enumerate(kinds)
        ]

    def begin(step, carry):
        for copy in copies(step):
            copy.start()
        return carry

    lax.fori_loop(1, n, begin, 0)

    def finish(step, carry):
        source = lax.rem(me + n - step, n)
        for i, kind in enumerate(kinds):
            remote(
                ins[i].at[source] if kind == "a2a" else ins[i], outs[i].at[source],
                send_sems.at[i, step - 1], recv_sems.at[i, step - 1], axis, source,
            ).wait()
        return carry

    lax.fori_loop(1, n, finish, 0)
    for copy in own:
        copy.wait()


def exchange(axis, collective, arrays):
    n = lax.axis_size(axis)
    kinds = tuple(kind for kind, _ in arrays)
    values = [value for _, value in arrays]
    shapes = [
        jax.ShapeDtypeStruct(value.shape if kind == "a2a" else (n,) + value.shape, value.dtype)
        for kind, value in arrays
    ]
    k = len(values)
    return pl.pallas_call(
        functools.partial(exchange_kernel, axis, n, kinds),
        out_shape=shapes,
        in_specs=[VM] * k,
        out_specs=[VM] * k,
        scratch_shapes=[
            pltpu.SemaphoreType.DMA((k, n - 1)),
            pltpu.SemaphoreType.DMA((k, n - 1)),
            pltpu.SemaphoreType.DMA((k,)),
        ],
        compiler_params=pltpu.CompilerParams(collective_id=collective, has_side_effects=True),
    )(*values)


def sum_kernel(chunks, x_ref, o_ref, r1, s2, r2, send_sems, recv_sems):
    me = lax.axis_index("mp")
    b0 = lax.rem(me, 2)
    b1 = me // 2
    p1 = me + 1 - 2 * b0
    p2 = lax.rem(me + 2, 4)
    half = r1.shape[1]
    quarter = half // 2
    barrier = pltpu.get_barrier_semaphore()
    for peer in (p1, p2):
        pl.semaphore_signal(barrier, inc=1, device_id={"mp": peer}, device_id_type=MESH)
    pl.semaphore_wait(barrier, 2)

    def rows(c, h, q, count):
        return pl.ds(pl.multiple_of(c * 2 * half + h * half + q * quarter, 16), count)

    def first(c):
        return remote(
            x_ref.at[rows(c, 1 - b0, 0, half)], r1.at[c], send_sems.at[c, 0], recv_sems.at[c, 0],
            "mp", p1,
        )

    def second(c):
        return remote(s2.at[c], r2.at[c], send_sems.at[c, 1], recv_sems.at[c, 1], "mp", p2)

    def third(c, q):
        place = o_ref.at[rows(c, b0, q, quarter)]
        return remote(place, place, send_sems.at[c, 2], recv_sems.at[c, 2], "mp", p2)

    def fourth(c, h):
        place = o_ref.at[rows(c, h, b1, quarter)]
        return remote(place, place, send_sems.at[c, 3], recv_sems.at[c, 3], "mp", p1)

    def fifth(c, h):
        place = o_ref.at[rows(c, h, 1 - b1, quarter)]
        return remote(place, place, send_sems.at[c, 4], recv_sems.at[c, 4], "mp", p1)

    def part(c, q):
        mine = x_ref[rows(c, b0, q, quarter)].astype(F32)
        theirs = r1[c, pl.ds(pl.multiple_of(q * quarter, 16), quarter)].astype(F32)
        return mine + theirs

    for c in range(chunks):
        first(c).start()
    for c in range(chunks):
        first(c).wait_recv()
        s2[c] = part(c, 1 - b1).astype(BF)
        second(c).start()
    for c in range(chunks):
        own = part(c, b1)
        second(c).wait_recv()
        o_ref[rows(c, b0, b1, quarter)] = (own + r2[c].astype(F32)).astype(BF)
        third(c, b1).start()
        fourth(c, b0).start()
    for c in range(chunks):
        third(c, 1 - b1).wait_recv()
        fifth(c, b0).start()
    for c in range(chunks):
        fourth(c, 1 - b0).wait_recv()
        fifth(c, 1 - b0).wait_recv()
        first(c).wait_send()
        second(c).wait_send()
        third(c, b1).wait_send()
        fourth(c, b0).wait_send()
        fifth(c, b0).wait_send()


def sum_mp(part, collective, chunks=2):
    total, width = part.shape
    half = total // chunks // 2
    return pl.pallas_call(
        functools.partial(sum_kernel, chunks),
        out_shape=jax.ShapeDtypeStruct((total, width), BF),
        in_specs=[VM],
        out_specs=VM,
        scratch_shapes=[
            pltpu.VMEM((chunks, half, width), BF),
            pltpu.VMEM((chunks, half // 2, width), BF),
            pltpu.VMEM((chunks, half // 2, width), BF),
            pltpu.SemaphoreType.DMA((chunks, 5)),
            pltpu.SemaphoreType.DMA((chunks, 5)),
        ],
        compiler_params=pltpu.CompilerParams(collective_id=collective, has_side_effects=True),
    )(part.astype(BF))


def shards(
    words, word_extra, span_pos, span_len, entity_shard, entity_row, targets, table, ent_proj,
    query_weight, w_key, w_value, w_out, gain_attn, bias_attn, w_up, w_down, gain_ffn, bias_ffn,
    w_head, gain_head, cot_words, cot_ents,
):
    n_dp = lax.axis_size("dp")
    n_mp = lax.axis_size("mp")
    seq_count, word_length, model_width = words.shape
    ent_len = span_pos.shape[1]
    masked_len = targets.shape[1]
    tokens_len = word_length + ent_len
    rows_dev, cols_dev = table.shape
    local_width = w_key.shape[1]
    heads_local = local_width // DH
    ent_total = seq_count * ent_len
    table_full = lax.all_gather(table, "mp", axis=1, tiled=True)

    owners = entity_shard.reshape(ent_total)
    wanted = entity_row.reshape(ent_total)
    capacity = max(16, 2 * ent_total // n_dp)
    owner_onehot = (owners[:, None] == jnp.arange(n_dp, dtype=jnp.int32)[None, :]).astype(BF)
    order_index = jnp.arange(ent_total, dtype=jnp.int32)
    earlier = (order_index[:, None] > order_index[None, :]).astype(BF)
    before = matmul(earlier, owner_onehot)
    slot_rank = jnp.sum(before * owner_onehot.astype(F32), axis=1).astype(jnp.int32)
    place = owners * capacity + slot_rank
    placed = place[:, None] == jnp.arange(n_dp * capacity, dtype=jnp.int32)[None, :]
    requests = jnp.sum(jnp.where(placed, wanted[:, None] + 1, 0), axis=0) - 1
    requests = jnp.pad(requests.reshape(n_dp, 1, capacity), ((0, 0), (0, 7), (0, LANES - capacity)))
    (received,) = exchange("dp", 0, [("a2a", requests)])
    received = received[:, 0, :capacity]
    present = received >= 0
    picked = jnp.take(table, jnp.maximum(received, 0), axis=0)
    picked = jnp.where(present[..., None], picked, jnp.zeros_like(picked))
    (back_rows,) = exchange("dp", 1, [("a2a", picked)])
    placed_low = placed.astype(BF)
    vec_cols = matmul(placed_low, back_rows.reshape(n_dp * capacity, cols_dev)).astype(BF)
    vec_all, proj_all = exchange("mp", 2, [("ag", vec_cols), ("ag", ent_proj)])
    ent_vectors = contract_product("mtc,mcd->td", vec_all, proj_all)

    word_count = word_length // 8 + word_extra
    span_start = span_pos * (word_count[:, None] - SPANW) // word_length
    positions = jnp.arange(word_length, dtype=jnp.int32)
    inside = (positions[None, None, :] >= span_start[..., None]) & (
        positions[None, None, :] < (span_start + span_len)[..., None]
    )
    span_total = contract_product("sep,spd->sed", inside.astype(BF), words)
    span_width = span_len.astype(F32)[..., None]
    ent_low = (
        ent_vectors.reshape(seq_count, ent_len, model_width) + span_total / span_width
    ).astype(BF)
    stream = jnp.concatenate([words, ent_low], axis=1)
    word_query = contract_product("rpa,gay->grpy", words, query_weight[:2])
    q_ent = contract_product("sed,kdh->kseh", ent_low, query_weight[2:])
    to_words = jnp.concatenate([word_query[0], q_ent[0]], axis=1).astype(BF)
    to_ents = jnp.concatenate([word_query[1], q_ent[1]], axis=1).astype(BF)
    key_rows = contract_product("snd,dh->snh", stream, w_key).astype(BF)
    value_rows = contract_product("snd,dh->snh", stream, w_value).astype(BF)
    head_shape = (seq_count, tokens_len, heads_local, DH)
    words_heads = to_words.reshape(head_shape)
    ents_heads = to_ents.reshape(head_shape)
    keys_heads = key_rows.reshape(head_shape)
    values_heads = value_rows.reshape(head_shape)
    key_valid = jnp.concatenate(
        [positions[None, :] < word_count[:, None], jnp.ones((seq_count, ent_len), dtype=bool)],
        axis=1,
    )

    def score_rows():
        word_part = contract_product("sqhc,skhc->shqk", words_heads, keys_heads[:, :word_length])
        ent_part = contract_product("sqhc,skhc->shqk", ents_heads, keys_heads[:, word_length:])
        raw_scores = jnp.concatenate([word_part, ent_part], axis=-1) * 0.125
        return jnp.where(key_valid[:, None, None, :], raw_scores, MASKED_SCORE)

    scores = score_rows()
    row_max = jnp.max(scores, axis=-1, keepdims=True)
    log_total = row_max + jnp.log(jnp.sum(jnp.exp(scores - row_max), axis=-1, keepdims=True))
    prob_low = jnp.exp(scores - log_total).astype(BF)
    context = (
        contract_product("shqk,skhc->sqhc", prob_low, values_heads)
        .reshape(seq_count * tokens_len, local_width)
        .astype(BF)
    )
    attn_sum = sum_mp(matmul(context, w_out), 3).astype(F32)
    pre_first = stream.reshape(seq_count * tokens_len, model_width).astype(F32) + attn_sum
    first_norm, first_back = jax.vjp(normalize, pre_first, gain_attn, bias_attn)
    first_low = first_norm.astype(BF)
    pre_act = matmul(first_low, w_up)
    hidden_f, gelu_back = jax.vjp(gelu_exact, pre_act)
    hidden = hidden_f.astype(BF)
    ffn_sum = sum_mp(matmul(hidden, w_down), 4).astype(F32)
    pre_second = first_norm + ffn_sum
    output, second_back = jax.vjp(normalize, pre_second, gain_ffn, bias_ffn)
    out_low = output.astype(BF).reshape(seq_count, tokens_len, model_width)
    out_words = out_low[:, :word_length]
    out_ents = out_low[:, word_length:]
    head_in = out_low[:, word_length : word_length + masked_len].reshape(
        seq_count * masked_len, model_width
    )
    head_pre = matmul(head_in, w_head)
    head_vec, head_back = jax.vjp(head_map, head_pre, gain_head)
    (all_head,) = exchange("dp", 5, [("ag", head_vec.astype(BF))])
    mine_total = head_vec.shape[0]
    masked_total = n_dp * mine_total
    ent_width = table_full.shape[1]
    all_head = all_head.reshape(masked_total, ent_width)
    row_offset = lax.axis_index("dp") * rows_dev
    local_target = targets.reshape(-1) - row_offset
    is_mine = (local_target >= 0) & (local_target < rows_dev)
    target_index = jnp.clip(local_target, 0, rows_dev - 1)
    target_rows = jnp.where(
        is_mine[:, None], jnp.take(table_full, target_index, axis=0), jnp.zeros((), BF)
    )
    target_logit = jnp.sum(all_head.astype(F32) * target_rows.astype(F32), axis=-1)
    block_rows = math.gcd(masked_total, 256)
    block_count = masked_total // block_rows
    head_blocks = all_head.reshape(block_count, block_rows, ent_width)

    def logits_of(head_block):
        return contract_product("md,rd->mr", head_block, table_full)

    def block_part(head_block):
        logits = logits_of(head_block)
        row_top = jnp.max(logits, axis=1)
        weights = jnp.exp(logits - row_top[:, None])
        return row_top, jnp.sum(weights, axis=1), matmul(weights.astype(BF), table_full)

    if block_count == 1:
        parts = [a[None] for a in block_part(head_blocks[0])]
    else:
        parts = lax.map(block_part, head_blocks)
    part_top, part_total = parts[0].reshape(masked_total), parts[1].reshape(masked_total)
    stats = jnp.zeros((8, masked_total), F32)
    stats = stats.at[0].set(part_top).at[1].set(part_total).at[2].set(target_logit)
    all_stats, all_parts, all_rows = exchange(
        "dp", 6,
        [
            ("ag", stats),
            ("a2a", parts[2].reshape(n_dp, mine_total, ent_width)),
            ("a2a", target_rows.reshape(n_dp, mine_total, ent_width)),
        ],
    )
    global_top = jnp.max(all_stats[:, 0], axis=0)
    shrink = jnp.exp(all_stats[:, 0] - global_top)
    global_total = jnp.sum(shrink * all_stats[:, 1], axis=0)
    head_total = global_top + jnp.log(global_total)
    loss = head_total - jnp.sum(all_stats[:, 2], axis=0)
    weight_all = shrink / global_total
    my_slots = lax.axis_index("dp") * mine_total
    my_weight = lax.dynamic_slice_in_dim(weight_all, my_slots, mine_total, 1)
    grad_head_mine = jnp.sum(
        all_parts * my_weight[..., None] - all_rows.astype(F32), axis=0
    )
    my_cols = lax.dynamic_slice_in_dim(all_head, lax.axis_index("mp") * cols_dev, cols_dev, 1)

    def block_back(running, inputs):
        head_block, col_block, total_block = inputs
        weight_low = jnp.exp(logits_of(head_block) - total_block[:, None]).astype(BF)
        return running + contract_product("mr,mc->rc", weight_low, col_block), None

    d_head_pre, grad_gain_head = head_back(grad_head_mine)
    d_head_low = d_head_pre.astype(BF)
    grad_head = contract_product("md,me->de", head_in, d_head_low)
    d_head_in = contract_product("me,de->md", d_head_low, w_head)
    d_output = jnp.concatenate([cot_words, cot_ents], axis=1).astype(F32)
    d_output = d_output.at[:, word_length : word_length + masked_len].add(
        d_head_in.reshape(seq_count, masked_len, model_width)
    )
    d_output = d_output.reshape(seq_count * tokens_len, model_width)
    d_second, grad_gain_ffn, grad_bias_ffn = second_back(d_output)
    d_ffn = d_second.astype(BF)
    grad_down = contract_product("tf,td->fd", hidden, d_ffn)
    d_hidden = contract_product("td,fd->tf", d_ffn, w_down)
    d_pre_act = gelu_back(d_hidden)[0].astype(BF)
    grad_up = contract_product("td,tf->df", first_low, d_pre_act)
    early = lax.psum(
        (grad_down.astype(BF), grad_up.astype(BF), grad_head.astype(BF)), "dp"
    )
    d_first = d_second + sum_mp(contract_product("tf,df->td", d_pre_act, w_up), 7).astype(F32)
    d_pre_first, grad_gain_attn, grad_bias_attn = first_back(d_first)
    d_attn = d_pre_first.astype(BF)
    grad_out = contract_product("th,td->hd", context, d_attn)
    d_context = contract_product("td,hd->th", d_attn, w_out).astype(BF).reshape(head_shape)
    prob_rows = jnp.exp(score_rows() - log_total)
    prob_again = prob_rows.astype(BF)
    d_probs = contract_product("sqhc,skhc->shqk", d_context, values_heads)
    d_values = (
        contract_product("shqk,sqhc->skhc", prob_again, d_context)
        .astype(BF)
        .reshape(seq_count, tokens_len, local_width)
    )
    d_scores = (
        prob_rows * (d_probs - jnp.sum(prob_rows * d_probs, axis=-1, keepdims=True))
    ).astype(BF)

    def bound(form, first_op, second_op):
        return (
            (contract_product(form, first_op, second_op) * 0.125)
            .astype(BF)
            .reshape(seq_count, -1, local_width)
        )

    d_score_words, d_score_ents = d_scores[..., :word_length], d_scores[..., word_length:]
    d_to_words = bound("shqk,skhc->sqhc", d_score_words, keys_heads[:, :word_length])
    d_to_ents = bound("shqk,skhc->sqhc", d_score_ents, keys_heads[:, word_length:])
    d_keys = jnp.concatenate(
        [
            bound("shqk,sqhc->skhc", d_score_words, words_heads),
            bound("shqk,sqhc->skhc", d_score_ents, ents_heads),
        ],
        axis=1,
    )
    grad_query = jnp.stack(
        [
            contract_product("yir,yiq->rq", words, d_to_words[:, :word_length]),
            contract_product("yir,yiq->rq", words, d_to_ents[:, :word_length]),
            contract_product("sed,seh->dh", ent_low, d_to_words[:, word_length:]),
            contract_product("sed,seh->dh", ent_low, d_to_ents[:, word_length:]),
        ]
    )
    grad_key = contract_product("snd,snh->dh", stream, d_keys)
    grad_value = contract_product("snd,snh->dh", stream, d_values)
    d_stream_word = contract_product(
        "vcr,er->vce", d_to_words[:, :word_length], query_weight[0]
    ) + contract_product("vcr,er->vce", d_to_ents[:, :word_length], query_weight[1])
    d_stream_ent = contract_product(
        "seh,dh->sed", d_to_words[:, word_length:], query_weight[2]
    ) + contract_product("seh,dh->sed", d_to_ents[:, word_length:], query_weight[3])
    d_stream = (
        jnp.concatenate([d_stream_word, d_stream_ent], axis=1)
        + contract_product("snh,dh->snd", d_keys, w_key)
        + contract_product("snh,dh->snd", d_values, w_value)
    )
    d_stream_sum = sum_mp(d_stream.reshape(seq_count * tokens_len, model_width), 8).astype(F32)
    d_total = (d_pre_first + d_stream_sum).reshape(seq_count, tokens_len, model_width)
    d_ent = d_total[:, word_length:].astype(BF)
    grad_words = d_total[:, :word_length] + contract_product(
        "sep,sed->spd", inside.astype(BF), (d_ent.astype(F32) / span_width).astype(BF)
    )
    d_ent_flat = d_ent.reshape(ent_total, model_width)
    grad_ent_proj = contract_product("tc,td->cd", vec_cols, d_ent_flat)
    d_vec = contract_product("td,cd->tc", d_ent_flat, ent_proj).astype(BF)
    outbox = contract_product("tp,tc->pc", placed_low, d_vec).astype(BF)
    (inbox,) = exchange("dp", 9, [("a2a", outbox.reshape(n_dp, capacity, cols_dev))])

    table_grad, _ = lax.scan(
        block_back,
        jnp.zeros((rows_dev, cols_dev), F32),
        (
            head_blocks,
            my_cols.reshape(block_count, block_rows, cols_dev),
            head_total.reshape(block_count, block_rows),
        ),
    )
    row_index = jnp.arange(rows_dev, dtype=jnp.int32)
    hit = jnp.concatenate([received.reshape(-1), jnp.where(is_mine, local_target, -1)])
    hit_rows = jnp.concatenate([inbox.reshape(-1, cols_dev), -my_cols])
    table_grad = table_grad + contract_product(
        "tr,tc->rc", (hit[:, None] == row_index[None, :]).astype(BF), hit_rows
    )
    late, early = lax.optimization_barrier(
        (
            (
                grad_query.astype(BF), grad_key.astype(BF), grad_value.astype(BF),
                grad_out.astype(BF), grad_ent_proj.astype(BF),
            ),
            early,
        )
    )
    late = lax.psum(late, "dp")
    small = lax.psum(
        (grad_gain_attn, grad_bias_attn, grad_gain_ffn, grad_bias_ffn, grad_gain_head), "dp"
    )
    grad_down, grad_up, grad_head = (a.astype(F32) for a in early)
    grad_query, grad_key, grad_value, grad_out, grad_ent_proj = (a.astype(F32) for a in late)
    grad_gain_attn, grad_bias_attn, grad_gain_ffn, grad_bias_ffn, grad_gain_head = small
    return (
        out_words, out_ents, loss, grad_words, table_grad, grad_ent_proj, grad_query, grad_key,
        grad_value, grad_out, grad_gain_attn, grad_bias_attn, grad_up, grad_down, grad_gain_ffn,
        grad_bias_ffn, grad_head, grad_gain_head,
    )


def solution(mesh):
    return jax.shard_map(
        shards,
        mesh=mesh,
        in_specs=(
            P("dp", None, None), P("dp"), P("dp", None), P("dp", None), P("dp", None, None),
            P("dp", None), P(), P("dp", "mp"), P("mp", None), P(None, None, "mp"), P(None, "mp"),
            P(None, "mp"), P("mp", None), P(), P(), P(None, "mp"), P("mp", None), P(), P(), P(),
            P(), P("dp", None, None), P("dp", None, None),
        ),
        out_specs=(
            P("dp", None, None), P("dp", None, None), P(), P("dp", None, None), P("dp", "mp"),
            P("mp", None), P(None, None, "mp"), P(None, "mp"), P(None, "mp"), P("mp", None), P(),
            P(), P(None, "mp"), P("mp", None), P(), P(), P(), P(),
        ),
        check_vma=False,
    )
```

```python
import functools
import math

import jax
import jax.numpy as jnp
from jax import lax
from jax.experimental import pallas as pl
from jax.experimental.pallas import tpu as pltpu
from jax.sharding import PartitionSpec as P

DH = 64
SPANW = 4
EPSILON = 1e-05
MASKED_SCORE = -1000000000.0
LANES = 128
BF = jnp.bfloat16
F32 = jnp.float32
MESH = pl.DeviceIdType.MESH
VM = pl.BlockSpec(memory_space=pltpu.VMEM)


def matmul(first_op, second_op):
    return jnp.dot(first_op, second_op, preferred_element_type=F32)


def contract_product(form, first_op, second_op):
    return jnp.einsum(form, first_op, second_op, preferred_element_type=F32)


def normalize(source, gain_vec, shift_vec):
    center = source - jnp.mean(source, axis=-1, keepdims=True)
    inv_scale = lax.rsqrt(jnp.mean(center * center, axis=-1, keepdims=True) + EPSILON)
    return center * inv_scale * gain_vec + shift_vec


def gelu_exact(source):
    return jax.nn.gelu(source, approximate=False)


def head_map(head_pre, gain_vec):
    return normalize(gelu_exact(head_pre), gain_vec, 0.0)


def remote(src, dst, send, recv, axis, peer):
    return pltpu.make_async_remote_copy(
        src_ref=src, dst_ref=dst, send_sem=send, recv_sem=recv,
        device_id={axis: peer}, device_id_type=MESH,
    )


def exchange_kernel(axis, n, kinds, *refs):
    k = len(kinds)
    ins, outs, (send_sems, recv_sems, own_sems) = refs[:k], refs[k:2 * k], refs[2 * k:]
    me = lax.axis_index(axis)
    barrier = pltpu.get_barrier_semaphore()

    def greet(step, carry):
        pl.semaphore_signal(
            barrier, inc=1, device_id={axis: lax.rem(me + step, n)}, device_id_type=MESH
        )
        return carry

    lax.fori_loop(1, n, greet, 0)
    own = []
    for i, kind in enumerate(kinds):
        src = ins[i].at[me] if kind == "a2a" else ins[i]
        own.append(pltpu.make_async_copy(src, outs[i].at[me], own_sems.at[i]))
        own[-1].start()
    pl.semaphore_wait(barrier, n - 1)

    def copies(step):
        peer = lax.rem(me + step, n)
        return [
            remote(
                ins[i].at[peer] if kind == "a2a" else ins[i], outs[i].at[me],
                send_sems.at[i, step - 1], recv_sems.at[i, step - 1], axis, peer,
            )
            for i, kind in enumerate(kinds)
        ]

    def begin(step, carry):
        for copy in copies(step):
            copy.start()
        return carry

    lax.fori_loop(1, n, begin, 0)

    def finish(step, carry):
        source = lax.rem(me + n - step, n)
        for i, kind in enumerate(kinds):
            remote(
                ins[i].at[source] if kind == "a2a" else ins[i], outs[i].at[source],
                send_sems.at[i, step - 1], recv_sems.at[i, step - 1], axis, source,
            ).wait()
        return carry

    lax.fori_loop(1, n, finish, 0)
    for copy in own:
        copy.wait()


def exchange(axis, collective, arrays):
    n = lax.axis_size(axis)
    kinds = tuple(kind for kind, _ in arrays)
    values = [value for _, value in arrays]
    shapes = [
        jax.ShapeDtypeStruct(value.shape if kind == "a2a" else (n,) + value.shape, value.dtype)
        for kind, value in arrays
    ]
    k = len(values)
    return pl.pallas_call(
        functools.partial(exchange_kernel, axis, n, kinds),
        out_shape=shapes,
        in_specs=[VM] * k,
        out_specs=[VM] * k,
        scratch_shapes=[
            pltpu.SemaphoreType.DMA((k, n - 1)),
            pltpu.SemaphoreType.DMA((k, n - 1)),
            pltpu.SemaphoreType.DMA((k,)),
        ],
        compiler_params=pltpu.CompilerParams(collective_id=collective, has_side_effects=True),
    )(*values)


def contract(first_op, second_op, first_dim, second_dim):
    return lax.dot_general(
        first_op, second_op, (((first_dim,), (second_dim,)), ((), ())), preferred_element_type=F32
    )


def span(start, count):
    return pl.ds(pl.multiple_of(start, 16), count)


def each(count, step, body, unroll=1):
    def run(index, carry):
        body(pl.multiple_of(index * step, step))
        return carry

    lax.fori_loop(0, count // step, run, 0, unroll=unroll)


def sum8(value):
    return jnp.sum(value.reshape(value.shape[0] // 8, 8, value.shape[1]), axis=0)


class Quarters:
    def __init__(self, part, r1, s2, r2, full, send, recv):
        self.part, self.r1, self.s2, self.r2, self.full = part, r1, s2, r2, full
        self.send, self.recv = send, recv
        me = lax.axis_index("mp")
        self.b0, self.b1 = lax.rem(me, 2), me // 2
        self.p1, self.p2 = me + 1 - 2 * self.b0, lax.rem(me + 2, 4)
        self.length = part.shape[1]
        self.half = self.length // 2
        self.quarter = self.length // 4

    def copy(self, s, k, src, dst, peer):
        return remote(src, dst, self.send.at[s, k], self.recv.at[s, k], "mp", peer)

    def first(self, s):
        rows = span((1 - self.b0) * self.half, self.half)
        return self.copy(s, 0, self.part.at[s, rows], self.r1.at[s], self.p1)

    def second(self, s):
        return self.copy(s, 1, self.s2.at[s], self.r2.at[s], self.p2)

    def place(self, s, h, q):
        return self.full.at[span(s * self.length + h * self.half + q * self.quarter, self.quarter)]

    def third(self, s, q):
        return self.copy(s, 2, self.place(s, self.b0, q), self.place(s, self.b0, q), self.p2)

    def fourth(self, s, h):
        return self.copy(s, 3, self.place(s, h, self.b1), self.place(s, h, self.b1), self.p1)

    def fifth(self, s, h):
        q = 1 - self.b1
        return self.copy(s, 4, self.place(s, h, q), self.place(s, h, q), self.p1)

    def both(self, s, q, row):
        mine = self.part[s, span(self.b0 * self.half + q * self.quarter + row, 16)]
        return mine.astype(F32) + self.r1[s, span(q * self.quarter + row, 16)].astype(F32)

    def begin(self, s):
        self.first(s).start()

    def pass_on(self, s):
        self.first(s).wait_recv()

        def body(row):
            self.s2[s, span(row, 16)] = self.both(s, 1 - self.b1, row).astype(BF)

        each(self.quarter, 16, body)
        self.second(s).start()

    def wait_sum(self, s):
        self.second(s).wait_recv()

    def total(self, s, row):
        return self.both(s, self.b1, row) + self.r2[s, span(row, 16)].astype(F32)

    def own_row(self, s, row):
        return s * self.length + self.b0 * self.half + self.b1 * self.quarter + row

    def spread(self, s):
        self.third(s, self.b1).start()
        self.fourth(s, self.b0).start()

    def forward(self, s):
        self.third(s, 1 - self.b1).wait_recv()
        self.fifth(s, self.b0).start()

    def wait_full(self, s):
        self.fourth(s, 1 - self.b0).wait_recv()
        self.fifth(s, 1 - self.b0).wait_recv()

    def drain(self, s):
        self.first(s).wait_send()
        self.second(s).wait_send()
        self.third(s, self.b1).wait_send()
        self.fourth(s, self.b0).wait_send()
        self.fifth(s, self.b0).wait_send()


def scaled(center):
    return lax.rsqrt(jnp.mean(center * center, axis=-1, keepdims=True) + EPSILON)


def scores_of(qkv, sT, h, cols, word_length):
    k_cols = pl.ds(cols.start, word_length), pl.ds(cols.start + word_length, cols.size - word_length)
    sT[0:word_length] = contract(qkv[h, 128:192, k_cols[0]], qkv[h, 0:64, cols], 0, 0)
    sT[word_length:] = contract(qkv[h, 128:192, k_cols[1]], qkv[h, 64:128, cols], 0, 0)


def forward_kernel(
    sizes, stream, query_weight, w_key, w_value, mask, w_out, w_up, w_down, norms,
    qkv, lse, ctx, wt_words, wt_ents, center1, first_low, hidden, slope, center2, out,
    sT, pT, pre, first, part1, r11, s21, r21, part2, r12, s22, r22,
    send1, recv1, send2, recv2,
):
    seqs, length, word_length, heads = sizes
    width = stream.shape[1]
    units = w_up.shape[1]
    one = Quarters(part1, r11, s21, r21, first_low, send1, recv1)
    two = Quarters(part2, r12, s22, r22, center2, send2, recv2)
    barrier = pltpu.get_barrier_semaphore()
    for peer in (one.p1, one.p2):
        pl.semaphore_signal(barrier, inc=1, device_id={"mp": peer}, device_id_type=MESH)

    for target, first_query in ((wt_words, 0), (wt_ents, 2)):
        sources = (query_weight[first_query], query_weight[first_query + 1], w_key[...], w_value[...])
        for g, source in enumerate(sources):
            turned = jnp.transpose(source)
            for h in range(heads):
                target[h, g * DH : (g + 1) * DH] = turned[h * DH : (h + 1) * DH]

    def project(s):
        for weight, start, count in ((wt_words, 0, word_length), (wt_ents, word_length, length - word_length)):
            base = s * length + start
            for h in range(heads):
                value = contract(weight[h], stream[base : base + count], 1, 1)
                qkv[h, 0:128, base : base + count] = (value[0:128] * 0.125).astype(BF)
                qkv[h, 128:256, base : base + count] = value[128:256].astype(BF)

    def attend(s, h):
        cols = pl.ds(s * length, length)
        scores_of(qkv, sT, h, cols, word_length)

        def body(col):
            here = pl.ds(col, LANES)
            words = sT[0:word_length, here] + mask[s]
            ents = sT[word_length:, here]
            top = jnp.maximum(
                jnp.max(words, axis=0, keepdims=True), jnp.max(ents, axis=0, keepdims=True)
            )
            words = jnp.exp(words - top)
            ents = jnp.exp(ents - top)
            total = jnp.sum(words, axis=0, keepdims=True) + jnp.sum(ents, axis=0, keepdims=True)
            pT[0:word_length, here] = words.astype(BF)
            pT[word_length:, here] = ents.astype(BF)
            lse[h, 0:1, pl.ds(pl.multiple_of(s * length + col, LANES), LANES)] = top + jnp.log(total)
            lse[h, 1:2, pl.ds(pl.multiple_of(s * length + col, LANES), LANES)] = 1.0 / total

        each(length, LANES, body)
        value = matmul(qkv[h, 192:256, cols], pT[...]) * lse[h, 1:2, cols]
        ctx[h * DH : (h + 1) * DH, cols] = value.astype(BF)

    def attention_part(s):
        value = contract(ctx[:, s * length : (s + 1) * length], w_out[...], 0, 0)
        part1[s] = value.astype(BF)

    def first_rows(s):
        def body(row):
            at = one.own_row(s, row)
            value = stream[span(at, 16)].astype(F32) + one.total(s, row)
            center = value - jnp.mean(value, axis=-1, keepdims=True)
            mine = span(s * one.quarter + row, 16)
            center1[mine] = center
            normed = center * scaled(center) * norms[0:1] + norms[1:2]
            first[mine] = normed
            first_low[span(at, 16)] = normed.astype(BF)

        each(one.quarter, 16, body)

    def second_rows(s):
        def body(row):
            at = two.own_row(s, row)
            value = first[span(s * two.quarter + row, 16)] + two.total(s, row)
            center = value - jnp.mean(value, axis=-1, keepdims=True)
            center2[span(at, 16)] = center.astype(BF)

        each(two.quarter, 16, body)

    def feed(s):
        rows = slice(s * length, (s + 1) * length)
        tile = 256
        for j in range(units // tile):
            cols = slice(j * tile, (j + 1) * tile)
            pre[...] = matmul(first_low[rows], w_up[:, cols])

            def body(row):
                value = pre[pl.ds(row, 32)]
                bell = lax.erf(value * 0.7071067811865476) * 0.5 + 0.5
                at = span(s * length + row, 32)
                hidden[at, cols] = (value * bell).astype(BF)
                slope[at, cols] = (
                    bell + value * jnp.exp(value * value * -0.5) * 0.3989422804014327
                ).astype(BF)

            each(length, 32, body)
        for j in range(width // tile):
            cols = slice(j * tile, (j + 1) * tile)
            part2[s, :, cols] = matmul(hidden[rows], w_down[:, cols]).astype(BF)

    def output_rows(s):
        def body(row):
            at = span(s * length + row, 16)
            center = center2[at].astype(F32)
            out[at] = (center * scaled(center) * norms[2:3] + norms[3:4]).astype(BF)

        each(length, 16, body)

    project(0)
    for h in range(heads):
        attend(0, h)
    attention_part(0)
    pl.semaphore_wait(barrier, 2)
    one.begin(0)
    project(1)
    attend(1, 0)
    one.pass_on(0)
    for h in range(1, heads):
        attend(1, h)
    attention_part(1)
    one.begin(1)
    one.wait_sum(0)
    first_rows(0)
    one.spread(0)
    one.pass_on(1)
    one.forward(0)
    one.wait_full(0)
    feed(0)
    two.begin(0)
    one.wait_sum(1)
    first_rows(1)
    one.spread(1)
    two.pass_on(0)
    one.forward(1)
    one.wait_full(1)
    feed(1)
    two.begin(1)
    two.wait_sum(0)
    second_rows(0)
    two.spread(0)
    two.pass_on(1)
    two.forward(0)
    two.wait_full(0)
    output_rows(0)
    two.wait_sum(1)
    second_rows(1)
    two.spread(1)
    two.forward(1)
    two.wait_full(1)
    output_rows(1)
    for s in range(seqs):
        one.drain(s)
        two.drain(s)


def quarter_scratch(seqs, length, width):
    return [
        pltpu.VMEM((seqs, length, width), BF),
        pltpu.VMEM((seqs, length // 2, width), BF),
        pltpu.VMEM((seqs, length // 4, width), BF),
        pltpu.VMEM((seqs, length // 4, width), BF),
    ]


def forward_layer(sizes, stream, query_weight, w_key, w_value, mask, w_out, w_up, w_down, norms):
    seqs, length, word_length, heads = sizes
    tokens, width = stream.shape
    local = heads * DH
    units = w_up.shape[1]

    def like(*shape, dtype=BF):
        return jax.ShapeDtypeStruct(shape, dtype)

    outs = [
        like(heads, 4 * DH, tokens), like(heads, 8, tokens, dtype=F32), like(local, tokens),
        like(heads, 4 * DH, width), like(heads, 4 * DH, width), like(tokens // 4, width, dtype=F32),
        like(tokens, width), like(tokens, units), like(tokens, units), like(tokens, width),
        like(tokens, width),
    ]
    return pl.pallas_call(
        functools.partial(forward_kernel, sizes),
        out_shape=outs,
        in_specs=[VM] * 9,
        out_specs=[VM] * len(outs),
        scratch_shapes=[
            pltpu.VMEM((length, length), F32),
            pltpu.VMEM((length, length), BF),
            pltpu.VMEM((length, 256), F32),
            pltpu.VMEM((tokens // 4, width), F32),
            *quarter_scratch(seqs, length, width),
            *quarter_scratch(seqs, length, width),
            pltpu.SemaphoreType.DMA((seqs, 5)), pltpu.SemaphoreType.DMA((seqs, 5)),
            pltpu.SemaphoreType.DMA((seqs, 5)), pltpu.SemaphoreType.DMA((seqs, 5)),
        ],
        compiler_params=pltpu.CompilerParams(
            collective_id=3, has_side_effects=True, vmem_limit_bytes=56 * 2**20
        ),
    )(stream, query_weight, w_key, w_value, mask, w_out, w_up, w_down, norms)


class Job:
    def __init__(self, buf, out, arrivals, send, recv, n):
        self.buf, self.out, self.arrivals, self.send, self.recv = buf, out, arrivals, send, recv
        self.me = lax.axis_index("dp")
        self.bits, self.halvings = job_plan(buf.shape[0], n)

    def bit(self, k):
        return lax.rem(self.me // 2**k, 2)

    def peer(self, k):
        return self.me + (1 - 2 * self.bit(k)) * 2**k

    def offset(self, k):
        start = 0
        for i in range(k):
            start = start + self.bit(i) * (self.buf.shape[0] >> (i + 1))
        return start

    def copy(self, index, k, src, dst):
        return remote(src, dst, self.send.at[index], self.recv.at[index], "dp", self.peer(k))

    def steps(self):
        rows = self.buf.shape[0]
        size = rows
        for k in range(self.bits):
            keep = self.offset(min(k, self.halvings))
            away = keep
            if k < self.halvings:
                size //= 2
                away = keep + (1 - self.bit(k)) * size
                keep = keep + self.bit(k) * size
            arrived = self.arrivals[k]
            copy = self.copy(k, k, self.buf.at[span(away, size)], arrived)
            copy.start()
            yield
            copy.wait()
            last = k == self.bits - 1

            def body(row, keep=keep, arrived=arrived, last=last):
                at = span(keep + row, 16)
                value = self.buf[at].astype(F32) + arrived[span(row, 16)].astype(F32)
                (self.out if last else self.buf)[at] = value.astype(BF)

            each(size, 16, body)
        for k in reversed(range(self.halvings)):
            done = self.out.at[span(self.offset(k + 1), size)]
            copy = self.copy(self.bits + k, k, done, done)
            copy.start()
            yield
            copy.wait()
            size *= 2


def job_plan(rows, n):
    bits, halvings, size = n.bit_length() - 1, 0, rows
    while halvings < bits - 1 and (size // 2) % 16 == 0:
        size, halvings = size // 2, halvings + 1
    return bits, halvings


def job_scratch(rows, width, n):
    bits, halvings = job_plan(rows, n)
    return [pltpu.VMEM((rows, width), BF)] + [
        pltpu.VMEM((rows >> min(k + 1, halvings), width), BF) for k in range(bits)
    ]


def backward_kernel(sizes, n, *refs):
    seqs, length, word_length, heads = sizes
    refs = list(refs)

    def take(count):
        taken = refs[:count]
        del refs[:count]
        return taken

    (
        cot_words, cot_ents, d_head, head_grad, center2, slope, hidden, first_low, center1, ctx, qkv, lse,
        wt_words, wt_ents, stream, mask, w_out, w_up, w_down, norms,
    ) = take(20)
    down_out, up_out, head_out, *per_head_out = take(3 + heads)
    gw, small = take(2)
    sums, d_own, d_ffn, d_pre, wide, d_attn, d_first, dctx, sT, dpT, pT, dsT, dcat = take(13)
    part, r1, s2, r2 = take(4)
    send1, recv1, send2, recv2, job_send, job_recv = take(6)
    width = stream.shape[1]
    units = w_up.shape[1]
    bits = n.bit_length() - 1
    jobs = []
    for index, out in enumerate([down_out, up_out, head_out, *per_head_out]):
        buf, *arrivals = take(1 + bits)
        jobs.append(Job(buf, out, arrivals, job_send.at[index], job_recv.at[index], n))
    down_job, up_job, head_job, *per_head = jobs
    one = Quarters(part, r1, s2, r2, d_attn, send1, recv1)
    two = Quarters(part, r1, s2, r2, gw, send2, recv2)
    barrier = pltpu.get_barrier_semaphore()
    for peer in (one.p1, one.p2):
        pl.semaphore_signal(barrier, inc=1, device_id={"mp": peer}, device_id_type=MESH)
    for k in range(bits):
        pl.semaphore_signal(
            barrier, inc=1, device_id={"dp": down_job.peer(k)}, device_id_type=MESH
        )
    active = []

    def launch(job):
        active.append(job.steps())
        next(active[-1])

    def advance(rounds=1):
        for _ in range(rounds):
            for steps in list(active):
                if next(steps, 0) == 0:
                    active.remove(steps)

    sums[...] = jnp.zeros_like(sums)

    def second_back(s):
        start = one.own_row(0, 0)

        def rows_of(row, cot):
            at = span(s * length + row, 16)
            center = center2[at].astype(F32)
            inv = scaled(center)
            normed = center * inv
            sums[0] += cot * normed
            sums[1] += cot
            grad = cot * norms[2:3]
            value = inv * (
                grad
                - jnp.mean(grad, axis=-1, keepdims=True)
                - normed * jnp.mean(grad * normed, axis=-1, keepdims=True)
            )
            d_ffn[at] = value.astype(BF)

            @pl.when((row >= start) & (row < start + one.quarter))
            def keep():
                d_own[span(s * one.quarter + row - start, 16)] = value

        scored = d_head.shape[1]

        def word_rows(row):
            rows_of(row, cot_words[s, span(row, 16)].astype(F32))

        def scored_rows(row):
            rows_of(row + word_length, cot_ents[s, span(row, 16)].astype(F32) + d_head[s, span(row, 16)])

        def other_rows(row):
            row = row + scored
            rows_of(row + word_length, cot_ents[s, span(row, 16)].astype(F32))

        each(word_length, 16, word_rows)
        each(scored, 16, scored_rows)
        each(length - word_length - scored, 16, other_rows)

    def feed_back(s):
        rows = slice(s * length, (s + 1) * length)
        tile = 256
        for j in range(units // tile):
            cols = slice(j * tile, (j + 1) * tile)
            wide[...] = contract(d_ffn[rows], w_down[cols], 1, 1)

            def body(row):
                at = span(s * length + row, 32)
                d_pre[at, cols] = (wide[pl.ds(row, 32)] * slope[at, cols].astype(F32)).astype(BF)

            each(length, 32, body)
        for j in range(width // tile):
            cols = slice(j * tile, (j + 1) * tile)
            part[s, :, cols] = contract(d_pre[rows], w_up[cols], 1, 1).astype(BF)

    def first_back(s):
        def body(row):
            at = one.own_row(s, row)
            mine = span(s * one.quarter + row, 16)
            value = d_own[mine] + one.total(s, row)
            center = center1[mine]
            inv = scaled(center)
            normed = center * inv
            sums[2] += value * normed
            sums[3] += value
            grad = value * norms[0:1]
            value = inv * (
                grad
                - jnp.mean(grad, axis=-1, keepdims=True)
                - normed * jnp.mean(grad * normed, axis=-1, keepdims=True)
            )
            d_first[mine] = value
            d_attn[span(at, 16)] = value.astype(BF)

        each(one.quarter, 16, body)

    def context_back(s):
        cols = slice(s * length, (s + 1) * length)
        dctx[:, cols] = contract(w_out[...], d_attn[cols], 1, 1).astype(BF)

    def attend_back(s, h):
        cols = pl.ds(s * length, length)
        w_cols = pl.ds(s * length, word_length)
        e_cols = pl.ds(s * length + word_length, length - word_length)
        mine = slice(h * DH, (h + 1) * DH)
        scores_of(qkv, sT, h, cols, word_length)
        dpT[...] = contract(qkv[h, 192:256, cols], dctx[mine, cols], 0, 0)

        def body(col):
            here = pl.ds(col, LANES)
            at = pl.ds(pl.multiple_of(s * length + col, LANES), LANES)
            delta = jnp.sum(
                ctx[mine, at].astype(F32) * dctx[mine, at].astype(F32), axis=0, keepdims=True
            )
            log_total = lse[h, 0:1, at]
            probs = jnp.exp(sT[0:word_length, here] + mask[s] - log_total)
            pT[0:word_length, here] = probs.astype(BF)
            dsT[0:word_length, here] = (probs * (dpT[0:word_length, here] - delta)).astype(BF)
            probs = jnp.exp(sT[word_length:, here] - log_total)
            pT[word_length:, here] = probs.astype(BF)
            dsT[word_length:, here] = (probs * (dpT[word_length:, here] - delta)).astype(BF)

        each(length, LANES, body)
        d_words, d_ents = dsT[0:word_length], dsT[word_length:]
        dcat[h, 0:64, cols] = (contract(qkv[h, 128:192, w_cols], d_words, 1, 0) * 0.125).astype(BF)
        dcat[h, 64:128, cols] = (contract(qkv[h, 128:192, e_cols], d_ents, 1, 0) * 0.125).astype(BF)
        dcat[h, 128:192, w_cols] = contract(qkv[h, 0:64, cols], d_words, 1, 1).astype(BF)
        dcat[h, 128:192, e_cols] = contract(qkv[h, 64:128, cols], d_ents, 1, 1).astype(BF)
        dcat[h, 192:256, cols] = contract(dctx[mine, cols], pT[...], 1, 1).astype(BF)

    def head_grads(h):
        buf = per_head[h].buf
        from_words, from_ents = None, None
        for s in range(seqs):
            middle, start, end = s * length + word_length, s * length, (s + 1) * length
            words = matmul(dcat[h, :, start:middle], stream[start:middle])
            ents = matmul(dcat[h, :, middle:end], stream[middle:end])
            from_words = words if s == 0 else from_words + words
            from_ents = ents if s == 0 else from_ents + ents
        buf[0:128] = from_words[0:128].astype(BF)
        buf[128:256] = (from_words[128:256] + from_ents[128:256]).astype(BF)
        buf[256:384] = from_ents[0:128].astype(BF)
        buf[384:448] = matmul(ctx[h * DH : (h + 1) * DH], d_attn[...]).astype(BF)

    def stream_part(s):
        for start in range(0, length, LANES):
            weight = wt_words if start < word_length else wt_ents
            cols = slice(s * length + start, s * length + start + LANES)
            value = contract(dcat[0, :, cols], weight[0], 0, 0)
            for h in range(1, heads):
                value = value + contract(dcat[h, :, cols], weight[h], 0, 0)
            part[s, start : start + LANES] = value.astype(BF)

    def last_rows(s):
        def body(row):
            at = two.own_row(s, row)
            value = d_first[span(s * two.quarter + row, 16)] + two.total(s, row)
            gw[span(at, 16)] = value.astype(BF)

        each(two.quarter, 16, body)

    def tile_grads(job, left, right):
        tile = 256
        for j in range(left.shape[1] // tile):
            cols = slice(j * tile, (j + 1) * tile)
            job.buf[cols] = contract(left[:, cols], right[...], 0, 0).astype(BF)

    head_job.buf[...] = head_grad[...]
    second_back(0)
    feed_back(0)
    pl.semaphore_wait(barrier, 2 + bits)
    one.begin(0)
    launch(head_job)
    second_back(1)
    one.pass_on(0)
    feed_back(1)
    one.begin(1)
    tile_grads(down_job, hidden, d_ffn)
    launch(down_job)
    one.wait_sum(0)
    first_back(0)
    one.spread(0)
    one.pass_on(1)
    tile_grads(up_job, first_low, d_pre)
    launch(up_job)
    one.forward(0)
    one.wait_sum(1)
    first_back(1)
    one.spread(1)
    advance()
    one.wait_full(0)
    context_back(0)
    attend_back(0, 0)
    one.forward(1)
    advance()
    one.wait_full(1)
    context_back(1)
    for s in range(seqs):
        one.drain(s)
    attend_back(1, 0)
    head_grads(0)
    advance()
    launch(per_head[0])
    for h in range(1, heads):
        attend_back(0, h)
        advance()
        attend_back(1, h)
        if h == heads - 1:
            for s in range(seqs):
                stream_part(s)
                two.begin(s)
        head_grads(h)
        advance()
        launch(per_head[h])
    two.pass_on(0)
    two.pass_on(1)
    advance()
    two.wait_sum(0)
    last_rows(0)
    two.spread(0)
    two.wait_sum(1)
    last_rows(1)
    two.spread(1)
    advance()
    two.forward(0)
    two.forward(1)
    for row in range(4):
        small[row : row + 1] = jnp.sum(sums[row], axis=0, keepdims=True)
    small[4:8] = jnp.zeros_like(small[4:8])
    advance()
    for s in range(seqs):
        two.wait_full(s)
        two.drain(s)
    while active:
        advance()


def backward_layer(sizes, n, arrays):
    seqs, length, word_length, heads = sizes
    stream, w_up = arrays[14], arrays[17]
    tokens, width = stream.shape
    units, local = w_up.shape[1], heads * DH
    head_width = arrays[3].shape[1]
    bits = n.bit_length() - 1
    job_shapes = [(units, width), (width, units), (width, head_width)] + [(7 * DH, width)] * heads
    outs = [jax.ShapeDtypeStruct(shape, BF) for shape in job_shapes + [(tokens, width)]]
    outs.append(jax.ShapeDtypeStruct((8, width), F32))
    scratch = [
        pltpu.VMEM((4, 16, width), F32), pltpu.VMEM((tokens // 4, width), F32),
        pltpu.VMEM((tokens, width), BF), pltpu.VMEM((tokens, units), BF),
        pltpu.VMEM((length, 256), F32), pltpu.VMEM((tokens, width), BF),
        pltpu.VMEM((tokens // 4, width), F32), pltpu.VMEM((local, tokens), BF),
        pltpu.VMEM((length, length), F32), pltpu.VMEM((length, length), F32),
        pltpu.VMEM((length, length), BF), pltpu.VMEM((length, length), BF),
        pltpu.VMEM((heads, 4 * DH, tokens), BF),
        *quarter_scratch(seqs, length, width),
        pltpu.SemaphoreType.DMA((seqs, 5)), pltpu.SemaphoreType.DMA((seqs, 5)),
        pltpu.SemaphoreType.DMA((seqs, 5)), pltpu.SemaphoreType.DMA((seqs, 5)),
        pltpu.SemaphoreType.DMA((len(job_shapes), 2 * bits)),
        pltpu.SemaphoreType.DMA((len(job_shapes), 2 * bits)),
    ]
    for rows, columns in job_shapes:
        scratch += job_scratch(rows, columns, n)
    return pl.pallas_call(
        functools.partial(backward_kernel, sizes, n),
        out_shape=outs,
        in_specs=[VM] * len(arrays),
        out_specs=[VM] * len(outs),
        scratch_shapes=scratch,
        compiler_params=pltpu.CompilerParams(
            collective_id=7, has_side_effects=True, vmem_limit_bytes=60 * 2**20
        ),
    )(*arrays)


def shards(
    words, word_extra, span_pos, span_len, entity_shard, entity_row, targets, table, ent_proj,
    query_weight, w_key, w_value, w_out, gain_attn, bias_attn, w_up, w_down, gain_ffn, bias_ffn,
    w_head, gain_head, cot_words, cot_ents,
):
    n_dp = lax.axis_size("dp")
    n_mp = lax.axis_size("mp")
    seq_count, word_length, model_width = words.shape
    ent_len = span_pos.shape[1]
    masked_len = targets.shape[1]
    tokens_len = word_length + ent_len
    rows_dev, cols_dev = table.shape
    local_width = w_key.shape[1]
    heads_local = local_width // DH
    ent_total = seq_count * ent_len
    table_full = lax.all_gather(table, "mp", axis=1, tiled=True)

    owners = entity_shard.reshape(ent_total)
    wanted = entity_row.reshape(ent_total)
    capacity = max(16, 2 * ent_total // n_dp)
    owner_onehot = (owners[:, None] == jnp.arange(n_dp, dtype=jnp.int32)[None, :]).astype(BF)
    order_index = jnp.arange(ent_total, dtype=jnp.int32)
    earlier = (order_index[:, None] > order_index[None, :]).astype(BF)
    before = matmul(earlier, owner_onehot)
    slot_rank = jnp.sum(before * owner_onehot.astype(F32), axis=1).astype(jnp.int32)
    place = owners * capacity + slot_rank
    placed = place[:, None] == jnp.arange(n_dp * capacity, dtype=jnp.int32)[None, :]
    requests = jnp.sum(jnp.where(placed, wanted[:, None] + 1, 0), axis=0) - 1
    requests = jnp.pad(requests.reshape(n_dp, 1, capacity), ((0, 0), (0, 7), (0, LANES - capacity)))
    (received,) = exchange("dp", 0, [("a2a", requests)])
    received = received[:, 0, :capacity]
    present = received >= 0
    picked = jnp.take(table, jnp.maximum(received, 0), axis=0)
    picked = jnp.where(present[..., None], picked, jnp.zeros_like(picked))
    (back_rows,) = exchange("dp", 1, [("a2a", picked)])
    placed_low = placed.astype(BF)
    vec_cols = matmul(placed_low, back_rows.reshape(n_dp * capacity, cols_dev)).astype(BF)
    vec_all, proj_all = exchange("mp", 2, [("ag", vec_cols), ("ag", ent_proj)])
    ent_vectors = contract_product("mtc,mcd->td", vec_all, proj_all)

    word_count = word_length // 8 + word_extra
    span_start = span_pos * (word_count[:, None] - SPANW) // word_length
    positions = jnp.arange(word_length, dtype=jnp.int32)
    inside = (positions[None, None, :] >= span_start[..., None]) & (
        positions[None, None, :] < (span_start + span_len)[..., None]
    )
    span_total = contract_product("sep,spd->sed", inside.astype(BF), words)
    span_width = span_len.astype(F32)[..., None]
    ent_low = (
        ent_vectors.reshape(seq_count, ent_len, model_width) + span_total / span_width
    ).astype(BF)
    stream = jnp.concatenate([words, ent_low], axis=1)
    key_valid = positions[None, :] < word_count[:, None]
    mask = jnp.broadcast_to(
        jnp.where(key_valid, 0.0, MASKED_SCORE)[..., None], (seq_count, word_length, LANES)
    )
    norms = jnp.stack([gain_attn, bias_attn, gain_ffn, bias_ffn])
    sizes = (seq_count, tokens_len, word_length, heads_local)
    qkv, lse, ctx, wt_words, wt_ents, center1, first_low, hidden, slope, center2, output = forward_layer(
        sizes, stream.reshape(seq_count * tokens_len, model_width), query_weight, w_key, w_value,
        mask, w_out, w_up, w_down, norms,
    )
    out_low = output.reshape(seq_count, tokens_len, model_width)
    out_words = out_low[:, :word_length]
    out_ents = out_low[:, word_length:]
    head_in = out_low[:, word_length : word_length + masked_len].reshape(
        seq_count * masked_len, model_width
    )
    head_pre = matmul(head_in, w_head)
    head_vec, head_back = jax.vjp(head_map, head_pre, gain_head)
    (all_head,) = exchange("dp", 5, [("ag", head_vec.astype(BF))])
    mine_total = head_vec.shape[0]
    masked_total = n_dp * mine_total
    ent_width = table_full.shape[1]
    all_head = all_head.reshape(masked_total, ent_width)
    row_offset = lax.axis_index("dp") * rows_dev
    local_target = targets.reshape(-1) - row_offset
    is_mine = (local_target >= 0) & (local_target < rows_dev)
    target_index = jnp.clip(local_target, 0, rows_dev - 1)
    target_rows = jnp.where(
        is_mine[:, None], jnp.take(table_full, target_index, axis=0), jnp.zeros((), BF)
    )
    target_logit = jnp.sum(all_head.astype(F32) * target_rows.astype(F32), axis=-1)
    block_rows = math.gcd(masked_total, 256)
    block_count = masked_total // block_rows
    head_blocks = all_head.reshape(block_count, block_rows, ent_width)

    def logits_of(head_block):
        return contract_product("md,rd->mr", head_block, table_full)

    def block_part(head_block):
        logits = logits_of(head_block)
        row_top = jnp.max(logits, axis=1)
        weights = jnp.exp(logits - row_top[:, None])
        return row_top, jnp.sum(weights, axis=1), matmul(weights.astype(BF), table_full)

    if block_count == 1:
        parts = [a[None] for a in block_part(head_blocks[0])]
    else:
        parts = lax.map(block_part, head_blocks)
    part_top, part_total = parts[0].reshape(masked_total), parts[1].reshape(masked_total)
    stats = jnp.zeros((8, masked_total), F32)
    stats = stats.at[0].set(part_top).at[1].set(part_total).at[2].set(target_logit)
    all_stats, all_parts, all_rows = exchange(
        "dp", 6,
        [
            ("ag", stats),
            ("a2a", parts[2].reshape(n_dp, mine_total, ent_width)),
            ("a2a", target_rows.reshape(n_dp, mine_total, ent_width)),
        ],
    )
    global_top = jnp.max(all_stats[:, 0], axis=0)
    shrink = jnp.exp(all_stats[:, 0] - global_top)
    global_total = jnp.sum(shrink * all_stats[:, 1], axis=0)
    head_total = global_top + jnp.log(global_total)
    loss = head_total - jnp.sum(all_stats[:, 2], axis=0)
    weight_all = shrink / global_total
    my_slots = lax.axis_index("dp") * mine_total
    my_weight = lax.dynamic_slice_in_dim(weight_all, my_slots, mine_total, 1)
    grad_head_mine = jnp.sum(
        all_parts * my_weight[..., None] - all_rows.astype(F32), axis=0
    )
    my_cols = lax.dynamic_slice_in_dim(all_head, lax.axis_index("mp") * cols_dev, cols_dev, 1)

    def block_back(running, inputs):
        head_block, col_block, total_block = inputs
        weight_low = jnp.exp(logits_of(head_block) - total_block[:, None]).astype(BF)
        return running + contract_product("mr,mc->rc", weight_low, col_block), None

    d_head_pre, grad_gain_head = head_back(grad_head_mine)
    d_head_low = d_head_pre.astype(BF)
    grad_head = contract_product("md,me->de", head_in, d_head_low)
    d_head_in = contract_product("me,de->md", d_head_low, w_head)
    *sums, d_total, small = backward_layer(
        sizes, n_dp,
        (
            cot_words, cot_ents, d_head_in.reshape(seq_count, masked_len, model_width),
            grad_head.astype(BF), center2, slope, hidden, first_low, center1, ctx, qkv, lse, wt_words,
            wt_ents, stream.reshape(seq_count * tokens_len, model_width), mask, w_out, w_up, w_down,
            norms,
        ),
    )
    grad_down, grad_up, grad_head, *per_head = (a.astype(F32) for a in sums)
    per_head = jnp.stack(per_head).reshape(heads_local, 7, DH, model_width)

    def columns_of(which):
        return per_head[:, which].transpose(2, 0, 1).reshape(model_width, local_width)

    grad_query = jnp.stack([columns_of(0), columns_of(1), columns_of(4), columns_of(5)])
    grad_key, grad_value = columns_of(2), columns_of(3)
    grad_out = per_head[:, 6].reshape(local_width, model_width)
    d_total = d_total.reshape(seq_count, tokens_len, model_width)
    d_ent = d_total[:, word_length:]
    grad_words = d_total[:, :word_length].astype(F32) + contract_product(
        "sep,sed->spd", inside.astype(BF), (d_ent.astype(F32) / span_width).astype(BF)
    )
    d_ent_flat = d_ent.reshape(ent_total, model_width)
    grad_ent_proj = contract_product("tc,td->cd", vec_cols, d_ent_flat)
    d_vec = contract_product("td,cd->tc", d_ent_flat, ent_proj).astype(BF)
    outbox = contract_product("tp,tc->pc", placed_low, d_vec).astype(BF)
    (inbox,) = exchange("dp", 9, [("a2a", outbox.reshape(n_dp, capacity, cols_dev))])

    table_grad, _ = lax.scan(
        block_back,
        jnp.zeros((rows_dev, cols_dev), F32),
        (
            head_blocks,
            my_cols.reshape(block_count, block_rows, cols_dev),
            head_total.reshape(block_count, block_rows),
        ),
    )
    row_index = jnp.arange(rows_dev, dtype=jnp.int32)
    hit = jnp.concatenate([received.reshape(-1), jnp.where(is_mine, local_target, -1)])
    hit_rows = jnp.concatenate([inbox.reshape(-1, cols_dev), -my_cols])
    table_grad = table_grad + contract_product(
        "tr,tc->rc", (hit[:, None] == row_index[None, :]).astype(BF), hit_rows
    )
    halves = lax.psum(small[2:4], "mp")
    grad_gain_ffn, grad_bias_ffn, grad_gain_attn, grad_bias_attn, grad_gain_head, grad_ent_proj = lax.psum(
        (small[0], small[1], halves[0], halves[1], grad_gain_head, grad_ent_proj), "dp"
    )
    return (
        out_words, out_ents, loss, grad_words, table_grad, grad_ent_proj, grad_query, grad_key,
        grad_value, grad_out, grad_gain_attn, grad_bias_attn, grad_up, grad_down, grad_gain_ffn,
        grad_bias_ffn, grad_head, grad_gain_head,
    )


def solution(mesh):
    return jax.shard_map(
        shards,
        mesh=mesh,
        in_specs=(
            P("dp", None, None), P("dp"), P("dp", None), P("dp", None), P("dp", None, None),
            P("dp", None), P(), P("dp", "mp"), P("mp", None), P(None, None, "mp"), P(None, "mp"),
            P(None, "mp"), P("mp", None), P(), P(), P(None, "mp"), P("mp", None), P(), P(), P(),
            P(), P("dp", None, None), P("dp", None, None),
        ),
        out_specs=(
            P("dp", None, None), P("dp", None, None), P(), P("dp", None, None), P("dp", "mp"),
            P("mp", None), P(None, None, "mp"), P(None, "mp"), P(None, "mp"), P("mp", None), P(),
            P(), P(None, "mp"), P("mp", None), P(), P(), P(), P(),
        ),
        check_vma=False,
    )
```

```python
import functools
import math

import jax
import jax.numpy as jnp
from jax import lax
from jax.experimental import pallas as pl
from jax.experimental.pallas import tpu as pltpu
from jax.sharding import PartitionSpec as P

DH = 64
SPANW = 4
EPSILON = 1e-05
MASKED_SCORE = -1000000000.0
LANES = 128
BF = jnp.bfloat16
F32 = jnp.float32
MESH = pl.DeviceIdType.MESH
VM = pl.BlockSpec(memory_space=pltpu.VMEM)


def matmul(first_op, second_op):
    return jnp.dot(first_op, second_op, preferred_element_type=F32)


def contract_product(form, first_op, second_op):
    return jnp.einsum(form, first_op, second_op, preferred_element_type=F32)


def normalize(source, gain_vec, shift_vec):
    center = source - jnp.mean(source, axis=-1, keepdims=True)
    inv_scale = lax.rsqrt(jnp.mean(center * center, axis=-1, keepdims=True) + EPSILON)
    return center * inv_scale * gain_vec + shift_vec


def gelu_exact(source):
    return jax.nn.gelu(source, approximate=False)


def head_map(head_pre, gain_vec):
    return normalize(gelu_exact(head_pre), gain_vec, 0.0)


def remote(src, dst, send, recv, axis, peer):
    return pltpu.make_async_remote_copy(
        src_ref=src, dst_ref=dst, send_sem=send, recv_sem=recv,
        device_id={axis: peer}, device_id_type=MESH,
    )


def exchange_kernel(axis, n, kinds, *refs):
    k = len(kinds)
    ins, outs, (send_sems, recv_sems, own_sems) = refs[:k], refs[k:2 * k], refs[2 * k:]
    me = lax.axis_index(axis)
    barrier = pltpu.get_barrier_semaphore()

    def greet(step, carry):
        pl.semaphore_signal(
            barrier, inc=1, device_id={axis: lax.rem(me + step, n)}, device_id_type=MESH
        )
        return carry

    lax.fori_loop(1, n, greet, 0)
    own = []
    for i, kind in enumerate(kinds):
        src = ins[i].at[me] if kind == "a2a" else ins[i]
        own.append(pltpu.make_async_copy(src, outs[i].at[me], own_sems.at[i]))
        own[-1].start()
    pl.semaphore_wait(barrier, n - 1)

    def copies(step):
        peer = lax.rem(me + step, n)
        return [
            remote(
                ins[i].at[peer] if kind == "a2a" else ins[i], outs[i].at[me],
                send_sems.at[i, step - 1], recv_sems.at[i, step - 1], axis, peer,
            )
            for i, kind in enumerate(kinds)
        ]

    def begin(step, carry):
        for copy in copies(step):
            copy.start()
        return carry

    lax.fori_loop(1, n, begin, 0)

    def finish(step, carry):
        source = lax.rem(me + n - step, n)
        for i, kind in enumerate(kinds):
            remote(
                ins[i].at[source] if kind == "a2a" else ins[i], outs[i].at[source],
                send_sems.at[i, step - 1], recv_sems.at[i, step - 1], axis, source,
            ).wait()
        return carry

    lax.fori_loop(1, n, finish, 0)
    for copy in own:
        copy.wait()


def exchange(axis, collective, arrays):
    n = lax.axis_size(axis)
    kinds = tuple(kind for kind, _ in arrays)
    values = [value for _, value in arrays]
    shapes = [
        jax.ShapeDtypeStruct(value.shape if kind == "a2a" else (n,) + value.shape, value.dtype)
        for kind, value in arrays
    ]
    k = len(values)
    return pl.pallas_call(
        functools.partial(exchange_kernel, axis, n, kinds),
        out_shape=shapes,
        in_specs=[VM] * k,
        out_specs=[VM] * k,
        scratch_shapes=[
            pltpu.SemaphoreType.DMA((k, n - 1)),
            pltpu.SemaphoreType.DMA((k, n - 1)),
            pltpu.SemaphoreType.DMA((k,)),
        ],
        compiler_params=pltpu.CompilerParams(collective_id=collective, has_side_effects=True),
    )(*values)


def contract(first_op, second_op, first_dim, second_dim):
    return lax.dot_general(
        first_op, second_op, (((first_dim,), (second_dim,)), ((), ())), preferred_element_type=F32
    )


def span(start, count):
    return pl.ds(pl.multiple_of(start, 16), count)


def each(count, step, body, unroll=1):
    while count // step % unroll:
        unroll -= 1

    def run(index, carry):
        for i in range(unroll):
            body(pl.multiple_of((index * unroll + i) * step, step))
        return carry

    lax.fori_loop(0, count // step // unroll, run, 0)


class Quarters:
    def __init__(self, part, r1, s2, r2, full, send, recv):
        self.part, self.r1, self.s2, self.r2, self.full = part, r1, s2, r2, full
        self.send, self.recv = send, recv
        me = lax.axis_index("mp")
        self.b0, self.b1 = lax.rem(me, 2), me // 2
        self.p1, self.p2 = me + 1 - 2 * self.b0, lax.rem(me + 2, 4)
        self.length = part.shape[1]
        self.half = self.length // 2
        self.quarter = self.length // 4

    def copy(self, s, k, src, dst, peer):
        return remote(src, dst, self.send.at[s, k], self.recv.at[s, k], "mp", peer)

    def first(self, s):
        rows = span((1 - self.b0) * self.half, self.half)
        return self.copy(s, 0, self.part.at[s, rows], self.r1.at[s], self.p1)

    def second(self, s):
        return self.copy(s, 1, self.s2.at[s], self.r2.at[s], self.p2)

    def place(self, s, h, q):
        return self.full.at[span(s * self.length + h * self.half + q * self.quarter, self.quarter)]

    def third(self, s, q):
        return self.copy(s, 2, self.place(s, self.b0, q), self.place(s, self.b0, q), self.p2)

    def fourth(self, s, h):
        return self.copy(s, 3, self.place(s, h, self.b1), self.place(s, h, self.b1), self.p1)

    def fifth(self, s, h):
        q = 1 - self.b1
        return self.copy(s, 4, self.place(s, h, q), self.place(s, h, q), self.p1)

    def both(self, s, q, row):
        mine = self.part[s, span(self.b0 * self.half + q * self.quarter + row, 16)]
        return mine.astype(F32) + self.r1[s, span(q * self.quarter + row, 16)].astype(F32)

    def begin(self, s):
        self.first(s).start()

    def pass_on(self, s):
        self.first(s).wait_recv()

        def body(row):
            self.s2[s, span(row, 16)] = self.both(s, 1 - self.b1, row).astype(BF)

        each(self.quarter, 16, body, 5)
        self.second(s).start()

    def wait_sum(self, s):
        self.second(s).wait_recv()

    def total(self, s, row):
        return self.both(s, self.b1, row) + self.r2[s, span(row, 16)].astype(F32)

    def own_row(self, s, row):
        return s * self.length + self.b0 * self.half + self.b1 * self.quarter + row

    def spread(self, s):
        self.third(s, self.b1).start()
        self.fourth(s, self.b0).start()

    def forward(self, s):
        self.third(s, 1 - self.b1).wait_recv()
        self.fifth(s, self.b0).start()

    def wait_full(self, s):
        self.fourth(s, 1 - self.b0).wait_recv()
        self.fifth(s, 1 - self.b0).wait_recv()

    def drain(self, s, sent=False):
        if not sent:
            self.first(s).wait_send()
        self.second(s).wait_send()
        self.third(s, self.b1).wait_send()
        self.fourth(s, self.b0).wait_send()
        self.fifth(s, self.b0).wait_send()


def scaled(center):
    return lax.rsqrt(jnp.mean(center * center, axis=-1, keepdims=True) + EPSILON)


def scores_of(qkv, sT, h, cols, word_length):
    k_cols = pl.ds(cols.start, word_length), pl.ds(cols.start + word_length, cols.size - word_length)
    sT[0:word_length] = contract(qkv[h, 128:192, k_cols[0]], qkv[h, 0:64, cols], 0, 0)
    sT[word_length:] = contract(qkv[h, 128:192, k_cols[1]], qkv[h, 64:128, cols], 0, 0)


def forward_kernel(
    sizes, stream, query_weight, w_key, w_value, mask, w_out, w_up, w_down, norms,
    qkv, lse, ctx, wt_words, wt_ents, center1, first_low, hidden, slope, center2, out,
    sT, pT, pre, first, part1, r11, s21, r21, part2, r12, s22, r22,
    send1, recv1, send2, recv2,
):
    seqs, length, word_length, heads = sizes
    width = stream.shape[1]
    units = w_up.shape[1]
    one = Quarters(part1, r11, s21, r21, first_low, send1, recv1)
    two = Quarters(part2, r12, s22, r22, center2, send2, recv2)
    barrier = pltpu.get_barrier_semaphore()
    for peer in (one.p1, one.p2):
        pl.semaphore_signal(barrier, inc=1, device_id={"mp": peer}, device_id_type=MESH)

    for target, first_query in ((wt_words, 0), (wt_ents, 2)):
        sources = (query_weight[first_query], query_weight[first_query + 1], w_key[...], w_value[...])
        for g, source in enumerate(sources):
            for h in range(heads):
                target[h, g * DH : (g + 1) * DH] = source[h * DH : (h + 1) * DH]

    def project(s):
        for weight, start, count in ((wt_words, 0, word_length), (wt_ents, word_length, length - word_length)):
            base = s * length + start
            for h in range(heads):
                value = contract(weight[h], stream[base : base + count], 1, 1)
                qkv[h, 0:128, base : base + count] = (value[0:128] * 0.125).astype(BF)
                qkv[h, 128:256, base : base + count] = value[128:256].astype(BF)

    def attend(s, h):
        cols = pl.ds(s * length, length)
        scores_of(qkv, sT, h, cols, word_length)

        def body(col):
            here = pl.ds(col, LANES)
            words = sT[0:word_length, here] + mask[s]
            ents = sT[word_length:, here]
            top = jnp.maximum(
                jnp.max(words, axis=0, keepdims=True), jnp.max(ents, axis=0, keepdims=True)
            )
            words = jnp.exp(words - top)
            ents = jnp.exp(ents - top)
            total = jnp.sum(words, axis=0, keepdims=True) + jnp.sum(ents, axis=0, keepdims=True)
            pT[0:word_length, here] = words.astype(BF)
            pT[word_length:, here] = ents.astype(BF)
            lse[h, 0:1, pl.ds(pl.multiple_of(s * length + col, LANES), LANES)] = top + jnp.log(total)
            lse[h, 1:2, pl.ds(pl.multiple_of(s * length + col, LANES), LANES)] = 1.0 / total

        each(length, LANES, body)
        value = matmul(qkv[h, 192:256, cols], pT[...]) * lse[h, 1:2, cols]
        ctx[h * DH : (h + 1) * DH, cols] = value.astype(BF)

    def attention_part(s):
        value = contract(ctx[:, s * length : (s + 1) * length], w_out[...], 0, 0)
        part1[s] = value.astype(BF)

    def first_rows(s):
        def body(row):
            at = one.own_row(s, row)
            value = stream[span(at, 16)].astype(F32) + one.total(s, row)
            center = value - jnp.mean(value, axis=-1, keepdims=True)
            mine = span(s * one.quarter + row, 16)
            center1[mine] = center
            normed = center * scaled(center) * norms[0:1] + norms[1:2]
            first[mine] = normed
            first_low[span(at, 16)] = normed.astype(BF)

        each(one.quarter, 16, body, 5)

    def second_rows(s):
        def body(row):
            at = two.own_row(s, row)
            value = first[span(s * two.quarter + row, 16)] + two.total(s, row)
            center = value - jnp.mean(value, axis=-1, keepdims=True)
            center2[span(at, 16)] = center.astype(BF)

        each(two.quarter, 16, body, 5)

    def feed(s):
        rows = slice(s * length, (s + 1) * length)
        tile = 256
        for j in range(units // tile):
            cols = slice(j * tile, (j + 1) * tile)
            pre[...] = matmul(first_low[rows], w_up[:, cols])

            def body(row):
                value = pre[pl.ds(row, 32)]
                bell = lax.erf(value * 0.7071067811865476) * 0.5 + 0.5
                at = span(s * length + row, 32)
                hidden[at, cols] = (value * bell).astype(BF)
                slope[at, cols] = (
                    bell + value * jnp.exp(value * value * -0.5) * 0.3989422804014327
                ).astype(BF)

            each(length, 32, body, 4)
        for j in range(width // tile):
            cols = slice(j * tile, (j + 1) * tile)
            part2[s, :, cols] = matmul(hidden[rows], w_down[:, cols]).astype(BF)

    def output_rows(s):
        def body(row):
            at = span(s * length + row, 16)
            center = center2[at].astype(F32)
            out[at] = (center * scaled(center) * norms[2:3] + norms[3:4]).astype(BF)

        each(length, 16, body, 5)

    project(0)
    for h in range(heads):
        attend(0, h)
    attention_part(0)
    pl.semaphore_wait(barrier, 2)
    one.begin(0)
    project(1)
    attend(1, 0)
    one.pass_on(0)
    for h in range(1, heads):
        attend(1, h)
    attention_part(1)
    one.begin(1)
    one.wait_sum(0)
    first_rows(0)
    one.spread(0)
    one.pass_on(1)
    one.forward(0)
    one.wait_full(0)
    feed(0)
    two.begin(0)
    one.wait_sum(1)
    first_rows(1)
    one.spread(1)
    two.pass_on(0)
    one.forward(1)
    one.wait_full(1)
    feed(1)
    two.begin(1)
    two.wait_sum(0)
    second_rows(0)
    two.spread(0)
    two.pass_on(1)
    two.forward(0)
    two.wait_full(0)
    output_rows(0)
    two.wait_sum(1)
    second_rows(1)
    two.spread(1)
    two.forward(1)
    two.wait_full(1)
    output_rows(1)
    for s in range(seqs):
        one.drain(s)
        two.drain(s)


def quarter_scratch(seqs, length, width):
    return [
        pltpu.VMEM((seqs, length, width), BF),
        pltpu.VMEM((seqs, length // 2, width), BF),
        pltpu.VMEM((seqs, length // 4, width), BF),
        pltpu.VMEM((seqs, length // 4, width), BF),
    ]


def forward_layer(sizes, stream, query_weight, w_key, w_value, mask, w_out, w_up, w_down, norms):
    seqs, length, word_length, heads = sizes
    tokens, width = stream.shape
    local = heads * DH
    units = w_up.shape[1]

    def like(*shape, dtype=BF):
        return jax.ShapeDtypeStruct(shape, dtype)

    outs = [
        like(heads, 4 * DH, tokens), like(heads, 8, tokens, dtype=F32), like(local, tokens),
        like(heads, 4 * DH, width), like(heads, 4 * DH, width), like(tokens // 4, width, dtype=F32),
        like(tokens, width), like(tokens, units), like(tokens, units), like(tokens, width),
        like(tokens, width),
    ]
    return pl.pallas_call(
        functools.partial(forward_kernel, sizes),
        out_shape=outs,
        in_specs=[VM] * 9,
        out_specs=[VM] * len(outs),
        scratch_shapes=[
            pltpu.VMEM((length, length), F32),
            pltpu.VMEM((length, length), BF),
            pltpu.VMEM((length, 256), F32),
            pltpu.VMEM((tokens // 4, width), F32),
            *quarter_scratch(seqs, length, width),
            *quarter_scratch(seqs, length, width),
            pltpu.SemaphoreType.DMA((seqs, 5)), pltpu.SemaphoreType.DMA((seqs, 5)),
            pltpu.SemaphoreType.DMA((seqs, 5)), pltpu.SemaphoreType.DMA((seqs, 5)),
        ],
        compiler_params=pltpu.CompilerParams(
            collective_id=3, has_side_effects=True, vmem_limit_bytes=56 * 2**20
        ),
    )(stream, query_weight, w_key, w_value, mask, w_out, w_up, w_down, norms)


class Job:
    def __init__(self, rows, buf, out, arrivals, send, recv, n, first=(0, 1, 2)):
        self.buf, self.out, self.arrivals, self.send, self.recv = buf, out, arrivals, send, recv
        self.rows = rows
        self.me = lax.axis_index("dp")
        self.bits, self.halvings = job_plan(rows, n)
        self.order = list(range(self.bits))
        if self.bits >= len(first):
            self.order[: len(first)] = first

    def bit(self, k):
        return lax.rem(self.me // 2 ** self.order[k], 2)

    def peer(self, k):
        return self.me + (1 - 2 * self.bit(k)) * 2 ** self.order[k]

    def offset(self, k):
        start = 0
        for i in range(k):
            start = start + self.bit(i) * (self.rows >> (i + 1))
        return start

    def copy(self, index, k, src, dst):
        return remote(src, dst, self.send.at[index], self.recv.at[index], "dp", self.peer(k))

    def steps(self):
        size = self.rows
        for k in range(self.bits):
            keep = self.offset(min(k, self.halvings))
            away = keep
            if k < self.halvings:
                size //= 2
                away = keep + (1 - self.bit(k)) * size
                keep = keep + self.bit(k) * size
            arrived = self.arrivals[k]
            copy = self.copy(k, k, self.buf.at[span(away, size)], arrived)
            copy.start()
            yield
            copy.wait()
            last = k == self.bits - 1

            def body(row, keep=keep, arrived=arrived, last=last):
                at = span(keep + row, 16)
                value = self.buf[at].astype(F32) + arrived[span(row, 16)].astype(F32)
                (self.out if last else self.buf)[at] = value.astype(BF)

            each(size, 16, body, 4)
        for k in reversed(range(self.halvings)):
            done = self.out.at[span(self.offset(k + 1), size)]
            copy = self.copy(self.bits + k, k, done, done)
            copy.start()
            yield
            copy.wait()
            size *= 2


def job_plan(rows, n):
    bits, halvings, size = n.bit_length() - 1, 0, rows
    while halvings < bits - 1 and (size // 2) % 16 == 0:
        size, halvings = size // 2, halvings + 1
    return bits, halvings


def job_cuts(units, width, head_rows, proj_rows, heads):
    orders = [
        ((1, 2, 0), (0, 1, 2), (1, 2, 0)),
        ((0, 1, 2), (0, 1, 2), (0, 1, 2)),
        ((1, 0, 2),),
        ((0, 1, 2),),
        ((1, 2, 0), (0, 1, 2)),
        ((0, 1, 2), (0, 1, 2)),
        ((0, 1, 2), (0, 1, 2)),
    ]
    cuts = [(units, [units // 3] * 3), (width, [width // 3] * 3)]
    cuts += [(head_rows, [head_rows]), (proj_rows, [proj_rows])]
    cuts += [(7 * DH, [4 * DH, 3 * DH])] * heads
    return [(rows, pieces, order) for (rows, pieces), order in zip(cuts, orders)]


def job_scratch(rows, width, n):
    bits, halvings = job_plan(rows, n)
    return [
        pltpu.VMEM((rows >> min(k + 1, halvings), width), BF) for k in range(bits)
    ]


class Spread:
    def __init__(self, axis, n, source_of, into, send, recv):
        self.axis, self.n, self.source_of, self.into = axis, n, source_of, into
        self.send, self.recv = send, recv
        self.me = lax.axis_index(axis)

    def copy(self, step, peer, slot):
        return remote(
            self.source_of(peer), self.into.at[slot], self.send.at[step - 1], self.recv.at[step - 1],
            self.axis, peer,
        )

    def start(self):
        def begin(step, carry):
            self.copy(step, lax.rem(self.me + step, self.n), self.me).start()
            return carry

        lax.fori_loop(1, self.n, begin, 0)

    def wait(self):
        def finish(step, carry):
            source = lax.rem(self.me + self.n - step, self.n)
            self.copy(step, source, source).wait()
            return carry

        lax.fori_loop(1, self.n, finish, 0)


def greet(barrier, axis, n):
    me = lax.axis_index(axis)

    def signal(step, carry):
        pl.semaphore_signal(
            barrier, inc=1, device_id={axis: lax.rem(me + step, n)}, device_id_type=MESH
        )
        return carry

    lax.fori_loop(1, n, signal, 0)


def backward_kernel(sizes, n, n_mp, *refs):
    seqs, length, word_length, heads = sizes
    refs = list(refs)

    def take(count):
        taken = refs[:count]
        del refs[:count]
        return taken

    cot_words, cot_ents = take(2)
    (
        d_head, head_grad, center2, slope, hidden, first_low, center1, w_up, w_down, norms,
        small_in, ent_proj, vec_rows, place,
    ) = take(14)
    late_in = take(8)
    down_out, up_out, head_all, proj_out, *per_head_out = take(4 + heads)
    gw, inbox, small = take(3)
    ctx, qkv, lse, wt_words, wt_ents, stream, mask, w_out = late = take(8)
    sums, d_ffn, d_pre, d_attn, d_first, dctx, sT, dpT, pT, dsT, dcat = take(11)
    head_out, small_mp, small_dp, outbox = take(4)
    part, r1, s2, r2 = take(4)
    (
        send1, recv1, send2, recv2, job_send, job_recv, late_sem, cot_sem,
        mp_send, mp_recv, dp_send, dp_recv,
    ) = take(12)
    width = stream.shape[1]
    units = w_up.shape[1]
    me_mp, me_dp = lax.axis_index("mp"), lax.axis_index("dp")
    bits = n.bit_length() - 1
    jobs = []
    groups = [[], [], [], []] + [[] for h in range(heads)]
    buffers = take(len(groups))
    for group, buf, out, (rows, cuts, orders) in zip(
        groups, buffers, [down_out, up_out, head_out, proj_out, *per_head_out],
        job_cuts(units, width, head_out.shape[0], proj_out.shape[0], heads),
    ):
        start = 0
        for count, order in zip(cuts, orders):
            at = pl.ds(start, count)
            start += count
            index = len(jobs)
            jobs.append(
                Job(
                    count, buf.at[at], out.at[at], take(bits), job_send.at[index],
                    job_recv.at[index], n, order,
                )
            )
            group.append(jobs[-1])
    down_jobs, up_jobs, (head_job,), (proj_job,), *heads_jobs = groups
    down_buf, up_buf, head_buf, proj_buf, *heads_buf = buffers
    one = Quarters(part, r1, s2, r2, d_attn, send1, recv1)
    two = Quarters(part, r1, s2, r2, gw, send2, recv2)
    barrier = pltpu.get_barrier_semaphore()
    greet(barrier, "mp", n_mp)
    greet(barrier, "dp", n)
    cots = []
    for s in range(seqs):
        for k, (source, start, count) in enumerate(
            ((cot_words, 0, word_length), (cot_ents, word_length, length - word_length))
        ):
            target = d_attn.at[pl.ds(s * length + start, count)]
            cots.append(pltpu.make_async_copy(source.at[s], target, cot_sem.at[s, k]))
            cots[-1].start()
    late_copies = [
        pltpu.make_async_copy(source, target, late_sem.at[i])
        for i, (source, target) in enumerate(zip(late_in, late))
    ]
    for copy in late_copies:
        copy.start()
    running = {}

    def launch(job):
        running[id(job)] = job.steps()
        next(running[id(job)])

    def step(*which):
        for job in which:
            next(running[id(job)], 0)

    def finish(job):
        for _ in running[id(job)]:
            pass

    sums[...] = jnp.zeros_like(sums)

    spare = d_first.shape[0] - 16

    def second_back(s):
        start = one.own_row(0, 0)

        def rows_of(row, extra=None):
            at = span(s * length + row, 16)
            cot = d_attn[at].astype(F32)
            if extra is not None:
                cot = cot + extra
            center = center2[at].astype(F32)
            inv = scaled(center)
            normed = center * inv
            sums[0] += cot * normed
            sums[1] += cot
            grad = cot * norms[2:3]
            value = inv * (
                grad
                - jnp.mean(grad, axis=-1, keepdims=True)
                - normed * jnp.mean(grad * normed, axis=-1, keepdims=True)
            )
            d_ffn[at] = value.astype(BF)

            own = (row >= start) & (row < start + one.quarter)
            d_first[span(jnp.where(own, s * one.quarter + row - start, spare), 16)] = value

        scored = d_head.shape[1]
        each(word_length, 16, rows_of, 4)
        each(scored, 16, lambda row: rows_of(row + word_length, d_head[s, span(row, 16)]))
        each(length - word_length - scored, 16, lambda row: rows_of(row + word_length + scored), 7)

    def feed_back(s):
        rows = slice(s * length, (s + 1) * length)
        tile = 256
        for j in range(units // tile):
            cols = slice(j * tile, (j + 1) * tile)
            sT[:, 0:tile] = contract(d_ffn[rows], w_down[cols], 1, 1)

            def body(row):
                at = span(s * length + row, 32)
                d_pre[at, cols] = (
                    sT[pl.ds(row, 32), 0:tile] * slope[at, cols].astype(F32)
                ).astype(BF)

            each(length, 32, body, 4)
        for j in range(width // tile):
            cols = slice(j * tile, (j + 1) * tile)
            part[s, :, cols] = contract(d_pre[rows], w_up[cols], 1, 1).astype(BF)

    def first_back(s):
        def body(row):
            at = one.own_row(s, row)
            mine = span(s * one.quarter + row, 16)
            value = d_first[mine] + one.total(s, row)
            center = center1[mine]
            inv = scaled(center)
            normed = center * inv
            sums[2] += value * normed
            sums[3] += value
            grad = value * norms[0:1]
            value = inv * (
                grad
                - jnp.mean(grad, axis=-1, keepdims=True)
                - normed * jnp.mean(grad * normed, axis=-1, keepdims=True)
            )
            d_first[mine] = value
            d_attn[span(at, 16)] = value.astype(BF)

        each(one.quarter, 16, body, 5)

    def context_back(s):
        cols = slice(s * length, (s + 1) * length)
        dctx[:, cols] = contract(w_out[...], d_attn[cols], 1, 1).astype(BF)

    def attend_back(s, h):
        cols = pl.ds(s * length, length)
        w_cols = pl.ds(s * length, word_length)
        e_cols = pl.ds(s * length + word_length, length - word_length)
        mine = slice(h * DH, (h + 1) * DH)
        scores_of(qkv, sT, h, cols, word_length)
        dpT[...] = contract(qkv[h, 192:256, cols], dctx[mine, cols], 0, 0)

        def body(col):
            here = pl.ds(col, LANES)
            at = pl.ds(pl.multiple_of(s * length + col, LANES), LANES)
            delta = jnp.sum(
                ctx[mine, at].astype(F32) * dctx[mine, at].astype(F32), axis=0, keepdims=True
            )
            log_total = lse[h, 0:1, at]
            probs = jnp.exp(sT[0:word_length, here] + mask[s] - log_total)
            pT[0:word_length, here] = probs.astype(BF)
            dsT[0:word_length, here] = (probs * (dpT[0:word_length, here] - delta)).astype(BF)
            probs = jnp.exp(sT[word_length:, here] - log_total)
            pT[word_length:, here] = probs.astype(BF)
            dsT[word_length:, here] = (probs * (dpT[word_length:, here] - delta)).astype(BF)

        each(length, LANES, body)
        d_words, d_ents = dsT[0:word_length], dsT[word_length:]
        dcat[h, 0:64, cols] = (contract(qkv[h, 128:192, w_cols], d_words, 1, 0) * 0.125).astype(BF)
        dcat[h, 64:128, cols] = (contract(qkv[h, 128:192, e_cols], d_ents, 1, 0) * 0.125).astype(BF)
        dcat[h, 128:192, w_cols] = contract(qkv[h, 0:64, cols], d_words, 1, 1).astype(BF)
        dcat[h, 128:192, e_cols] = contract(qkv[h, 64:128, cols], d_ents, 1, 1).astype(BF)
        dcat[h, 192:256, cols] = contract(dctx[mine, cols], pT[...], 1, 1).astype(BF)

    def head_grads(h):
        buf = heads_buf[h]
        from_words, from_ents = None, None
        for s in range(seqs):
            middle, start, end = s * length + word_length, s * length, (s + 1) * length
            words = matmul(dcat[h, :, start:middle], stream[start:middle])
            ents = matmul(dcat[h, :, middle:end], stream[middle:end])
            from_words = words if s == 0 else from_words + words
            from_ents = ents if s == 0 else from_ents + ents
        buf[0:128] = from_words[0:128].astype(BF)
        buf[128:256] = (from_words[128:256] + from_ents[128:256]).astype(BF)
        buf[256:384] = from_ents[0:128].astype(BF)
        buf[384:448] = matmul(ctx[h * DH : (h + 1) * DH], d_attn[...]).astype(BF)

    def stream_part(s):
        for start in range(0, length, LANES):
            weight = wt_words if start < word_length else wt_ents
            cols = slice(s * length + start, s * length + start + LANES)
            value = contract(dcat[0, :, cols], weight[0], 0, 0)
            for h in range(1, heads):
                value = value + contract(dcat[h, :, cols], weight[h], 0, 0)
            part[s, start : start + LANES] = value.astype(BF)

    def last_rows(s):
        def body(row):
            at = two.own_row(s, row)
            value = d_first[span(s * two.quarter + row, 16)] + two.total(s, row)
            gw[span(at, 16)] = value.astype(BF)

        each(two.quarter, 16, body, 5)

    def down_tile(j):
        cols = slice(j * 256, (j + 1) * 256)
        down_buf[cols] = contract(hidden[:, cols], d_ffn[...], 0, 0).astype(BF)

    def up_tile(j):
        cols = slice(j * 256, (j + 1) * 256)
        up_buf[cols] = contract(first_low[:, cols], d_pre[...], 0, 0).astype(BF)

    def wait_cots(s):
        for copy in cots[2 * s : 2 * s + 2]:
            copy.wait()

    def wait_late():
        for copy in late_copies:
            copy.wait()

    small_over_mp = Spread(
        "mp", n_mp, lambda peer: small_mp.at[me_mp], small_mp, mp_send.at[0], mp_recv.at[0]
    )
    small_over_dp = Spread(
        "dp", n, lambda peer: small_dp.at[me_dp], small_dp, dp_send.at[0], dp_recv.at[0]
    )
    boxes = Spread("dp", n, lambda peer: outbox.at[peer], inbox, dp_send.at[1], dp_recv.at[1])
    head_rows = head_out.shape[0]
    head_place = span(me_mp * head_rows, head_rows)

    def head_copy(distance, peer, owner):
        return remote(
            head_out, head_all.at[span(owner * head_rows, head_rows)], mp_send.at[1, distance - 1],
            mp_recv.at[1, distance - 1], "mp", peer,
        )

    def small_first():
        mine = small_in[...]
        mine = mine + jnp.concatenate(
            [jnp.sum(sums[row], axis=0, keepdims=True) for row in range(4)]
            + [jnp.zeros((4, width), F32)]
        )
        small_mp[me_mp] = mine
        small_over_mp.start()

    def small_second():
        small_over_mp.wait()
        total = small_mp[0]
        for device in range(1, n_mp):
            total = total + small_mp[device]
        row = lax.broadcasted_iota(jnp.int32, total.shape, 0)
        small_dp[me_dp] = jnp.where((row == 2) | (row == 3), total, small_mp[me_mp])
        small_over_dp.start()

    def small_last():
        small_over_dp.wait()

        def add(device, total):
            return total + small_dp[device]

        small[...] = lax.fori_loop(1, n, add, small_dp[0])

    def head_first():
        head_all[head_place] = head_out[...]
        for distance in range(1, n_mp):
            head_copy(distance, lax.rem(me_mp + distance, n_mp), me_mp).start()

    def head_last():
        for distance in range(1, n_mp):
            source = lax.rem(me_mp + n_mp - distance, n_mp)
            head_copy(distance, source, source).wait()

    def entities():
        grads, rows = None, []
        count = length - word_length
        for s in range(seqs):
            d_ent = gw[s * length + word_length : (s + 1) * length]
            value = matmul(vec_rows[:, s * count : (s + 1) * count], d_ent)
            grads = value if s == 0 else grads + value
            rows.append(contract(ent_proj[...], d_ent, 1, 1).astype(BF))
        proj_buf[...] = grads.astype(BF)
        launch(proj_job)
        rows = jnp.concatenate(rows, axis=1)
        slot = lax.broadcasted_iota(jnp.int32, (LANES, seqs * count), 0)

        def fill(owner, carry):
            placed = jnp.where(slot + owner * LANES == place[...], 1.0, 0.0).astype(BF)
            outbox[owner] = contract(rows, placed, 1, 1).astype(BF)
            return carry

        lax.fori_loop(0, n, fill, 0)
        inbox[me_dp] = outbox[me_dp]
        boxes.start()

    head_buf[...] = head_grad[...]
    wait_cots(0)
    second_back(0)
    feed_back(0)
    pl.semaphore_wait(barrier, n_mp - 1 + n - 1)
    one.begin(0)
    launch(head_job)
    wait_cots(1)
    second_back(1)
    one.pass_on(0)
    step(head_job)
    down_tile(0)
    launch(down_jobs[0])
    down_tile(1)
    launch(down_jobs[1])
    down_tile(2)
    launch(down_jobs[2])
    feed_back(1)
    one.begin(1)
    step(head_job)
    up_tile(0)
    launch(up_jobs[0])
    up_tile(1)
    launch(up_jobs[1])
    up_tile(2)
    launch(up_jobs[2])
    step(down_jobs[0])
    one.pass_on(1)
    step(down_jobs[1], head_job)
    one.wait_sum(0)
    first_back(0)
    one.spread(0)
    step(down_jobs[2], up_jobs[0], down_jobs[1], down_jobs[0])
    one.wait_sum(1)
    first_back(1)
    one.spread(1)
    small_first()
    step(up_jobs[1], up_jobs[0], down_jobs[2])
    one.forward(0)
    step(up_jobs[2], up_jobs[1], head_job, down_jobs[1])
    one.wait_full(0)
    small_second()
    wait_late()
    context_back(0)
    step(down_jobs[0])
    attend_back(0, 0)
    step(up_jobs[2], down_jobs[2], head_job)
    finish(head_job)
    head_first()
    step(up_jobs[0])
    attend_back(0, 1)
    step(down_jobs[1])
    attend_back(0, 2)
    one.first(0).wait_send()
    stream_part(0)
    two.begin(0)
    step(up_jobs[1], up_jobs[0])
    one.forward(1)
    one.wait_full(1)
    one.drain(0, True)
    one.drain(1)
    context_back(1)
    step(down_jobs[1], down_jobs[0], up_jobs[1])
    attend_back(1, 0)
    two.pass_on(0)
    head_grads(0)
    launch(heads_jobs[0][0])
    launch(heads_jobs[0][1])
    step(up_jobs[0], up_jobs[2])
    attend_back(1, 1)
    head_grads(1)
    launch(heads_jobs[1][0])
    launch(heads_jobs[1][1])
    step(down_jobs[0])
    attend_back(1, 2)
    step(up_jobs[1], down_jobs[2])
    stream_part(1)
    two.begin(1)
    head_grads(2)
    launch(heads_jobs[2][0])
    launch(heads_jobs[2][1])
    step(heads_jobs[0][0], heads_jobs[0][1], up_jobs[2])
    two.pass_on(1)
    two.wait_sum(0)
    last_rows(0)
    two.spread(0)
    small_last()
    step(heads_jobs[1][0], down_jobs[2], heads_jobs[0][0], heads_jobs[1][1])
    step(heads_jobs[0][1])
    two.wait_sum(1)
    step(heads_jobs[1][0])
    last_rows(1)
    two.spread(1)
    step(heads_jobs[1][1], heads_jobs[2][0], heads_jobs[0][1], heads_jobs[2][1])
    two.forward(0)
    step(heads_jobs[2][0], heads_jobs[1][0], heads_jobs[0][1], up_jobs[2])
    step(heads_jobs[2][1])
    two.forward(1)
    two.wait_full(0)
    step(heads_jobs[1][1], heads_jobs[0][0], heads_jobs[1][0])
    two.wait_full(1)
    entities()
    step(heads_jobs[1][1], heads_jobs[0][1], heads_jobs[2][0], heads_jobs[2][1])
    step(heads_jobs[1][0], heads_jobs[2][0], proj_job, heads_jobs[2][1])
    step(proj_job, heads_jobs[0][0], heads_jobs[1][1], proj_job)
    step(heads_jobs[2][0], heads_jobs[0][0], proj_job, heads_jobs[2][1])
    step(proj_job)
    boxes.wait()
    head_last()
    for s in range(seqs):
        two.drain(s)
    for job in jobs:
        finish(job)


def backward_layer(sizes, n, cots, now, late):
    seqs, length, word_length, heads = sizes
    stream, w_up, ent_proj = late[5], now[7], now[11]
    n_mp = lax.axis_size("mp")
    tokens, width = stream.shape
    units, local = w_up.shape[1], heads * DH
    head_rows, head_width = now[1].shape
    bits = n.bit_length() - 1
    outs = [(units, width), (width, units), (n_mp * head_rows, head_width), ent_proj.shape]
    outs += [(7 * DH, width)] * heads + [(tokens, width), (n, ent_proj.shape[0], LANES)]
    outs = [jax.ShapeDtypeStruct(shape, BF) for shape in outs]
    outs.append(jax.ShapeDtypeStruct((8, width), F32))
    cuts = job_cuts(units, width, head_rows, ent_proj.shape[0], heads)
    widths = [width, units, head_width] + [width] * (1 + heads)
    job_count = sum(len(sizes) for _, sizes, _ in cuts)
    scratch = [pltpu.VMEM(value.shape, value.dtype) for value in late]
    scratch += [
        pltpu.VMEM((4, 16, width), F32), pltpu.VMEM((tokens, width), BF),
        pltpu.VMEM((tokens, units), BF), pltpu.VMEM((tokens, width), BF),
        pltpu.VMEM((tokens // 4 + 16, width), F32), pltpu.VMEM((local, tokens), BF),
        pltpu.VMEM((length, length), F32), pltpu.VMEM((length, length), F32),
        pltpu.VMEM((length, length), BF), pltpu.VMEM((length, length), BF),
        pltpu.VMEM((heads, 4 * DH, tokens), BF),
        pltpu.VMEM((head_rows, head_width), BF), pltpu.VMEM((n_mp, 8, width), F32),
        pltpu.VMEM((n, 8, width), F32), pltpu.VMEM((n, ent_proj.shape[0], LANES), BF),
        *quarter_scratch(seqs, length, width),
        pltpu.SemaphoreType.DMA((seqs, 5)), pltpu.SemaphoreType.DMA((seqs, 5)),
        pltpu.SemaphoreType.DMA((seqs, 5)), pltpu.SemaphoreType.DMA((seqs, 5)),
        pltpu.SemaphoreType.DMA((job_count, 2 * bits)),
        pltpu.SemaphoreType.DMA((job_count, 2 * bits)),
        pltpu.SemaphoreType.DMA((len(late),)), pltpu.SemaphoreType.DMA((seqs, 2)),
        pltpu.SemaphoreType.DMA((2, n_mp - 1)), pltpu.SemaphoreType.DMA((2, n_mp - 1)),
        pltpu.SemaphoreType.DMA((2, n - 1)), pltpu.SemaphoreType.DMA((2, n - 1)),
    ]
    scratch += [pltpu.VMEM((rows, columns), BF) for (rows, _, _), columns in zip(cuts, widths)]
    for (_, counts, _), columns in zip(cuts, widths):
        for count in counts:
            scratch += job_scratch(count, columns, n)
    hbm = pl.BlockSpec(memory_space=pl.ANY)
    return pl.pallas_call(
        functools.partial(backward_kernel, sizes, n, n_mp),
        out_shape=outs,
        in_specs=[hbm] * len(cots) + [VM] * len(now) + [hbm] * len(late),
        out_specs=[VM] * len(outs),
        scratch_shapes=scratch,
        compiler_params=pltpu.CompilerParams(
            collective_id=7, has_side_effects=True, vmem_limit_bytes=61 * 2**20
        ),
    )(*cots, *now, *late)


def shards(
    words, word_extra, span_pos, span_len, entity_shard, entity_row, targets, table, ent_proj,
    query_weight, w_key, w_value, w_out, gain_attn, bias_attn, w_up, w_down, gain_ffn, bias_ffn,
    w_head, gain_head, cot_words, cot_ents,
):
    n_dp = lax.axis_size("dp")
    n_mp = lax.axis_size("mp")
    seq_count, word_length, model_width = words.shape
    ent_len = span_pos.shape[1]
    masked_len = targets.shape[1]
    tokens_len = word_length + ent_len
    rows_dev, cols_dev = table.shape
    local_width = w_key.shape[1]
    heads_local = local_width // DH
    ent_total = seq_count * ent_len
    table_full = lax.all_gather(table, "mp", axis=1, tiled=True)

    owners = entity_shard.reshape(ent_total)
    wanted = entity_row.reshape(ent_total)
    capacity = max(16, 2 * ent_total // n_dp)
    owner_onehot = (owners[:, None] == jnp.arange(n_dp, dtype=jnp.int32)[None, :]).astype(BF)
    order_index = jnp.arange(ent_total, dtype=jnp.int32)
    earlier = (order_index[:, None] > order_index[None, :]).astype(BF)
    before = matmul(earlier, owner_onehot)
    slot_rank = jnp.sum(before * owner_onehot.astype(F32), axis=1).astype(jnp.int32)
    place = owners * capacity + slot_rank
    placed = place[:, None] == jnp.arange(n_dp * capacity, dtype=jnp.int32)[None, :]
    requests = jnp.sum(jnp.where(placed, wanted[:, None] + 1, 0), axis=0) - 1
    requests = jnp.pad(requests.reshape(n_dp, 1, capacity), ((0, 0), (0, 7), (0, LANES - capacity)))
    (received,) = exchange("dp", 0, [("a2a", requests)])
    received = received[:, 0, :capacity]
    present = received >= 0
    picked = jnp.take(table, jnp.maximum(received, 0), axis=0)
    picked = jnp.where(present[..., None], picked, jnp.zeros_like(picked))
    (back_rows,) = exchange("dp", 1, [("a2a", picked)])
    placed_low = placed.astype(BF)
    vec_cols = matmul(placed_low, back_rows.reshape(n_dp * capacity, cols_dev)).astype(BF)
    vec_all, proj_all = exchange("mp", 2, [("ag", vec_cols), ("ag", ent_proj)])
    ent_vectors = contract_product("mtc,mcd->td", vec_all, proj_all)

    word_count = word_length // 8 + word_extra
    span_start = span_pos * (word_count[:, None] - SPANW) // word_length
    positions = jnp.arange(word_length, dtype=jnp.int32)
    inside = (positions[None, None, :] >= span_start[..., None]) & (
        positions[None, None, :] < (span_start + span_len)[..., None]
    )
    span_total = contract_product("sep,spd->sed", inside.astype(BF), words)
    span_width = span_len.astype(F32)[..., None]
    ent_low = (
        ent_vectors.reshape(seq_count, ent_len, model_width) + span_total / span_width
    ).astype(BF)
    stream = jnp.concatenate([words, ent_low], axis=1)
    key_valid = positions[None, :] < word_count[:, None]
    mask = jnp.broadcast_to(
        jnp.where(key_valid, 0.0, MASKED_SCORE)[..., None], (seq_count, word_length, LANES)
    )
    norms = jnp.stack([gain_attn, bias_attn, gain_ffn, bias_ffn])
    sizes = (seq_count, tokens_len, word_length, heads_local)
    qkv, lse, ctx, wt_words, wt_ents, center1, first_low, hidden, slope, center2, output = forward_layer(
        sizes, stream.reshape(seq_count * tokens_len, model_width), query_weight.transpose(0, 2, 1),
        w_key.T, w_value.T, mask, w_out, w_up, w_down, norms,
    )
    out_low = output.reshape(seq_count, tokens_len, model_width)
    out_words = out_low[:, :word_length]
    out_ents = out_low[:, word_length:]
    head_in = out_low[:, word_length : word_length + masked_len].reshape(
        seq_count * masked_len, model_width
    )
    head_pre = matmul(head_in, w_head)
    head_vec, head_back = jax.vjp(head_map, head_pre, gain_head)
    (all_head,) = exchange("dp", 5, [("ag", head_vec.astype(BF))])
    mine_total = head_vec.shape[0]
    masked_total = n_dp * mine_total
    ent_width = table_full.shape[1]
    all_head = all_head.reshape(masked_total, ent_width)
    row_offset = lax.axis_index("dp") * rows_dev
    local_target = targets.reshape(-1) - row_offset
    is_mine = (local_target >= 0) & (local_target < rows_dev)
    target_index = jnp.clip(local_target, 0, rows_dev - 1)
    target_rows = jnp.where(
        is_mine[:, None], jnp.take(table_full, target_index, axis=0), jnp.zeros((), BF)
    )
    target_logit = jnp.sum(all_head.astype(F32) * target_rows.astype(F32), axis=-1)
    block_rows = math.gcd(masked_total, 256)
    block_count = masked_total // block_rows
    head_blocks = all_head.reshape(block_count, block_rows, ent_width)

    def logits_of(head_block):
        return contract_product("md,rd->mr", head_block, table_full)

    def block_part(head_block):
        logits = logits_of(head_block)
        row_top = jnp.max(logits, axis=1)
        weights = jnp.exp(logits - row_top[:, None])
        return row_top, jnp.sum(weights, axis=1), matmul(weights.astype(BF), table_full)

    if block_count == 1:
        parts = [a[None] for a in block_part(head_blocks[0])]
    else:
        parts = lax.map(block_part, head_blocks)
    part_top, part_total = parts[0].reshape(masked_total), parts[1].reshape(masked_total)
    stats = jnp.zeros((8, masked_total), F32)
    stats = stats.at[0].set(part_top).at[1].set(part_total).at[2].set(target_logit)
    all_stats, all_parts, all_rows = exchange(
        "dp", 6,
        [
            ("ag", stats),
            ("a2a", parts[2].reshape(n_dp, mine_total, ent_width)),
            ("a2a", target_rows.reshape(n_dp, mine_total, ent_width)),
        ],
    )
    global_top = jnp.max(all_stats[:, 0], axis=0)
    shrink = jnp.exp(all_stats[:, 0] - global_top)
    global_total = jnp.sum(shrink * all_stats[:, 1], axis=0)
    head_total = global_top + jnp.log(global_total)
    loss = head_total - jnp.sum(all_stats[:, 2], axis=0)
    weight_all = shrink / global_total
    my_slots = lax.axis_index("dp") * mine_total
    my_weight = lax.dynamic_slice_in_dim(weight_all, my_slots, mine_total, 1)
    grad_head_mine = jnp.sum(
        all_parts * my_weight[..., None] - all_rows.astype(F32), axis=0
    )
    my_cols = lax.dynamic_slice_in_dim(all_head, lax.axis_index("mp") * cols_dev, cols_dev, 1)

    def block_back(running, inputs):
        head_block, col_block, total_block = inputs
        weight_low = jnp.exp(logits_of(head_block) - total_block[:, None]).astype(BF)
        return running + contract_product("mc,mr->cr", col_block, weight_low), None

    d_head_pre, grad_gain_head = head_back(grad_head_mine)
    d_head_low = d_head_pre.astype(BF)
    grad_head = contract_product("md,me->de", head_in, d_head_low)
    d_head_in = contract_product("me,de->md", d_head_low, w_head)
    head_rows = model_width // n_mp
    head_mine = lax.dynamic_slice_in_dim(
        grad_head.astype(BF), lax.axis_index("mp") * head_rows, head_rows, 0
    )
    small = jnp.zeros((8, model_width), F32).at[4, :ent_width].set(grad_gain_head)
    wide_place = (owners * LANES + slot_rank)[None]
    *sums, d_total, inbox, small = backward_layer(
        sizes, n_dp,
        (cot_words, cot_ents),
        (
            d_head_in.reshape(seq_count, masked_len, model_width), head_mine, center2, slope, hidden,
            first_low, center1, w_up, w_down, norms, small, ent_proj, vec_cols.T, wide_place,
        ),
        (
            ctx, qkv, lse, wt_words, wt_ents, stream.reshape(seq_count * tokens_len, model_width),
            mask, w_out,
        ),
    )
    grad_down, grad_up, grad_head, grad_ent_proj, *per_head = (a.astype(F32) for a in sums)
    per_head = [a.reshape(7, DH, model_width) for a in per_head]

    def columns_of(which):
        return jnp.concatenate([a[which] for a in per_head])

    grad_query = jnp.stack([columns_of(i) for i in (0, 1, 4, 5)]).transpose(0, 2, 1)
    grad_key, grad_value, grad_out = columns_of(2).T, columns_of(3).T, columns_of(6)
    d_total = d_total.reshape(seq_count, tokens_len, model_width)
    d_ent = d_total[:, word_length:]
    grad_words = d_total[:, :word_length].astype(F32) + contract_product(
        "sep,sed->spd", inside.astype(BF), (d_ent.astype(F32) / span_width).astype(BF)
    )
    table_grad, _ = lax.scan(
        block_back,
        jnp.zeros((cols_dev, rows_dev), F32),
        (
            head_blocks,
            my_cols.reshape(block_count, block_rows, cols_dev),
            head_total.reshape(block_count, block_rows),
        ),
    )
    row_index = jnp.arange(rows_dev, dtype=jnp.int32)
    hit = jnp.concatenate([received.reshape(-1), jnp.where(is_mine, local_target, -1)])
    hit_rows = jnp.concatenate(
        [inbox[:, :, :capacity].transpose(1, 0, 2).reshape(cols_dev, -1), -my_cols.T], axis=1
    )
    table_grad = table_grad + contract_product(
        "ct,tr->cr", hit_rows, (hit[:, None] == row_index[None, :]).astype(BF)
    )
    table_grad = table_grad.T
    grad_gain_ffn, grad_bias_ffn, grad_gain_attn, grad_bias_attn = (small[i] for i in range(4))
    grad_gain_head = small[4, :ent_width]
    return (
        out_words, out_ents, loss, grad_words, table_grad, grad_ent_proj, grad_query, grad_key,
        grad_value, grad_out, grad_gain_attn, grad_bias_attn, grad_up, grad_down, grad_gain_ffn,
        grad_bias_ffn, grad_head, grad_gain_head,
    )


def solution(mesh):
    return jax.shard_map(
        shards,
        mesh=mesh,
        in_specs=(
            P("dp", None, None), P("dp"), P("dp", None), P("dp", None), P("dp", None, None),
            P("dp", None), P(), P("dp", "mp"), P("mp", None), P(None, None, "mp"), P(None, "mp"),
            P(None, "mp"), P("mp", None), P(), P(), P(None, "mp"), P("mp", None), P(), P(), P(),
            P(), P("dp", None, None), P("dp", None, None),
        ),
        out_specs=(
            P("dp", None, None), P("dp", None, None), P(), P("dp", None, None), P("dp", "mp"),
            P("mp", None), P(None, None, "mp"), P(None, "mp"), P(None, "mp"), P("mp", None), P(),
            P(), P(None, "mp"), P("mp", None), P(), P(), P(), P(),
        ),
        check_vma=False,
    )
```

```python
import functools
import math

import jax
import jax.numpy as jnp
from jax import lax
from jax.experimental import pallas as pl
from jax.experimental.pallas import tpu as pltpu
from jax.sharding import PartitionSpec as P

DH = 64
SPANW = 4
EPSILON = 1e-05
MASKED_SCORE = -1000000000.0
LANES = 128
BF = jnp.bfloat16
F32 = jnp.float32
MESH = pl.DeviceIdType.MESH
VM = pl.BlockSpec(memory_space=pltpu.VMEM)


def matmul(first_op, second_op):
    return jnp.dot(first_op, second_op, preferred_element_type=F32)


def contract_product(form, first_op, second_op):
    return jnp.einsum(form, first_op, second_op, preferred_element_type=F32)


def normalize(source, gain_vec, shift_vec):
    center = source - jnp.mean(source, axis=-1, keepdims=True)
    inv_scale = lax.rsqrt(jnp.mean(center * center, axis=-1, keepdims=True) + EPSILON)
    return center * inv_scale * gain_vec + shift_vec


def gelu_exact(source):
    return jax.nn.gelu(source, approximate=False)


def head_map(head_pre, gain_vec):
    return normalize(gelu_exact(head_pre), gain_vec, 0.0)


def remote(src, dst, send, recv, axis, peer):
    return pltpu.make_async_remote_copy(
        src_ref=src, dst_ref=dst, send_sem=send, recv_sem=recv,
        device_id={axis: peer}, device_id_type=MESH,
    )


def contract(first_op, second_op, first_dim, second_dim):
    return lax.dot_general(
        first_op, second_op, (((first_dim,), (second_dim,)), ((), ())), preferred_element_type=F32
    )


def span(start, count):
    return pl.ds(pl.multiple_of(start, 16), count)


def each(count, step, body, unroll=1):
    while count // step % unroll:
        unroll -= 1

    def run(index, carry):
        for i in range(unroll):
            body(pl.multiple_of((index * unroll + i) * step, step))
        return carry

    lax.fori_loop(0, count // step // unroll, run, 0)


class Quarters:
    def __init__(self, part, r1, s2, r2, full, send, recv):
        self.part, self.r1, self.s2, self.r2, self.full = part, r1, s2, r2, full
        self.send, self.recv = send, recv
        me = lax.axis_index("mp")
        self.b0, self.b1 = lax.rem(me, 2), me // 2
        self.p1, self.p2 = me + 1 - 2 * self.b0, lax.rem(me + 2, 4)
        self.length = part.shape[1]
        self.half = self.length // 2
        self.quarter = self.length // 4

    def copy(self, s, k, src, dst, peer):
        return remote(src, dst, self.send.at[s, k], self.recv.at[s, k], "mp", peer)

    def first(self, s):
        rows = span((1 - self.b0) * self.half, self.half)
        return self.copy(s, 0, self.part.at[s, rows], self.r1.at[s], self.p1)

    def second(self, s):
        return self.copy(s, 1, self.s2.at[s], self.r2.at[s], self.p2)

    def place(self, s, h, q):
        return self.full.at[span(s * self.length + h * self.half + q * self.quarter, self.quarter)]

    def third(self, s, q):
        return self.copy(s, 2, self.place(s, self.b0, q), self.place(s, self.b0, q), self.p2)

    def fourth(self, s, h):
        return self.copy(s, 3, self.place(s, h, self.b1), self.place(s, h, self.b1), self.p1)

    def fifth(self, s, h):
        q = 1 - self.b1
        return self.copy(s, 4, self.place(s, h, q), self.place(s, h, q), self.p1)

    def both(self, s, q, row):
        mine = self.part[s, span(self.b0 * self.half + q * self.quarter + row, 16)]
        return mine.astype(F32) + self.r1[s, span(q * self.quarter + row, 16)].astype(F32)

    def begin(self, s):
        self.first(s).start()

    def pass_on(self, s):
        self.first(s).wait_recv()

        def body(row):
            self.s2[s, span(row, 16)] = self.both(s, 1 - self.b1, row).astype(BF)

        each(self.quarter, 16, body, 5)
        self.second(s).start()

    def wait_sum(self, s):
        self.second(s).wait_recv()

    def total(self, s, row):
        return self.both(s, self.b1, row) + self.r2[s, span(row, 16)].astype(F32)

    def own_row(self, s, row):
        return s * self.length + self.b0 * self.half + self.b1 * self.quarter + row

    def spread(self, s):
        self.third(s, self.b1).start()
        self.fourth(s, self.b0).start()

    def forward(self, s):
        self.third(s, 1 - self.b1).wait_recv()
        self.fifth(s, self.b0).start()

    def wait_full(self, s):
        self.fourth(s, 1 - self.b0).wait_recv()
        self.fifth(s, 1 - self.b0).wait_recv()

    def drain(self, s, sent=False):
        if not sent:
            self.first(s).wait_send()
        self.second(s).wait_send()
        self.third(s, self.b1).wait_send()
        self.fourth(s, self.b0).wait_send()
        self.fifth(s, self.b0).wait_send()


class Spread:
    def __init__(self, axis, n, source_of, into, send, recv):
        self.axis, self.n, self.source_of, self.into = axis, n, source_of, into
        self.send, self.recv = send, recv
        self.me = lax.axis_index(axis)

    def copy(self, step, peer, slot):
        return remote(
            self.source_of(peer), self.into.at[slot], self.send.at[step - 1], self.recv.at[step - 1],
            self.axis, peer,
        )

    def start(self):
        def begin(step, carry):
            self.copy(step, lax.rem(self.me + step, self.n), self.me).start()
            return carry

        lax.fori_loop(1, self.n, begin, 0)

    def wait(self):
        def finish(step, carry):
            source = lax.rem(self.me + self.n - step, self.n)
            self.copy(step, source, source).wait()
            return carry

        lax.fori_loop(1, self.n, finish, 0)


def greet(barrier, axis, n):
    me = lax.axis_index(axis)

    def signal(step, carry):
        pl.semaphore_signal(
            barrier, inc=1, device_id={axis: lax.rem(me + step, n)}, device_id_type=MESH
        )
        return carry

    lax.fori_loop(1, n, signal, 0)


def scaled(center):
    return lax.rsqrt(jnp.mean(center * center, axis=-1, keepdims=True) + EPSILON)


def scores_of(qkv, sT, h, cols, word_length):
    k_cols = pl.ds(cols.start, word_length), pl.ds(cols.start + word_length, cols.size - word_length)
    sT[0:word_length] = contract(qkv[h, 128:192, k_cols[0]], qkv[h, 0:64, cols], 0, 0)
    sT[word_length:] = contract(qkv[h, 128:192, k_cols[1]], qkv[h, 64:128, cols], 0, 0)


def forward_kernel(
    sizes, n, n_mp, capacity,
    words, requests, place, table, ent_proj, inside, spans, query_weight, w_key, w_value, mask, w_out,
    w_up, w_down, norms,
    received, vec_rows, stream, qkv, lse, ctx, wt_words, wt_ents, center1, first_low, hidden, slope,
    center2, out_words, out_ents, head_in,
    sT, pT, pre, first, part1, r11, s21, r21, part2, r12, s22, r22,
    onehot, answers, answered, vec_all, proj_all, spanned,
    send1, recv1, send2, recv2, word_sem, dp_send, dp_recv, mp_send, mp_recv,
):
    seqs, length, word_length, heads = sizes
    width = stream.shape[1]
    me_dp, me_mp = lax.axis_index("dp"), lax.axis_index("mp")
    units = w_up.shape[1]
    one = Quarters(part1, r11, s21, r21, first_low, send1, recv1)
    two = Quarters(part2, r12, s22, r22, center2, send2, recv2)
    barrier = pltpu.get_barrier_semaphore()
    greet(barrier, "dp", n)
    greet(barrier, "mp", n_mp)
    word_copies = [
        pltpu.make_async_copy(
            words.at[s], stream.at[pl.ds(s * length, word_length)], word_sem.at[s]
        )
        for s in range(seqs)
    ]
    for copy in word_copies:
        copy.start()
    asks = Spread("dp", n, lambda peer: requests.at[peer], received, dp_send.at[0], dp_recv.at[0])
    backs = Spread("dp", n, lambda peer: answers.at[peer], answered, dp_send.at[1], dp_recv.at[1])
    projs = Spread("mp", n_mp, lambda peer: ent_proj, proj_all, mp_send.at[0], mp_recv.at[0])
    vecs = Spread(
        "mp", n_mp, lambda peer: vec_all.at[me_mp], vec_all, mp_send.at[1], mp_recv.at[1]
    )
    ent_count = length - word_length

    def answer():
        ids = jnp.concatenate([received[source, 0:1, 0:capacity] for source in range(n)], axis=1)

        def body(row):
            index = lax.broadcasted_iota(jnp.int32, (80, n * capacity), 0) + row
            onehot[span(row, 80)] = jnp.where(index == ids, 1.0, 0.0).astype(BF)

        each(table.shape[1], 80, body)
        found = matmul(table[...], onehot[...]).astype(BF)
        for source in range(n):
            answers[source, :, 0:capacity] = found[:, source * capacity : (source + 1) * capacity]

    def collect():
        slot = lax.broadcasted_iota(jnp.int32, (capacity, seqs * ent_count), 0)

        def add(owner, total):
            placed = jnp.where(slot + owner * LANES == place[...], 1.0, 0.0).astype(BF)
            return total + matmul(answered[owner, :, 0:capacity], placed)

        total = lax.fori_loop(0, n, add, jnp.zeros(vec_rows.shape, F32))
        vec_rows[...] = total.astype(BF)
        vec_all[me_mp] = total.astype(BF)

    def span_means():
        for s in range(seqs):
            at = slice(s * ent_count, (s + 1) * ent_count)
            start = s * length
            spanned[at] = matmul(inside[s], stream[start : start + word_length]) / spans[at]

    def entity_rows():
        vectors = vec_all[...].reshape(n_mp * vec_rows.shape[0], seqs * ent_count)
        projection = proj_all[...].reshape(n_mp * vec_rows.shape[0], width)
        value = (contract(vectors, projection, 0, 0) + spanned[...]).astype(BF)
        for s in range(seqs):
            at = s * length + word_length
            stream[at : at + ent_count] = value[s * ent_count : (s + 1) * ent_count]

    pl.semaphore_wait(barrier, n + n_mp - 2)
    received[me_dp] = requests[me_dp]
    asks.start()
    proj_all[me_mp] = ent_proj[...]
    projs.start()

    for target, first_query in ((wt_words, 0), (wt_ents, 2)):
        sources = (query_weight[first_query], query_weight[first_query + 1], w_key[...], w_value[...])
        for g, source in enumerate(sources):
            for h in range(heads):
                target[h, g * DH : (g + 1) * DH] = source[h * DH : (h + 1) * DH]

    def project(s, weight, start, count):
        base = s * length + start
        for h in range(heads):
            value = contract(weight[h], stream[base : base + count], 1, 1)
            qkv[h, 0:128, base : base + count] = (value[0:128] * 0.125).astype(BF)
            qkv[h, 128:256, base : base + count] = value[128:256].astype(BF)

    def attend(s, h):
        cols = pl.ds(s * length, length)
        scores_of(qkv, sT, h, cols, word_length)

        def body(col):
            here = pl.ds(col, LANES)
            words = sT[0:word_length, here] + mask[s]
            ents = sT[word_length:, here]
            top = jnp.maximum(
                jnp.max(words, axis=0, keepdims=True), jnp.max(ents, axis=0, keepdims=True)
            )
            words = jnp.exp(words - top)
            ents = jnp.exp(ents - top)
            total = jnp.sum(words, axis=0, keepdims=True) + jnp.sum(ents, axis=0, keepdims=True)
            pT[0:word_length, here] = words.astype(BF)
            pT[word_length:, here] = ents.astype(BF)
            lse[h, 0:1, pl.ds(pl.multiple_of(s * length + col, LANES), LANES)] = top + jnp.log(total)
            lse[h, 1:2, pl.ds(pl.multiple_of(s * length + col, LANES), LANES)] = 1.0 / total

        each(length, LANES, body)
        value = matmul(qkv[h, 192:256, cols], pT[...]) * lse[h, 1:2, cols]
        ctx[h * DH : (h + 1) * DH, cols] = value.astype(BF)

    def attention_part(s):
        value = contract(ctx[:, s * length : (s + 1) * length], w_out[...], 0, 0)
        part1[s] = value.astype(BF)

    def first_rows(s):
        def body(row):
            at = one.own_row(s, row)
            value = stream[span(at, 16)].astype(F32) + one.total(s, row)
            center = value - jnp.mean(value, axis=-1, keepdims=True)
            mine = span(s * one.quarter + row, 16)
            center1[mine] = center
            normed = center * scaled(center) * norms[0:1] + norms[1:2]
            first[mine] = normed
            first_low[span(at, 16)] = normed.astype(BF)

        each(one.quarter, 16, body, 5)

    def second_rows(s):
        def body(row):
            at = two.own_row(s, row)
            value = first[span(s * two.quarter + row, 16)] + two.total(s, row)
            center = value - jnp.mean(value, axis=-1, keepdims=True)
            center2[span(at, 16)] = center.astype(BF)

        each(two.quarter, 16, body, 5)

    def feed(s):
        rows = slice(s * length, (s + 1) * length)
        tile = 256
        for j in range(units // tile):
            cols = slice(j * tile, (j + 1) * tile)
            pre[...] = matmul(first_low[rows], w_up[:, cols])

            def body(row):
                value = pre[pl.ds(row, 32)]
                bell = lax.erf(value * 0.7071067811865476) * 0.5 + 0.5
                at = span(s * length + row, 32)
                hidden[at, cols] = (value * bell).astype(BF)
                slope[at, cols] = (
                    bell + value * jnp.exp(value * value * -0.5) * 0.3989422804014327
                ).astype(BF)

            each(length, 32, body, 4)
        for j in range(width // tile):
            cols = slice(j * tile, (j + 1) * tile)
            part2[s, :, cols] = matmul(hidden[rows], w_down[:, cols]).astype(BF)

    def output_rows(s):
        def rows_of(row):
            center = center2[span(s * length + row, 16)].astype(F32)
            return (center * scaled(center) * norms[2:3] + norms[3:4]).astype(BF)

        def word_rows(row):
            out_words[s, span(row, 16)] = rows_of(row)

        def ent_rows(row):
            out_ents[s, span(row, 16)] = rows_of(row + word_length)

        each(word_length, 16, word_rows, 4)
        each(ent_count, 16, ent_rows, 4)
        scored = head_in.shape[0] // seqs
        head_in[s * scored : (s + 1) * scored] = out_ents[s, 0:scored]

    for copy in word_copies:
        copy.wait()
    project(0, wt_words, 0, word_length)
    asks.wait()
    answer()
    answered[me_dp] = answers[me_dp]
    backs.start()
    span_means()
    project(1, wt_words, 0, word_length)
    backs.wait()
    collect()
    vecs.start()
    projs.wait()
    vecs.wait()
    entity_rows()
    project(0, wt_ents, word_length, ent_count)
    for h in range(heads):
        attend(0, h)
    attention_part(0)
    one.begin(0)
    project(1, wt_ents, word_length, ent_count)
    attend(1, 0)
    one.pass_on(0)
    for h in range(1, heads):
        attend(1, h)
    attention_part(1)
    one.begin(1)
    one.wait_sum(0)
    first_rows(0)
    one.spread(0)
    one.pass_on(1)
    one.forward(0)
    one.wait_full(0)
    feed(0)
    two.begin(0)
    one.wait_sum(1)
    first_rows(1)
    one.spread(1)
    two.pass_on(0)
    one.forward(1)
    one.wait_full(1)
    feed(1)
    two.begin(1)
    two.wait_sum(0)
    second_rows(0)
    two.spread(0)
    two.pass_on(1)
    two.forward(0)
    two.wait_full(0)
    output_rows(0)
    two.wait_sum(1)
    second_rows(1)
    two.spread(1)
    two.forward(1)
    two.wait_full(1)
    output_rows(1)
    for s in range(seqs):
        one.drain(s)
        two.drain(s)


def quarter_scratch(seqs, length, width):
    return [
        pltpu.VMEM((seqs, length, width), BF),
        pltpu.VMEM((seqs, length // 2, width), BF),
        pltpu.VMEM((seqs, length // 4, width), BF),
        pltpu.VMEM((seqs, length // 4, width), BF),
    ]


def forward_layer(sizes, scored, capacity, words, arrays):
    seqs, length, word_length, heads = sizes
    n, n_mp = lax.axis_size("dp"), lax.axis_size("mp")
    width = words.shape[2]
    tokens = seqs * length
    local, ents = heads * DH, seqs * (length - word_length)
    requests, table, w_up = arrays[0], arrays[2], arrays[11]
    cols_dev, rows_dev = table.shape
    units = w_up.shape[1]

    def like(*shape, dtype=BF):
        return jax.ShapeDtypeStruct(shape, dtype)

    outs = [
        like(*requests.shape, dtype=jnp.int32), like(cols_dev, ents), like(tokens, width),
        like(heads, 4 * DH, tokens), like(heads, 8, tokens, dtype=F32), like(local, tokens),
        like(heads, 4 * DH, width), like(heads, 4 * DH, width), like(tokens // 4, width, dtype=F32),
        like(tokens, width), like(tokens, units), like(tokens, units), like(tokens, width),
        like(seqs, word_length, width), like(seqs, length - word_length, width),
        like(seqs * scored, width),
    ]
    return pl.pallas_call(
        functools.partial(forward_kernel, sizes, n, n_mp, capacity),
        out_shape=outs,
        in_specs=[pl.BlockSpec(memory_space=pl.ANY)] + [VM] * len(arrays),
        out_specs=[VM] * len(outs),
        scratch_shapes=[
            pltpu.VMEM((length, length), F32),
            pltpu.VMEM((length, length), BF),
            pltpu.VMEM((length, 256), F32),
            pltpu.VMEM((tokens // 4, width), F32),
            *quarter_scratch(seqs, length, width),
            *quarter_scratch(seqs, length, width),
            pltpu.VMEM((rows_dev, n * capacity), BF),
            pltpu.VMEM((n, cols_dev, LANES), BF), pltpu.VMEM((n, cols_dev, LANES), BF),
            pltpu.VMEM((n_mp, cols_dev, ents), BF), pltpu.VMEM((n_mp, cols_dev, width), BF),
            pltpu.VMEM((ents, width), F32),
            pltpu.SemaphoreType.DMA((seqs, 5)), pltpu.SemaphoreType.DMA((seqs, 5)),
            pltpu.SemaphoreType.DMA((seqs, 5)), pltpu.SemaphoreType.DMA((seqs, 5)),
            pltpu.SemaphoreType.DMA((seqs,)),
            pltpu.SemaphoreType.DMA((2, n - 1)), pltpu.SemaphoreType.DMA((2, n - 1)),
            pltpu.SemaphoreType.DMA((2, n_mp - 1)), pltpu.SemaphoreType.DMA((2, n_mp - 1)),
        ],
        compiler_params=pltpu.CompilerParams(
            collective_id=3, has_side_effects=True, vmem_limit_bytes=60 * 2**20
        ),
    )(words, *arrays)


class Job:
    def __init__(self, rows, buf, out, arrivals, send, recv, n, first=(0, 1, 2)):
        self.buf, self.out, self.arrivals, self.send, self.recv = buf, out, arrivals, send, recv
        self.rows = rows
        self.me = lax.axis_index("dp")
        self.bits, self.halvings = job_plan(rows, n)
        self.order = list(range(self.bits))
        if self.bits >= len(first):
            self.order[: len(first)] = first

    def bit(self, k):
        return lax.rem(self.me // 2 ** self.order[k], 2)

    def peer(self, k):
        return self.me + (1 - 2 * self.bit(k)) * 2 ** self.order[k]

    def offset(self, k):
        start = 0
        for i in range(k):
            start = start + self.bit(i) * (self.rows >> (i + 1))
        return start

    def copy(self, index, k, src, dst):
        return remote(src, dst, self.send.at[index], self.recv.at[index], "dp", self.peer(k))

    def steps(self):
        size = self.rows
        for k in range(self.bits):
            keep = self.offset(min(k, self.halvings))
            away = keep
            if k < self.halvings:
                size //= 2
                away = keep + (1 - self.bit(k)) * size
                keep = keep + self.bit(k) * size
            arrived = self.arrivals[k]
            copy = self.copy(k, k, self.buf.at[span(away, size)], arrived)
            copy.start()
            yield
            copy.wait()
            last = k == self.bits - 1

            def body(row, keep=keep, arrived=arrived, last=last):
                at = span(keep + row, 16)
                value = self.buf[at].astype(F32) + arrived[span(row, 16)].astype(F32)
                (self.out if last else self.buf)[at] = value.astype(BF)

            each(size, 16, body, 4)
        for k in reversed(range(self.halvings)):
            done = self.out.at[span(self.offset(k + 1), size)]
            copy = self.copy(self.bits + k, k, done, done)
            copy.start()
            yield
            copy.wait()
            size *= 2


def job_plan(rows, n):
    bits, halvings, size = n.bit_length() - 1, 0, rows
    while halvings < bits - 1 and (size // 2) % 16 == 0:
        size, halvings = size // 2, halvings + 1
    return bits, halvings


def job_cuts(units, width, head_rows, proj_rows, heads):
    orders = [
        ((1, 2, 0), (0, 1, 2), (1, 2, 0)),
        ((0, 1, 2), (0, 1, 2), (0, 1, 2)),
        ((1, 0, 2),),
        ((0, 1, 2),),
        ((1, 2, 0), (0, 1, 2)),
        ((0, 1, 2), (0, 1, 2)),
        ((0, 1, 2), (0, 1, 2)),
    ]
    cuts = [(units, [units // 3] * 3), (width, [width // 3] * 3)]
    cuts += [(head_rows, [head_rows]), (proj_rows, [proj_rows])]
    cuts += [(7 * DH, [4 * DH, 3 * DH])] * heads
    return [(rows, pieces, order) for (rows, pieces), order in zip(cuts, orders)]


def job_scratch(rows, width, n):
    bits, halvings = job_plan(rows, n)
    return [
        pltpu.VMEM((rows >> min(k + 1, halvings), width), BF) for k in range(bits)
    ]


def backward_kernel(sizes, n, n_mp, *refs):
    seqs, length, word_length, heads = sizes
    refs = list(refs)

    def take(count):
        taken = refs[:count]
        del refs[:count]
        return taken

    cot_words, cot_ents = take(2)
    (
        d_head, head_grad, center2, slope, hidden, first_low, center1, w_up, w_down, norms,
        small_in, ent_proj, vec_rows, place,
    ) = take(14)
    late_in = take(8)
    down_out, up_out, head_all, proj_out, *per_head_out = take(4 + heads)
    gw, inbox, small = take(3)
    ctx, qkv, lse, wt_words, wt_ents, stream, mask, w_out = late = take(8)
    sums, d_ffn, d_pre, d_attn, d_first, dctx, sT, dpT, pT, dsT, dcat = take(11)
    head_out, small_mp, small_dp, outbox = take(4)
    part, r1, s2, r2 = take(4)
    (
        send1, recv1, send2, recv2, job_send, job_recv, late_sem, cot_sem,
        mp_send, mp_recv, dp_send, dp_recv,
    ) = take(12)
    width = stream.shape[1]
    units = w_up.shape[1]
    me_mp, me_dp = lax.axis_index("mp"), lax.axis_index("dp")
    bits = n.bit_length() - 1
    jobs = []
    groups = [[], [], [], []] + [[] for h in range(heads)]
    buffers = take(len(groups))
    for group, buf, out, (rows, cuts, orders) in zip(
        groups, buffers, [down_out, up_out, head_out, proj_out, *per_head_out],
        job_cuts(units, width, head_out.shape[0], proj_out.shape[0], heads),
    ):
        start = 0
        for count, order in zip(cuts, orders):
            at = pl.ds(start, count)
            start += count
            index = len(jobs)
            jobs.append(
                Job(
                    count, buf.at[at], out.at[at], take(bits), job_send.at[index],
                    job_recv.at[index], n, order,
                )
            )
            group.append(jobs[-1])
    down_jobs, up_jobs, (head_job,), (proj_job,), *heads_jobs = groups
    down_buf, up_buf, head_buf, proj_buf, *heads_buf = buffers
    one = Quarters(part, r1, s2, r2, d_attn, send1, recv1)
    two = Quarters(part, r1, s2, r2, gw, send2, recv2)
    barrier = pltpu.get_barrier_semaphore()
    greet(barrier, "mp", n_mp)
    greet(barrier, "dp", n)
    cots = []
    for s in range(seqs):
        for k, (source, start, count) in enumerate(
            ((cot_words, 0, word_length), (cot_ents, word_length, length - word_length))
        ):
            target = d_attn.at[pl.ds(s * length + start, count)]
            cots.append(pltpu.make_async_copy(source.at[s], target, cot_sem.at[s, k]))
            cots[-1].start()
    late_copies = [
        pltpu.make_async_copy(source, target, late_sem.at[i])
        for i, (source, target) in enumerate(zip(late_in, late))
    ]
    for copy in late_copies:
        copy.start()
    running = {}

    def launch(job):
        running[id(job)] = job.steps()
        next(running[id(job)])

    def step(*which):
        for job in which:
            next(running[id(job)], 0)

    def finish(job):
        for _ in running[id(job)]:
            pass

    sums[...] = jnp.zeros_like(sums)

    spare = d_first.shape[0] - 16

    def second_back(s):
        start = one.own_row(0, 0)

        def rows_of(row, extra=None):
            at = span(s * length + row, 16)
            cot = d_attn[at].astype(F32)
            if extra is not None:
                cot = cot + extra
            center = center2[at].astype(F32)
            inv = scaled(center)
            normed = center * inv
            sums[0] += cot * normed
            sums[1] += cot
            grad = cot * norms[2:3]
            value = inv * (
                grad
                - jnp.mean(grad, axis=-1, keepdims=True)
                - normed * jnp.mean(grad * normed, axis=-1, keepdims=True)
            )
            d_ffn[at] = value.astype(BF)

            own = (row >= start) & (row < start + one.quarter)
            d_first[span(jnp.where(own, s * one.quarter + row - start, spare), 16)] = value

        scored = d_head.shape[1]
        each(word_length, 16, rows_of, 4)
        each(scored, 16, lambda row: rows_of(row + word_length, d_head[s, span(row, 16)]))
        each(length - word_length - scored, 16, lambda row: rows_of(row + word_length + scored), 7)

    def feed_back(s):
        rows = slice(s * length, (s + 1) * length)
        tile = 256
        for j in range(units // tile):
            cols = slice(j * tile, (j + 1) * tile)
            sT[:, 0:tile] = contract(d_ffn[rows], w_down[cols], 1, 1)

            def body(row):
                at = span(s * length + row, 32)
                d_pre[at, cols] = (
                    sT[pl.ds(row, 32), 0:tile] * slope[at, cols].astype(F32)
                ).astype(BF)

            each(length, 32, body, 4)
        for j in range(width // tile):
            cols = slice(j * tile, (j + 1) * tile)
            part[s, :, cols] = contract(d_pre[rows], w_up[cols], 1, 1).astype(BF)

    def first_back(s):
        def body(row):
            at = one.own_row(s, row)
            mine = span(s * one.quarter + row, 16)
            value = d_first[mine] + one.total(s, row)
            center = center1[mine]
            inv = scaled(center)
            normed = center * inv
            sums[2] += value * normed
            sums[3] += value
            grad = value * norms[0:1]
            value = inv * (
                grad
                - jnp.mean(grad, axis=-1, keepdims=True)
                - normed * jnp.mean(grad * normed, axis=-1, keepdims=True)
            )
            d_first[mine] = value
            d_attn[span(at, 16)] = value.astype(BF)

        each(one.quarter, 16, body, 5)

    def context_back(s):
        cols = slice(s * length, (s + 1) * length)
        dctx[:, cols] = contract(w_out[...], d_attn[cols], 1, 1).astype(BF)

    def attend_back(s, h):
        cols = pl.ds(s * length, length)
        w_cols = pl.ds(s * length, word_length)
        e_cols = pl.ds(s * length + word_length, length - word_length)
        mine = slice(h * DH, (h + 1) * DH)
        scores_of(qkv, sT, h, cols, word_length)
        dpT[...] = contract(qkv[h, 192:256, cols], dctx[mine, cols], 0, 0)

        def body(col):
            here = pl.ds(col, LANES)
            at = pl.ds(pl.multiple_of(s * length + col, LANES), LANES)
            delta = jnp.sum(
                ctx[mine, at].astype(F32) * dctx[mine, at].astype(F32), axis=0, keepdims=True
            )
            log_total = lse[h, 0:1, at]
            probs = jnp.exp(sT[0:word_length, here] + mask[s] - log_total)
            pT[0:word_length, here] = probs.astype(BF)
            dsT[0:word_length, here] = (probs * (dpT[0:word_length, here] - delta)).astype(BF)
            probs = jnp.exp(sT[word_length:, here] - log_total)
            pT[word_length:, here] = probs.astype(BF)
            dsT[word_length:, here] = (probs * (dpT[word_length:, here] - delta)).astype(BF)

        each(length, LANES, body)
        d_words, d_ents = dsT[0:word_length], dsT[word_length:]
        dcat[h, 0:64, cols] = (contract(qkv[h, 128:192, w_cols], d_words, 1, 0) * 0.125).astype(BF)
        dcat[h, 64:128, cols] = (contract(qkv[h, 128:192, e_cols], d_ents, 1, 0) * 0.125).astype(BF)
        dcat[h, 128:192, w_cols] = contract(qkv[h, 0:64, cols], d_words, 1, 1).astype(BF)
        dcat[h, 128:192, e_cols] = contract(qkv[h, 64:128, cols], d_ents, 1, 1).astype(BF)
        dcat[h, 192:256, cols] = contract(dctx[mine, cols], pT[...], 1, 1).astype(BF)

    def head_grads(h):
        buf = heads_buf[h]
        from_words, from_ents = None, None
        for s in range(seqs):
            middle, start, end = s * length + word_length, s * length, (s + 1) * length
            words = matmul(dcat[h, :, start:middle], stream[start:middle])
            ents = matmul(dcat[h, :, middle:end], stream[middle:end])
            from_words = words if s == 0 else from_words + words
            from_ents = ents if s == 0 else from_ents + ents
        buf[0:128] = from_words[0:128].astype(BF)
        buf[128:256] = (from_words[128:256] + from_ents[128:256]).astype(BF)
        buf[256:384] = from_ents[0:128].astype(BF)
        buf[384:448] = matmul(ctx[h * DH : (h + 1) * DH], d_attn[...]).astype(BF)

    def stream_part(s):
        for start in range(0, length, LANES):
            weight = wt_words if start < word_length else wt_ents
            cols = slice(s * length + start, s * length + start + LANES)
            value = contract(dcat[0, :, cols], weight[0], 0, 0)
            for h in range(1, heads):
                value = value + contract(dcat[h, :, cols], weight[h], 0, 0)
            part[s, start : start + LANES] = value.astype(BF)

    def last_rows(s):
        def body(row):
            at = two.own_row(s, row)
            value = d_first[span(s * two.quarter + row, 16)] + two.total(s, row)
            gw[span(at, 16)] = value.astype(BF)

        each(two.quarter, 16, body, 5)

    def down_tile(j):
        cols = slice(j * 256, (j + 1) * 256)
        down_buf[cols] = contract(hidden[:, cols], d_ffn[...], 0, 0).astype(BF)

    def up_tile(j):
        cols = slice(j * 256, (j + 1) * 256)
        up_buf[cols] = contract(first_low[:, cols], d_pre[...], 0, 0).astype(BF)

    def wait_cots(s):
        for copy in cots[2 * s : 2 * s + 2]:
            copy.wait()

    def wait_late():
        for copy in late_copies:
            copy.wait()

    small_over_mp = Spread(
        "mp", n_mp, lambda peer: small_mp.at[me_mp], small_mp, mp_send.at[0], mp_recv.at[0]
    )
    small_over_dp = Spread(
        "dp", n, lambda peer: small_dp.at[me_dp], small_dp, dp_send.at[0], dp_recv.at[0]
    )
    boxes = Spread("dp", n, lambda peer: outbox.at[peer], inbox, dp_send.at[1], dp_recv.at[1])
    head_rows = head_out.shape[0]
    head_place = span(me_mp * head_rows, head_rows)

    def head_copy(distance, peer, owner):
        return remote(
            head_out, head_all.at[span(owner * head_rows, head_rows)], mp_send.at[1, distance - 1],
            mp_recv.at[1, distance - 1], "mp", peer,
        )

    def small_first():
        mine = small_in[...]
        mine = mine + jnp.concatenate(
            [jnp.sum(sums[row], axis=0, keepdims=True) for row in range(4)]
            + [jnp.zeros((4, width), F32)]
        )
        small_mp[me_mp] = mine
        small_over_mp.start()

    def small_second():
        small_over_mp.wait()
        total = small_mp[0]
        for device in range(1, n_mp):
            total = total + small_mp[device]
        row = lax.broadcasted_iota(jnp.int32, total.shape, 0)
        small_dp[me_dp] = jnp.where((row == 2) | (row == 3), total, small_mp[me_mp])
        small_over_dp.start()

    def small_last():
        small_over_dp.wait()

        def add(device, total):
            return total + small_dp[device]

        small[...] = lax.fori_loop(1, n, add, small_dp[0])

    def head_first():
        head_all[head_place] = head_out[...]
        for distance in range(1, n_mp):
            head_copy(distance, lax.rem(me_mp + distance, n_mp), me_mp).start()

    def head_last():
        for distance in range(1, n_mp):
            source = lax.rem(me_mp + n_mp - distance, n_mp)
            head_copy(distance, source, source).wait()

    def entities():
        grads, rows = None, []
        count = length - word_length
        for s in range(seqs):
            d_ent = gw[s * length + word_length : (s + 1) * length]
            value = matmul(vec_rows[:, s * count : (s + 1) * count], d_ent)
            grads = value if s == 0 else grads + value
            rows.append(contract(ent_proj[...], d_ent, 1, 1).astype(BF))
        proj_buf[...] = grads.astype(BF)
        launch(proj_job)
        rows = jnp.concatenate(rows, axis=1)
        slot = lax.broadcasted_iota(jnp.int32, (LANES, seqs * count), 0)

        def fill(owner, carry):
            placed = jnp.where(slot + owner * LANES == place[...], 1.0, 0.0).astype(BF)
            outbox[owner] = contract(rows, placed, 1, 1).astype(BF)
            return carry

        lax.fori_loop(0, n, fill, 0)
        inbox[me_dp] = outbox[me_dp]
        boxes.start()

    head_buf[...] = head_grad[head_place]
    wait_cots(0)
    second_back(0)
    feed_back(0)
    pl.semaphore_wait(barrier, n_mp - 1 + n - 1)
    one.begin(0)
    launch(head_job)
    wait_cots(1)
    second_back(1)
    one.pass_on(0)
    step(head_job)
    down_tile(0)
    launch(down_jobs[0])
    down_tile(1)
    launch(down_jobs[1])
    down_tile(2)
    launch(down_jobs[2])
    feed_back(1)
    one.begin(1)
    step(head_job)
    up_tile(0)
    launch(up_jobs[0])
    up_tile(1)
    launch(up_jobs[1])
    up_tile(2)
    launch(up_jobs[2])
    step(down_jobs[0])
    one.pass_on(1)
    step(down_jobs[1], head_job)
    one.wait_sum(0)
    first_back(0)
    one.spread(0)
    step(down_jobs[2], up_jobs[0], down_jobs[1], down_jobs[0])
    one.wait_sum(1)
    first_back(1)
    one.spread(1)
    small_first()
    step(up_jobs[1], up_jobs[0], down_jobs[2])
    one.forward(0)
    step(up_jobs[2], up_jobs[1], head_job, down_jobs[1])
    one.wait_full(0)
    small_second()
    wait_late()
    context_back(0)
    step(down_jobs[0])
    attend_back(0, 0)
    step(up_jobs[2], down_jobs[2], head_job)
    finish(head_job)
    head_first()
    step(up_jobs[0])
    attend_back(0, 1)
    step(down_jobs[1])
    attend_back(0, 2)
    one.first(0).wait_send()
    stream_part(0)
    two.begin(0)
    step(up_jobs[1], up_jobs[0])
    one.forward(1)
    one.wait_full(1)
    one.drain(0, True)
    one.drain(1)
    context_back(1)
    step(down_jobs[1], down_jobs[0], up_jobs[1])
    attend_back(1, 0)
    two.pass_on(0)
    head_grads(0)
    launch(heads_jobs[0][0])
    launch(heads_jobs[0][1])
    step(up_jobs[0], up_jobs[2])
    attend_back(1, 1)
    head_grads(1)
    launch(heads_jobs[1][0])
    launch(heads_jobs[1][1])
    step(down_jobs[0])
    attend_back(1, 2)
    step(up_jobs[1], down_jobs[2])
    stream_part(1)
    two.begin(1)
    head_grads(2)
    launch(heads_jobs[2][0])
    launch(heads_jobs[2][1])
    step(heads_jobs[0][0], heads_jobs[0][1], up_jobs[2])
    two.pass_on(1)
    two.wait_sum(0)
    last_rows(0)
    two.spread(0)
    small_last()
    step(heads_jobs[1][0], down_jobs[2], heads_jobs[0][0], heads_jobs[1][1])
    step(heads_jobs[0][1])
    two.wait_sum(1)
    step(heads_jobs[1][0])
    last_rows(1)
    two.spread(1)
    step(heads_jobs[1][1], heads_jobs[2][0], heads_jobs[0][1], heads_jobs[2][1])
    two.forward(0)
    step(heads_jobs[2][0], heads_jobs[1][0], heads_jobs[0][1], up_jobs[2])
    step(heads_jobs[2][1])
    two.forward(1)
    two.wait_full(0)
    step(heads_jobs[1][1], heads_jobs[0][0], heads_jobs[1][0])
    two.wait_full(1)
    entities()
    step(heads_jobs[1][1], heads_jobs[0][1], heads_jobs[2][0], heads_jobs[2][1])
    step(heads_jobs[1][0], heads_jobs[2][0], proj_job, heads_jobs[2][1])
    step(proj_job, heads_jobs[0][0], heads_jobs[1][1], proj_job)
    step(heads_jobs[2][0], heads_jobs[0][0], proj_job, heads_jobs[2][1])
    step(proj_job)
    boxes.wait()
    head_last()
    for s in range(seqs):
        two.drain(s)
    for job in jobs:
        finish(job)


def backward_layer(sizes, n, cots, now, late):
    seqs, length, word_length, heads = sizes
    stream, w_up, ent_proj = late[5], now[7], now[11]
    n_mp = lax.axis_size("mp")
    tokens, width = stream.shape
    units, local = w_up.shape[1], heads * DH
    head_rows, head_width = now[1].shape[0] // n_mp, now[1].shape[1]
    bits = n.bit_length() - 1
    outs = [(units, width), (width, units), (n_mp * head_rows, head_width), ent_proj.shape]
    outs += [(7 * DH, width)] * heads + [(tokens, width), (n, ent_proj.shape[0], LANES)]
    outs = [jax.ShapeDtypeStruct(shape, BF) for shape in outs]
    outs.append(jax.ShapeDtypeStruct((8, width), F32))
    cuts = job_cuts(units, width, head_rows, ent_proj.shape[0], heads)
    widths = [width, units, head_width] + [width] * (1 + heads)
    job_count = sum(len(sizes) for _, sizes, _ in cuts)
    scratch = [pltpu.VMEM(value.shape, value.dtype) for value in late]
    scratch += [
        pltpu.VMEM((4, 16, width), F32), pltpu.VMEM((tokens, width), BF),
        pltpu.VMEM((tokens, units), BF), pltpu.VMEM((tokens, width), BF),
        pltpu.VMEM((tokens // 4 + 16, width), F32), pltpu.VMEM((local, tokens), BF),
        pltpu.VMEM((length, length), F32), pltpu.VMEM((length, length), F32),
        pltpu.VMEM((length, length), BF), pltpu.VMEM((length, length), BF),
        pltpu.VMEM((heads, 4 * DH, tokens), BF),
        pltpu.VMEM((head_rows, head_width), BF), pltpu.VMEM((n_mp, 8, width), F32),
        pltpu.VMEM((n, 8, width), F32), pltpu.VMEM((n, ent_proj.shape[0], LANES), BF),
        *quarter_scratch(seqs, length, width),
        pltpu.SemaphoreType.DMA((seqs, 5)), pltpu.SemaphoreType.DMA((seqs, 5)),
        pltpu.SemaphoreType.DMA((seqs, 5)), pltpu.SemaphoreType.DMA((seqs, 5)),
        pltpu.SemaphoreType.DMA((job_count, 2 * bits)),
        pltpu.SemaphoreType.DMA((job_count, 2 * bits)),
        pltpu.SemaphoreType.DMA((len(late),)), pltpu.SemaphoreType.DMA((seqs, 2)),
        pltpu.SemaphoreType.DMA((2, n_mp - 1)), pltpu.SemaphoreType.DMA((2, n_mp - 1)),
        pltpu.SemaphoreType.DMA((2, n - 1)), pltpu.SemaphoreType.DMA((2, n - 1)),
    ]
    scratch += [pltpu.VMEM((rows, columns), BF) for (rows, _, _), columns in zip(cuts, widths)]
    for (_, counts, _), columns in zip(cuts, widths):
        for count in counts:
            scratch += job_scratch(count, columns, n)
    hbm = pl.BlockSpec(memory_space=pl.ANY)
    return pl.pallas_call(
        functools.partial(backward_kernel, sizes, n, n_mp),
        out_shape=outs,
        in_specs=[hbm] * len(cots) + [VM] * len(now) + [hbm] * len(late),
        out_specs=[VM] * len(outs),
        scratch_shapes=scratch,
        compiler_params=pltpu.CompilerParams(
            collective_id=7, has_side_effects=True, vmem_limit_bytes=61 * 2**20
        ),
    )(*cots, *now, *late)


def chunks_of(total, size):
    return [(start, min(size, total - start)) for start in range(0, total, size)]


def head_kernel(
    n, head_in, w_head, gain, table, target, d_head, grad_head, small, loss, table_grad,
    all_head, logits, probs, onehot, turned, tops, parts_out, parts_in, rows_out, rows_in,
    stats_out, stats_in, send, recv,
):
    me_dp, me_mp = lax.axis_index("dp"), lax.axis_index("mp")
    mine, vec_width = all_head.shape[1:]
    total = n * mine
    rows_dev = table.shape[1]
    cols_dev = table_grad.shape[0]
    block = logits.shape[0]
    blocks = total // block
    owners = block // mine
    barrier = pltpu.get_barrier_semaphore()
    greet(barrier, "dp", n)

    pre = matmul(head_in[...], w_head[...])
    bell = lax.erf(pre * 0.7071067811865476) * 0.5 + 0.5
    value = pre * bell
    center = value - jnp.mean(value, axis=-1, keepdims=True)
    inv = scaled(center)
    normed = center * inv
    all_head[me_dp] = (normed * gain[...]).astype(BF)
    pl.semaphore_wait(barrier, n - 1)
    heads = Spread("dp", n, lambda peer: all_head.at[me_dp], all_head, send.at[0], recv.at[0])
    heads.start()

    def fill_onehot(b):
        wanted = target[b]

        def body(row):
            index = lax.broadcasted_iota(jnp.int32, (80, block), 0) + row
            onehot[span(row, 80)] = jnp.where(index == wanted, 1.0, 0.0).astype(BF)

        each(rows_dev, 80, body)

    def slots_of(b):
        return all_head[pl.ds(b * owners, owners)].reshape(block, vec_width)

    def fill_probs(b):
        slots = slots_of(b)
        for start, count in chunks_of(rows_dev, 1024):
            logits[:, start : start + count] = matmul(slots, table[:, start : start + count])

        def body(row):
            x = logits[span(row, 16)]
            top = jnp.max(x, axis=-1, keepdims=True)
            x = jnp.exp(x - top)
            lane = lax.broadcasted_iota(jnp.int32, (16, LANES), 1)
            amount = jnp.sum(x, axis=-1, keepdims=True)
            tops[span(row, 16)] = jnp.where(lane == 0, top, jnp.where(lane == 1, amount, 0.0))
            probs[span(row, 16)] = x.astype(BF)

        each(block, 16, body, 2)

    def over_blocks(body):
        if blocks == 1:
            body(0)
        else:
            lax.fori_loop(0, blocks, lambda b, carry: (body(b), carry)[1], 0)

    def target_part(b):
        fill_onehot(b)
        found = matmul(table[...], onehot[...])
        turned[...] = found
        rows = jnp.transpose(found).astype(BF).reshape(owners, mine, vec_width)
        rows_out[pl.ds(b * owners, owners)] = rows

    def block_part(b):
        if blocks > 1:
            target_part(b)
        slots = jnp.transpose(slots_of(b).astype(F32))
        own = jnp.sum(slots * turned[...], axis=0, keepdims=True)
        fill_probs(b)
        part = contract(probs[...], table[...], 1, 1)
        at = pl.ds(b * owners, owners)
        parts_out[at, :, 0:vec_width] = part.reshape(owners, mine, vec_width)
        parts_out[at, :, vec_width:] = tops[...].reshape(owners, mine, LANES)
        columns = pl.ds(pl.multiple_of(b * block, LANES), block)
        stats_out[0:2, columns] = jnp.transpose(tops[...])[0:2]
        stats_out[2:3, columns] = own

    if blocks == 1:
        target_part(0)
    heads.wait()
    stats_out[...] = jnp.zeros_like(stats_out)
    over_blocks(block_part)
    exchanges = [
        Spread("dp", n, lambda peer: parts_out.at[peer], parts_in, send.at[1], recv.at[1]),
        Spread("dp", n, lambda peer: rows_out.at[peer], rows_in, send.at[2], recv.at[2]),
        Spread("dp", n, lambda peer: stats_out, stats_in, send.at[3], recv.at[3]),
    ]
    for exchange_one in exchanges:
        exchange_one.start()
    parts_in[me_dp] = parts_out[me_dp]
    rows_in[me_dp] = rows_out[me_dp]
    stats_in[me_dp] = stats_out[...]
    for exchange_one in exchanges:
        exchange_one.wait()

    def combine(source, state):
        top, amount, sums, targets = state
        part = parts_in[source]
        other = part[:, vec_width : vec_width + 1]
        new_top = jnp.maximum(top, other)
        old, new = jnp.exp(top - new_top), jnp.exp(other - new_top)
        amount = amount * old + part[:, vec_width + 1 : vec_width + 2] * new
        sums = sums * old + part[:, 0:vec_width] * new
        return new_top, amount, sums, targets + rows_in[source].astype(F32)

    first = parts_in[0]
    state = (
        first[:, vec_width : vec_width + 1], first[:, vec_width + 1 : vec_width + 2],
        first[:, 0:vec_width], rows_in[0].astype(F32),
    )
    _, amount, sums, targets = lax.fori_loop(1, n, combine, state)
    d_vec = sums / amount - targets
    small[...] = jnp.zeros_like(small)
    small[4:5, 0:vec_width] = jnp.sum(d_vec * normed, axis=0, keepdims=True)
    grad = d_vec * gain[...]
    d_value = inv * (
        grad
        - jnp.mean(grad, axis=-1, keepdims=True)
        - normed * jnp.mean(grad * normed, axis=-1, keepdims=True)
    )
    d_pre = d_value * (bell + pre * jnp.exp(pre * pre * -0.5) * 0.3989422804014327)
    d_low = d_pre.astype(BF)
    d_head[...] = contract(d_low, w_head[...], 1, 1)
    grad_head[...] = contract(head_in[...], d_low, 0, 0).astype(BF)

    def stat(row):
        def top_of(source, top):
            return jnp.maximum(top, stats_in[source, 0:1])

        top = lax.fori_loop(1, n, top_of, stats_in[0, 0:1])

        def add(source, state):
            amount, targets = state
            amount = amount + stats_in[source, 1:2] * jnp.exp(stats_in[source, 0:1] - top)
            return amount, targets + stats_in[source, 2:3]

        zero = jnp.zeros_like(top)
        amount, targets = lax.fori_loop(0, n, add, (zero, zero))
        return top + jnp.log(amount), targets

    log_total, targets = stat(0)
    loss[...] = jnp.broadcast_to(log_total - targets, loss.shape)
    stats_out[3:4] = jnp.exp(stats_out[0:1] - log_total)

    def table_part(b):
        if blocks > 1:
            fill_onehot(b)
            fill_probs(b)
        columns = pl.ds(pl.multiple_of(b * block, LANES), block)
        turned[...] = jnp.transpose(slots_of(b).astype(F32))
        own = turned[span(me_mp * cols_dev, cols_dev)]
        scaled_own = (own * stats_out[3:4, columns]).astype(BF)
        own = own.astype(BF)
        for start, count in chunks_of(rows_dev, 1024):
            at = slice(start, start + count)
            value = matmul(scaled_own, probs[:, at]) - contract(own, onehot[at], 1, 1)
            if blocks == 1:
                table_grad[:, at] = value
            else:
                table_grad[:, at] += value

    if blocks > 1:
        table_grad[...] = jnp.zeros_like(table_grad)
    over_blocks(table_part)


def head_layer(n, head_in, w_head, gain, table, target, cols_dev):
    mine, width = head_in.shape
    vec_width = w_head.shape[1]
    total = n * mine
    rows_dev = table.shape[1]
    block = math.gcd(total, 256)
    shapes = [
        ((mine, width), F32), ((width, vec_width), BF), ((8, width), F32), ((8, total), F32),
        ((cols_dev, rows_dev), F32),
    ]
    return pl.pallas_call(
        functools.partial(head_kernel, n),
        out_shape=[jax.ShapeDtypeStruct(*shape) for shape in shapes],
        in_specs=[VM] * 5,
        out_specs=[VM] * 5,
        scratch_shapes=[
            pltpu.VMEM((n, mine, vec_width), BF), pltpu.VMEM((block, rows_dev), F32),
            pltpu.VMEM((block, rows_dev), BF), pltpu.VMEM((rows_dev, block), BF),
            pltpu.VMEM((vec_width, block), F32), pltpu.VMEM((block, LANES), F32),
            pltpu.VMEM((n, mine, vec_width + LANES), F32), pltpu.VMEM((n, mine, vec_width + LANES), F32),
            pltpu.VMEM((n, mine, vec_width), BF), pltpu.VMEM((n, mine, vec_width), BF),
            pltpu.VMEM((8, total), F32), pltpu.VMEM((n, 8, total), F32),
            pltpu.SemaphoreType.DMA((4, n - 1)), pltpu.SemaphoreType.DMA((4, n - 1)),
        ],
        compiler_params=pltpu.CompilerParams(
            collective_id=5, has_side_effects=True, vmem_limit_bytes=56 * 2**20
        ),
    )(head_in, w_head, gain, table, target.reshape(total // block, 1, block))


def shards(
    words, word_extra, span_pos, span_len, entity_shard, entity_row, targets, table, ent_proj,
    query_weight, w_key, w_value, w_out, gain_attn, bias_attn, w_up, w_down, gain_ffn, bias_ffn,
    w_head, gain_head, cot_words, cot_ents,
):
    n_dp = lax.axis_size("dp")
    n_mp = lax.axis_size("mp")
    seq_count, word_length, model_width = words.shape
    ent_len = span_pos.shape[1]
    masked_len = targets.shape[1]
    tokens_len = word_length + ent_len
    rows_dev, cols_dev = table.shape
    local_width = w_key.shape[1]
    heads_local = local_width // DH
    ent_total = seq_count * ent_len
    table_rows = lax.all_gather(table.T, "mp", axis=0, tiled=True)

    owners = entity_shard.reshape(ent_total)
    wanted = entity_row.reshape(ent_total)
    capacity = max(16, 2 * ent_total // n_dp)
    owner_onehot = (owners[:, None] == jnp.arange(n_dp, dtype=jnp.int32)[None, :]).astype(BF)
    order_index = jnp.arange(ent_total, dtype=jnp.int32)
    earlier = (order_index[:, None] > order_index[None, :]).astype(BF)
    before = matmul(earlier, owner_onehot)
    slot_rank = jnp.sum(before * owner_onehot.astype(F32), axis=1).astype(jnp.int32)
    place = (owners * LANES + slot_rank)[None]
    taken = place[0][:, None] == jnp.arange(n_dp * LANES, dtype=jnp.int32)[None, :]
    requests = jnp.sum(jnp.where(taken, wanted[:, None] + 1, 0), axis=0) - 1
    requests = jnp.broadcast_to(requests.reshape(n_dp, 1, LANES), (n_dp, 8, LANES))

    word_count = word_length // 8 + word_extra
    span_start = span_pos * (word_count[:, None] - SPANW) // word_length
    positions = jnp.arange(word_length, dtype=jnp.int32)
    inside = (positions[None, None, :] >= span_start[..., None]) & (
        positions[None, None, :] < (span_start + span_len)[..., None]
    )
    span_width = span_len.astype(F32)[..., None]
    key_valid = positions[None, :] < word_count[:, None]
    mask = jnp.broadcast_to(
        jnp.where(key_valid, 0.0, MASKED_SCORE)[..., None], (seq_count, word_length, LANES)
    )
    norms = jnp.stack([gain_attn, bias_attn, gain_ffn, bias_ffn])
    sizes = (seq_count, tokens_len, word_length, heads_local)
    (
        received, vec_rows, stream, qkv, lse, ctx, wt_words, wt_ents, center1, first_low, hidden, slope,
        center2, out_words, out_ents, head_in,
    ) = forward_layer(
        sizes, masked_len, capacity, words,
        (
            requests, place, table.T, ent_proj, inside.astype(BF), span_width.reshape(ent_total, 1),
            query_weight.transpose(0, 2, 1), w_key.T, w_value.T, mask, w_out, w_up, w_down, norms,
        ),
    )
    local_target = targets.reshape(-1) - lax.axis_index("dp") * rows_dev
    d_head, grad_head, small, loss, table_grad = head_layer(
        n_dp, head_in, w_head, gain_head[None], table_rows, local_target, cols_dev
    )
    loss = loss[0]
    *sums, d_total, inbox, small = backward_layer(
        sizes, n_dp,
        (cot_words, cot_ents),
        (
            d_head.reshape(seq_count, masked_len, model_width), grad_head, center2, slope, hidden,
            first_low, center1, w_up, w_down, norms, small, ent_proj, vec_rows, place,
        ),
        (
            ctx, qkv, lse, wt_words, wt_ents, stream, mask, w_out,
        ),
    )
    grad_down, grad_up, grad_head, grad_ent_proj, *per_head = (a.astype(F32) for a in sums)
    per_head = [a.reshape(7, DH, model_width) for a in per_head]

    def columns_of(which):
        return jnp.concatenate([a[which] for a in per_head])

    grad_query = jnp.stack([columns_of(i) for i in (0, 1, 4, 5)]).transpose(0, 2, 1)
    grad_key, grad_value, grad_out = columns_of(2).T, columns_of(3).T, columns_of(6)
    d_total = d_total.reshape(seq_count, tokens_len, model_width)
    d_ent = d_total[:, word_length:]
    grad_words = d_total[:, :word_length].astype(F32) + contract_product(
        "sep,sed->spd", inside.astype(BF), (d_ent.astype(F32) / span_width).astype(BF)
    )
    row_index = jnp.arange(rows_dev, dtype=jnp.int32)
    received = received[:, 0, :capacity]
    hit_rows = inbox[:, :, :capacity].transpose(1, 0, 2).reshape(cols_dev, -1)
    table_grad = table_grad + contract_product(
        "ct,tr->cr", hit_rows, (received.reshape(-1)[:, None] == row_index[None, :]).astype(BF)
    )
    table_grad = table_grad.T
    grad_gain_ffn, grad_bias_ffn, grad_gain_attn, grad_bias_attn = (small[i] for i in range(4))
    grad_gain_head = small[4, : w_head.shape[1]]
    return (
        out_words, out_ents, loss, grad_words, table_grad, grad_ent_proj, grad_query, grad_key,
        grad_value, grad_out, grad_gain_attn, grad_bias_attn, grad_up, grad_down, grad_gain_ffn,
        grad_bias_ffn, grad_head, grad_gain_head,
    )


def solution(mesh):
    return jax.shard_map(
        shards,
        mesh=mesh,
        in_specs=(
            P("dp", None, None), P("dp"), P("dp", None), P("dp", None), P("dp", None, None),
            P("dp", None), P(), P("dp", "mp"), P("mp", None), P(None, None, "mp"), P(None, "mp"),
            P(None, "mp"), P("mp", None), P(), P(), P(None, "mp"), P("mp", None), P(), P(), P(),
            P(), P("dp", None, None), P("dp", None, None),
        ),
        out_specs=(
            P("dp", None, None), P("dp", None, None), P(), P("dp", None, None), P("dp", "mp"),
            P("mp", None), P(None, None, "mp"), P(None, "mp"), P(None, "mp"), P("mp", None), P(),
            P(), P(None, "mp"), P("mp", None), P(), P(), P(), P(),
        ),
        check_vma=False,
    )
```

```python
import functools
import math

import jax
import jax.numpy as jnp
from jax import lax
from jax.experimental import pallas as pl
from jax.experimental.pallas import tpu as pltpu
from jax.sharding import PartitionSpec as P

DH = 64
SPANW = 4
EPSILON = 1e-05
MASKED_SCORE = -1000000000.0
LANES = 128
BF = jnp.bfloat16
F32 = jnp.float32
MESH = pl.DeviceIdType.MESH
VM = pl.BlockSpec(memory_space=pltpu.VMEM)


def matmul(first_op, second_op):
    return jnp.dot(first_op, second_op, preferred_element_type=F32)


def normalize(source, gain_vec, shift_vec):
    center = source - jnp.mean(source, axis=-1, keepdims=True)
    inv_scale = lax.rsqrt(jnp.mean(center * center, axis=-1, keepdims=True) + EPSILON)
    return center * inv_scale * gain_vec + shift_vec


def gelu_exact(source):
    return jax.nn.gelu(source, approximate=False)


def remote(src, dst, send, recv, axis, peer):
    return pltpu.make_async_remote_copy(
        src_ref=src, dst_ref=dst, send_sem=send, recv_sem=recv,
        device_id={axis: peer}, device_id_type=MESH,
    )


def contract(first_op, second_op, first_dim, second_dim):
    return lax.dot_general(
        first_op, second_op, (((first_dim,), (second_dim,)), ((), ())), preferred_element_type=F32
    )


def span(start, count):
    return pl.ds(pl.multiple_of(start, 16), count)


def each(count, step, body, unroll=1):
    while count // step % unroll:
        unroll -= 1

    def run(index, carry):
        for i in range(unroll):
            body(pl.multiple_of((index * unroll + i) * step, step))
        return carry

    lax.fori_loop(0, count // step // unroll, run, 0)


class Quarters:
    def __init__(self, part, r1, s2, r2, full, send, recv):
        self.part, self.r1, self.s2, self.r2, self.full = part, r1, s2, r2, full
        self.send, self.recv = send, recv
        me = lax.axis_index("mp")
        self.b0, self.b1 = lax.rem(me, 2), me // 2
        self.p1, self.p2 = me + 1 - 2 * self.b0, lax.rem(me + 2, 4)
        self.length = part.shape[1]
        self.half = self.length // 2
        self.quarter = self.length // 4

    def copy(self, s, k, src, dst, peer):
        return remote(src, dst, self.send.at[s, k], self.recv.at[s, k], "mp", peer)

    def first(self, s):
        rows = span((1 - self.b0) * self.half, self.half)
        return self.copy(s, 0, self.part.at[s, rows], self.r1.at[s], self.p1)

    def second(self, s):
        return self.copy(s, 1, self.s2.at[s], self.r2.at[s], self.p2)

    def place(self, s, h, q):
        return self.full.at[span(s * self.length + h * self.half + q * self.quarter, self.quarter)]

    def third(self, s, q):
        return self.copy(s, 2, self.place(s, self.b0, q), self.place(s, self.b0, q), self.p2)

    def fourth(self, s, h):
        return self.copy(s, 3, self.place(s, h, self.b1), self.place(s, h, self.b1), self.p1)

    def fifth(self, s, h):
        q = 1 - self.b1
        return self.copy(s, 4, self.place(s, h, q), self.place(s, h, q), self.p1)

    def both(self, s, q, row):
        mine = self.part[s, span(self.b0 * self.half + q * self.quarter + row, 16)]
        return mine.astype(F32) + self.r1[s, span(q * self.quarter + row, 16)].astype(F32)

    def begin(self, s):
        self.first(s).start()

    def pass_on(self, s):
        self.first(s).wait_recv()

        def body(row):
            self.s2[s, span(row, 16)] = self.both(s, 1 - self.b1, row).astype(BF)

        each(self.quarter, 16, body, 5)
        self.second(s).start()

    def wait_sum(self, s):
        self.second(s).wait_recv()

    def total(self, s, row):
        return self.both(s, self.b1, row) + self.r2[s, span(row, 16)].astype(F32)

    def own_row(self, s, row):
        return s * self.length + self.b0 * self.half + self.b1 * self.quarter + row

    def spread(self, s):
        self.third(s, self.b1).start()
        self.fourth(s, self.b0).start()

    def forward(self, s):
        self.third(s, 1 - self.b1).wait_recv()
        self.fifth(s, self.b0).start()

    def wait_full(self, s):
        self.fourth(s, 1 - self.b0).wait_recv()
        self.fifth(s, 1 - self.b0).wait_recv()

    def drain(self, s, sent=False):
        if not sent:
            self.first(s).wait_send()
        self.second(s).wait_send()
        self.third(s, self.b1).wait_send()
        self.fourth(s, self.b0).wait_send()
        self.fifth(s, self.b0).wait_send()


class Spread:
    def __init__(self, axis, n, source_of, into, send, recv):
        self.axis, self.n, self.source_of, self.into = axis, n, source_of, into
        self.send, self.recv = send, recv
        self.me = lax.axis_index(axis)

    def copy(self, step, peer, slot):
        return remote(
            self.source_of(peer), self.into.at[slot], self.send.at[step - 1], self.recv.at[step - 1],
            self.axis, peer,
        )

    def start(self):
        def begin(step, carry):
            self.copy(step, lax.rem(self.me + step, self.n), self.me).start()
            return carry

        lax.fori_loop(1, self.n, begin, 0)

    def wait(self):
        def finish(step, carry):
            source = lax.rem(self.me + self.n - step, self.n)
            self.copy(step, source, source).wait()
            return carry

        lax.fori_loop(1, self.n, finish, 0)


def greet(barrier, axis, n):
    me = lax.axis_index(axis)

    def signal(step, carry):
        pl.semaphore_signal(
            barrier, inc=1, device_id={axis: lax.rem(me + step, n)}, device_id_type=MESH
        )
        return carry

    lax.fori_loop(1, n, signal, 0)


def chunks_of(total, size):
    return [(start, min(size, total - start)) for start in range(0, total, size)]


def scaled(center):
    return lax.rsqrt(jnp.mean(center * center, axis=-1, keepdims=True) + EPSILON)


def scores_of(qkv, sT, h, cols, word_length):
    k_cols = pl.ds(cols.start, word_length), pl.ds(cols.start + word_length, cols.size - word_length)
    sT[0:word_length] = contract(qkv[h, 128:192, k_cols[0]], qkv[h, 0:64, cols], 0, 0)
    sT[word_length:] = contract(qkv[h, 128:192, k_cols[1]], qkv[h, 64:128, cols], 0, 0)


def forward_kernel(
    sizes, n, n_mp, capacity,
    words, word_extra, span_pos, span_len, shard, wanted, table, ent_proj, query_weight, w_key, w_value,
    w_out, w_up, w_down, gain_attn, bias_attn, gain_ffn, bias_ffn,
    received, place, inside, spans, mask, norms, vec_rows, stream, qkv, lse, ctx, wt_words, wt_ents, center1, first_low, hidden, slope,
    center2, out_words, out_ents, head_in,
    sT, pT, pre, first, part1, r11, s21, r21, part2, r12, s22, r22,
    onehot, answers, answered, vec_all, proj_all, spanned, requests,
    send1, recv1, send2, recv2, word_sem, dp_send, dp_recv, mp_send, mp_recv,
):
    seqs, length, word_length, heads = sizes
    width = stream.shape[1]
    me_dp, me_mp = lax.axis_index("dp"), lax.axis_index("mp")
    units = w_up.shape[1]
    one = Quarters(part1, r11, s21, r21, first_low, send1, recv1)
    two = Quarters(part2, r12, s22, r22, center2, send2, recv2)
    barrier = pltpu.get_barrier_semaphore()
    greet(barrier, "dp", n)
    greet(barrier, "mp", n_mp)
    word_copies = [
        pltpu.make_async_copy(
            words.at[s], stream.at[pl.ds(s * length, word_length)], word_sem.at[s]
        )
        for s in range(seqs)
    ]
    for copy in word_copies:
        copy.start()
    asks = Spread("dp", n, lambda peer: requests.at[peer], received, dp_send.at[0], dp_recv.at[0])
    backs = Spread("dp", n, lambda peer: answers.at[peer], answered, dp_send.at[1], dp_recv.at[1])
    projs = Spread("mp", n_mp, lambda peer: ent_proj, proj_all, mp_send.at[0], mp_recv.at[0])
    vecs = Spread(
        "mp", n_mp, lambda peer: vec_all.at[me_mp], vec_all, mp_send.at[1], mp_recv.at[1]
    )
    ent_count = length - word_length
    ents = seqs * ent_count

    def rows_joined(ref):
        return jnp.concatenate([ref[s : s + 1] for s in range(seqs)], axis=1)

    def prepare():
        owner = rows_joined(shard).astype(F32)
        owner_of = jnp.transpose(jnp.broadcast_to(owner, (ents, ents)))
        earlier = lax.broadcasted_iota(jnp.int32, (ents, ents), 0) < lax.broadcasted_iota(
            jnp.int32, (ents, ents), 1
        )
        rank = jnp.sum(jnp.where(earlier & (owner_of == owner), 1.0, 0.0), axis=0, keepdims=True)
        spot = owner * LANES + rank
        place[...] = spot.astype(jnp.int32)
        spot_of = jnp.transpose(jnp.broadcast_to(spot, (LANES, ents)))
        row_of = jnp.transpose(jnp.broadcast_to(rows_joined(wanted).astype(F32) + 1.0, (LANES, ents)))
        lane = lax.broadcasted_iota(jnp.int32, (ents, LANES), 1).astype(F32)

        def ask_of(peer, carry):
            first_spot = (peer * LANES).astype(F32)
            asked = jnp.where(spot_of == lane + first_spot, row_of, 0.0)
            asked = jnp.sum(asked, axis=0, keepdims=True) - 1.0
            requests[peer] = jnp.broadcast_to(asked.astype(jnp.int32), (8, LANES))
            return carry

        lax.fori_loop(0, n, ask_of, 0)

    def prepare_spans():
        for row, source in enumerate((gain_attn, bias_attn, gain_ffn, bias_ffn)):
            norms[row : row + 1] = source[...].reshape(1, width)
        for s in range(seqs):
            count = word_length // 8 + word_extra[s]
            position = lax.broadcasted_iota(jnp.int32, (word_length, LANES), 0)
            mask[s] = jnp.where(position < count, 0.0, MASKED_SCORE)
            many = span_len[s : s + 1]
            start = lax.shift_right_logical(
                span_pos[s : s + 1] * (count - SPANW), word_length.bit_length() - 1
            )
            position = lax.broadcasted_iota(jnp.int32, (word_length, ent_count), 0)
            within = (position >= start) & (position < start + many)
            inside[s] = jnp.where(within, 1.0, 0.0).astype(BF)
            spans[s * ent_count : (s + 1) * ent_count] = jnp.transpose(
                jnp.broadcast_to(many.astype(F32), (LANES, ent_count))
            )

    def answer():
        ids = jnp.concatenate([received[source, 0:1, 0:capacity] for source in range(n)], axis=1)

        def body(row):
            index = lax.broadcasted_iota(jnp.int32, (80, n * capacity), 0) + row
            onehot[span(row, 80)] = jnp.where(index == ids, 1.0, 0.0).astype(BF)

        each(table.shape[1], 80, body)
        found = matmul(table[...], onehot[...]).astype(BF)
        for source in range(n):
            answers[source, :, 0:capacity] = found[:, source * capacity : (source + 1) * capacity]

    def collect():
        slot = lax.broadcasted_iota(jnp.int32, (capacity, seqs * ent_count), 0)

        def add(owner, total):
            placed = jnp.where(slot + owner * LANES == place[...], 1.0, 0.0).astype(BF)
            return total + matmul(answered[owner, :, 0:capacity], placed)

        total = lax.fori_loop(0, n, add, jnp.zeros(vec_rows.shape, F32))
        vec_rows[...] = total.astype(BF)
        vec_all[me_mp] = total.astype(BF)

    def span_means():
        for s in range(seqs):
            at = slice(s * ent_count, (s + 1) * ent_count)
            start = s * length
            spanned[at] = (
                contract(inside[s], stream[start : start + word_length], 0, 0) / spans[at, 0:1]
            )

    def entity_rows():
        vectors = vec_all[...].reshape(n_mp * vec_rows.shape[0], seqs * ent_count)
        projection = proj_all[...].reshape(n_mp * vec_rows.shape[0], width)
        value = (contract(vectors, projection, 0, 0) + spanned[...]).astype(BF)
        for s in range(seqs):
            at = s * length + word_length
            stream[at : at + ent_count] = value[s * ent_count : (s + 1) * ent_count]

    prepare()
    pl.semaphore_wait(barrier, n + n_mp - 2)
    received[me_dp] = requests[me_dp]
    asks.start()
    proj_all[me_mp] = ent_proj[...]
    projs.start()
    prepare_spans()

    for target, first_query in ((wt_words, 0), (wt_ents, 2)):
        sources = (query_weight[first_query], query_weight[first_query + 1], w_key[...], w_value[...])
        for g, source in enumerate(sources):
            for h in range(heads):
                target[h, g * DH : (g + 1) * DH] = source[h * DH : (h + 1) * DH]

    def project(s, weight, start, count):
        base = s * length + start
        for h in range(heads):
            value = contract(weight[h], stream[base : base + count], 1, 1)
            qkv[h, 0:128, base : base + count] = (value[0:128] * 0.125).astype(BF)
            qkv[h, 128:256, base : base + count] = value[128:256].astype(BF)

    def attend(s, h):
        cols = pl.ds(s * length, length)
        scores_of(qkv, sT, h, cols, word_length)

        def body(col):
            here = pl.ds(col, LANES)
            words = sT[0:word_length, here] + mask[s]
            ents = sT[word_length:, here]
            top = jnp.maximum(
                jnp.max(words, axis=0, keepdims=True), jnp.max(ents, axis=0, keepdims=True)
            )
            words = jnp.exp(words - top)
            ents = jnp.exp(ents - top)
            total = jnp.sum(words, axis=0, keepdims=True) + jnp.sum(ents, axis=0, keepdims=True)
            pT[0:word_length, here] = words.astype(BF)
            pT[word_length:, here] = ents.astype(BF)
            lse[h, 0:1, pl.ds(pl.multiple_of(s * length + col, LANES), LANES)] = top + jnp.log(total)
            lse[h, 1:2, pl.ds(pl.multiple_of(s * length + col, LANES), LANES)] = 1.0 / total

        each(length, LANES, body)
        value = matmul(qkv[h, 192:256, cols], pT[...]) * lse[h, 1:2, cols]
        ctx[h * DH : (h + 1) * DH, cols] = value.astype(BF)

    def attention_part(s):
        value = contract(ctx[:, s * length : (s + 1) * length], w_out[...], 0, 0)
        part1[s] = value.astype(BF)

    def first_rows(s):
        def body(row):
            at = one.own_row(s, row)
            value = stream[span(at, 16)].astype(F32) + one.total(s, row)
            center = value - jnp.mean(value, axis=-1, keepdims=True)
            mine = span(s * one.quarter + row, 16)
            center1[mine] = center
            normed = center * scaled(center) * norms[0:1] + norms[1:2]
            first[mine] = normed
            first_low[span(at, 16)] = normed.astype(BF)

        each(one.quarter, 16, body, 5)

    def second_rows(s):
        def body(row):
            at = two.own_row(s, row)
            value = first[span(s * two.quarter + row, 16)] + two.total(s, row)
            center = value - jnp.mean(value, axis=-1, keepdims=True)
            center2[span(at, 16)] = center.astype(BF)

        each(two.quarter, 16, body, 5)

    def feed(s):
        rows = slice(s * length, (s + 1) * length)
        tile = 256
        for j in range(units // tile):
            cols = slice(j * tile, (j + 1) * tile)
            pre[...] = matmul(first_low[rows], w_up[:, cols])

            def body(row):
                value = pre[pl.ds(row, 32)]
                bell = lax.erf(value * 0.7071067811865476) * 0.5 + 0.5
                at = span(s * length + row, 32)
                hidden[at, cols] = (value * bell).astype(BF)
                slope[at, cols] = (
                    bell + value * jnp.exp(value * value * -0.5) * 0.3989422804014327
                ).astype(BF)

            each(length, 32, body, 4)
        for j in range(width // tile):
            cols = slice(j * tile, (j + 1) * tile)
            part2[s, :, cols] = matmul(hidden[rows], w_down[:, cols]).astype(BF)

    def output_rows(s):
        def rows_of(row):
            center = center2[span(s * length + row, 16)].astype(F32)
            return (center * scaled(center) * norms[2:3] + norms[3:4]).astype(BF)

        def word_rows(row):
            out_words[s, span(row, 16)] = rows_of(row)

        def ent_rows(row):
            out_ents[s, span(row, 16)] = rows_of(row + word_length)

        each(word_length, 16, word_rows, 4)
        each(ent_count, 16, ent_rows, 4)
        scored = head_in.shape[0] // seqs
        head_in[s * scored : (s + 1) * scored] = out_ents[s, 0:scored]

    for copy in word_copies:
        copy.wait()
    project(0, wt_words, 0, word_length)
    asks.wait()
    answer()
    answered[me_dp] = answers[me_dp]
    backs.start()
    span_means()
    project(1, wt_words, 0, word_length)
    backs.wait()
    collect()
    vecs.start()
    projs.wait()
    vecs.wait()
    entity_rows()
    project(0, wt_ents, word_length, ent_count)
    for h in range(heads):
        attend(0, h)
    attention_part(0)
    one.begin(0)
    project(1, wt_ents, word_length, ent_count)
    attend(1, 0)
    one.pass_on(0)
    for h in range(1, heads):
        attend(1, h)
    attention_part(1)
    one.begin(1)
    one.wait_sum(0)
    first_rows(0)
    one.spread(0)
    one.pass_on(1)
    one.forward(0)
    one.wait_full(0)
    feed(0)
    two.begin(0)
    one.wait_sum(1)
    first_rows(1)
    one.spread(1)
    two.pass_on(0)
    one.forward(1)
    one.wait_full(1)
    feed(1)
    two.begin(1)
    two.wait_sum(0)
    second_rows(0)
    two.spread(0)
    two.pass_on(1)
    two.forward(0)
    two.wait_full(0)
    output_rows(0)
    two.wait_sum(1)
    second_rows(1)
    two.spread(1)
    two.forward(1)
    two.wait_full(1)
    output_rows(1)
    for s in range(seqs):
        one.drain(s)
        two.drain(s)


def quarter_scratch(seqs, length, width):
    return [
        pltpu.VMEM((seqs, length, width), BF),
        pltpu.VMEM((seqs, length // 2, width), BF),
        pltpu.VMEM((seqs, length // 4, width), BF),
        pltpu.VMEM((seqs, length // 4, width), BF),
    ]


def forward_layer(sizes, scored, capacity, words, arrays):
    seqs, length, word_length, heads = sizes
    n, n_mp = lax.axis_size("dp"), lax.axis_size("mp")
    width = words.shape[2]
    tokens = seqs * length
    local, ents = heads * DH, seqs * (length - word_length)
    table, w_up = arrays[5], arrays[11]
    cols_dev, rows_dev = table.shape
    units = w_up.shape[1]

    def like(*shape, dtype=BF):
        return jax.ShapeDtypeStruct(shape, dtype)

    outs = [
        like(n, 8, LANES, dtype=jnp.int32), like(1, ents, dtype=jnp.int32),
        like(seqs, word_length, length - word_length), like(ents, LANES, dtype=F32),
        like(seqs, word_length, LANES, dtype=F32), like(4, width, dtype=F32),
        like(cols_dev, ents), like(tokens, width),
        like(heads, 4 * DH, tokens), like(heads, 8, tokens, dtype=F32), like(local, tokens),
        like(heads, 4 * DH, width), like(heads, 4 * DH, width), like(tokens // 4, width, dtype=F32),
        like(tokens, width), like(tokens, units), like(tokens, units), like(tokens, width),
        like(seqs, word_length, width), like(seqs, length - word_length, width),
        like(seqs * scored, width),
    ]
    return pl.pallas_call(
        functools.partial(forward_kernel, sizes, n, n_mp, capacity),
        out_shape=outs,
        in_specs=[pl.BlockSpec(memory_space=pl.ANY), pl.BlockSpec(memory_space=pltpu.SMEM)]
        + [VM] * (len(arrays) - 1),
        out_specs=[VM] * len(outs),
        scratch_shapes=[
            pltpu.VMEM((length, length), F32),
            pltpu.VMEM((length, length), BF),
            pltpu.VMEM((length, 256), F32),
            pltpu.VMEM((tokens // 4, width), F32),
            *quarter_scratch(seqs, length, width),
            *quarter_scratch(seqs, length, width),
            pltpu.VMEM((rows_dev, n * capacity), BF),
            pltpu.VMEM((n, cols_dev, LANES), BF), pltpu.VMEM((n, cols_dev, LANES), BF),
            pltpu.VMEM((n_mp, cols_dev, ents), BF), pltpu.VMEM((n_mp, cols_dev, width), BF),
            pltpu.VMEM((ents, width), F32), pltpu.VMEM((n, 8, LANES), jnp.int32),
            pltpu.SemaphoreType.DMA((seqs, 5)), pltpu.SemaphoreType.DMA((seqs, 5)),
            pltpu.SemaphoreType.DMA((seqs, 5)), pltpu.SemaphoreType.DMA((seqs, 5)),
            pltpu.SemaphoreType.DMA((seqs,)),
            pltpu.SemaphoreType.DMA((2, n - 1)), pltpu.SemaphoreType.DMA((2, n - 1)),
            pltpu.SemaphoreType.DMA((2, n_mp - 1)), pltpu.SemaphoreType.DMA((2, n_mp - 1)),
        ],
        compiler_params=pltpu.CompilerParams(
            collective_id=3, has_side_effects=True, vmem_limit_bytes=60 * 2**20
        ),
    )(words, *arrays)


class Job:
    def __init__(self, rows, buf, out, arrivals, send, recv, n, first=(0, 1, 2)):
        self.buf, self.out, self.arrivals, self.send, self.recv = buf, out, arrivals, send, recv
        self.rows = rows
        self.me = lax.axis_index("dp")
        self.bits, self.halvings = job_plan(rows, n)
        self.order = list(range(self.bits))
        if self.bits >= len(first):
            self.order[: len(first)] = first

    def bit(self, k):
        return lax.rem(self.me // 2 ** self.order[k], 2)

    def peer(self, k):
        return self.me + (1 - 2 * self.bit(k)) * 2 ** self.order[k]

    def offset(self, k):
        start = 0
        for i in range(k):
            start = start + self.bit(i) * (self.rows >> (i + 1))
        return start

    def copy(self, index, k, src, dst):
        return remote(src, dst, self.send.at[index], self.recv.at[index], "dp", self.peer(k))

    def steps(self):
        size = self.rows
        for k in range(self.bits):
            keep = self.offset(min(k, self.halvings))
            away = keep
            if k < self.halvings:
                size //= 2
                away = keep + (1 - self.bit(k)) * size
                keep = keep + self.bit(k) * size
            arrived = self.arrivals[k]
            copy = self.copy(k, k, self.buf.at[span(away, size)], arrived)
            copy.start()
            yield
            copy.wait()
            last = k == self.bits - 1

            def body(row, keep=keep, arrived=arrived, last=last):
                at = span(keep + row, 16)
                value = self.buf[at].astype(F32) + arrived[span(row, 16)].astype(F32)
                (self.out if last else self.buf)[at] = value.astype(BF)

            each(size, 16, body, 4)
        for k in reversed(range(self.halvings)):
            done = self.out.at[span(self.offset(k + 1), size)]
            copy = self.copy(self.bits + k, k, done, done)
            copy.start()
            yield
            copy.wait()
            size *= 2


def job_plan(rows, n):
    bits, halvings, size = n.bit_length() - 1, 0, rows
    while halvings < bits - 1 and (size // 2) % 16 == 0:
        size, halvings = size // 2, halvings + 1
    return bits, halvings


def job_cuts(units, width, head_rows, proj_rows, heads):
    orders = [
        ((1, 2, 0), (0, 1, 2), (1, 2, 0)),
        ((0, 1, 2), (0, 1, 2), (0, 1, 2)),
        ((1, 0, 2),),
        ((0, 1, 2),),
        ((1, 2, 0), (0, 1, 2)),
        ((0, 1, 2), (0, 1, 2)),
        ((0, 1, 2), (0, 1, 2)),
    ]
    cuts = [(units, [units // 3] * 3), (width, [width // 3] * 3)]
    cuts += [(head_rows, [head_rows]), (proj_rows, [proj_rows])]
    cuts += [(7 * DH, [4 * DH, 3 * DH])] * heads
    return [(rows, pieces, order) for (rows, pieces), order in zip(cuts, orders)]


def job_scratch(rows, width, n):
    bits, halvings = job_plan(rows, n)
    return [
        pltpu.VMEM((rows >> min(k + 1, halvings), width), BF) for k in range(bits)
    ]


def backward_kernel(sizes, n, n_mp, *refs):
    seqs, length, word_length, heads = sizes
    refs = list(refs)

    def take(count):
        taken = refs[:count]
        del refs[:count]
        return taken

    cot_words, cot_ents = take(2)
    (
        d_head, head_grad, center2, slope, hidden, first_low, center1, w_up, w_down, norms,
        small_in, ent_proj, vec_rows, place, received, inside, spans,
    ) = take(17)
    late_in = take(8)
    down_out, up_out, head_all, proj_out, *per_head_out = take(4 + heads)
    word_grads, table_hits, small = take(3)
    ctx, qkv, lse, wt_words, wt_ents, stream, mask, w_out = late = take(8)
    sums, d_ffn, d_pre, d_attn, d_first, dctx, sT, dpT, pT, dsT, dcat = take(11)
    head_out, small_mp, small_dp, outbox, gw, inbox, onehot = take(7)
    part, r1, s2, r2 = take(4)
    (
        send1, recv1, send2, recv2, job_send, job_recv, late_sem, cot_sem,
        mp_send, mp_recv, dp_send, dp_recv, out_sem,
    ) = take(13)
    width = stream.shape[1]
    units = w_up.shape[1]
    me_mp, me_dp = lax.axis_index("mp"), lax.axis_index("dp")
    bits = n.bit_length() - 1
    jobs = []
    groups = [[], [], [], []] + [[] for h in range(heads)]
    buffers = take(len(groups))
    for group, buf, out, (rows, cuts, orders) in zip(
        groups, buffers, [down_out, up_out, head_out, proj_out, *per_head_out],
        job_cuts(units, width, head_out.shape[0], proj_out.shape[0], heads),
    ):
        start = 0
        for count, order in zip(cuts, orders):
            at = pl.ds(start, count)
            start += count
            index = len(jobs)
            jobs.append(
                Job(
                    count, buf.at[at], out.at[at], take(bits), job_send.at[index],
                    job_recv.at[index], n, order,
                )
            )
            group.append(jobs[-1])
    down_jobs, up_jobs, (head_job,), (proj_job,), *heads_jobs = groups
    down_buf, up_buf, head_buf, proj_buf, *heads_buf = buffers
    one = Quarters(part, r1, s2, r2, d_attn, send1, recv1)
    two = Quarters(part, r1, s2, r2, gw, send2, recv2)
    barrier = pltpu.get_barrier_semaphore()
    greet(barrier, "mp", n_mp)
    greet(barrier, "dp", n)
    cots = []
    for s in range(seqs):
        for k, (source, start, count) in enumerate(
            ((cot_words, 0, word_length), (cot_ents, word_length, length - word_length))
        ):
            target = d_attn.at[pl.ds(s * length + start, count)]
            cots.append(pltpu.make_async_copy(source.at[s], target, cot_sem.at[s, k]))
            cots[-1].start()
    late_copies = [
        pltpu.make_async_copy(source, target, late_sem.at[i])
        for i, (source, target) in enumerate(zip(late_in, late))
    ]
    for copy in late_copies:
        copy.start()
    running = {}

    def launch(job):
        running[id(job)] = job.steps()
        next(running[id(job)])

    def step(*which):
        for job in which:
            next(running[id(job)], 0)

    def finish(job):
        for _ in running[id(job)]:
            pass

    sums[...] = jnp.zeros_like(sums)

    spare = d_first.shape[0] - 16

    def second_back(s):
        start = one.own_row(0, 0)

        def rows_of(row, extra=None):
            at = span(s * length + row, 16)
            cot = d_attn[at].astype(F32)
            if extra is not None:
                cot = cot + extra
            center = center2[at].astype(F32)
            inv = scaled(center)
            normed = center * inv
            sums[0] += cot * normed
            sums[1] += cot
            grad = cot * norms[2:3]
            value = inv * (
                grad
                - jnp.mean(grad, axis=-1, keepdims=True)
                - normed * jnp.mean(grad * normed, axis=-1, keepdims=True)
            )
            d_ffn[at] = value.astype(BF)

            own = (row >= start) & (row < start + one.quarter)
            d_first[span(jnp.where(own, s * one.quarter + row - start, spare), 16)] = value

        scored = d_head.shape[1]
        each(word_length, 16, rows_of, 4)
        each(scored, 16, lambda row: rows_of(row + word_length, d_head[s, span(row, 16)]))
        each(length - word_length - scored, 16, lambda row: rows_of(row + word_length + scored), 7)

    def feed_back(s):
        rows = slice(s * length, (s + 1) * length)
        tile = 256
        for j in range(units // tile):
            cols = slice(j * tile, (j + 1) * tile)
            sT[:, 0:tile] = contract(d_ffn[rows], w_down[cols], 1, 1)

            def body(row):
                at = span(s * length + row, 32)
                d_pre[at, cols] = (
                    sT[pl.ds(row, 32), 0:tile] * slope[at, cols].astype(F32)
                ).astype(BF)

            each(length, 32, body, 4)
        for j in range(width // tile):
            cols = slice(j * tile, (j + 1) * tile)
            part[s, :, cols] = contract(d_pre[rows], w_up[cols], 1, 1).astype(BF)

    def first_back(s):
        def body(row):
            at = one.own_row(s, row)
            mine = span(s * one.quarter + row, 16)
            value = d_first[mine] + one.total(s, row)
            center = center1[mine]
            inv = scaled(center)
            normed = center * inv
            sums[2] += value * normed
            sums[3] += value
            grad = value * norms[0:1]
            value = inv * (
                grad
                - jnp.mean(grad, axis=-1, keepdims=True)
                - normed * jnp.mean(grad * normed, axis=-1, keepdims=True)
            )
            d_first[mine] = value
            d_attn[span(at, 16)] = value.astype(BF)

        each(one.quarter, 16, body, 5)

    def context_back(s):
        cols = slice(s * length, (s + 1) * length)
        dctx[:, cols] = contract(w_out[...], d_attn[cols], 1, 1).astype(BF)

    def attend_back(s, h):
        cols = pl.ds(s * length, length)
        w_cols = pl.ds(s * length, word_length)
        e_cols = pl.ds(s * length + word_length, length - word_length)
        mine = slice(h * DH, (h + 1) * DH)
        scores_of(qkv, sT, h, cols, word_length)
        dpT[...] = contract(qkv[h, 192:256, cols], dctx[mine, cols], 0, 0)

        def body(col):
            here = pl.ds(col, LANES)
            at = pl.ds(pl.multiple_of(s * length + col, LANES), LANES)
            delta = jnp.sum(
                ctx[mine, at].astype(F32) * dctx[mine, at].astype(F32), axis=0, keepdims=True
            )
            log_total = lse[h, 0:1, at]
            probs = jnp.exp(sT[0:word_length, here] + mask[s] - log_total)
            pT[0:word_length, here] = probs.astype(BF)
            dsT[0:word_length, here] = (probs * (dpT[0:word_length, here] - delta)).astype(BF)
            probs = jnp.exp(sT[word_length:, here] - log_total)
            pT[word_length:, here] = probs.astype(BF)
            dsT[word_length:, here] = (probs * (dpT[word_length:, here] - delta)).astype(BF)

        each(length, LANES, body)
        d_words, d_ents = dsT[0:word_length], dsT[word_length:]
        dcat[h, 0:64, cols] = (contract(qkv[h, 128:192, w_cols], d_words, 1, 0) * 0.125).astype(BF)
        dcat[h, 64:128, cols] = (contract(qkv[h, 128:192, e_cols], d_ents, 1, 0) * 0.125).astype(BF)
        dcat[h, 128:192, w_cols] = contract(qkv[h, 0:64, cols], d_words, 1, 1).astype(BF)
        dcat[h, 128:192, e_cols] = contract(qkv[h, 64:128, cols], d_ents, 1, 1).astype(BF)
        dcat[h, 192:256, cols] = contract(dctx[mine, cols], pT[...], 1, 1).astype(BF)

    def head_grads(h):
        buf = heads_buf[h]
        from_words, from_ents = None, None
        for s in range(seqs):
            middle, start, end = s * length + word_length, s * length, (s + 1) * length
            words = matmul(dcat[h, :, start:middle], stream[start:middle])
            ents = matmul(dcat[h, :, middle:end], stream[middle:end])
            from_words = words if s == 0 else from_words + words
            from_ents = ents if s == 0 else from_ents + ents
        buf[0:128] = from_words[0:128].astype(BF)
        buf[128:256] = (from_words[128:256] + from_ents[128:256]).astype(BF)
        buf[256:384] = from_ents[0:128].astype(BF)
        buf[384:448] = matmul(ctx[h * DH : (h + 1) * DH], d_attn[...]).astype(BF)

    def stream_part(s):
        for start in range(0, length, LANES):
            weight = wt_words if start < word_length else wt_ents
            cols = slice(s * length + start, s * length + start + LANES)
            value = contract(dcat[0, :, cols], weight[0], 0, 0)
            for h in range(1, heads):
                value = value + contract(dcat[h, :, cols], weight[h], 0, 0)
            part[s, start : start + LANES] = value.astype(BF)

    def last_rows(s):
        def body(row):
            at = two.own_row(s, row)
            value = d_first[span(s * two.quarter + row, 16)] + two.total(s, row)
            gw[span(at, 16)] = value.astype(BF)

        each(two.quarter, 16, body, 5)

    def down_tile(j):
        cols = slice(j * 256, (j + 1) * 256)
        down_buf[cols] = contract(hidden[:, cols], d_ffn[...], 0, 0).astype(BF)

    def up_tile(j):
        cols = slice(j * 256, (j + 1) * 256)
        up_buf[cols] = contract(first_low[:, cols], d_pre[...], 0, 0).astype(BF)

    def wait_cots(s):
        for copy in cots[2 * s : 2 * s + 2]:
            copy.wait()

    def wait_late():
        for copy in late_copies:
            copy.wait()

    small_over_mp = Spread(
        "mp", n_mp, lambda peer: small_mp.at[me_mp], small_mp, mp_send.at[0], mp_recv.at[0]
    )
    small_over_dp = Spread(
        "dp", n, lambda peer: small_dp.at[me_dp], small_dp, dp_send.at[0], dp_recv.at[0]
    )
    boxes = Spread("dp", n, lambda peer: outbox.at[peer], inbox, dp_send.at[1], dp_recv.at[1])
    head_rows = head_out.shape[0]
    head_place = span(me_mp * head_rows, head_rows)

    def head_copy(distance, peer, owner):
        return remote(
            head_out, head_all.at[span(owner * head_rows, head_rows)], mp_send.at[1, distance - 1],
            mp_recv.at[1, distance - 1], "mp", peer,
        )

    def small_first():
        mine = small_in[...]
        mine = mine + jnp.concatenate(
            [jnp.sum(sums[row], axis=0, keepdims=True) for row in range(4)]
            + [jnp.zeros((4, width), F32)]
        )
        small_mp[me_mp] = mine
        small_over_mp.start()

    def small_second():
        small_over_mp.wait()
        total = small_mp[0]
        for device in range(1, n_mp):
            total = total + small_mp[device]
        row = lax.broadcasted_iota(jnp.int32, total.shape, 0)
        small_dp[me_dp] = jnp.where((row == 2) | (row == 3), total, small_mp[me_mp])
        small_over_dp.start()

    def small_last():
        small_over_dp.wait()

        def add(device, total):
            return total + small_dp[device]

        small[...] = lax.fori_loop(1, n, add, small_dp[0])

    def head_first():
        head_all[head_place] = head_out[...]
        for distance in range(1, n_mp):
            head_copy(distance, lax.rem(me_mp + distance, n_mp), me_mp).start()

    def head_last():
        for distance in range(1, n_mp):
            source = lax.rem(me_mp + n_mp - distance, n_mp)
            head_copy(distance, source, source).wait()

    def entities():
        grads, rows = None, []
        count = length - word_length
        for s in range(seqs):
            d_ent = gw[s * length + word_length : (s + 1) * length]
            value = matmul(vec_rows[:, s * count : (s + 1) * count], d_ent)
            grads = value if s == 0 else grads + value
            rows.append(contract(ent_proj[...], d_ent, 1, 1).astype(BF))
        proj_buf[...] = grads.astype(BF)
        launch(proj_job)
        rows = jnp.concatenate(rows, axis=1)
        slot = lax.broadcasted_iota(jnp.int32, (LANES, seqs * count), 0)

        def fill(owner, carry):
            placed = jnp.where(slot + owner * LANES == place[...], 1.0, 0.0).astype(BF)
            outbox[owner] = contract(rows, placed, 1, 1).astype(BF)
            return carry

        lax.fori_loop(0, n, fill, 0)
        inbox[me_dp] = outbox[me_dp]
        boxes.start()

    out_copies = []

    def words_out(s):
        width_part = width // 2
        rows = slice(s * length, s * length + word_length)
        at = slice(s * (length - word_length), (s + 1) * (length - word_length))
        shared = gw[s * length + word_length : (s + 1) * length].astype(F32) / spans[at, 0:1]
        for half, source in enumerate((sT, dpT)):
            if s > 0:
                out_copies[2 * (s - 1) + half].wait()
            cols = slice(half * width_part, (half + 1) * width_part)
            source[0:word_length, 0:width_part] = gw[rows, cols].astype(F32) + matmul(
                inside[s], shared[:, cols].astype(BF)
            )
            out_copies.append(
                pltpu.make_async_copy(
                    source.at[pl.ds(0, word_length), pl.ds(0, width_part)],
                    word_grads.at[s, :, pl.ds(half * width_part, width_part)], out_sem.at[s, half],
                )
            )
            out_copies[-1].start()

    pieces = chunks_of(table_hits.shape[1], onehot.shape[0])
    parts = (len(pieces) + 3) // 4

    def table_part(part):
        capacity = onehot.shape[1] // n
        ids = jnp.concatenate([received[source, 0:1, 0:capacity] for source in range(n)], axis=1)
        rows = jnp.concatenate([inbox[source, :, 0:capacity] for source in range(n)], axis=1)
        for start, count in pieces[part * parts : (part + 1) * parts]:

            def body(row, start=start):
                index = lax.broadcasted_iota(jnp.int32, (32, n * capacity), 0) + (row + start)
                onehot[span(row, 32)] = jnp.where(index == ids, 1.0, 0.0).astype(BF)

            each(count, 32, body, 2)
            table_hits[:, start : start + count] = contract(rows, onehot[0:count], 1, 1)

    head_buf[...] = head_grad[head_place]
    wait_cots(0)
    second_back(0)
    feed_back(0)
    pl.semaphore_wait(barrier, n_mp - 1 + n - 1)
    one.begin(0)
    launch(head_job)
    wait_cots(1)
    second_back(1)
    one.pass_on(0)
    step(head_job)
    down_tile(0)
    launch(down_jobs[0])
    down_tile(1)
    launch(down_jobs[1])
    down_tile(2)
    launch(down_jobs[2])
    feed_back(1)
    one.begin(1)
    step(head_job)
    up_tile(0)
    launch(up_jobs[0])
    up_tile(1)
    launch(up_jobs[1])
    up_tile(2)
    launch(up_jobs[2])
    step(down_jobs[0])
    one.pass_on(1)
    step(down_jobs[1], head_job)
    one.wait_sum(0)
    first_back(0)
    one.spread(0)
    step(down_jobs[2], up_jobs[0], down_jobs[1], down_jobs[0])
    one.wait_sum(1)
    first_back(1)
    one.spread(1)
    small_first()
    step(up_jobs[1], up_jobs[0], down_jobs[2])
    one.forward(0)
    step(up_jobs[2], up_jobs[1], head_job, down_jobs[1])
    one.wait_full(0)
    small_second()
    wait_late()
    context_back(0)
    step(down_jobs[0])
    attend_back(0, 0)
    step(up_jobs[2], down_jobs[2], head_job)
    finish(head_job)
    head_first()
    step(up_jobs[0])
    attend_back(0, 1)
    step(down_jobs[1])
    attend_back(0, 2)
    one.first(0).wait_send()
    stream_part(0)
    two.begin(0)
    step(up_jobs[1], up_jobs[0])
    one.forward(1)
    one.wait_full(1)
    one.drain(0, True)
    one.drain(1)
    context_back(1)
    step(down_jobs[1], down_jobs[0], up_jobs[1])
    attend_back(1, 0)
    two.pass_on(0)
    head_grads(0)
    launch(heads_jobs[0][0])
    launch(heads_jobs[0][1])
    step(up_jobs[0], up_jobs[2])
    attend_back(1, 1)
    head_grads(1)
    launch(heads_jobs[1][0])
    launch(heads_jobs[1][1])
    step(down_jobs[0])
    attend_back(1, 2)
    step(up_jobs[1], down_jobs[2])
    stream_part(1)
    two.begin(1)
    head_grads(2)
    launch(heads_jobs[2][0])
    launch(heads_jobs[2][1])
    step(heads_jobs[0][0], heads_jobs[0][1], up_jobs[2])
    two.pass_on(1)
    two.wait_sum(0)
    last_rows(0)
    two.spread(0)
    small_last()
    step(heads_jobs[1][0], down_jobs[2], heads_jobs[0][0], heads_jobs[1][1])
    step(heads_jobs[0][1])
    two.wait_sum(1)
    step(heads_jobs[1][0])
    last_rows(1)
    two.spread(1)
    step(heads_jobs[1][1], heads_jobs[2][0], heads_jobs[0][1], heads_jobs[2][1])
    two.forward(0)
    step(heads_jobs[2][0], heads_jobs[1][0], heads_jobs[0][1], up_jobs[2])
    step(heads_jobs[2][1])
    two.forward(1)
    two.wait_full(0)
    step(heads_jobs[1][1], heads_jobs[0][0], heads_jobs[1][0])
    two.wait_full(1)
    entities()
    words_out(0)
    step(heads_jobs[1][1], heads_jobs[0][1], heads_jobs[2][0])
    words_out(1)
    step(heads_jobs[2][1], heads_jobs[1][0], heads_jobs[2][0], proj_job)
    boxes.wait()
    table_part(0)
    table_part(1)
    step(heads_jobs[2][1], heads_jobs[0][0], proj_job, heads_jobs[1][1])
    table_part(2)
    table_part(3)
    step(proj_job, heads_jobs[2][0], heads_jobs[0][0], proj_job)
    step(heads_jobs[2][1], proj_job)
    head_last()
    for s in range(seqs):
        two.drain(s)
    for copy in out_copies[-2:]:
        copy.wait()
    for job in jobs:
        finish(job)


def backward_layer(sizes, n, capacity, rows_dev, cots, now, late):
    seqs, length, word_length, heads = sizes
    stream, w_up, ent_proj = late[5], now[7], now[11]
    n_mp = lax.axis_size("mp")
    tokens, width = stream.shape
    units, local = w_up.shape[1], heads * DH
    head_rows, head_width = now[1].shape[0] // n_mp, now[1].shape[1]
    bits = n.bit_length() - 1
    outs = [(units, width), (width, units), (n_mp * head_rows, head_width), ent_proj.shape]
    outs += [(7 * DH, width)] * heads
    outs = [jax.ShapeDtypeStruct(shape, BF) for shape in outs]
    outs += [
        jax.ShapeDtypeStruct((seqs, word_length, width), F32),
        jax.ShapeDtypeStruct((ent_proj.shape[0], rows_dev), F32),
        jax.ShapeDtypeStruct((8, width), F32),
    ]
    cuts = job_cuts(units, width, head_rows, ent_proj.shape[0], heads)
    widths = [width, units, head_width] + [width] * (1 + heads)
    job_count = sum(len(sizes) for _, sizes, _ in cuts)
    scratch = [pltpu.VMEM(value.shape, value.dtype) for value in late]
    scratch += [
        pltpu.VMEM((4, 16, width), F32), pltpu.VMEM((tokens, width), BF),
        pltpu.VMEM((tokens, units), BF), pltpu.VMEM((tokens, width), BF),
        pltpu.VMEM((tokens // 4 + 16, width), F32), pltpu.VMEM((local, tokens), BF),
        pltpu.VMEM((length, length), F32), pltpu.VMEM((length, length), F32),
        pltpu.VMEM((length, length), BF), pltpu.VMEM((length, length), BF),
        pltpu.VMEM((heads, 4 * DH, tokens), BF),
        pltpu.VMEM((head_rows, head_width), BF), pltpu.VMEM((n_mp, 8, width), F32),
        pltpu.VMEM((n, 8, width), F32), pltpu.VMEM((n, ent_proj.shape[0], LANES), BF),
        pltpu.VMEM((tokens, width), BF), pltpu.VMEM((n, ent_proj.shape[0], LANES), BF),
        pltpu.VMEM((256, n * capacity), BF),
        *quarter_scratch(seqs, length, width),
        pltpu.SemaphoreType.DMA((seqs, 5)), pltpu.SemaphoreType.DMA((seqs, 5)),
        pltpu.SemaphoreType.DMA((seqs, 5)), pltpu.SemaphoreType.DMA((seqs, 5)),
        pltpu.SemaphoreType.DMA((job_count, 2 * bits)),
        pltpu.SemaphoreType.DMA((job_count, 2 * bits)),
        pltpu.SemaphoreType.DMA((len(late),)), pltpu.SemaphoreType.DMA((seqs, 2)),
        pltpu.SemaphoreType.DMA((2, n_mp - 1)), pltpu.SemaphoreType.DMA((2, n_mp - 1)),
        pltpu.SemaphoreType.DMA((2, n - 1)), pltpu.SemaphoreType.DMA((2, n - 1)),
        pltpu.SemaphoreType.DMA((seqs, 2)),
    ]
    scratch += [pltpu.VMEM((rows, columns), BF) for (rows, _, _), columns in zip(cuts, widths)]
    for (_, counts, _), columns in zip(cuts, widths):
        for count in counts:
            scratch += job_scratch(count, columns, n)
    hbm = pl.BlockSpec(memory_space=pl.ANY)
    return pl.pallas_call(
        functools.partial(backward_kernel, sizes, n, n_mp),
        out_shape=outs,
        in_specs=[hbm] * len(cots) + [VM] * len(now) + [hbm] * len(late),
        out_specs=[VM] * (len(outs) - 3) + [hbm, VM, VM],
        scratch_shapes=scratch,
        compiler_params=pltpu.CompilerParams(
            collective_id=7, has_side_effects=True, vmem_limit_bytes=62 * 2**20
        ),
    )(*cots, *now, *late)


def head_kernel(
    n, head_in, w_head, gain, table, target, d_head, grad_head, small, loss, table_grad,
    all_head, logits, probs, onehot, turned, tops, parts_out, parts_in, rows_out, rows_in,
    stats_out, stats_in, send, recv,
):
    me_dp, me_mp = lax.axis_index("dp"), lax.axis_index("mp")
    mine, vec_width = all_head.shape[1:]
    total = n * mine
    rows_dev = table.shape[1]
    cols_dev = table_grad.shape[0]
    block = logits.shape[0]
    blocks = total // block
    owners = block // mine
    barrier = pltpu.get_barrier_semaphore()
    greet(barrier, "dp", n)

    pre = matmul(head_in[...], w_head[...])
    bell = lax.erf(pre * 0.7071067811865476) * 0.5 + 0.5
    value = pre * bell
    center = value - jnp.mean(value, axis=-1, keepdims=True)
    inv = scaled(center)
    normed = center * inv
    all_head[me_dp] = (normed * gain[...]).astype(BF)
    pl.semaphore_wait(barrier, n - 1)
    heads = Spread("dp", n, lambda peer: all_head.at[me_dp], all_head, send.at[0], recv.at[0])
    heads.start()

    def fill_onehot(b):
        count = block // target.shape[1]
        rows = target[pl.ds(pl.multiple_of(b * count, count), count)]
        wanted = jnp.concatenate([rows[i : i + 1] for i in range(count)], axis=1) - me_dp * rows_dev

        def body(row):
            index = lax.broadcasted_iota(jnp.int32, (80, block), 0) + row
            onehot[span(row, 80)] = jnp.where(index == wanted, 1.0, 0.0).astype(BF)

        each(rows_dev, 80, body)

    def slots_of(b):
        return all_head[pl.ds(b * owners, owners)].reshape(block, vec_width)

    def fill_probs(b):
        slots = slots_of(b)
        for start, count in chunks_of(rows_dev, 1024):
            logits[:, start : start + count] = matmul(slots, table[:, start : start + count])

        def body(row):
            x = logits[span(row, 16)]
            top = jnp.max(x, axis=-1, keepdims=True)
            x = jnp.exp(x - top)
            lane = lax.broadcasted_iota(jnp.int32, (16, LANES), 1)
            amount = jnp.sum(x, axis=-1, keepdims=True)
            tops[span(row, 16)] = jnp.where(lane == 0, top, jnp.where(lane == 1, amount, 0.0))
            probs[span(row, 16)] = x.astype(BF)

        each(block, 16, body, 2)

    def over_blocks(body):
        if blocks == 1:
            body(0)
        else:
            lax.fori_loop(0, blocks, lambda b, carry: (body(b), carry)[1], 0)

    def target_part(b):
        fill_onehot(b)
        found = matmul(table[...], onehot[...])
        turned[...] = found
        rows = jnp.transpose(found).astype(BF).reshape(owners, mine, vec_width)
        rows_out[pl.ds(b * owners, owners)] = rows

    def block_part(b):
        if blocks > 1:
            target_part(b)
        slots = jnp.transpose(slots_of(b).astype(F32))
        own = jnp.sum(slots * turned[...], axis=0, keepdims=True)
        fill_probs(b)
        part = contract(probs[...], table[...], 1, 1)
        at = pl.ds(b * owners, owners)
        parts_out[at, :, 0:vec_width] = part.reshape(owners, mine, vec_width)
        parts_out[at, :, vec_width:] = tops[...].reshape(owners, mine, LANES)
        columns = pl.ds(pl.multiple_of(b * block, LANES), block)
        stats_out[0:2, columns] = jnp.transpose(tops[...])[0:2]
        stats_out[2:3, columns] = own

    if blocks == 1:
        target_part(0)
    heads.wait()
    stats_out[...] = jnp.zeros_like(stats_out)
    over_blocks(block_part)
    exchanges = [
        Spread("dp", n, lambda peer: parts_out.at[peer], parts_in, send.at[1], recv.at[1]),
        Spread("dp", n, lambda peer: rows_out.at[peer], rows_in, send.at[2], recv.at[2]),
        Spread("dp", n, lambda peer: stats_out, stats_in, send.at[3], recv.at[3]),
    ]
    for exchange_one in exchanges:
        exchange_one.start()
    parts_in[me_dp] = parts_out[me_dp]
    rows_in[me_dp] = rows_out[me_dp]
    stats_in[me_dp] = stats_out[...]
    for exchange_one in exchanges:
        exchange_one.wait()

    def combine(source, state):
        top, amount, sums, targets = state
        part = parts_in[source]
        other = part[:, vec_width : vec_width + 1]
        new_top = jnp.maximum(top, other)
        old, new = jnp.exp(top - new_top), jnp.exp(other - new_top)
        amount = amount * old + part[:, vec_width + 1 : vec_width + 2] * new
        sums = sums * old + part[:, 0:vec_width] * new
        return new_top, amount, sums, targets + rows_in[source].astype(F32)

    first = parts_in[0]
    state = (
        first[:, vec_width : vec_width + 1], first[:, vec_width + 1 : vec_width + 2],
        first[:, 0:vec_width], rows_in[0].astype(F32),
    )
    _, amount, sums, targets = lax.fori_loop(1, n, combine, state)
    d_vec = sums / amount - targets
    small[...] = jnp.zeros_like(small)
    small[4:5, 0:vec_width] = jnp.sum(d_vec * normed, axis=0, keepdims=True)
    grad = d_vec * gain[...]
    d_value = inv * (
        grad
        - jnp.mean(grad, axis=-1, keepdims=True)
        - normed * jnp.mean(grad * normed, axis=-1, keepdims=True)
    )
    d_pre = d_value * (bell + pre * jnp.exp(pre * pre * -0.5) * 0.3989422804014327)
    d_low = d_pre.astype(BF)
    d_head[...] = contract(d_low, w_head[...], 1, 1)
    grad_head[...] = contract(head_in[...], d_low, 0, 0).astype(BF)

    def stat(row):
        def top_of(source, top):
            return jnp.maximum(top, stats_in[source, 0:1])

        top = lax.fori_loop(1, n, top_of, stats_in[0, 0:1])

        def add(source, state):
            amount, targets = state
            amount = amount + stats_in[source, 1:2] * jnp.exp(stats_in[source, 0:1] - top)
            return amount, targets + stats_in[source, 2:3]

        zero = jnp.zeros_like(top)
        amount, targets = lax.fori_loop(0, n, add, (zero, zero))
        return top + jnp.log(amount), targets

    log_total, targets = stat(0)
    loss[...] = jnp.broadcast_to(log_total - targets, loss.shape)
    stats_out[3:4] = jnp.exp(stats_out[0:1] - log_total)

    def table_part(b):
        if blocks > 1:
            fill_onehot(b)
            fill_probs(b)
        columns = pl.ds(pl.multiple_of(b * block, LANES), block)
        turned[...] = jnp.transpose(slots_of(b).astype(F32))
        own = turned[span(me_mp * cols_dev, cols_dev)]
        scaled_own = (own * stats_out[3:4, columns]).astype(BF)
        own = own.astype(BF)
        for start, count in chunks_of(rows_dev, 1024):
            at = slice(start, start + count)
            value = matmul(scaled_own, probs[:, at]) - contract(own, onehot[at], 1, 1)
            if blocks == 1:
                table_grad[:, at] = value
            else:
                table_grad[:, at] += value

    if blocks > 1:
        table_grad[...] = jnp.zeros_like(table_grad)
    over_blocks(table_part)


def head_layer(n, head_in, w_head, gain, table, target, cols_dev):
    mine, width = head_in.shape
    vec_width = w_head.shape[1]
    total = n * mine
    rows_dev = table.shape[1]
    block = math.gcd(total, 256)
    shapes = [
        ((mine, width), F32), ((width, vec_width), BF), ((8, width), F32), ((8, total), F32),
        ((cols_dev, rows_dev), F32),
    ]
    return pl.pallas_call(
        functools.partial(head_kernel, n),
        out_shape=[jax.ShapeDtypeStruct(*shape) for shape in shapes],
        in_specs=[VM] * 5,
        out_specs=[VM] * 5,
        scratch_shapes=[
            pltpu.VMEM((n, mine, vec_width), BF), pltpu.VMEM((block, rows_dev), F32),
            pltpu.VMEM((block, rows_dev), BF), pltpu.VMEM((rows_dev, block), BF),
            pltpu.VMEM((vec_width, block), F32), pltpu.VMEM((block, LANES), F32),
            pltpu.VMEM((n, mine, vec_width + LANES), F32), pltpu.VMEM((n, mine, vec_width + LANES), F32),
            pltpu.VMEM((n, mine, vec_width), BF), pltpu.VMEM((n, mine, vec_width), BF),
            pltpu.VMEM((8, total), F32), pltpu.VMEM((n, 8, total), F32),
            pltpu.SemaphoreType.DMA((4, n - 1)), pltpu.SemaphoreType.DMA((4, n - 1)),
        ],
        compiler_params=pltpu.CompilerParams(
            collective_id=5, has_side_effects=True, vmem_limit_bytes=56 * 2**20
        ),
    )(head_in, w_head, gain, table, target)


def shards(
    words, word_extra, span_pos, span_len, entity_shard, entity_row, targets, table, ent_proj,
    query_weight, w_key, w_value, w_out, gain_attn, bias_attn, w_up, w_down, gain_ffn, bias_ffn,
    w_head, gain_head, cot_words, cot_ents,
):
    n_dp = lax.axis_size("dp")
    n_mp = lax.axis_size("mp")
    seq_count, word_length, model_width = words.shape
    ent_len = span_pos.shape[1]
    masked_len = targets.shape[1]
    tokens_len = word_length + ent_len
    rows_dev, cols_dev = table.shape
    local_width = w_key.shape[1]
    heads_local = local_width // DH
    ent_total = seq_count * ent_len
    table_rows = lax.all_gather(table.T, "mp", axis=0, tiled=True)

    capacity = max(16, 2 * ent_total // n_dp)
    sizes = (seq_count, tokens_len, word_length, heads_local)
    (
        received, place, inside, spans, mask, norms, vec_rows, stream, qkv, lse, ctx, wt_words, wt_ents,
        center1, first_low, hidden, slope, center2, out_words, out_ents, head_in,
    ) = forward_layer(
        sizes, masked_len, capacity, words,
        (
            word_extra, span_pos, span_len, entity_shard.reshape(seq_count, ent_len), entity_row,
            table.T, ent_proj, query_weight.transpose(0, 2, 1), w_key.T, w_value.T, w_out, w_up, w_down,
            gain_attn, bias_attn, gain_ffn, bias_ffn,
        ),
    )
    d_head, grad_head, small, loss, table_grad = head_layer(
        n_dp, head_in, w_head, gain_head[None], table_rows, targets, cols_dev
    )
    loss = loss[0]
    *sums, grad_words, table_hits, small = backward_layer(
        sizes, n_dp, capacity, rows_dev,
        (cot_words, cot_ents),
        (
            d_head.reshape(seq_count, masked_len, model_width), grad_head, center2, slope, hidden,
            first_low, center1, w_up, w_down, norms, small, ent_proj, vec_rows, place,
            received, inside, spans,
        ),
        (
            ctx, qkv, lse, wt_words, wt_ents, stream, mask, w_out,
        ),
    )
    grad_down, grad_up, grad_head, grad_ent_proj, *per_head = (a.astype(F32) for a in sums)
    per_head = [a.reshape(7, DH, model_width) for a in per_head]

    def columns_of(which):
        return jnp.concatenate([a[which] for a in per_head])

    grad_query = jnp.stack([columns_of(i) for i in (0, 1, 4, 5)]).transpose(0, 2, 1)
    grad_key, grad_value, grad_out = columns_of(2).T, columns_of(3).T, columns_of(6)
    table_grad = (table_grad + table_hits).T
    grad_gain_ffn, grad_bias_ffn, grad_gain_attn, grad_bias_attn = (small[i] for i in range(4))
    grad_gain_head = small[4, : w_head.shape[1]]
    return (
        out_words, out_ents, loss, grad_words, table_grad, grad_ent_proj, grad_query, grad_key,
        grad_value, grad_out, grad_gain_attn, grad_bias_attn, grad_up, grad_down, grad_gain_ffn,
        grad_bias_ffn, grad_head, grad_gain_head,
    )


def solution(mesh):
    return jax.shard_map(
        shards,
        mesh=mesh,
        in_specs=(
            P("dp", None, None), P("dp"), P("dp", None), P("dp", None), P("dp", None, None),
            P("dp", None), P(), P("dp", "mp"), P("mp", None), P(None, None, "mp"), P(None, "mp"),
            P(None, "mp"), P("mp", None), P(), P(), P(None, "mp"), P("mp", None), P(), P(), P(),
            P(), P("dp", None, None), P("dp", None, None),
        ),
        out_specs=(
            P("dp", None, None), P("dp", None, None), P(), P("dp", None, None), P("dp", "mp"),
            P("mp", None), P(None, None, "mp"), P(None, "mp"), P(None, "mp"), P("mp", None), P(),
            P(), P(None, "mp"), P("mp", None), P(), P(), P(), P(),
        ),
        check_vma=False,
    )
```

```python
import functools
import math

import jax
import jax.numpy as jnp
from jax import lax
from jax.experimental import pallas as pl
from jax.experimental.pallas import tpu as pltpu
from jax.sharding import PartitionSpec as P

DH = 64
SPANW = 4
EPSILON = 1e-05
MASKED_SCORE = -1000000000.0
LANES = 128
BF = jnp.bfloat16
F32 = jnp.float32
MESH = pl.DeviceIdType.MESH
VM = pl.BlockSpec(memory_space=pltpu.VMEM)


def matmul(first_op, second_op):
    return jnp.dot(first_op, second_op, preferred_element_type=F32)


def normalize(source, gain_vec, shift_vec):
    center = source - jnp.mean(source, axis=-1, keepdims=True)
    inv_scale = lax.rsqrt(jnp.mean(center * center, axis=-1, keepdims=True) + EPSILON)
    return center * inv_scale * gain_vec + shift_vec


def gelu_exact(source):
    return jax.nn.gelu(source, approximate=False)


def remote(src, dst, send, recv, axis, peer):
    return pltpu.make_async_remote_copy(
        src_ref=src, dst_ref=dst, send_sem=send, recv_sem=recv,
        device_id={axis: peer}, device_id_type=MESH,
    )


def contract(first_op, second_op, first_dim, second_dim):
    return lax.dot_general(
        first_op, second_op, (((first_dim,), (second_dim,)), ((), ())), preferred_element_type=F32
    )


def span(start, count):
    return pl.ds(pl.multiple_of(start, 16), count)


def each(count, step, body, unroll=1):
    while count // step % unroll:
        unroll -= 1

    def run(index, carry):
        for i in range(unroll):
            body(pl.multiple_of((index * unroll + i) * step, step))
        return carry

    lax.fori_loop(0, count // step // unroll, run, 0)


class Quarters:
    def __init__(self, part, r1, s2, r2, full, send, recv):
        self.part, self.r1, self.s2, self.r2, self.full = part, r1, s2, r2, full
        self.send, self.recv = send, recv
        me = lax.axis_index("mp")
        self.b0, self.b1 = lax.rem(me, 2), me // 2
        self.p1, self.p2 = me + 1 - 2 * self.b0, lax.rem(me + 2, 4)
        self.length = part.shape[1]
        self.half = self.length // 2
        self.quarter = self.length // 4

    def copy(self, s, k, src, dst, peer):
        return remote(src, dst, self.send.at[s, k], self.recv.at[s, k], "mp", peer)

    def first(self, s):
        rows = span((1 - self.b0) * self.half, self.half)
        return self.copy(s, 0, self.part.at[s, rows], self.r1.at[s], self.p1)

    def second(self, s):
        return self.copy(s, 1, self.s2.at[s], self.r2.at[s], self.p2)

    def place(self, s, h, q):
        return self.full.at[span(s * self.length + h * self.half + q * self.quarter, self.quarter)]

    def third(self, s, q):
        return self.copy(s, 2, self.place(s, self.b0, q), self.place(s, self.b0, q), self.p2)

    def fourth(self, s, h):
        return self.copy(s, 3, self.place(s, h, self.b1), self.place(s, h, self.b1), self.p1)

    def fifth(self, s, h):
        q = 1 - self.b1
        return self.copy(s, 4, self.place(s, h, q), self.place(s, h, q), self.p1)

    def both(self, s, q, row):
        mine = self.part[s, span(self.b0 * self.half + q * self.quarter + row, 16)]
        return mine.astype(F32) + self.r1[s, span(q * self.quarter + row, 16)].astype(F32)

    def begin(self, s):
        self.first(s).start()

    def pass_on(self, s):
        self.first(s).wait_recv()

        def body(row):
            self.s2[s, span(row, 16)] = self.both(s, 1 - self.b1, row).astype(BF)

        each(self.quarter, 16, body, 5)
        self.second(s).start()

    def wait_sum(self, s):
        self.second(s).wait_recv()

    def total(self, s, row):
        return self.both(s, self.b1, row) + self.r2[s, span(row, 16)].astype(F32)

    def own_row(self, s, row):
        return s * self.length + self.b0 * self.half + self.b1 * self.quarter + row

    def spread(self, s):
        self.third(s, self.b1).start()
        self.fourth(s, self.b0).start()

    def forward(self, s):
        self.third(s, 1 - self.b1).wait_recv()
        self.fifth(s, self.b0).start()

    def wait_full(self, s):
        self.fourth(s, 1 - self.b0).wait_recv()
        self.fifth(s, 1 - self.b0).wait_recv()

    def drain(self, s, sent=False):
        if not sent:
            self.first(s).wait_send()
        self.second(s).wait_send()
        self.third(s, self.b1).wait_send()
        self.fourth(s, self.b0).wait_send()
        self.fifth(s, self.b0).wait_send()


class Spread:
    def __init__(self, axis, n, source_of, into, send, recv):
        self.axis, self.n, self.source_of, self.into = axis, n, source_of, into
        self.send, self.recv = send, recv
        self.me = lax.axis_index(axis)

    def copy(self, step, peer, slot):
        return remote(
            self.source_of(peer), self.into.at[slot], self.send.at[step - 1], self.recv.at[step - 1],
            self.axis, peer,
        )

    def start(self):
        def begin(step, carry):
            self.copy(step, lax.rem(self.me + step, self.n), self.me).start()
            return carry

        lax.fori_loop(1, self.n, begin, 0)

    def wait(self):
        def finish(step, carry):
            source = lax.rem(self.me + self.n - step, self.n)
            self.copy(step, source, source).wait()
            return carry

        lax.fori_loop(1, self.n, finish, 0)


def greet(barrier, axis, n):
    me = lax.axis_index(axis)

    def signal(step, carry):
        pl.semaphore_signal(
            barrier, inc=1, device_id={axis: lax.rem(me + step, n)}, device_id_type=MESH
        )
        return carry

    lax.fori_loop(1, n, signal, 0)


def chunks_of(total, size):
    return [(start, min(size, total - start)) for start in range(0, total, size)]


def scaled(center):
    return lax.rsqrt(jnp.mean(center * center, axis=-1, keepdims=True) + EPSILON)


def scores_of(qkv, sT, h, cols, word_length):
    k_cols = pl.ds(cols.start, word_length), pl.ds(cols.start + word_length, cols.size - word_length)
    sT[0:word_length] = contract(qkv[h, 128:192, k_cols[0]], qkv[h, 0:64, cols], 0, 0)
    sT[word_length:] = contract(qkv[h, 128:192, k_cols[1]], qkv[h, 64:128, cols], 0, 0)


def forward_kernel(
    sizes, n, n_mp, capacity,
    words, word_extra, span_pos, span_len, shard, wanted, table, ent_proj, query_weight, w_key, w_value,
    w_out, w_up, w_down, gain_attn, bias_attn, gain_ffn, bias_ffn,
    received, place, inside, spans, mask, norms, vec_rows, stream, qkv, lse, ctx, wt_words, wt_ents, center1, first_low, hidden, slope,
    center2, out_words, out_ents, head_in, table_all,
    sT, pT, pre, first, part1, r11, s21, r21, part2, r12, s22, r22,
    onehot, answers, answered, vec_all, proj_all, spanned, requests,
    send1, recv1, send2, recv2, word_sem, dp_send, dp_recv, mp_send, mp_recv,
    table_send, table_recv,
):
    seqs, length, word_length, heads = sizes
    width = stream.shape[1]
    me_dp, me_mp = lax.axis_index("dp"), lax.axis_index("mp")
    units = w_up.shape[1]
    one = Quarters(part1, r11, s21, r21, first_low, send1, recv1)
    two = Quarters(part2, r12, s22, r22, center2, send2, recv2)
    barrier = pltpu.get_barrier_semaphore()
    greet(barrier, "dp", n)
    greet(barrier, "mp", n_mp)
    word_copies = [
        pltpu.make_async_copy(
            words.at[s], stream.at[pl.ds(s * length, word_length)], word_sem.at[s]
        )
        for s in range(seqs)
    ]
    for copy in word_copies:
        copy.start()
    asks = Spread("dp", n, lambda peer: requests.at[peer], received, dp_send.at[0], dp_recv.at[0])
    backs = Spread("dp", n, lambda peer: answers.at[peer], answered, dp_send.at[1], dp_recv.at[1])
    projs = Spread("mp", n_mp, lambda peer: ent_proj, proj_all, mp_send.at[0], mp_recv.at[0])
    vecs = Spread(
        "mp", n_mp, lambda peer: vec_all.at[me_mp], vec_all, mp_send.at[1], mp_recv.at[1]
    )
    ent_count = length - word_length
    ents = seqs * ent_count

    pieces = table_send.shape[1]
    cols_dev = table.shape[0]
    piece_rows = cols_dev // pieces

    def table_copy(kind, owner, piece):
        place_all = table_all.at[span(owner * cols_dev + piece * piece_rows, piece_rows)]
        source = place_all if kind == 2 else table.at[span(piece * piece_rows, piece_rows)]
        return remote(
            source, place_all, table_send.at[kind, piece], table_recv.at[kind, piece], "mp",
            one.p2 if kind == 1 else one.p1,
        )

    own_table = pltpu.make_async_copy(
        table, table_all.at[span(me_mp * cols_dev, cols_dev)], word_sem.at[seqs]
    )

    def table_begin(kind, first_piece, last_piece):
        for piece in range(first_piece, last_piece):
            table_copy(kind, me_mp, piece).start()

    def table_forward(first_piece, last_piece):
        for piece in range(first_piece, last_piece):
            table_copy(1, one.p2, piece).wait_recv()
            table_copy(2, one.p2, piece).start()

    def table_end():
        own_table.wait()
        for piece in range(pieces):
            table_copy(0, one.p1, piece).wait_recv()
            table_copy(2, lax.rem(one.p1 + 2, n_mp), piece).wait_recv()
            table_copy(0, me_mp, piece).wait_send()
            table_copy(1, me_mp, piece).wait_send()
            table_copy(2, one.p2, piece).wait_send()

    def rows_joined(ref):
        return jnp.concatenate([ref[s : s + 1] for s in range(seqs)], axis=1)

    def prepare():
        owner = rows_joined(shard).astype(F32)
        owner_of = jnp.transpose(jnp.broadcast_to(owner, (ents, ents)))
        earlier = lax.broadcasted_iota(jnp.int32, (ents, ents), 0) < lax.broadcasted_iota(
            jnp.int32, (ents, ents), 1
        )
        rank = jnp.sum(jnp.where(earlier & (owner_of == owner), 1.0, 0.0), axis=0, keepdims=True)
        spot = owner * LANES + rank
        place[...] = spot.astype(jnp.int32)
        spot_of = jnp.transpose(jnp.broadcast_to(spot, (LANES, ents)))
        row_of = jnp.transpose(jnp.broadcast_to(rows_joined(wanted).astype(F32) + 1.0, (LANES, ents)))
        lane = lax.broadcasted_iota(jnp.int32, (ents, LANES), 1).astype(F32)

        def ask_of(peer, carry):
            first_spot = (peer * LANES).astype(F32)
            asked = jnp.where(spot_of == lane + first_spot, row_of, 0.0)
            asked = jnp.sum(asked, axis=0, keepdims=True) - 1.0
            requests[peer] = jnp.broadcast_to(asked.astype(jnp.int32), (8, LANES))
            return carry

        lax.fori_loop(0, n, ask_of, 0)

    def prepare_spans():
        for row, source in enumerate((gain_attn, bias_attn, gain_ffn, bias_ffn)):
            norms[row : row + 1] = source[...].reshape(1, width)
        for s in range(seqs):
            count = word_length // 8 + word_extra[s]
            position = lax.broadcasted_iota(jnp.int32, (word_length, LANES), 0)
            mask[s] = jnp.where(position < count, 0.0, MASKED_SCORE)
            many = span_len[s : s + 1]
            start = lax.shift_right_logical(
                span_pos[s : s + 1] * (count - SPANW), word_length.bit_length() - 1
            )
            position = lax.broadcasted_iota(jnp.int32, (word_length, ent_count), 0)
            within = (position >= start) & (position < start + many)
            inside[s] = jnp.where(within, 1.0, 0.0).astype(BF)
            spans[s * ent_count : (s + 1) * ent_count] = jnp.transpose(
                jnp.broadcast_to(many.astype(F32), (LANES, ent_count))
            )

    def answer():
        ids = jnp.concatenate([received[source, 0:1, 0:capacity] for source in range(n)], axis=1)

        def body(row):
            index = lax.broadcasted_iota(jnp.int32, (80, n * capacity), 0) + row
            onehot[span(row, 80)] = jnp.where(index == ids, 1.0, 0.0).astype(BF)

        each(table.shape[1], 80, body)
        found = matmul(table[...], onehot[...]).astype(BF)
        for source in range(n):
            answers[source, :, 0:capacity] = found[:, source * capacity : (source + 1) * capacity]

    def collect():
        slot = lax.broadcasted_iota(jnp.int32, (capacity, seqs * ent_count), 0)

        def add(owner, total):
            placed = jnp.where(slot + owner * LANES == place[...], 1.0, 0.0).astype(BF)
            return total + matmul(answered[owner, :, 0:capacity], placed)

        total = lax.fori_loop(0, n, add, jnp.zeros(vec_rows.shape, F32))
        vec_rows[...] = total.astype(BF)
        vec_all[me_mp] = total.astype(BF)

    def span_means():
        for s in range(seqs):
            at = slice(s * ent_count, (s + 1) * ent_count)
            start = s * length
            spanned[at] = (
                contract(inside[s], stream[start : start + word_length], 0, 0) / spans[at, 0:1]
            )

    def entity_rows():
        vectors = vec_all[...].reshape(n_mp * vec_rows.shape[0], seqs * ent_count)
        projection = proj_all[...].reshape(n_mp * vec_rows.shape[0], width)
        value = (contract(vectors, projection, 0, 0) + spanned[...]).astype(BF)
        for s in range(seqs):
            at = s * length + word_length
            stream[at : at + ent_count] = value[s * ent_count : (s + 1) * ent_count]

    prepare()
    pl.semaphore_wait(barrier, n + n_mp - 2)
    received[me_dp] = requests[me_dp]
    asks.start()
    proj_all[me_mp] = ent_proj[...]
    projs.start()
    own_table.start()
    table_begin(1, 0, pieces // 2)
    table_begin(0, 0, pieces)
    prepare_spans()

    for target, first_query in ((wt_words, 0), (wt_ents, 2)):
        sources = (query_weight[first_query], query_weight[first_query + 1], w_key[...], w_value[...])
        for g, source in enumerate(sources):
            for h in range(heads):
                target[h, g * DH : (g + 1) * DH] = source[h * DH : (h + 1) * DH]

    def project(s, weight, start, count):
        base = s * length + start
        for h in range(heads):
            value = contract(weight[h], stream[base : base + count], 1, 1)
            qkv[h, 0:128, base : base + count] = (value[0:128] * 0.125).astype(BF)
            qkv[h, 128:256, base : base + count] = value[128:256].astype(BF)

    def attend(s, h):
        cols = pl.ds(s * length, length)
        scores_of(qkv, sT, h, cols, word_length)

        def body(col):
            here = pl.ds(col, LANES)
            words = sT[0:word_length, here] + mask[s]
            ents = sT[word_length:, here]
            top = jnp.maximum(
                jnp.max(words, axis=0, keepdims=True), jnp.max(ents, axis=0, keepdims=True)
            )
            words = jnp.exp(words - top)
            ents = jnp.exp(ents - top)
            total = jnp.sum(words, axis=0, keepdims=True) + jnp.sum(ents, axis=0, keepdims=True)
            pT[0:word_length, here] = words.astype(BF)
            pT[word_length:, here] = ents.astype(BF)
            lse[h, 0:1, pl.ds(pl.multiple_of(s * length + col, LANES), LANES)] = top + jnp.log(total)
            lse[h, 1:2, pl.ds(pl.multiple_of(s * length + col, LANES), LANES)] = 1.0 / total

        each(length, LANES, body)
        value = matmul(qkv[h, 192:256, cols], pT[...]) * lse[h, 1:2, cols]
        ctx[h * DH : (h + 1) * DH, cols] = value.astype(BF)

    def attention_part(s):
        value = contract(ctx[:, s * length : (s + 1) * length], w_out[...], 0, 0)
        part1[s] = value.astype(BF)

    def first_rows(s):
        def body(row):
            at = one.own_row(s, row)
            value = stream[span(at, 16)].astype(F32) + one.total(s, row)
            center = value - jnp.mean(value, axis=-1, keepdims=True)
            mine = span(s * one.quarter + row, 16)
            center1[mine] = center
            normed = center * scaled(center) * norms[0:1] + norms[1:2]
            first[mine] = normed
            first_low[span(at, 16)] = normed.astype(BF)

        each(one.quarter, 16, body, 5)

    def second_rows(s):
        def body(row):
            at = two.own_row(s, row)
            value = first[span(s * two.quarter + row, 16)] + two.total(s, row)
            center = value - jnp.mean(value, axis=-1, keepdims=True)
            center2[span(at, 16)] = center.astype(BF)

        each(two.quarter, 16, body, 5)

    def feed(s):
        rows = slice(s * length, (s + 1) * length)
        tile = 256
        for j in range(units // tile):
            cols = slice(j * tile, (j + 1) * tile)
            pre[...] = matmul(first_low[rows], w_up[:, cols])

            def body(row):
                value = pre[pl.ds(row, 32)]
                bell = lax.erf(value * 0.7071067811865476) * 0.5 + 0.5
                at = span(s * length + row, 32)
                hidden[at, cols] = (value * bell).astype(BF)
                slope[at, cols] = (
                    bell + value * jnp.exp(value * value * -0.5) * 0.3989422804014327
                ).astype(BF)

            each(length, 32, body, 4)
        for j in range(width // tile):
            cols = slice(j * tile, (j + 1) * tile)
            part2[s, :, cols] = matmul(hidden[rows], w_down[:, cols]).astype(BF)

    def output_rows(s):
        def rows_of(row):
            center = center2[span(s * length + row, 16)].astype(F32)
            return (center * scaled(center) * norms[2:3] + norms[3:4]).astype(BF)

        def word_rows(row):
            out_words[s, span(row, 16)] = rows_of(row)

        def ent_rows(row):
            out_ents[s, span(row, 16)] = rows_of(row + word_length)

        each(word_length, 16, word_rows, 4)
        each(ent_count, 16, ent_rows, 4)
        scored = head_in.shape[0] // seqs
        head_in[s * scored : (s + 1) * scored] = out_ents[s, 0:scored]

    for copy in word_copies:
        copy.wait()
    project(0, wt_words, 0, word_length)
    asks.wait()
    answer()
    answered[me_dp] = answers[me_dp]
    backs.start()
    span_means()
    project(1, wt_words, 0, word_length)
    backs.wait()
    collect()
    vecs.start()
    projs.wait()
    vecs.wait()
    table_begin(1, pieces // 2, pieces)
    entity_rows()
    project(0, wt_ents, word_length, ent_count)
    for h in range(heads):
        attend(0, h)
    attention_part(0)
    one.begin(0)
    table_forward(0, pieces // 2)
    project(1, wt_ents, word_length, ent_count)
    attend(1, 0)
    one.pass_on(0)
    for h in range(1, heads):
        attend(1, h)
    attention_part(1)
    one.begin(1)
    table_forward(pieces // 2, pieces)
    one.wait_sum(0)
    first_rows(0)
    one.spread(0)
    one.pass_on(1)
    one.forward(0)
    one.wait_full(0)
    feed(0)
    two.begin(0)
    one.wait_sum(1)
    first_rows(1)
    one.spread(1)
    two.pass_on(0)
    one.forward(1)
    one.wait_full(1)
    feed(1)
    two.begin(1)
    two.wait_sum(0)
    second_rows(0)
    two.spread(0)
    two.pass_on(1)
    two.forward(0)
    two.wait_full(0)
    output_rows(0)
    two.wait_sum(1)
    second_rows(1)
    two.spread(1)
    two.forward(1)
    two.wait_full(1)
    output_rows(1)
    for s in range(seqs):
        one.drain(s)
        two.drain(s)
    table_end()


def quarter_scratch(seqs, length, width):
    return [
        pltpu.VMEM((seqs, length, width), BF),
        pltpu.VMEM((seqs, length // 2, width), BF),
        pltpu.VMEM((seqs, length // 4, width), BF),
        pltpu.VMEM((seqs, length // 4, width), BF),
    ]


def forward_layer(sizes, scored, capacity, words, arrays):
    seqs, length, word_length, heads = sizes
    n, n_mp = lax.axis_size("dp"), lax.axis_size("mp")
    width = words.shape[2]
    tokens = seqs * length
    local, ents = heads * DH, seqs * (length - word_length)
    table, w_up = arrays[5], arrays[11]
    cols_dev, rows_dev = table.shape
    units = w_up.shape[1]

    def like(*shape, dtype=BF):
        return jax.ShapeDtypeStruct(shape, dtype)

    outs = [
        like(n, 8, LANES, dtype=jnp.int32), like(1, ents, dtype=jnp.int32),
        like(seqs, word_length, length - word_length), like(ents, LANES, dtype=F32),
        like(seqs, word_length, LANES, dtype=F32), like(4, width, dtype=F32),
        like(cols_dev, ents), like(tokens, width),
        like(heads, 4 * DH, tokens), like(heads, 8, tokens, dtype=F32), like(local, tokens),
        like(heads, 4 * DH, width), like(heads, 4 * DH, width), like(tokens // 4, width, dtype=F32),
        like(tokens, width), like(tokens, units), like(tokens, units), like(tokens, width),
        like(seqs, word_length, width), like(seqs, length - word_length, width),
        like(seqs * scored, width), like(n_mp * cols_dev, rows_dev),
    ]
    return pl.pallas_call(
        functools.partial(forward_kernel, sizes, n, n_mp, capacity),
        out_shape=outs,
        in_specs=[pl.BlockSpec(memory_space=pl.ANY), pl.BlockSpec(memory_space=pltpu.SMEM)]
        + [VM] * (len(arrays) - 1),
        out_specs=[VM] * (len(outs) - 1) + [pl.BlockSpec(memory_space=pl.ANY)],
        scratch_shapes=[
            pltpu.VMEM((length, length), F32),
            pltpu.VMEM((length, length), BF),
            pltpu.VMEM((length, 256), F32),
            pltpu.VMEM((tokens // 4, width), F32),
            *quarter_scratch(seqs, length, width),
            *quarter_scratch(seqs, length, width),
            pltpu.VMEM((rows_dev, n * capacity), BF),
            pltpu.VMEM((n, cols_dev, LANES), BF), pltpu.VMEM((n, cols_dev, LANES), BF),
            pltpu.VMEM((n_mp, cols_dev, ents), BF), pltpu.VMEM((n_mp, cols_dev, width), BF),
            pltpu.VMEM((ents, width), F32), pltpu.VMEM((n, 8, LANES), jnp.int32),
            pltpu.SemaphoreType.DMA((seqs, 5)), pltpu.SemaphoreType.DMA((seqs, 5)),
            pltpu.SemaphoreType.DMA((seqs, 5)), pltpu.SemaphoreType.DMA((seqs, 5)),
            pltpu.SemaphoreType.DMA((seqs + 1,)),
            pltpu.SemaphoreType.DMA((2, n - 1)), pltpu.SemaphoreType.DMA((2, n - 1)),
            pltpu.SemaphoreType.DMA((2, n_mp - 1)), pltpu.SemaphoreType.DMA((2, n_mp - 1)),
            pltpu.SemaphoreType.DMA((3, cols_dev // 16)), pltpu.SemaphoreType.DMA((3, cols_dev // 16)),
        ],
        compiler_params=pltpu.CompilerParams(
            collective_id=3, has_side_effects=True, vmem_limit_bytes=60 * 2**20
        ),
    )(words, *arrays)


class Job:
    def __init__(self, rows, buf, out, arrivals, send, recv, n, first=(0, 1, 2)):
        self.buf, self.out, self.arrivals, self.send, self.recv = buf, out, arrivals, send, recv
        self.rows = rows
        self.me = lax.axis_index("dp")
        self.bits, self.halvings = job_plan(rows, n)
        self.order = list(range(self.bits))
        if self.bits >= len(first):
            self.order[: len(first)] = first

    def bit(self, k):
        return lax.rem(self.me // 2 ** self.order[k], 2)

    def peer(self, k):
        return self.me + (1 - 2 * self.bit(k)) * 2 ** self.order[k]

    def offset(self, k):
        start = 0
        for i in range(k):
            start = start + self.bit(i) * (self.rows >> (i + 1))
        return start

    def copy(self, index, k, src, dst):
        return remote(src, dst, self.send.at[index], self.recv.at[index], "dp", self.peer(k))

    def steps(self):
        size = self.rows
        for k in range(self.bits):
            keep = self.offset(min(k, self.halvings))
            away = keep
            if k < self.halvings:
                size //= 2
                away = keep + (1 - self.bit(k)) * size
                keep = keep + self.bit(k) * size
            arrived = self.arrivals[k]
            copy = self.copy(k, k, self.buf.at[span(away, size)], arrived)
            copy.start()
            yield
            copy.wait()
            last = k == self.bits - 1

            def body(row, keep=keep, arrived=arrived, last=last):
                at = span(keep + row, 16)
                value = self.buf[at].astype(F32) + arrived[span(row, 16)].astype(F32)
                (self.out if last else self.buf)[at] = value.astype(BF)

            each(size, 16, body, 4)
        for k in reversed(range(self.halvings)):
            done = self.out.at[span(self.offset(k + 1), size)]
            copy = self.copy(self.bits + k, k, done, done)
            copy.start()
            yield
            copy.wait()
            size *= 2


def job_plan(rows, n):
    bits, halvings, size = n.bit_length() - 1, 0, rows
    while halvings < bits - 1 and (size // 2) % 16 == 0:
        size, halvings = size // 2, halvings + 1
    return bits, halvings


def job_cuts(units, width, head_rows, proj_rows, heads):
    orders = [
        ((1, 2, 0), (0, 1, 2), (1, 2, 0)),
        ((0, 1, 2), (0, 1, 2), (0, 1, 2)),
        ((1, 0, 2),),
        ((0, 1, 2),),
        ((1, 2, 0), (0, 1, 2)),
        ((0, 1, 2), (0, 1, 2)),
        ((0, 1, 2), (0, 1, 2)),
    ]
    cuts = [(units, [units // 3] * 3), (width, [width // 3] * 3)]
    cuts += [(head_rows, [head_rows]), (proj_rows, [proj_rows])]
    cuts += [(7 * DH, [4 * DH, 3 * DH])] * heads
    return [(rows, pieces, order) for (rows, pieces), order in zip(cuts, orders)]


def job_scratch(rows, width, n):
    bits, halvings = job_plan(rows, n)
    return [
        pltpu.VMEM((rows >> min(k + 1, halvings), width), BF) for k in range(bits)
    ]


def backward_kernel(sizes, n, n_mp, *refs):
    seqs, length, word_length, heads = sizes
    refs = list(refs)

    def take(count):
        taken = refs[:count]
        del refs[:count]
        return taken

    cot_words, cot_ents = take(2)
    (
        d_head, head_grad, center2, slope, hidden, first_low, center1, w_up, w_down, norms,
        small_in, ent_proj, vec_rows, place, received, inside, spans,
    ) = take(17)
    late_in = take(8)
    down_out, up_out, head_all, proj_out, *per_head_out = take(4 + heads)
    word_grads, table_hits, small = take(3)
    ctx, qkv, lse, wt_words, wt_ents, stream, mask, w_out = late = take(8)
    sums, d_ffn, d_pre, d_attn, d_first, dctx, sT, dpT, pT, dsT, dcat = take(11)
    head_out, small_mp, small_dp, outbox, gw, inbox, onehot = take(7)
    part, r1, s2, r2 = take(4)
    (
        send1, recv1, send2, recv2, job_send, job_recv, late_sem, cot_sem,
        mp_send, mp_recv, dp_send, dp_recv, out_sem,
    ) = take(13)
    width = stream.shape[1]
    units = w_up.shape[1]
    me_mp, me_dp = lax.axis_index("mp"), lax.axis_index("dp")
    bits = n.bit_length() - 1
    jobs = []
    groups = [[], [], [], []] + [[] for h in range(heads)]
    buffers = take(len(groups))
    for group, buf, out, (rows, cuts, orders) in zip(
        groups, buffers, [down_out, up_out, head_out, proj_out, *per_head_out],
        job_cuts(units, width, head_out.shape[0], proj_out.shape[0], heads),
    ):
        start = 0
        for count, order in zip(cuts, orders):
            at = pl.ds(start, count)
            start += count
            index = len(jobs)
            jobs.append(
                Job(
                    count, buf.at[at], out.at[at], take(bits), job_send.at[index],
                    job_recv.at[index], n, order,
                )
            )
            group.append(jobs[-1])
    down_jobs, up_jobs, (head_job,), (proj_job,), *heads_jobs = groups
    down_buf, up_buf, head_buf, proj_buf, *heads_buf = buffers
    one = Quarters(part, r1, s2, r2, d_attn, send1, recv1)
    two = Quarters(part, r1, s2, r2, gw, send2, recv2)
    barrier = pltpu.get_barrier_semaphore()
    greet(barrier, "mp", n_mp)
    greet(barrier, "dp", n)
    cots = []
    for s in range(seqs):
        for k, (source, start, count) in enumerate(
            ((cot_words, 0, word_length), (cot_ents, word_length, length - word_length))
        ):
            target = d_attn.at[pl.ds(s * length + start, count)]
            cots.append(pltpu.make_async_copy(source.at[s], target, cot_sem.at[s, k]))
            cots[-1].start()
    late_copies = [
        pltpu.make_async_copy(source, target, late_sem.at[i])
        for i, (source, target) in enumerate(zip(late_in, late))
    ]
    for copy in late_copies:
        copy.start()
    running = {}

    def launch(job):
        running[id(job)] = job.steps()
        next(running[id(job)])

    def step(*which):
        for job in which:
            next(running[id(job)], 0)

    def finish(job):
        for _ in running[id(job)]:
            pass

    sums[...] = jnp.zeros_like(sums)

    spare = d_first.shape[0] - 16

    def second_back(s):
        start = one.own_row(0, 0)

        def rows_of(row, extra=None):
            at = span(s * length + row, 16)
            cot = d_attn[at].astype(F32)
            if extra is not None:
                cot = cot + extra
            center = center2[at].astype(F32)
            inv = scaled(center)
            normed = center * inv
            sums[0] += cot * normed
            sums[1] += cot
            grad = cot * norms[2:3]
            value = inv * (
                grad
                - jnp.mean(grad, axis=-1, keepdims=True)
                - normed * jnp.mean(grad * normed, axis=-1, keepdims=True)
            )
            d_ffn[at] = value.astype(BF)

            own = (row >= start) & (row < start + one.quarter)
            d_first[span(jnp.where(own, s * one.quarter + row - start, spare), 16)] = value

        scored = d_head.shape[1]
        each(word_length, 16, rows_of, 4)
        each(scored, 16, lambda row: rows_of(row + word_length, d_head[s, span(row, 16)]))
        each(length - word_length - scored, 16, lambda row: rows_of(row + word_length + scored), 7)

    def feed_back(s):
        rows = slice(s * length, (s + 1) * length)
        tile = 256
        for j in range(units // tile):
            cols = slice(j * tile, (j + 1) * tile)
            sT[:, 0:tile] = contract(d_ffn[rows], w_down[cols], 1, 1)

            def body(row):
                at = span(s * length + row, 32)
                d_pre[at, cols] = (
                    sT[pl.ds(row, 32), 0:tile] * slope[at, cols].astype(F32)
                ).astype(BF)

            each(length, 32, body, 4)
        for j in range(width // tile):
            cols = slice(j * tile, (j + 1) * tile)
            part[s, :, cols] = contract(d_pre[rows], w_up[cols], 1, 1).astype(BF)

    def first_back(s):
        def body(row):
            at = one.own_row(s, row)
            mine = span(s * one.quarter + row, 16)
            value = d_first[mine] + one.total(s, row)
            center = center1[mine]
            inv = scaled(center)
            normed = center * inv
            sums[2] += value * normed
            sums[3] += value
            grad = value * norms[0:1]
            value = inv * (
                grad
                - jnp.mean(grad, axis=-1, keepdims=True)
                - normed * jnp.mean(grad * normed, axis=-1, keepdims=True)
            )
            d_first[mine] = value
            d_attn[span(at, 16)] = value.astype(BF)

        each(one.quarter, 16, body, 5)

    def context_back(s):
        cols = slice(s * length, (s + 1) * length)
        dctx[:, cols] = contract(w_out[...], d_attn[cols], 1, 1).astype(BF)

    def attend_back(s, h):
        cols = pl.ds(s * length, length)
        w_cols = pl.ds(s * length, word_length)
        e_cols = pl.ds(s * length + word_length, length - word_length)
        mine = slice(h * DH, (h + 1) * DH)
        scores_of(qkv, sT, h, cols, word_length)
        dpT[...] = contract(qkv[h, 192:256, cols], dctx[mine, cols], 0, 0)

        def body(col):
            here = pl.ds(col, LANES)
            at = pl.ds(pl.multiple_of(s * length + col, LANES), LANES)
            delta = jnp.sum(
                ctx[mine, at].astype(F32) * dctx[mine, at].astype(F32), axis=0, keepdims=True
            )
            log_total = lse[h, 0:1, at]
            probs = jnp.exp(sT[0:word_length, here] + mask[s] - log_total)
            pT[0:word_length, here] = probs.astype(BF)
            dsT[0:word_length, here] = (probs * (dpT[0:word_length, here] - delta)).astype(BF)
            probs = jnp.exp(sT[word_length:, here] - log_total)
            pT[word_length:, here] = probs.astype(BF)
            dsT[word_length:, here] = (probs * (dpT[word_length:, here] - delta)).astype(BF)

        each(length, LANES, body)
        d_words, d_ents = dsT[0:word_length], dsT[word_length:]
        dcat[h, 0:64, cols] = (contract(qkv[h, 128:192, w_cols], d_words, 1, 0) * 0.125).astype(BF)
        dcat[h, 64:128, cols] = (contract(qkv[h, 128:192, e_cols], d_ents, 1, 0) * 0.125).astype(BF)
        dcat[h, 128:192, w_cols] = contract(qkv[h, 0:64, cols], d_words, 1, 1).astype(BF)
        dcat[h, 128:192, e_cols] = contract(qkv[h, 64:128, cols], d_ents, 1, 1).astype(BF)
        dcat[h, 192:256, cols] = contract(dctx[mine, cols], pT[...], 1, 1).astype(BF)

    def head_grads(h):
        buf = heads_buf[h]
        from_words, from_ents = None, None
        for s in range(seqs):
            middle, start, end = s * length + word_length, s * length, (s + 1) * length
            words = matmul(dcat[h, :, start:middle], stream[start:middle])
            ents = matmul(dcat[h, :, middle:end], stream[middle:end])
            from_words = words if s == 0 else from_words + words
            from_ents = ents if s == 0 else from_ents + ents
        buf[0:128] = from_words[0:128].astype(BF)
        buf[128:256] = (from_words[128:256] + from_ents[128:256]).astype(BF)
        buf[256:384] = from_ents[0:128].astype(BF)
        buf[384:448] = matmul(ctx[h * DH : (h + 1) * DH], d_attn[...]).astype(BF)

    def stream_part(s):
        for start in range(0, length, LANES):
            weight = wt_words if start < word_length else wt_ents
            cols = slice(s * length + start, s * length + start + LANES)
            value = contract(dcat[0, :, cols], weight[0], 0, 0)
            for h in range(1, heads):
                value = value + contract(dcat[h, :, cols], weight[h], 0, 0)
            part[s, start : start + LANES] = value.astype(BF)

    def last_rows(s):
        def body(row):
            at = two.own_row(s, row)
            value = d_first[span(s * two.quarter + row, 16)] + two.total(s, row)
            gw[span(at, 16)] = value.astype(BF)

        each(two.quarter, 16, body, 5)

    def down_tile(j):
        cols = slice(j * 256, (j + 1) * 256)
        down_buf[cols] = contract(hidden[:, cols], d_ffn[...], 0, 0).astype(BF)

    def up_tile(j):
        cols = slice(j * 256, (j + 1) * 256)
        up_buf[cols] = contract(first_low[:, cols], d_pre[...], 0, 0).astype(BF)

    def wait_cots(s):
        for copy in cots[2 * s : 2 * s + 2]:
            copy.wait()

    def wait_late():
        for copy in late_copies:
            copy.wait()

    small_over_mp = Spread(
        "mp", n_mp, lambda peer: small_mp.at[me_mp], small_mp, mp_send.at[0], mp_recv.at[0]
    )
    small_over_dp = Spread(
        "dp", n, lambda peer: small_dp.at[me_dp], small_dp, dp_send.at[0], dp_recv.at[0]
    )
    boxes = Spread("dp", n, lambda peer: outbox.at[peer], inbox, dp_send.at[1], dp_recv.at[1])
    head_rows = head_out.shape[0]
    head_place = span(me_mp * head_rows, head_rows)

    def head_copy(distance, peer, owner):
        return remote(
            head_out, head_all.at[span(owner * head_rows, head_rows)], mp_send.at[1, distance - 1],
            mp_recv.at[1, distance - 1], "mp", peer,
        )

    def small_first():
        mine = small_in[...]
        mine = mine + jnp.concatenate(
            [jnp.sum(sums[row], axis=0, keepdims=True) for row in range(4)]
            + [jnp.zeros((4, width), F32)]
        )
        small_mp[me_mp] = mine
        small_over_mp.start()

    def small_second():
        small_over_mp.wait()
        total = small_mp[0]
        for device in range(1, n_mp):
            total = total + small_mp[device]
        row = lax.broadcasted_iota(jnp.int32, total.shape, 0)
        small_dp[me_dp] = jnp.where((row == 2) | (row == 3), total, small_mp[me_mp])
        small_over_dp.start()

    def small_last():
        small_over_dp.wait()

        def add(device, total):
            return total + small_dp[device]

        small[...] = lax.fori_loop(1, n, add, small_dp[0])

    def head_first():
        head_all[head_place] = head_out[...]
        for distance in range(1, n_mp):
            head_copy(distance, lax.rem(me_mp + distance, n_mp), me_mp).start()

    def head_last():
        for distance in range(1, n_mp):
            source = lax.rem(me_mp + n_mp - distance, n_mp)
            head_copy(distance, source, source).wait()

    def entities():
        grads, rows = None, []
        count = length - word_length
        for s in range(seqs):
            d_ent = gw[s * length + word_length : (s + 1) * length]
            value = matmul(vec_rows[:, s * count : (s + 1) * count], d_ent)
            grads = value if s == 0 else grads + value
            rows.append(contract(ent_proj[...], d_ent, 1, 1).astype(BF))
        proj_buf[...] = grads.astype(BF)
        launch(proj_job)
        rows = jnp.concatenate(rows, axis=1)
        slot = lax.broadcasted_iota(jnp.int32, (LANES, seqs * count), 0)

        def fill(owner, carry):
            placed = jnp.where(slot + owner * LANES == place[...], 1.0, 0.0).astype(BF)
            outbox[owner] = contract(rows, placed, 1, 1).astype(BF)
            return carry

        lax.fori_loop(0, n, fill, 0)
        inbox[me_dp] = outbox[me_dp]
        boxes.start()

    out_copies = []

    def words_out(s):
        width_part = width // 2
        rows = slice(s * length, s * length + word_length)
        at = slice(s * (length - word_length), (s + 1) * (length - word_length))
        shared = gw[s * length + word_length : (s + 1) * length].astype(F32) / spans[at, 0:1]
        for half, source in enumerate((sT, dpT)):
            if s > 0:
                out_copies[2 * (s - 1) + half].wait()
            cols = slice(half * width_part, (half + 1) * width_part)
            source[0:word_length, 0:width_part] = gw[rows, cols].astype(F32) + matmul(
                inside[s], shared[:, cols].astype(BF)
            )
            out_copies.append(
                pltpu.make_async_copy(
                    source.at[pl.ds(0, word_length), pl.ds(0, width_part)],
                    word_grads.at[s, :, pl.ds(half * width_part, width_part)], out_sem.at[s, half],
                )
            )
            out_copies[-1].start()

    pieces = chunks_of(table_hits.shape[1], onehot.shape[0])
    parts = (len(pieces) + 3) // 4

    def table_part(part):
        capacity = onehot.shape[1] // n
        ids = jnp.concatenate([received[source, 0:1, 0:capacity] for source in range(n)], axis=1)
        rows = jnp.concatenate([inbox[source, :, 0:capacity] for source in range(n)], axis=1)
        for start, count in pieces[part * parts : (part + 1) * parts]:

            def body(row, start=start):
                index = lax.broadcasted_iota(jnp.int32, (32, n * capacity), 0) + (row + start)
                onehot[span(row, 32)] = jnp.where(index == ids, 1.0, 0.0).astype(BF)

            each(count, 32, body, 2)
            table_hits[:, start : start + count] = contract(rows, onehot[0:count], 1, 1)

    head_buf[...] = head_grad[head_place]
    wait_cots(0)
    second_back(0)
    feed_back(0)
    pl.semaphore_wait(barrier, n_mp - 1 + n - 1)
    one.begin(0)
    launch(head_job)
    wait_cots(1)
    second_back(1)
    one.pass_on(0)
    step(head_job)
    down_tile(0)
    launch(down_jobs[0])
    down_tile(1)
    launch(down_jobs[1])
    down_tile(2)
    launch(down_jobs[2])
    feed_back(1)
    one.begin(1)
    step(head_job)
    up_tile(0)
    launch(up_jobs[0])
    up_tile(1)
    launch(up_jobs[1])
    up_tile(2)
    launch(up_jobs[2])
    step(down_jobs[0])
    one.pass_on(1)
    step(down_jobs[1], head_job)
    one.wait_sum(0)
    first_back(0)
    one.spread(0)
    step(down_jobs[2], up_jobs[0], down_jobs[1], down_jobs[0])
    one.wait_sum(1)
    first_back(1)
    one.spread(1)
    small_first()
    step(up_jobs[1], up_jobs[0], down_jobs[2])
    one.forward(0)
    step(up_jobs[2], up_jobs[1], head_job, down_jobs[1])
    one.wait_full(0)
    small_second()
    wait_late()
    context_back(0)
    step(down_jobs[0])
    attend_back(0, 0)
    step(up_jobs[2], down_jobs[2], head_job)
    finish(head_job)
    head_first()
    step(up_jobs[0])
    attend_back(0, 1)
    step(down_jobs[1])
    attend_back(0, 2)
    one.first(0).wait_send()
    stream_part(0)
    two.begin(0)
    step(up_jobs[1], up_jobs[0])
    one.forward(1)
    one.wait_full(1)
    one.drain(0, True)
    one.drain(1)
    context_back(1)
    step(down_jobs[1], down_jobs[0], up_jobs[1])
    attend_back(1, 0)
    two.pass_on(0)
    head_grads(0)
    launch(heads_jobs[0][0])
    launch(heads_jobs[0][1])
    step(up_jobs[0], up_jobs[2])
    attend_back(1, 1)
    head_grads(1)
    launch(heads_jobs[1][0])
    launch(heads_jobs[1][1])
    step(down_jobs[0])
    attend_back(1, 2)
    step(up_jobs[1], down_jobs[2])
    stream_part(1)
    two.begin(1)
    head_grads(2)
    launch(heads_jobs[2][0])
    launch(heads_jobs[2][1])
    step(heads_jobs[0][0], heads_jobs[0][1], up_jobs[2])
    two.pass_on(1)
    two.wait_sum(0)
    last_rows(0)
    two.spread(0)
    small_last()
    step(heads_jobs[1][0], down_jobs[2], heads_jobs[0][0], heads_jobs[1][1])
    step(heads_jobs[0][1])
    two.wait_sum(1)
    step(heads_jobs[1][0])
    last_rows(1)
    two.spread(1)
    step(heads_jobs[1][1], heads_jobs[2][0], heads_jobs[0][1], heads_jobs[2][1])
    two.forward(0)
    step(heads_jobs[2][0], heads_jobs[1][0], heads_jobs[0][1], up_jobs[2])
    step(heads_jobs[2][1])
    two.forward(1)
    two.wait_full(0)
    step(heads_jobs[1][1], heads_jobs[0][0], heads_jobs[1][0])
    two.wait_full(1)
    entities()
    words_out(0)
    step(heads_jobs[1][1], heads_jobs[0][1], heads_jobs[2][0])
    words_out(1)
    step(heads_jobs[2][1], heads_jobs[1][0], heads_jobs[2][0], proj_job)
    boxes.wait()
    table_part(0)
    table_part(1)
    step(heads_jobs[2][1], heads_jobs[0][0], proj_job, heads_jobs[1][1])
    table_part(2)
    table_part(3)
    step(proj_job, heads_jobs[2][0], heads_jobs[0][0], proj_job)
    step(heads_jobs[2][1], proj_job)
    head_last()
    for s in range(seqs):
        two.drain(s)
    for copy in out_copies[-2:]:
        copy.wait()
    for job in jobs:
        finish(job)


def backward_layer(sizes, n, capacity, rows_dev, cots, now, late):
    seqs, length, word_length, heads = sizes
    stream, w_up, ent_proj = late[5], now[7], now[11]
    n_mp = lax.axis_size("mp")
    tokens, width = stream.shape
    units, local = w_up.shape[1], heads * DH
    head_rows, head_width = now[1].shape[0] // n_mp, now[1].shape[1]
    bits = n.bit_length() - 1
    outs = [(units, width), (width, units), (n_mp * head_rows, head_width), ent_proj.shape]
    outs += [(7 * DH, width)] * heads
    outs = [jax.ShapeDtypeStruct(shape, BF) for shape in outs]
    outs += [
        jax.ShapeDtypeStruct((seqs, word_length, width), F32),
        jax.ShapeDtypeStruct((ent_proj.shape[0], rows_dev), F32),
        jax.ShapeDtypeStruct((8, width), F32),
    ]
    cuts = job_cuts(units, width, head_rows, ent_proj.shape[0], heads)
    widths = [width, units, head_width] + [width] * (1 + heads)
    job_count = sum(len(sizes) for _, sizes, _ in cuts)
    scratch = [pltpu.VMEM(value.shape, value.dtype) for value in late]
    scratch += [
        pltpu.VMEM((4, 16, width), F32), pltpu.VMEM((tokens, width), BF),
        pltpu.VMEM((tokens, units), BF), pltpu.VMEM((tokens, width), BF),
        pltpu.VMEM((tokens // 4 + 16, width), F32), pltpu.VMEM((local, tokens), BF),
        pltpu.VMEM((length, length), F32), pltpu.VMEM((length, length), F32),
        pltpu.VMEM((length, length), BF), pltpu.VMEM((length, length), BF),
        pltpu.VMEM((heads, 4 * DH, tokens), BF),
        pltpu.VMEM((head_rows, head_width), BF), pltpu.VMEM((n_mp, 8, width), F32),
        pltpu.VMEM((n, 8, width), F32), pltpu.VMEM((n, ent_proj.shape[0], LANES), BF),
        pltpu.VMEM((tokens, width), BF), pltpu.VMEM((n, ent_proj.shape[0], LANES), BF),
        pltpu.VMEM((256, n * capacity), BF),
        *quarter_scratch(seqs, length, width),
        pltpu.SemaphoreType.DMA((seqs, 5)), pltpu.SemaphoreType.DMA((seqs, 5)),
        pltpu.SemaphoreType.DMA((seqs, 5)), pltpu.SemaphoreType.DMA((seqs, 5)),
        pltpu.SemaphoreType.DMA((job_count, 2 * bits)),
        pltpu.SemaphoreType.DMA((job_count, 2 * bits)),
        pltpu.SemaphoreType.DMA((len(late),)), pltpu.SemaphoreType.DMA((seqs, 2)),
        pltpu.SemaphoreType.DMA((2, n_mp - 1)), pltpu.SemaphoreType.DMA((2, n_mp - 1)),
        pltpu.SemaphoreType.DMA((2, n - 1)), pltpu.SemaphoreType.DMA((2, n - 1)),
        pltpu.SemaphoreType.DMA((seqs, 2)),
    ]
    scratch += [pltpu.VMEM((rows, columns), BF) for (rows, _, _), columns in zip(cuts, widths)]
    for (_, counts, _), columns in zip(cuts, widths):
        for count in counts:
            scratch += job_scratch(count, columns, n)
    hbm = pl.BlockSpec(memory_space=pl.ANY)
    return pl.pallas_call(
        functools.partial(backward_kernel, sizes, n, n_mp),
        out_shape=outs,
        in_specs=[hbm] * len(cots) + [VM] * len(now) + [hbm] * len(late),
        out_specs=[VM] * (len(outs) - 3) + [hbm, VM, VM],
        scratch_shapes=scratch,
        compiler_params=pltpu.CompilerParams(
            collective_id=7, has_side_effects=True, vmem_limit_bytes=62 * 2**20
        ),
    )(*cots, *now, *late)


def head_kernel(
    n, head_in, w_head, gain, table, target, d_head, grad_head, small, loss, table_grad,
    all_head, logits, probs, onehot, turned, tops, parts_out, parts_in, rows_out, rows_in,
    stats_out, stats_in, send, recv,
):
    me_dp, me_mp = lax.axis_index("dp"), lax.axis_index("mp")
    mine, vec_width = all_head.shape[1:]
    total = n * mine
    rows_dev = table.shape[1]
    cols_dev = table_grad.shape[0]
    block = logits.shape[0]
    blocks = total // block
    owners = block // mine
    barrier = pltpu.get_barrier_semaphore()
    greet(barrier, "dp", n)

    pre = matmul(head_in[...], w_head[...])
    bell = lax.erf(pre * 0.7071067811865476) * 0.5 + 0.5
    value = pre * bell
    center = value - jnp.mean(value, axis=-1, keepdims=True)
    inv = scaled(center)
    normed = center * inv
    all_head[me_dp] = (normed * gain[...]).astype(BF)
    pl.semaphore_wait(barrier, n - 1)
    heads = Spread("dp", n, lambda peer: all_head.at[me_dp], all_head, send.at[0], recv.at[0])
    heads.start()

    def fill_onehot(b):
        count = block // target.shape[1]
        rows = target[pl.ds(pl.multiple_of(b * count, count), count)]
        wanted = jnp.concatenate([rows[i : i + 1] for i in range(count)], axis=1) - me_dp * rows_dev

        def body(row):
            index = lax.broadcasted_iota(jnp.int32, (80, block), 0) + row
            onehot[span(row, 80)] = jnp.where(index == wanted, 1.0, 0.0).astype(BF)

        each(rows_dev, 80, body)

    def slots_of(b):
        return all_head[pl.ds(b * owners, owners)].reshape(block, vec_width)

    def fill_probs(b):
        slots = slots_of(b)
        for start, count in chunks_of(rows_dev, 1024):
            logits[:, start : start + count] = matmul(slots, table[:, start : start + count])

        def body(row):
            x = logits[span(row, 16)]
            top = jnp.max(x, axis=-1, keepdims=True)
            x = jnp.exp(x - top)
            lane = lax.broadcasted_iota(jnp.int32, (16, LANES), 1)
            amount = jnp.sum(x, axis=-1, keepdims=True)
            tops[span(row, 16)] = jnp.where(lane == 0, top, jnp.where(lane == 1, amount, 0.0))
            probs[span(row, 16)] = x.astype(BF)

        each(block, 16, body, 2)

    def over_blocks(body):
        if blocks == 1:
            body(0)
        else:
            lax.fori_loop(0, blocks, lambda b, carry: (body(b), carry)[1], 0)

    def target_part(b):
        fill_onehot(b)
        found = matmul(table[...], onehot[...])
        turned[...] = found
        rows = jnp.transpose(found).astype(BF).reshape(owners, mine, vec_width)
        rows_out[pl.ds(b * owners, owners)] = rows

    def block_part(b):
        if blocks > 1:
            target_part(b)
        slots = jnp.transpose(slots_of(b).astype(F32))
        own = jnp.sum(slots * turned[...], axis=0, keepdims=True)
        fill_probs(b)
        part = contract(probs[...], table[...], 1, 1)
        at = pl.ds(b * owners, owners)
        parts_out[at, :, 0:vec_width] = part.reshape(owners, mine, vec_width)
        parts_out[at, :, vec_width:] = tops[...].reshape(owners, mine, LANES)
        columns = pl.ds(pl.multiple_of(b * block, LANES), block)
        stats_out[0:2, columns] = jnp.transpose(tops[...])[0:2]
        stats_out[2:3, columns] = own

    if blocks == 1:
        target_part(0)
    heads.wait()
    stats_out[...] = jnp.zeros_like(stats_out)
    over_blocks(block_part)
    exchanges = [
        Spread("dp", n, lambda peer: parts_out.at[peer], parts_in, send.at[1], recv.at[1]),
        Spread("dp", n, lambda peer: rows_out.at[peer], rows_in, send.at[2], recv.at[2]),
        Spread("dp", n, lambda peer: stats_out, stats_in, send.at[3], recv.at[3]),
    ]
    for exchange_one in exchanges:
        exchange_one.start()
    parts_in[me_dp] = parts_out[me_dp]
    rows_in[me_dp] = rows_out[me_dp]
    stats_in[me_dp] = stats_out[...]
    for exchange_one in exchanges:
        exchange_one.wait()

    def combine(source, state):
        top, amount, sums, targets = state
        part = parts_in[source]
        other = part[:, vec_width : vec_width + 1]
        new_top = jnp.maximum(top, other)
        old, new = jnp.exp(top - new_top), jnp.exp(other - new_top)
        amount = amount * old + part[:, vec_width + 1 : vec_width + 2] * new
        sums = sums * old + part[:, 0:vec_width] * new
        return new_top, amount, sums, targets + rows_in[source].astype(F32)

    first = parts_in[0]
    state = (
        first[:, vec_width : vec_width + 1], first[:, vec_width + 1 : vec_width + 2],
        first[:, 0:vec_width], rows_in[0].astype(F32),
    )
    _, amount, sums, targets = lax.fori_loop(1, n, combine, state)
    d_vec = sums / amount - targets
    small[...] = jnp.zeros_like(small)
    small[4:5, 0:vec_width] = jnp.sum(d_vec * normed, axis=0, keepdims=True)
    grad = d_vec * gain[...]
    d_value = inv * (
        grad
        - jnp.mean(grad, axis=-1, keepdims=True)
        - normed * jnp.mean(grad * normed, axis=-1, keepdims=True)
    )
    d_pre = d_value * (bell + pre * jnp.exp(pre * pre * -0.5) * 0.3989422804014327)
    d_low = d_pre.astype(BF)
    d_head[...] = contract(d_low, w_head[...], 1, 1)
    grad_head[...] = contract(head_in[...], d_low, 0, 0).astype(BF)

    def stat(row):
        def top_of(source, top):
            return jnp.maximum(top, stats_in[source, 0:1])

        top = lax.fori_loop(1, n, top_of, stats_in[0, 0:1])

        def add(source, state):
            amount, targets = state
            amount = amount + stats_in[source, 1:2] * jnp.exp(stats_in[source, 0:1] - top)
            return amount, targets + stats_in[source, 2:3]

        zero = jnp.zeros_like(top)
        amount, targets = lax.fori_loop(0, n, add, (zero, zero))
        return top + jnp.log(amount), targets

    log_total, targets = stat(0)
    loss[...] = jnp.broadcast_to(log_total - targets, loss.shape)
    stats_out[3:4] = jnp.exp(stats_out[0:1] - log_total)

    def table_part(b):
        if blocks > 1:
            fill_onehot(b)
            fill_probs(b)
        columns = pl.ds(pl.multiple_of(b * block, LANES), block)
        turned[...] = jnp.transpose(slots_of(b).astype(F32))
        own = turned[span(me_mp * cols_dev, cols_dev)]
        scaled_own = (own * stats_out[3:4, columns]).astype(BF)
        own = own.astype(BF)
        for start, count in chunks_of(rows_dev, 1024):
            at = slice(start, start + count)
            value = matmul(scaled_own, probs[:, at]) - contract(own, onehot[at], 1, 1)
            if blocks == 1:
                table_grad[:, at] = value
            else:
                table_grad[:, at] += value

    if blocks > 1:
        table_grad[...] = jnp.zeros_like(table_grad)
    over_blocks(table_part)


def head_layer(n, head_in, w_head, gain, table, target, cols_dev):
    mine, width = head_in.shape
    vec_width = w_head.shape[1]
    total = n * mine
    rows_dev = table.shape[1]
    block = math.gcd(total, 256)
    shapes = [
        ((mine, width), F32), ((width, vec_width), BF), ((8, width), F32), ((8, total), F32),
        ((cols_dev, rows_dev), F32),
    ]
    return pl.pallas_call(
        functools.partial(head_kernel, n),
        out_shape=[jax.ShapeDtypeStruct(*shape) for shape in shapes],
        in_specs=[VM] * 5,
        out_specs=[VM] * 5,
        scratch_shapes=[
            pltpu.VMEM((n, mine, vec_width), BF), pltpu.VMEM((block, rows_dev), F32),
            pltpu.VMEM((block, rows_dev), BF), pltpu.VMEM((rows_dev, block), BF),
            pltpu.VMEM((vec_width, block), F32), pltpu.VMEM((block, LANES), F32),
            pltpu.VMEM((n, mine, vec_width + LANES), F32), pltpu.VMEM((n, mine, vec_width + LANES), F32),
            pltpu.VMEM((n, mine, vec_width), BF), pltpu.VMEM((n, mine, vec_width), BF),
            pltpu.VMEM((8, total), F32), pltpu.VMEM((n, 8, total), F32),
            pltpu.SemaphoreType.DMA((4, n - 1)), pltpu.SemaphoreType.DMA((4, n - 1)),
        ],
        compiler_params=pltpu.CompilerParams(
            collective_id=5, has_side_effects=True, vmem_limit_bytes=56 * 2**20
        ),
    )(head_in, w_head, gain, table, target)


def shards(
    words, word_extra, span_pos, span_len, entity_shard, entity_row, targets, table, ent_proj,
    query_weight, w_key, w_value, w_out, gain_attn, bias_attn, w_up, w_down, gain_ffn, bias_ffn,
    w_head, gain_head, cot_words, cot_ents,
):
    n_dp = lax.axis_size("dp")
    n_mp = lax.axis_size("mp")
    seq_count, word_length, model_width = words.shape
    ent_len = span_pos.shape[1]
    masked_len = targets.shape[1]
    tokens_len = word_length + ent_len
    rows_dev, cols_dev = table.shape
    local_width = w_key.shape[1]
    heads_local = local_width // DH
    ent_total = seq_count * ent_len

    capacity = max(16, 2 * ent_total // n_dp)
    sizes = (seq_count, tokens_len, word_length, heads_local)
    (
        received, place, inside, spans, mask, norms, vec_rows, stream, qkv, lse, ctx, wt_words, wt_ents,
        center1, first_low, hidden, slope, center2, out_words, out_ents, head_in, table_rows,
    ) = forward_layer(
        sizes, masked_len, capacity, words,
        (
            word_extra, span_pos, span_len, entity_shard.reshape(seq_count, ent_len), entity_row,
            table.T, ent_proj, query_weight.transpose(0, 2, 1), w_key.T, w_value.T, w_out, w_up, w_down,
            gain_attn, bias_attn, gain_ffn, bias_ffn,
        ),
    )
    d_head, grad_head, small, loss, table_grad = head_layer(
        n_dp, head_in, w_head, gain_head[None], table_rows, targets, cols_dev
    )
    loss = loss[0]
    *sums, grad_words, table_hits, small = backward_layer(
        sizes, n_dp, capacity, rows_dev,
        (cot_words, cot_ents),
        (
            d_head.reshape(seq_count, masked_len, model_width), grad_head, center2, slope, hidden,
            first_low, center1, w_up, w_down, norms, small, ent_proj, vec_rows, place,
            received, inside, spans,
        ),
        (
            ctx, qkv, lse, wt_words, wt_ents, stream, mask, w_out,
        ),
    )
    grad_down, grad_up, grad_head, grad_ent_proj, *per_head = (a.astype(F32) for a in sums)
    per_head = [a.reshape(7, DH, model_width) for a in per_head]

    def columns_of(which):
        return jnp.concatenate([a[which] for a in per_head])

    grad_query = jnp.stack([columns_of(i) for i in (0, 1, 4, 5)]).transpose(0, 2, 1)
    grad_key, grad_value, grad_out = columns_of(2).T, columns_of(3).T, columns_of(6)
    table_grad = (table_grad + table_hits).T
    grad_gain_ffn, grad_bias_ffn, grad_gain_attn, grad_bias_attn = (small[i] for i in range(4))
    grad_gain_head = small[4, : w_head.shape[1]]
    return (
        out_words, out_ents, loss, grad_words, table_grad, grad_ent_proj, grad_query, grad_key,
        grad_value, grad_out, grad_gain_attn, grad_bias_attn, grad_up, grad_down, grad_gain_ffn,
        grad_bias_ffn, grad_head, grad_gain_head,
    )


def solution(mesh):
    return jax.shard_map(
        shards,
        mesh=mesh,
        in_specs=(
            P("dp", None, None), P("dp"), P("dp", None), P("dp", None), P("dp", None, None),
            P("dp", None), P(), P("dp", "mp"), P("mp", None), P(None, None, "mp"), P(None, "mp"),
            P(None, "mp"), P("mp", None), P(), P(), P(None, "mp"), P("mp", None), P(), P(), P(),
            P(), P("dp", None, None), P("dp", None, None),
        ),
        out_specs=(
            P("dp", None, None), P("dp", None, None), P(), P("dp", None, None), P("dp", "mp"),
            P("mp", None), P(None, None, "mp"), P(None, "mp"), P(None, "mp"), P("mp", None), P(),
            P(), P(None, "mp"), P("mp", None), P(), P(), P(), P(),
        ),
        check_vma=False,
    )
```

```python
import functools
import math

import jax
import jax.numpy as jnp
from jax import lax
from jax.experimental import pallas as pl
from jax.experimental.pallas import tpu as pltpu
from jax.sharding import PartitionSpec as P

DH = 64
SPANW = 4
EPSILON = 1e-05
MASKED_SCORE = -1000000000.0
LANES = 128
BF = jnp.bfloat16
F32 = jnp.float32
MESH = pl.DeviceIdType.MESH
VM = pl.BlockSpec(memory_space=pltpu.VMEM)


def matmul(first_op, second_op):
    return jnp.dot(first_op, second_op, preferred_element_type=F32)


def normalize(source, gain_vec, shift_vec):
    center = source - jnp.mean(source, axis=-1, keepdims=True)
    inv_scale = lax.rsqrt(jnp.mean(center * center, axis=-1, keepdims=True) + EPSILON)
    return center * inv_scale * gain_vec + shift_vec


def gelu_exact(source):
    return jax.nn.gelu(source, approximate=False)


def remote(src, dst, send, recv, axis, peer):
    return pltpu.make_async_remote_copy(
        src_ref=src, dst_ref=dst, send_sem=send, recv_sem=recv,
        device_id={axis: peer}, device_id_type=MESH,
    )


def contract(first_op, second_op, first_dim, second_dim):
    return lax.dot_general(
        first_op, second_op, (((first_dim,), (second_dim,)), ((), ())), preferred_element_type=F32
    )


def span(start, count):
    return pl.ds(pl.multiple_of(start, 16), count)


def each(count, step, body, unroll=1):
    while count // step % unroll:
        unroll -= 1

    def run(index, carry):
        for i in range(unroll):
            body(pl.multiple_of((index * unroll + i) * step, step))
        return carry

    lax.fori_loop(0, count // step // unroll, run, 0)


class Quarters:
    def __init__(self, part, r1, s2, r2, full, send, recv):
        self.part, self.r1, self.s2, self.r2, self.full = part, r1, s2, r2, full
        self.send, self.recv = send, recv
        me = lax.axis_index("mp")
        self.b0, self.b1 = lax.rem(me, 2), me // 2
        self.p1, self.p2 = me + 1 - 2 * self.b0, lax.rem(me + 2, 4)
        self.length = part.shape[1]
        self.half = self.length // 2
        self.quarter = self.length // 4

    def copy(self, s, k, src, dst, peer):
        return remote(src, dst, self.send.at[s, k], self.recv.at[s, k], "mp", peer)

    def first(self, s):
        rows = span((1 - self.b0) * self.half, self.half)
        return self.copy(s, 0, self.part.at[s, rows], self.r1.at[s], self.p1)

    def second(self, s):
        return self.copy(s, 1, self.s2.at[s], self.r2.at[s], self.p2)

    def place(self, s, h, q):
        return self.full.at[span(s * self.length + h * self.half + q * self.quarter, self.quarter)]

    def third(self, s, q):
        return self.copy(s, 2, self.place(s, self.b0, q), self.place(s, self.b0, q), self.p2)

    def fourth(self, s, h):
        return self.copy(s, 3, self.place(s, h, self.b1), self.place(s, h, self.b1), self.p1)

    def fifth(self, s, h):
        q = 1 - self.b1
        return self.copy(s, 4, self.place(s, h, q), self.place(s, h, q), self.p1)

    def both(self, s, q, row):
        mine = self.part[s, span(self.b0 * self.half + q * self.quarter + row, 16)]
        return mine.astype(F32) + self.r1[s, span(q * self.quarter + row, 16)].astype(F32)

    def begin(self, s):
        self.first(s).start()

    def pass_on(self, s):
        self.first(s).wait_recv()

        def body(row):
            self.s2[s, span(row, 16)] = self.both(s, 1 - self.b1, row).astype(BF)

        each(self.quarter, 16, body, 5)
        self.second(s).start()

    def wait_sum(self, s):
        self.second(s).wait_recv()

    def total(self, s, row):
        return self.both(s, self.b1, row) + self.r2[s, span(row, 16)].astype(F32)

    def own_row(self, s, row):
        return s * self.length + self.b0 * self.half + self.b1 * self.quarter + row

    def spread(self, s):
        self.third(s, self.b1).start()
        self.fourth(s, self.b0).start()

    def forward(self, s):
        self.third(s, 1 - self.b1).wait_recv()
        self.fifth(s, self.b0).start()

    def wait_full(self, s):
        self.fourth(s, 1 - self.b0).wait_recv()
        self.fifth(s, 1 - self.b0).wait_recv()

    def drain(self, s, sent=False):
        if not sent:
            self.first(s).wait_send()
        self.second(s).wait_send()
        self.third(s, self.b1).wait_send()
        self.fourth(s, self.b0).wait_send()
        self.fifth(s, self.b0).wait_send()


class Spread:
    def __init__(self, axis, n, source_of, into, send, recv):
        self.axis, self.n, self.source_of, self.into = axis, n, source_of, into
        self.send, self.recv = send, recv
        self.me = lax.axis_index(axis)

    def copy(self, step, peer, slot):
        return remote(
            self.source_of(peer), self.into.at[slot], self.send.at[step - 1], self.recv.at[step - 1],
            self.axis, peer,
        )

    def start(self):
        def begin(step, carry):
            self.copy(step, lax.rem(self.me + step, self.n), self.me).start()
            return carry

        lax.fori_loop(1, self.n, begin, 0)

    def wait(self):
        def finish(step, carry):
            source = lax.rem(self.me + self.n - step, self.n)
            self.copy(step, source, source).wait()
            return carry

        lax.fori_loop(1, self.n, finish, 0)


def greet(barrier, axis, n):
    me = lax.axis_index(axis)

    def signal(step, carry):
        pl.semaphore_signal(
            barrier, inc=1, device_id={axis: lax.rem(me + step, n)}, device_id_type=MESH
        )
        return carry

    lax.fori_loop(1, n, signal, 0)


def chunks_of(total, size):
    return [(start, min(size, total - start)) for start in range(0, total, size)]


def scaled(center):
    return lax.rsqrt(jnp.mean(center * center, axis=-1, keepdims=True) + EPSILON)


def scores_of(qkv, sT, h, cols, word_length):
    k_cols = pl.ds(cols.start, word_length), pl.ds(cols.start + word_length, cols.size - word_length)
    sT[0:word_length] = contract(qkv[h, 128:192, k_cols[0]], qkv[h, 0:64, cols], 0, 0)
    sT[word_length:] = contract(qkv[h, 128:192, k_cols[1]], qkv[h, 64:128, cols], 0, 0)


def forward_kernel(
    sizes, n, n_mp, capacity,
    words, word_extra, span_pos, span_len, shard, wanted, table, ent_proj, query_weight, w_key, w_value,
    w_out, w_up, w_down, gain_attn, bias_attn, gain_ffn, bias_ffn,
    received, place, inside, spans, mask, norms, vec_rows, stream, qkv, lse, ctx, wt_words, wt_ents, center1, first_low, hidden, slope,
    center2, out_words, out_ents, head_in, table_all,
    sT, pT, pre, first, part1, r11, s21, r21, part2, r12, s22, r22,
    onehot, answers, answered, vec_all, proj_all, spanned, requests,
    send1, recv1, send2, recv2, word_sem, dp_send, dp_recv, mp_send, mp_recv,
    table_send, table_recv,
):
    seqs, length, word_length, heads = sizes
    width = stream.shape[1]
    me_dp, me_mp = lax.axis_index("dp"), lax.axis_index("mp")
    units = w_up.shape[1]
    one = Quarters(part1, r11, s21, r21, first_low, send1, recv1)
    two = Quarters(part2, r12, s22, r22, center2, send2, recv2)
    barrier = pltpu.get_barrier_semaphore()
    greet(barrier, "dp", n)
    greet(barrier, "mp", n_mp)
    word_copies = [
        pltpu.make_async_copy(
            words.at[s], stream.at[pl.ds(s * length, word_length)], word_sem.at[s]
        )
        for s in range(seqs)
    ]
    for copy in word_copies:
        copy.start()
    asks = Spread("dp", n, lambda peer: requests.at[peer], received, dp_send.at[0], dp_recv.at[0])
    backs = Spread("dp", n, lambda peer: answers.at[peer], answered, dp_send.at[1], dp_recv.at[1])
    projs = Spread("mp", n_mp, lambda peer: ent_proj, proj_all, mp_send.at[0], mp_recv.at[0])
    vecs = Spread(
        "mp", n_mp, lambda peer: vec_all.at[me_mp], vec_all, mp_send.at[1], mp_recv.at[1]
    )
    ent_count = length - word_length
    ents = seqs * ent_count

    pieces = table_send.shape[1]
    cols_dev = table.shape[0]
    piece_rows = cols_dev // pieces

    def table_copy(kind, owner, piece):
        place_all = table_all.at[span(owner * cols_dev + piece * piece_rows, piece_rows)]
        source = place_all if kind == 2 else table.at[span(piece * piece_rows, piece_rows)]
        return remote(
            source, place_all, table_send.at[kind, piece], table_recv.at[kind, piece], "mp",
            one.p2 if kind == 1 else one.p1,
        )

    own_table = pltpu.make_async_copy(
        table, table_all.at[span(me_mp * cols_dev, cols_dev)], word_sem.at[seqs]
    )

    def table_begin(kind, first_piece, last_piece):
        for piece in range(first_piece, last_piece):
            table_copy(kind, me_mp, piece).start()

    def table_forward(first_piece, last_piece):
        for piece in range(first_piece, last_piece):
            table_copy(1, one.p2, piece).wait_recv()
            table_copy(2, one.p2, piece).start()

    def table_end():
        own_table.wait()
        for piece in range(pieces):
            table_copy(0, one.p1, piece).wait_recv()
            table_copy(2, lax.rem(one.p1 + 2, n_mp), piece).wait_recv()
            table_copy(0, me_mp, piece).wait_send()
            table_copy(1, me_mp, piece).wait_send()
            table_copy(2, one.p2, piece).wait_send()

    def rows_joined(ref):
        return jnp.concatenate([ref[s : s + 1] for s in range(seqs)], axis=1)

    def prepare():
        owner = rows_joined(shard).astype(F32)
        owner_of = jnp.transpose(jnp.broadcast_to(owner, (ents, ents)))
        earlier = lax.broadcasted_iota(jnp.int32, (ents, ents), 0) < lax.broadcasted_iota(
            jnp.int32, (ents, ents), 1
        )
        rank = jnp.sum(jnp.where(earlier & (owner_of == owner), 1.0, 0.0), axis=0, keepdims=True)
        spot = owner * LANES + rank
        place[...] = spot.astype(jnp.int32)
        spot_of = jnp.transpose(jnp.broadcast_to(spot, (LANES, ents)))
        row_of = jnp.transpose(jnp.broadcast_to(rows_joined(wanted).astype(F32) + 1.0, (LANES, ents)))
        lane = lax.broadcasted_iota(jnp.int32, (ents, LANES), 1).astype(F32)

        def ask_of(peer, carry):
            first_spot = (peer * LANES).astype(F32)
            asked = jnp.where(spot_of == lane + first_spot, row_of, 0.0)
            asked = jnp.sum(asked, axis=0, keepdims=True) - 1.0
            requests[peer] = jnp.broadcast_to(asked.astype(jnp.int32), (8, LANES))
            return carry

        lax.fori_loop(0, n, ask_of, 0)

    def prepare_spans():
        for row, source in enumerate((gain_attn, bias_attn, gain_ffn, bias_ffn)):
            norms[row : row + 1] = source[...].reshape(1, width)
        for s in range(seqs):
            count = word_length // 8 + word_extra[s]
            position = lax.broadcasted_iota(jnp.int32, (word_length, LANES), 0)
            mask[s] = jnp.where(position < count, 0.0, MASKED_SCORE)
            many = span_len[s : s + 1]
            start = lax.shift_right_logical(
                span_pos[s : s + 1] * (count - SPANW), word_length.bit_length() - 1
            )
            position = lax.broadcasted_iota(jnp.int32, (word_length, ent_count), 0)
            within = (position >= start) & (position < start + many)
            inside[s] = jnp.where(within, 1.0, 0.0).astype(BF)
            spans[s * ent_count : (s + 1) * ent_count] = jnp.transpose(
                jnp.broadcast_to(many.astype(F32), (LANES, ent_count))
            )

    def answer():
        ids = jnp.concatenate([received[source, 0:1, 0:capacity] for source in range(n)], axis=1)

        def body(row):
            index = lax.broadcasted_iota(jnp.int32, (80, n * capacity), 0) + row
            onehot[span(row, 80)] = jnp.where(index == ids, 1.0, 0.0).astype(BF)

        each(table.shape[1], 80, body)
        found = matmul(table[...], onehot[...]).astype(BF)
        for source in range(n):
            answers[source, :, 0:capacity] = found[:, source * capacity : (source + 1) * capacity]

    def collect():
        slot = lax.broadcasted_iota(jnp.int32, (capacity, seqs * ent_count), 0)

        def add(owner, total):
            placed = jnp.where(slot + owner * LANES == place[...], 1.0, 0.0).astype(BF)
            return total + matmul(answered[owner, :, 0:capacity], placed)

        total = lax.fori_loop(0, n, add, jnp.zeros(vec_rows.shape, F32))
        vec_rows[...] = total.astype(BF)
        vec_all[me_mp] = total.astype(BF)

    def span_means():
        for s in range(seqs):
            at = slice(s * ent_count, (s + 1) * ent_count)
            start = s * length
            spanned[at] = (
                contract(inside[s], stream[start : start + word_length], 0, 0) / spans[at, 0:1]
            )

    def entity_rows():
        vectors = vec_all[...].reshape(n_mp * vec_rows.shape[0], seqs * ent_count)
        projection = proj_all[...].reshape(n_mp * vec_rows.shape[0], width)
        value = (contract(vectors, projection, 0, 0) + spanned[...]).astype(BF)
        for s in range(seqs):
            at = s * length + word_length
            stream[at : at + ent_count] = value[s * ent_count : (s + 1) * ent_count]

    prepare()
    pl.semaphore_wait(barrier, n + n_mp - 2)
    received[me_dp] = requests[me_dp]
    asks.start()
    proj_all[me_mp] = ent_proj[...]
    projs.start()
    own_table.start()
    table_begin(1, 0, pieces // 2)
    table_begin(0, 0, pieces)
    prepare_spans()

    for target, first_query in ((wt_words, 0), (wt_ents, 2)):
        sources = (query_weight[first_query], query_weight[first_query + 1], w_key[...], w_value[...])
        for g, source in enumerate(sources):
            for h in range(heads):
                target[h, g * DH : (g + 1) * DH] = source[h * DH : (h + 1) * DH]

    def project(s, weight, start, count):
        base = s * length + start
        for h in range(heads):
            value = contract(weight[h], stream[base : base + count], 1, 1)
            qkv[h, 0:128, base : base + count] = (value[0:128] * 0.125).astype(BF)
            qkv[h, 128:256, base : base + count] = value[128:256].astype(BF)

    def attend(s, h):
        cols = pl.ds(s * length, length)
        scores_of(qkv, sT, h, cols, word_length)

        def body(col):
            here = pl.ds(col, LANES)
            words = sT[0:word_length, here] + mask[s]
            ents = sT[word_length:, here]
            top = jnp.maximum(
                jnp.max(words, axis=0, keepdims=True), jnp.max(ents, axis=0, keepdims=True)
            )
            words = jnp.exp(words - top)
            ents = jnp.exp(ents - top)
            total = jnp.sum(words, axis=0, keepdims=True) + jnp.sum(ents, axis=0, keepdims=True)
            pT[0:word_length, here] = words.astype(BF)
            pT[word_length:, here] = ents.astype(BF)
            lse[h, 0:1, pl.ds(pl.multiple_of(s * length + col, LANES), LANES)] = top + jnp.log(total)
            lse[h, 1:2, pl.ds(pl.multiple_of(s * length + col, LANES), LANES)] = 1.0 / total

        each(length, LANES, body)
        value = matmul(qkv[h, 192:256, cols], pT[...]) * lse[h, 1:2, cols]
        ctx[h * DH : (h + 1) * DH, cols] = value.astype(BF)

    def attention_part(s):
        value = contract(ctx[:, s * length : (s + 1) * length], w_out[...], 0, 0)
        part1[s] = value.astype(BF)

    def first_rows(s):
        def body(row):
            at = one.own_row(s, row)
            value = stream[span(at, 16)].astype(F32) + one.total(s, row)
            center = value - jnp.mean(value, axis=-1, keepdims=True)
            mine = span(s * one.quarter + row, 16)
            center1[mine] = center
            normed = center * scaled(center) * norms[0:1] + norms[1:2]
            first[mine] = normed
            first_low[span(at, 16)] = normed.astype(BF)

        each(one.quarter, 16, body, 5)

    def second_rows(s):
        def body(row):
            at = two.own_row(s, row)
            value = first[span(s * two.quarter + row, 16)] + two.total(s, row)
            center = value - jnp.mean(value, axis=-1, keepdims=True)
            center2[span(at, 16)] = center.astype(BF)

        each(two.quarter, 16, body, 5)

    def feed(s):
        rows = slice(s * length, (s + 1) * length)
        tile = 256
        for j in range(units // tile):
            cols = slice(j * tile, (j + 1) * tile)
            pre[...] = matmul(first_low[rows], w_up[:, cols])

            def body(row):
                value = pre[pl.ds(row, 32)]
                bell = lax.erf(value * 0.7071067811865476) * 0.5 + 0.5
                at = span(s * length + row, 32)
                hidden[at, cols] = (value * bell).astype(BF)
                slope[at, cols] = (
                    bell + value * jnp.exp(value * value * -0.5) * 0.3989422804014327
                ).astype(BF)

            each(length, 32, body, 4)
        for j in range(width // tile):
            cols = slice(j * tile, (j + 1) * tile)
            part2[s, :, cols] = matmul(hidden[rows], w_down[:, cols]).astype(BF)

    def output_rows(s):
        def rows_of(row):
            center = center2[span(s * length + row, 16)].astype(F32)
            return (center * scaled(center) * norms[2:3] + norms[3:4]).astype(BF)

        def word_rows(row):
            out_words[s, span(row, 16)] = rows_of(row)

        def ent_rows(row):
            out_ents[s, span(row, 16)] = rows_of(row + word_length)

        each(word_length, 16, word_rows, 4)
        each(ent_count, 16, ent_rows, 4)
        scored = head_in.shape[0] // seqs
        head_in[s * scored : (s + 1) * scored] = out_ents[s, 0:scored]

    for copy in word_copies:
        copy.wait()
    project(0, wt_words, 0, word_length)
    asks.wait()
    answer()
    answered[me_dp] = answers[me_dp]
    backs.start()
    span_means()
    project(1, wt_words, 0, word_length)
    backs.wait()
    collect()
    vecs.start()
    projs.wait()
    vecs.wait()
    table_begin(1, pieces // 2, pieces)
    entity_rows()
    project(0, wt_ents, word_length, ent_count)
    for h in range(heads):
        attend(0, h)
    attention_part(0)
    one.begin(0)
    table_forward(0, pieces // 2)
    project(1, wt_ents, word_length, ent_count)
    attend(1, 0)
    one.pass_on(0)
    for h in range(1, heads):
        attend(1, h)
    attention_part(1)
    one.begin(1)
    table_forward(pieces // 2, pieces)
    one.wait_sum(0)
    first_rows(0)
    one.spread(0)
    one.pass_on(1)
    one.forward(0)
    one.wait_full(0)
    feed(0)
    two.begin(0)
    one.wait_sum(1)
    first_rows(1)
    one.spread(1)
    two.pass_on(0)
    one.forward(1)
    one.wait_full(1)
    feed(1)
    two.begin(1)
    two.wait_sum(0)
    second_rows(0)
    two.spread(0)
    two.pass_on(1)
    two.forward(0)
    two.wait_full(0)
    output_rows(0)
    two.wait_sum(1)
    second_rows(1)
    two.spread(1)
    two.forward(1)
    two.wait_full(1)
    output_rows(1)
    for s in range(seqs):
        one.drain(s)
        two.drain(s)
    table_end()


def quarter_scratch(seqs, length, width):
    return [
        pltpu.VMEM((seqs, length, width), BF),
        pltpu.VMEM((seqs, length // 2, width), BF),
        pltpu.VMEM((seqs, length // 4, width), BF),
        pltpu.VMEM((seqs, length // 4, width), BF),
    ]


def forward_layer(sizes, scored, capacity, words, arrays):
    seqs, length, word_length, heads = sizes
    n, n_mp = lax.axis_size("dp"), lax.axis_size("mp")
    width = words.shape[2]
    tokens = seqs * length
    local, ents = heads * DH, seqs * (length - word_length)
    table, w_up = arrays[5], arrays[11]
    cols_dev, rows_dev = table.shape
    units = w_up.shape[1]

    def like(*shape, dtype=BF):
        return jax.ShapeDtypeStruct(shape, dtype)

    outs = [
        like(n, 8, LANES, dtype=jnp.int32), like(1, ents, dtype=jnp.int32),
        like(seqs, word_length, length - word_length), like(ents, LANES, dtype=F32),
        like(seqs, word_length, LANES, dtype=F32), like(4, width, dtype=F32),
        like(cols_dev, ents), like(tokens, width),
        like(heads, 4 * DH, tokens), like(heads, 8, tokens, dtype=F32), like(local, tokens),
        like(heads, 4 * DH, width), like(heads, 4 * DH, width), like(tokens // 4, width, dtype=F32),
        like(tokens, width), like(tokens, units), like(tokens, units), like(tokens, width),
        like(seqs, word_length, width), like(seqs, length - word_length, width),
        like(seqs * scored, width), like(n_mp * cols_dev, rows_dev),
    ]
    return pl.pallas_call(
        functools.partial(forward_kernel, sizes, n, n_mp, capacity),
        out_shape=outs,
        in_specs=[pl.BlockSpec(memory_space=pl.ANY), pl.BlockSpec(memory_space=pltpu.SMEM)]
        + [VM] * (len(arrays) - 1),
        out_specs=[VM] * (len(outs) - 1) + [pl.BlockSpec(memory_space=pl.ANY)],
        scratch_shapes=[
            pltpu.VMEM((length, length), F32),
            pltpu.VMEM((length, length), BF),
            pltpu.VMEM((length, 256), F32),
            pltpu.VMEM((tokens // 4, width), F32),
            *quarter_scratch(seqs, length, width),
            *quarter_scratch(seqs, length, width),
            pltpu.VMEM((rows_dev, n * capacity), BF),
            pltpu.VMEM((n, cols_dev, LANES), BF), pltpu.VMEM((n, cols_dev, LANES), BF),
            pltpu.VMEM((n_mp, cols_dev, ents), BF), pltpu.VMEM((n_mp, cols_dev, width), BF),
            pltpu.VMEM((ents, width), F32), pltpu.VMEM((n, 8, LANES), jnp.int32),
            pltpu.SemaphoreType.DMA((seqs, 5)), pltpu.SemaphoreType.DMA((seqs, 5)),
            pltpu.SemaphoreType.DMA((seqs, 5)), pltpu.SemaphoreType.DMA((seqs, 5)),
            pltpu.SemaphoreType.DMA((seqs + 1,)),
            pltpu.SemaphoreType.DMA((2, n - 1)), pltpu.SemaphoreType.DMA((2, n - 1)),
            pltpu.SemaphoreType.DMA((2, n_mp - 1)), pltpu.SemaphoreType.DMA((2, n_mp - 1)),
            pltpu.SemaphoreType.DMA((3, cols_dev // 16)), pltpu.SemaphoreType.DMA((3, cols_dev // 16)),
        ],
        compiler_params=pltpu.CompilerParams(
            collective_id=3, has_side_effects=True, vmem_limit_bytes=60 * 2**20
        ),
    )(words, *arrays)


class Job:
    def __init__(self, rows, buf, out, arrivals, send, recv, n, first=(0, 1, 2)):
        self.buf, self.out, self.arrivals, self.send, self.recv = buf, out, arrivals, send, recv
        self.rows = rows
        self.me = lax.axis_index("dp")
        self.bits, self.halvings = job_plan(rows, n)
        self.order = list(range(self.bits))
        if self.bits >= len(first):
            self.order[: len(first)] = first

    def bit(self, k):
        return lax.rem(self.me // 2 ** self.order[k], 2)

    def peer(self, k):
        return self.me + (1 - 2 * self.bit(k)) * 2 ** self.order[k]

    def offset(self, k):
        start = 0
        for i in range(k):
            start = start + self.bit(i) * (self.rows >> (i + 1))
        return start

    def copy(self, index, k, src, dst):
        return remote(src, dst, self.send.at[index], self.recv.at[index], "dp", self.peer(k))

    def steps(self):
        size = self.rows
        for k in range(self.bits):
            keep = self.offset(min(k, self.halvings))
            away = keep
            if k < self.halvings:
                size //= 2
                away = keep + (1 - self.bit(k)) * size
                keep = keep + self.bit(k) * size
            arrived = self.arrivals[k]
            copy = self.copy(k, k, self.buf.at[span(away, size)], arrived)
            copy.start()
            yield
            copy.wait()
            last = k == self.bits - 1

            def body(row, keep=keep, arrived=arrived, last=last):
                at = span(keep + row, 16)
                value = self.buf[at].astype(F32) + arrived[span(row, 16)].astype(F32)
                (self.out if last else self.buf)[at] = value.astype(BF)

            each(size, 16, body, 4)
        for k in reversed(range(self.halvings)):
            done = self.out.at[span(self.offset(k + 1), size)]
            copy = self.copy(self.bits + k, k, done, done)
            copy.start()
            yield
            copy.wait()
            size *= 2


def job_plan(rows, n):
    bits, halvings, size = n.bit_length() - 1, 0, rows
    while halvings < bits - 1 and (size // 2) % 16 == 0:
        size, halvings = size // 2, halvings + 1
    return bits, halvings


def job_cuts(units, width, head_rows, proj_rows, heads):
    orders = [
        ((1, 0, 2), (0, 1, 2), (1, 0, 2)),
        ((0, 1, 2), (0, 1, 2), (0, 1, 2)),
        ((0, 1, 2),),
        ((0, 1, 2),),
        ((0, 1, 2), (1, 0, 2)),
        ((0, 1, 2), (1, 0, 2)),
        ((0, 1, 2), (1, 0, 2)),
    ]
    cuts = [(units, [units // 3] * 3), (width, [width // 3] * 3)]
    cuts += [(head_rows, [head_rows]), (proj_rows, [proj_rows])]
    cuts += [(7 * DH, [4 * DH, 3 * DH])] * heads
    return [(rows, pieces, order) for (rows, pieces), order in zip(cuts, orders)]


def job_scratch(rows, width, n):
    bits, halvings = job_plan(rows, n)
    return [
        pltpu.VMEM((rows >> min(k + 1, halvings), width), BF) for k in range(bits)
    ]


def backward_kernel(sizes, n, n_mp, *refs):
    seqs, length, word_length, heads = sizes
    refs = list(refs)

    def take(count):
        taken = refs[:count]
        del refs[:count]
        return taken

    cot_words, cot_ents = take(2)
    (
        d_head, head_grad, center2, slope, hidden, first_low, center1, w_up, w_down, norms,
        small_in, ent_proj, vec_rows, place, received, inside, spans,
    ) = take(17)
    late_in = take(8)
    down_out, up_out, head_all, proj_out, *per_head_out = take(4 + heads)
    word_grads, table_hits, small = take(3)
    ctx, qkv, lse, wt_words, wt_ents, stream, mask, w_out = late = take(8)
    sums, d_ffn, d_pre, d_attn, d_first, dctx, sT, dpT, pT, dsT, dcat = take(11)
    head_out, small_mp, small_dp, outbox, gw, inbox, onehot = take(7)
    part, r1, s2, r2 = take(4)
    (
        send1, recv1, send2, recv2, job_send, job_recv, late_sem, cot_sem,
        mp_send, mp_recv, dp_send, dp_recv, out_sem,
    ) = take(13)
    width = stream.shape[1]
    units = w_up.shape[1]
    me_mp, me_dp = lax.axis_index("mp"), lax.axis_index("dp")
    bits = n.bit_length() - 1
    jobs = []
    groups = [[], [], [], []] + [[] for h in range(heads)]
    buffers = take(len(groups))
    for group, buf, out, (rows, cuts, orders) in zip(
        groups, buffers, [down_out, up_out, head_out, proj_out, *per_head_out],
        job_cuts(units, width, head_out.shape[0], proj_out.shape[0], heads),
    ):
        start = 0
        for count, order in zip(cuts, orders):
            at = pl.ds(start, count)
            start += count
            index = len(jobs)
            jobs.append(
                Job(
                    count, buf.at[at], out.at[at], take(bits), job_send.at[index],
                    job_recv.at[index], n, order,
                )
            )
            group.append(jobs[-1])
    down_jobs, up_jobs, (head_job,), (proj_job,), *heads_jobs = groups
    down_buf, up_buf, head_buf, proj_buf, *heads_buf = buffers
    one = Quarters(part, r1, s2, r2, d_attn, send1, recv1)
    two = Quarters(part, r1, s2, r2, gw, send2, recv2)
    barrier = pltpu.get_barrier_semaphore()
    greet(barrier, "mp", n_mp)
    greet(barrier, "dp", n)
    cots = []
    for s in range(seqs):
        for k, (source, start, count) in enumerate(
            ((cot_words, 0, word_length), (cot_ents, word_length, length - word_length))
        ):
            target = d_attn.at[pl.ds(s * length + start, count)]
            cots.append(pltpu.make_async_copy(source.at[s], target, cot_sem.at[s, k]))
            cots[-1].start()
    late_copies = [
        pltpu.make_async_copy(source, target, late_sem.at[i])
        for i, (source, target) in enumerate(zip(late_in, late))
    ]
    for copy in late_copies:
        copy.start()
    running = {}

    def launch(job):
        running[id(job)] = job.steps()
        next(running[id(job)])

    def step(*which):
        for job in which:
            next(running[id(job)], 0)

    def finish(job):
        for _ in running[id(job)]:
            pass

    sums[...] = jnp.zeros_like(sums)

    spare = d_first.shape[0] - 16

    def second_back(s):
        start = one.own_row(0, 0)

        def rows_of(row, extra=None):
            at = span(s * length + row, 16)
            cot = d_attn[at].astype(F32)
            if extra is not None:
                cot = cot + extra
            center = center2[at].astype(F32)
            inv = scaled(center)
            normed = center * inv
            sums[0] += cot * normed
            sums[1] += cot
            grad = cot * norms[2:3]
            value = inv * (
                grad
                - jnp.mean(grad, axis=-1, keepdims=True)
                - normed * jnp.mean(grad * normed, axis=-1, keepdims=True)
            )
            d_ffn[at] = value.astype(BF)

            own = (row >= start) & (row < start + one.quarter)
            d_first[span(jnp.where(own, s * one.quarter + row - start, spare), 16)] = value

        scored = d_head.shape[1]
        each(word_length, 16, rows_of, 4)
        each(scored, 16, lambda row: rows_of(row + word_length, d_head[s, span(row, 16)]))
        each(length - word_length - scored, 16, lambda row: rows_of(row + word_length + scored), 7)

    def feed_back(s):
        rows = slice(s * length, (s + 1) * length)
        tile = 256
        for j in range(units // tile):
            cols = slice(j * tile, (j + 1) * tile)
            sT[:, 0:tile] = contract(d_ffn[rows], w_down[cols], 1, 1)

            def body(row):
                at = span(s * length + row, 32)
                d_pre[at, cols] = (
                    sT[pl.ds(row, 32), 0:tile] * slope[at, cols].astype(F32)
                ).astype(BF)

            each(length, 32, body, 4)
        for j in range(width // tile):
            cols = slice(j * tile, (j + 1) * tile)
            part[s, :, cols] = contract(d_pre[rows], w_up[cols], 1, 1).astype(BF)

    def first_back(s):
        def body(row):
            at = one.own_row(s, row)
            mine = span(s * one.quarter + row, 16)
            value = d_first[mine] + one.total(s, row)
            center = center1[mine]
            inv = scaled(center)
            normed = center * inv
            sums[2] += value * normed
            sums[3] += value
            grad = value * norms[0:1]
            value = inv * (
                grad
                - jnp.mean(grad, axis=-1, keepdims=True)
                - normed * jnp.mean(grad * normed, axis=-1, keepdims=True)
            )
            d_first[mine] = value
            d_attn[span(at, 16)] = value.astype(BF)

        each(one.quarter, 16, body, 5)

    def context_back(s):
        cols = slice(s * length, (s + 1) * length)
        dctx[:, cols] = contract(w_out[...], d_attn[cols], 1, 1).astype(BF)

    def attend_back(s, h):
        cols = pl.ds(s * length, length)
        w_cols = pl.ds(s * length, word_length)
        e_cols = pl.ds(s * length + word_length, length - word_length)
        mine = slice(h * DH, (h + 1) * DH)
        scores_of(qkv, sT, h, cols, word_length)
        dpT[...] = contract(qkv[h, 192:256, cols], dctx[mine, cols], 0, 0)

        def body(col):
            here = pl.ds(col, LANES)
            at = pl.ds(pl.multiple_of(s * length + col, LANES), LANES)
            delta = jnp.sum(
                ctx[mine, at].astype(F32) * dctx[mine, at].astype(F32), axis=0, keepdims=True
            )
            log_total = lse[h, 0:1, at]
            probs = jnp.exp(sT[0:word_length, here] + mask[s] - log_total)
            pT[0:word_length, here] = probs.astype(BF)
            dsT[0:word_length, here] = (probs * (dpT[0:word_length, here] - delta)).astype(BF)
            probs = jnp.exp(sT[word_length:, here] - log_total)
            pT[word_length:, here] = probs.astype(BF)
            dsT[word_length:, here] = (probs * (dpT[word_length:, here] - delta)).astype(BF)

        each(length, LANES, body)
        d_words, d_ents = dsT[0:word_length], dsT[word_length:]
        dcat[h, 0:64, cols] = (contract(qkv[h, 128:192, w_cols], d_words, 1, 0) * 0.125).astype(BF)
        dcat[h, 64:128, cols] = (contract(qkv[h, 128:192, e_cols], d_ents, 1, 0) * 0.125).astype(BF)
        dcat[h, 128:192, w_cols] = contract(qkv[h, 0:64, cols], d_words, 1, 1).astype(BF)
        dcat[h, 128:192, e_cols] = contract(qkv[h, 64:128, cols], d_ents, 1, 1).astype(BF)
        dcat[h, 192:256, cols] = contract(dctx[mine, cols], pT[...], 1, 1).astype(BF)

    def head_grads(h):
        buf = heads_buf[h]
        from_words, from_ents = None, None
        for s in range(seqs):
            middle, start, end = s * length + word_length, s * length, (s + 1) * length
            words = matmul(dcat[h, :, start:middle], stream[start:middle])
            ents = matmul(dcat[h, :, middle:end], stream[middle:end])
            from_words = words if s == 0 else from_words + words
            from_ents = ents if s == 0 else from_ents + ents
        buf[0:128] = from_words[0:128].astype(BF)
        buf[128:256] = (from_words[128:256] + from_ents[128:256]).astype(BF)
        buf[256:384] = from_ents[0:128].astype(BF)
        buf[384:448] = matmul(ctx[h * DH : (h + 1) * DH], d_attn[...]).astype(BF)

    def stream_part(s):
        for start in range(0, length, LANES):
            weight = wt_words if start < word_length else wt_ents
            cols = slice(s * length + start, s * length + start + LANES)
            value = contract(dcat[0, :, cols], weight[0], 0, 0)
            for h in range(1, heads):
                value = value + contract(dcat[h, :, cols], weight[h], 0, 0)
            part[s, start : start + LANES] = value.astype(BF)

    def last_rows(s):
        def body(row):
            at = two.own_row(s, row)
            value = d_first[span(s * two.quarter + row, 16)] + two.total(s, row)
            gw[span(at, 16)] = value.astype(BF)

        each(two.quarter, 16, body, 5)

    def down_tile(j):
        cols = slice(j * 256, (j + 1) * 256)
        down_buf[cols] = contract(hidden[:, cols], d_ffn[...], 0, 0).astype(BF)

    def up_tile(j):
        cols = slice(j * 256, (j + 1) * 256)
        up_buf[cols] = contract(first_low[:, cols], d_pre[...], 0, 0).astype(BF)

    def wait_cots(s):
        for copy in cots[2 * s : 2 * s + 2]:
            copy.wait()

    def wait_late():
        for copy in late_copies:
            copy.wait()

    small_over_mp = Spread(
        "mp", n_mp, lambda peer: small_mp.at[me_mp], small_mp, mp_send.at[0], mp_recv.at[0]
    )
    small_over_dp = Spread(
        "dp", n, lambda peer: small_dp.at[me_dp], small_dp, dp_send.at[0], dp_recv.at[0]
    )
    boxes = Spread("dp", n, lambda peer: outbox.at[peer], inbox, dp_send.at[1], dp_recv.at[1])
    head_rows = head_out.shape[0]
    head_place = span(me_mp * head_rows, head_rows)

    def head_copy(distance, peer, owner):
        return remote(
            head_out, head_all.at[span(owner * head_rows, head_rows)], mp_send.at[1, distance - 1],
            mp_recv.at[1, distance - 1], "mp", peer,
        )

    def small_first():
        mine = small_in[...]
        mine = mine + jnp.concatenate(
            [jnp.sum(sums[row], axis=0, keepdims=True) for row in range(4)]
            + [jnp.zeros((4, width), F32)]
        )
        small_mp[me_mp] = mine
        small_over_mp.start()

    def small_second():
        small_over_mp.wait()
        total = small_mp[0]
        for device in range(1, n_mp):
            total = total + small_mp[device]
        row = lax.broadcasted_iota(jnp.int32, total.shape, 0)
        small_dp[me_dp] = jnp.where((row == 2) | (row == 3), total, small_mp[me_mp])
        small_over_dp.start()

    def small_last():
        small_over_dp.wait()

        def add(device, total):
            return total + small_dp[device]

        small[...] = lax.fori_loop(1, n, add, small_dp[0])

    def head_first():
        head_all[head_place] = head_out[...]
        for distance in range(1, n_mp):
            head_copy(distance, lax.rem(me_mp + distance, n_mp), me_mp).start()

    def head_last():
        for distance in range(1, n_mp):
            source = lax.rem(me_mp + n_mp - distance, n_mp)
            head_copy(distance, source, source).wait()

    def entities():
        grads, rows = None, []
        count = length - word_length
        for s in range(seqs):
            d_ent = gw[s * length + word_length : (s + 1) * length]
            value = matmul(vec_rows[:, s * count : (s + 1) * count], d_ent)
            grads = value if s == 0 else grads + value
            rows.append(contract(ent_proj[...], d_ent, 1, 1).astype(BF))
        proj_buf[...] = grads.astype(BF)
        launch(proj_job)
        rows = jnp.concatenate(rows, axis=1)
        slot = lax.broadcasted_iota(jnp.int32, (LANES, seqs * count), 0)

        def fill(owner, carry):
            placed = jnp.where(slot + owner * LANES == place[...], 1.0, 0.0).astype(BF)
            outbox[owner] = contract(rows, placed, 1, 1).astype(BF)
            return carry

        lax.fori_loop(0, n, fill, 0)
        inbox[me_dp] = outbox[me_dp]
        boxes.start()

    out_copies = []

    def words_out(s):
        width_part = width // 2
        rows = slice(s * length, s * length + word_length)
        at = slice(s * (length - word_length), (s + 1) * (length - word_length))
        shared = gw[s * length + word_length : (s + 1) * length].astype(F32) / spans[at, 0:1]
        for half, source in enumerate((sT, dpT)):
            if s > 0:
                out_copies[2 * (s - 1) + half].wait()
            cols = slice(half * width_part, (half + 1) * width_part)
            source[0:word_length, 0:width_part] = gw[rows, cols].astype(F32) + matmul(
                inside[s], shared[:, cols].astype(BF)
            )
            out_copies.append(
                pltpu.make_async_copy(
                    source.at[pl.ds(0, word_length), pl.ds(0, width_part)],
                    word_grads.at[s, :, pl.ds(half * width_part, width_part)], out_sem.at[s, half],
                )
            )
            out_copies[-1].start()

    pieces = chunks_of(table_hits.shape[1], onehot.shape[0])
    parts = (len(pieces) + 3) // 4

    def table_part(part):
        capacity = onehot.shape[1] // n
        ids = jnp.concatenate([received[source, 0:1, 0:capacity] for source in range(n)], axis=1)
        rows = jnp.concatenate([inbox[source, :, 0:capacity] for source in range(n)], axis=1)
        for start, count in pieces[part * parts : (part + 1) * parts]:

            def body(row, start=start):
                index = lax.broadcasted_iota(jnp.int32, (32, n * capacity), 0) + (row + start)
                onehot[span(row, 32)] = jnp.where(index == ids, 1.0, 0.0).astype(BF)

            each(count, 32, body, 2)
            table_hits[:, start : start + count] = contract(rows, onehot[0:count], 1, 1)

    head_buf[...] = head_grad[head_place]
    wait_cots(0)
    second_back(0)
    feed_back(0)
    pl.semaphore_wait(barrier, n_mp - 1 + n - 1)
    one.begin(0)
    launch(head_job)
    wait_cots(1)
    second_back(1)
    one.pass_on(0)
    feed_back(1)
    one.begin(1)
    step(head_job)
    down_tile(0)
    launch(down_jobs[0])
    down_tile(1)
    launch(down_jobs[1])
    down_tile(2)
    launch(down_jobs[2])
    up_tile(0)
    launch(up_jobs[0])
    up_tile(1)
    launch(up_jobs[1])
    up_tile(2)
    launch(up_jobs[2])
    one.pass_on(1)
    step(head_job)
    one.wait_sum(0)
    first_back(0)
    one.spread(0)
    step(down_jobs[0], head_job, down_jobs[1])
    one.wait_sum(1)
    first_back(1)
    one.spread(1)
    small_first()
    step(down_jobs[2], head_job, up_jobs[0], down_jobs[1])
    one.forward(0)
    step(up_jobs[1], up_jobs[0])
    one.wait_full(0)
    small_second()
    wait_late()
    context_back(0)
    attend_back(0, 0)
    step(up_jobs[2])
    attend_back(0, 1)
    step(down_jobs[1], up_jobs[1], down_jobs[0])
    attend_back(0, 2)
    step(down_jobs[2], head_job)
    finish(head_job)
    head_first()
    step(up_jobs[0], up_jobs[2])
    one.first(0).wait_send()
    stream_part(0)
    two.begin(0)
    one.forward(1)
    step(down_jobs[1], up_jobs[1])
    one.wait_full(1)
    one.drain(0, True)
    one.drain(1)
    context_back(1)
    step(up_jobs[0])
    attend_back(1, 0)
    two.pass_on(0)
    head_grads(0)
    launch(heads_jobs[0][0])
    launch(heads_jobs[0][1])
    step(down_jobs[0], down_jobs[1], up_jobs[1])
    attend_back(1, 1)
    head_grads(1)
    launch(heads_jobs[1][0])
    launch(heads_jobs[1][1])
    step(down_jobs[2], up_jobs[0])
    attend_back(1, 2)
    step(heads_jobs[0][1])
    stream_part(1)
    two.begin(1)
    step(up_jobs[2], heads_jobs[0][0])
    head_grads(2)
    launch(heads_jobs[2][0])
    launch(heads_jobs[2][1])
    step(heads_jobs[1][1], down_jobs[0])
    two.pass_on(1)
    two.wait_sum(0)
    last_rows(0)
    two.spread(0)
    small_last()
    step(up_jobs[2], up_jobs[1], heads_jobs[0][0])
    two.wait_sum(1)
    last_rows(1)
    two.spread(1)
    step(heads_jobs[2][1], heads_jobs[1][0], down_jobs[2], heads_jobs[0][1])
    step(down_jobs[0], heads_jobs[0][0])
    two.forward(0)
    step(heads_jobs[1][0], heads_jobs[2][0], heads_jobs[1][1])
    two.forward(1)
    two.wait_full(0)
    step(heads_jobs[0][1], down_jobs[2])
    two.wait_full(1)
    entities()
    step(heads_jobs[0][0], up_jobs[2])
    words_out(0)
    step(heads_jobs[1][0], heads_jobs[2][0], heads_jobs[2][1])
    words_out(1)
    step(heads_jobs[0][1], heads_jobs[1][1], proj_job)
    boxes.wait()
    table_part(0)
    step(heads_jobs[1][0])
    table_part(1)
    step(heads_jobs[0][0])
    table_part(2)
    step(heads_jobs[2][0], heads_jobs[0][1], heads_jobs[1][1], proj_job)
    table_part(3)
    step(heads_jobs[2][1], heads_jobs[1][0], proj_job, heads_jobs[2][0])
    step(heads_jobs[2][1], heads_jobs[1][1], proj_job, heads_jobs[2][0])
    step(heads_jobs[2][1], proj_job)
    head_last()
    for s in range(seqs):
        two.drain(s)
    for copy in out_copies[-2:]:
        copy.wait()
    for job in jobs:
        finish(job)


def backward_layer(sizes, n, capacity, rows_dev, cots, now, late):
    seqs, length, word_length, heads = sizes
    stream, w_up, ent_proj = late[5], now[7], now[11]
    n_mp = lax.axis_size("mp")
    tokens, width = stream.shape
    units, local = w_up.shape[1], heads * DH
    head_rows, head_width = now[1].shape[0] // n_mp, now[1].shape[1]
    bits = n.bit_length() - 1
    outs = [(units, width), (width, units), (n_mp * head_rows, head_width), ent_proj.shape]
    outs += [(7 * DH, width)] * heads
    outs = [jax.ShapeDtypeStruct(shape, BF) for shape in outs]
    outs += [
        jax.ShapeDtypeStruct((seqs, word_length, width), F32),
        jax.ShapeDtypeStruct((ent_proj.shape[0], rows_dev), F32),
        jax.ShapeDtypeStruct((8, width), F32),
    ]
    cuts = job_cuts(units, width, head_rows, ent_proj.shape[0], heads)
    widths = [width, units, head_width] + [width] * (1 + heads)
    job_count = sum(len(sizes) for _, sizes, _ in cuts)
    scratch = [pltpu.VMEM(value.shape, value.dtype) for value in late]
    scratch += [
        pltpu.VMEM((4, 16, width), F32), pltpu.VMEM((tokens, width), BF),
        pltpu.VMEM((tokens, units), BF), pltpu.VMEM((tokens, width), BF),
        pltpu.VMEM((tokens // 4 + 16, width), F32), pltpu.VMEM((local, tokens), BF),
        pltpu.VMEM((length, length), F32), pltpu.VMEM((length, length), F32),
        pltpu.VMEM((length, length), BF), pltpu.VMEM((length, length), BF),
        pltpu.VMEM((heads, 4 * DH, tokens), BF),
        pltpu.VMEM((head_rows, head_width), BF), pltpu.VMEM((n_mp, 8, width), F32),
        pltpu.VMEM((n, 8, width), F32), pltpu.VMEM((n, ent_proj.shape[0], LANES), BF),
        pltpu.VMEM((tokens, width), BF), pltpu.VMEM((n, ent_proj.shape[0], LANES), BF),
        pltpu.VMEM((256, n * capacity), BF),
        *quarter_scratch(seqs, length, width),
        pltpu.SemaphoreType.DMA((seqs, 5)), pltpu.SemaphoreType.DMA((seqs, 5)),
        pltpu.SemaphoreType.DMA((seqs, 5)), pltpu.SemaphoreType.DMA((seqs, 5)),
        pltpu.SemaphoreType.DMA((job_count, 2 * bits)),
        pltpu.SemaphoreType.DMA((job_count, 2 * bits)),
        pltpu.SemaphoreType.DMA((len(late),)), pltpu.SemaphoreType.DMA((seqs, 2)),
        pltpu.SemaphoreType.DMA((2, n_mp - 1)), pltpu.SemaphoreType.DMA((2, n_mp - 1)),
        pltpu.SemaphoreType.DMA((2, n - 1)), pltpu.SemaphoreType.DMA((2, n - 1)),
        pltpu.SemaphoreType.DMA((seqs, 2)),
    ]
    scratch += [pltpu.VMEM((rows, columns), BF) for (rows, _, _), columns in zip(cuts, widths)]
    for (_, counts, _), columns in zip(cuts, widths):
        for count in counts:
            scratch += job_scratch(count, columns, n)
    hbm = pl.BlockSpec(memory_space=pl.ANY)
    return pl.pallas_call(
        functools.partial(backward_kernel, sizes, n, n_mp),
        out_shape=outs,
        in_specs=[hbm] * len(cots) + [VM] * len(now) + [hbm] * len(late),
        out_specs=[VM] * (len(outs) - 3) + [hbm, VM, VM],
        scratch_shapes=scratch,
        compiler_params=pltpu.CompilerParams(
            collective_id=7, has_side_effects=True, vmem_limit_bytes=62 * 2**20
        ),
    )(*cots, *now, *late)


def head_kernel(
    n, head_in, w_head, gain, table, target, d_head, grad_head, small, loss, table_grad,
    all_head, logits, probs, onehot, turned, tops, parts_out, parts_in, rows_out, rows_in,
    stats_out, stats_in, send, recv,
):
    me_dp, me_mp = lax.axis_index("dp"), lax.axis_index("mp")
    mine, vec_width = all_head.shape[1:]
    total = n * mine
    rows_dev = table.shape[1]
    cols_dev = table_grad.shape[0]
    block = logits.shape[0]
    blocks = total // block
    owners = block // mine
    barrier = pltpu.get_barrier_semaphore()
    greet(barrier, "dp", n)

    pre = matmul(head_in[...], w_head[...])
    bell = lax.erf(pre * 0.7071067811865476) * 0.5 + 0.5
    value = pre * bell
    center = value - jnp.mean(value, axis=-1, keepdims=True)
    inv = scaled(center)
    normed = center * inv
    all_head[me_dp] = (normed * gain[...]).astype(BF)
    pl.semaphore_wait(barrier, n - 1)
    heads = Spread("dp", n, lambda peer: all_head.at[me_dp], all_head, send.at[0], recv.at[0])
    heads.start()

    def fill_onehot(b):
        count = block // target.shape[1]
        rows = target[pl.ds(pl.multiple_of(b * count, count), count)]
        wanted = jnp.concatenate([rows[i : i + 1] for i in range(count)], axis=1) - me_dp * rows_dev

        def body(row):
            index = lax.broadcasted_iota(jnp.int32, (80, block), 0) + row
            onehot[span(row, 80)] = jnp.where(index == wanted, 1.0, 0.0).astype(BF)

        each(rows_dev, 80, body)

    def slots_of(b):
        return all_head[pl.ds(b * owners, owners)].reshape(block, vec_width)

    def fill_probs(b):
        slots = slots_of(b)
        for start, count in chunks_of(rows_dev, 1024):
            logits[:, start : start + count] = matmul(slots, table[:, start : start + count])

        def body(row):
            x = logits[span(row, 16)]
            top = jnp.max(x, axis=-1, keepdims=True)
            x = jnp.exp(x - top)
            lane = lax.broadcasted_iota(jnp.int32, (16, LANES), 1)
            amount = jnp.sum(x, axis=-1, keepdims=True)
            tops[span(row, 16)] = jnp.where(lane == 0, top, jnp.where(lane == 1, amount, 0.0))
            probs[span(row, 16)] = x.astype(BF)

        each(block, 16, body, 2)

    def over_blocks(body):
        if blocks == 1:
            body(0)
        else:
            lax.fori_loop(0, blocks, lambda b, carry: (body(b), carry)[1], 0)

    def target_part(b):
        fill_onehot(b)
        found = matmul(table[...], onehot[...])
        turned[...] = found
        rows = jnp.transpose(found).astype(BF).reshape(owners, mine, vec_width)
        rows_out[pl.ds(b * owners, owners)] = rows

    def block_part(b):
        if blocks > 1:
            target_part(b)
        slots = jnp.transpose(slots_of(b).astype(F32))
        own = jnp.sum(slots * turned[...], axis=0, keepdims=True)
        fill_probs(b)
        part = contract(probs[...], table[...], 1, 1)
        at = pl.ds(b * owners, owners)
        parts_out[at] = part.astype(BF).reshape(owners, mine, vec_width)
        columns = pl.ds(pl.multiple_of(b * block, LANES), block)
        stats_out[0:2, columns] = jnp.transpose(tops[...])[0:2]
        stats_out[2:3, columns] = own

    row_exchange = Spread("dp", n, lambda peer: rows_out.at[peer], rows_in, send.at[2], recv.at[2])
    if blocks == 1:
        target_part(0)
        row_exchange.start()
    heads.wait()
    stats_out[...] = jnp.zeros_like(stats_out)
    over_blocks(block_part)
    exchanges = [
        Spread("dp", n, lambda peer: parts_out.at[peer], parts_in, send.at[1], recv.at[1]),
        Spread("dp", n, lambda peer: stats_out, stats_in, send.at[3], recv.at[3]),
    ]
    for exchange_one in exchanges:
        exchange_one.start()
    if blocks > 1:
        row_exchange.start()
    parts_in[me_dp] = parts_out[me_dp]
    rows_in[me_dp] = rows_out[me_dp]
    stats_in[me_dp] = stats_out[...]
    row_exchange.wait()
    for exchange_one in exchanges:
        exchange_one.wait()
    chosen = lax.broadcasted_iota(jnp.int32, (mine, total), 0) + me_dp * mine
    chosen = jnp.where(lax.broadcasted_iota(jnp.int32, (mine, total), 1) == chosen, 1.0, 0.0)

    def columns_of(source):
        return lax.dot_general(
            chosen, stats_in[source], (((1,), (1,)), ((), ())), precision=lax.Precision.HIGHEST,
            preferred_element_type=F32,
        )

    def combine(source, state):
        top, amount, sums, targets = state
        columns = columns_of(source)
        other = columns[:, 0:1]
        new_top = jnp.maximum(top, other)
        old, new = jnp.exp(top - new_top), jnp.exp(other - new_top)
        amount = amount * old + columns[:, 1:2] * new
        sums = sums * old + parts_in[source].astype(F32) * new
        return new_top, amount, sums, targets + rows_in[source].astype(F32)

    columns = columns_of(0)
    state = (columns[:, 0:1], columns[:, 1:2], parts_in[0].astype(F32), rows_in[0].astype(F32))
    _, amount, sums, targets = lax.fori_loop(1, n, combine, state)
    d_vec = sums / amount - targets
    small[...] = jnp.zeros_like(small)
    small[4:5, 0:vec_width] = jnp.sum(d_vec * normed, axis=0, keepdims=True)
    grad = d_vec * gain[...]
    d_value = inv * (
        grad
        - jnp.mean(grad, axis=-1, keepdims=True)
        - normed * jnp.mean(grad * normed, axis=-1, keepdims=True)
    )
    d_pre = d_value * (bell + pre * jnp.exp(pre * pre * -0.5) * 0.3989422804014327)
    d_low = d_pre.astype(BF)
    d_head[...] = contract(d_low, w_head[...], 1, 1)
    grad_head[...] = contract(head_in[...], d_low, 0, 0).astype(BF)

    def stat(row):
        def top_of(source, top):
            return jnp.maximum(top, stats_in[source, 0:1])

        top = lax.fori_loop(1, n, top_of, stats_in[0, 0:1])

        def add(source, state):
            amount, targets = state
            amount = amount + stats_in[source, 1:2] * jnp.exp(stats_in[source, 0:1] - top)
            return amount, targets + stats_in[source, 2:3]

        zero = jnp.zeros_like(top)
        amount, targets = lax.fori_loop(0, n, add, (zero, zero))
        return top + jnp.log(amount), targets

    log_total, targets = stat(0)
    loss[...] = jnp.broadcast_to(log_total - targets, loss.shape)
    stats_out[3:4] = jnp.exp(stats_out[0:1] - log_total)

    def table_part(b):
        if blocks > 1:
            fill_onehot(b)
            fill_probs(b)
        columns = pl.ds(pl.multiple_of(b * block, LANES), block)
        turned[...] = jnp.transpose(slots_of(b).astype(F32))
        own = turned[span(me_mp * cols_dev, cols_dev)]
        scaled_own = (own * stats_out[3:4, columns]).astype(BF)
        own = own.astype(BF)
        for start, count in chunks_of(rows_dev, 1024):
            at = slice(start, start + count)
            value = matmul(scaled_own, probs[:, at]) - contract(own, onehot[at], 1, 1)
            if blocks == 1:
                table_grad[:, at] = value
            else:
                table_grad[:, at] += value

    if blocks > 1:
        table_grad[...] = jnp.zeros_like(table_grad)
    over_blocks(table_part)


def head_layer(n, head_in, w_head, gain, table, target, cols_dev):
    mine, width = head_in.shape
    vec_width = w_head.shape[1]
    total = n * mine
    rows_dev = table.shape[1]
    block = math.gcd(total, 256)
    shapes = [
        ((mine, width), F32), ((width, vec_width), BF), ((8, width), F32), ((8, total), F32),
        ((cols_dev, rows_dev), F32),
    ]
    return pl.pallas_call(
        functools.partial(head_kernel, n),
        out_shape=[jax.ShapeDtypeStruct(*shape) for shape in shapes],
        in_specs=[VM] * 5,
        out_specs=[VM] * 5,
        scratch_shapes=[
            pltpu.VMEM((n, mine, vec_width), BF), pltpu.VMEM((block, rows_dev), F32),
            pltpu.VMEM((block, rows_dev), BF), pltpu.VMEM((rows_dev, block), BF),
            pltpu.VMEM((vec_width, block), F32), pltpu.VMEM((block, LANES), F32),
            pltpu.VMEM((n, mine, vec_width), BF), pltpu.VMEM((n, mine, vec_width), BF),
            pltpu.VMEM((n, mine, vec_width), BF), pltpu.VMEM((n, mine, vec_width), BF),
            pltpu.VMEM((8, total), F32), pltpu.VMEM((n, 8, total), F32),
            pltpu.SemaphoreType.DMA((4, n - 1)), pltpu.SemaphoreType.DMA((4, n - 1)),
        ],
        compiler_params=pltpu.CompilerParams(
            collective_id=5, has_side_effects=True, vmem_limit_bytes=56 * 2**20
        ),
    )(head_in, w_head, gain, table, target)


def shards(
    words, word_extra, span_pos, span_len, entity_shard, entity_row, targets, table, ent_proj,
    query_weight, w_key, w_value, w_out, gain_attn, bias_attn, w_up, w_down, gain_ffn, bias_ffn,
    w_head, gain_head, cot_words, cot_ents,
):
    n_dp = lax.axis_size("dp")
    n_mp = lax.axis_size("mp")
    seq_count, word_length, model_width = words.shape
    ent_len = span_pos.shape[1]
    masked_len = targets.shape[1]
    tokens_len = word_length + ent_len
    rows_dev, cols_dev = table.shape
    local_width = w_key.shape[1]
    heads_local = local_width // DH
    ent_total = seq_count * ent_len

    capacity = max(16, 2 * ent_total // n_dp)
    sizes = (seq_count, tokens_len, word_length, heads_local)
    (
        received, place, inside, spans, mask, norms, vec_rows, stream, qkv, lse, ctx, wt_words, wt_ents,
        center1, first_low, hidden, slope, center2, out_words, out_ents, head_in, table_rows,
    ) = forward_layer(
        sizes, masked_len, capacity, words,
        (
            word_extra, span_pos, span_len, entity_shard.reshape(seq_count, ent_len), entity_row,
            table.T, ent_proj, query_weight.transpose(0, 2, 1), w_key.T, w_value.T, w_out, w_up, w_down,
            gain_attn, bias_attn, gain_ffn, bias_ffn,
        ),
    )
    d_head, grad_head, small, loss, table_grad = head_layer(
        n_dp, head_in, w_head, gain_head[None], table_rows, targets, cols_dev
    )
    loss = loss[0]
    *sums, grad_words, table_hits, small = backward_layer(
        sizes, n_dp, capacity, rows_dev,
        (cot_words, cot_ents),
        (
            d_head.reshape(seq_count, masked_len, model_width), grad_head, center2, slope, hidden,
            first_low, center1, w_up, w_down, norms, small, ent_proj, vec_rows, place,
            received, inside, spans,
        ),
        (
            ctx, qkv, lse, wt_words, wt_ents, stream, mask, w_out,
        ),
    )
    grad_down, grad_up, grad_head, grad_ent_proj, *per_head = (a.astype(F32) for a in sums)
    per_head = [a.reshape(7, DH, model_width) for a in per_head]

    def columns_of(which):
        return jnp.concatenate([a[which] for a in per_head])

    grad_query = jnp.stack([columns_of(i) for i in (0, 1, 4, 5)]).transpose(0, 2, 1)
    grad_key, grad_value, grad_out = columns_of(2).T, columns_of(3).T, columns_of(6)
    table_grad = (table_grad + table_hits).T
    grad_gain_ffn, grad_bias_ffn, grad_gain_attn, grad_bias_attn = (small[i] for i in range(4))
    grad_gain_head = small[4, : w_head.shape[1]]
    return (
        out_words, out_ents, loss, grad_words, table_grad, grad_ent_proj, grad_query, grad_key,
        grad_value, grad_out, grad_gain_attn, grad_bias_attn, grad_up, grad_down, grad_gain_ffn,
        grad_bias_ffn, grad_head, grad_gain_head,
    )


def solution(mesh):
    return jax.shard_map(
        shards,
        mesh=mesh,
        in_specs=(
            P("dp", None, None), P("dp"), P("dp", None), P("dp", None), P("dp", None, None),
            P("dp", None), P(), P("dp", "mp"), P("mp", None), P(None, None, "mp"), P(None, "mp"),
            P(None, "mp"), P("mp", None), P(), P(), P(None, "mp"), P("mp", None), P(), P(), P(),
            P(), P("dp", None, None), P("dp", None, None),
        ),
        out_specs=(
            P("dp", None, None), P("dp", None, None), P(), P("dp", None, None), P("dp", "mp"),
            P("mp", None), P(None, None, "mp"), P(None, "mp"), P(None, "mp"), P("mp", None), P(),
            P(), P(None, "mp"), P("mp", None), P(), P(), P(), P(),
        ),
        check_vma=False,
    )
```

```python
import functools
import math

import jax
import jax.numpy as jnp
from jax import lax
from jax.experimental import pallas as pl
from jax.experimental.pallas import tpu as pltpu
from jax.sharding import PartitionSpec as P

DH = 64
SPANW = 4
EPSILON = 1e-05
MASKED_SCORE = -1000000000.0
LANES = 128
BF = jnp.bfloat16
F32 = jnp.float32
MESH = pl.DeviceIdType.MESH
VM = pl.BlockSpec(memory_space=pltpu.VMEM)


def matmul(first_op, second_op):
    return jnp.dot(first_op, second_op, preferred_element_type=F32)


def normalize(source, gain_vec, shift_vec):
    center = source - jnp.mean(source, axis=-1, keepdims=True)
    inv_scale = lax.rsqrt(jnp.mean(center * center, axis=-1, keepdims=True) + EPSILON)
    return center * inv_scale * gain_vec + shift_vec


def gelu_exact(source):
    return jax.nn.gelu(source, approximate=False)


def remote(src, dst, send, recv, axis, peer):
    return pltpu.make_async_remote_copy(
        src_ref=src, dst_ref=dst, send_sem=send, recv_sem=recv,
        device_id={axis: peer}, device_id_type=MESH,
    )


def contract(first_op, second_op, first_dim, second_dim):
    return lax.dot_general(
        first_op, second_op, (((first_dim,), (second_dim,)), ((), ())), preferred_element_type=F32
    )


def span(start, count):
    return pl.ds(pl.multiple_of(start, 16), count)


def each(count, step, body, unroll=1):
    while count // step % unroll:
        unroll -= 1

    def run(index, carry):
        for i in range(unroll):
            body(pl.multiple_of((index * unroll + i) * step, step))
        return carry

    lax.fori_loop(0, count // step // unroll, run, 0)


class Quarters:
    def __init__(self, part, r1, s2, r2, full, send, recv):
        self.part, self.r1, self.s2, self.r2, self.full = part, r1, s2, r2, full
        self.send, self.recv = send, recv
        me = lax.axis_index("mp")
        self.b0, self.b1 = lax.rem(me, 2), me // 2
        self.p1, self.p2 = me + 1 - 2 * self.b0, lax.rem(me + 2, 4)
        self.length = part.shape[1]
        self.half = self.length // 2
        self.quarter = self.length // 4

    def copy(self, s, k, src, dst, peer):
        return remote(src, dst, self.send.at[s, k], self.recv.at[s, k], "mp", peer)

    def first(self, s):
        rows = span((1 - self.b0) * self.half, self.half)
        return self.copy(s, 0, self.part.at[s, rows], self.r1.at[s], self.p1)

    def second(self, s):
        return self.copy(s, 1, self.s2.at[s], self.r2.at[s], self.p2)

    def place(self, s, h, q):
        return self.full.at[span(s * self.length + h * self.half + q * self.quarter, self.quarter)]

    def third(self, s, q):
        return self.copy(s, 2, self.place(s, self.b0, q), self.place(s, self.b0, q), self.p2)

    def fourth(self, s, h):
        return self.copy(s, 3, self.place(s, h, self.b1), self.place(s, h, self.b1), self.p1)

    def fifth(self, s, h):
        q = 1 - self.b1
        return self.copy(s, 4, self.place(s, h, q), self.place(s, h, q), self.p1)

    def both(self, s, q, row):
        mine = self.part[s, span(self.b0 * self.half + q * self.quarter + row, 16)]
        return mine.astype(F32) + self.r1[s, span(q * self.quarter + row, 16)].astype(F32)

    def begin(self, s):
        self.first(s).start()

    def pass_on(self, s):
        self.first(s).wait_recv()

        def body(row):
            self.s2[s, span(row, 16)] = self.both(s, 1 - self.b1, row).astype(BF)

        each(self.quarter, 16, body, 5)
        self.second(s).start()

    def wait_sum(self, s):
        self.second(s).wait_recv()

    def total(self, s, row):
        return self.both(s, self.b1, row) + self.r2[s, span(row, 16)].astype(F32)

    def own_row(self, s, row):
        return s * self.length + self.b0 * self.half + self.b1 * self.quarter + row

    def spread(self, s):
        self.third(s, self.b1).start()
        self.fourth(s, self.b0).start()

    def forward(self, s):
        self.third(s, 1 - self.b1).wait_recv()
        self.fifth(s, self.b0).start()

    def wait_full(self, s):
        self.fourth(s, 1 - self.b0).wait_recv()
        self.fifth(s, 1 - self.b0).wait_recv()

    def drain(self, s, sent=False):
        if not sent:
            self.first(s).wait_send()
        self.second(s).wait_send()
        self.third(s, self.b1).wait_send()
        self.fourth(s, self.b0).wait_send()
        self.fifth(s, self.b0).wait_send()


class Spread:
    def __init__(self, axis, n, source_of, into, send, recv):
        self.axis, self.n, self.source_of, self.into = axis, n, source_of, into
        self.send, self.recv = send, recv
        self.me = lax.axis_index(axis)

    def copy(self, step, peer, slot):
        return remote(
            self.source_of(peer), self.into.at[slot], self.send.at[step - 1], self.recv.at[step - 1],
            self.axis, peer,
        )

    def start(self):
        def begin(step, carry):
            self.copy(step, lax.rem(self.me + step, self.n), self.me).start()
            return carry

        lax.fori_loop(1, self.n, begin, 0)

    def wait(self):
        def finish(step, carry):
            source = lax.rem(self.me + self.n - step, self.n)
            self.copy(step, source, source).wait()
            return carry

        lax.fori_loop(1, self.n, finish, 0)


def greet(barrier, axis, n):
    me = lax.axis_index(axis)

    def signal(step, carry):
        pl.semaphore_signal(
            barrier, inc=1, device_id={axis: lax.rem(me + step, n)}, device_id_type=MESH
        )
        return carry

    lax.fori_loop(1, n, signal, 0)


def chunks_of(total, size):
    return [(start, min(size, total - start)) for start in range(0, total, size)]


def scaled(center):
    return lax.rsqrt(jnp.mean(center * center, axis=-1, keepdims=True) + EPSILON)


def scores_of(qkv, sT, h, cols, word_length):
    k_cols = pl.ds(cols.start, word_length), pl.ds(cols.start + word_length, cols.size - word_length)
    sT[0:word_length] = contract(qkv[h, 128:192, k_cols[0]], qkv[h, 0:64, cols], 0, 0)
    sT[word_length:] = contract(qkv[h, 128:192, k_cols[1]], qkv[h, 64:128, cols], 0, 0)


def forward_kernel(
    sizes, n, n_mp, capacity,
    words, word_extra, span_pos, span_len, shard, wanted, table, ent_proj, query_weight, w_key, w_value,
    w_out, w_up, w_down, gain_attn, bias_attn, gain_ffn, bias_ffn,
    received, place, inside, spans, mask, norms, vec_rows, stream, qkv, lse, ctx, wt_words, wt_ents, center1, first_low, hidden, slope,
    center2, out_words, out_ents, head_in, table_all,
    sT, pT, pre, first, part1, r11, s21, r21, part2, r12, s22, r22,
    onehot, answers, answered, vec_all, proj_all, spanned, requests,
    send1, recv1, send2, recv2, word_sem, dp_send, dp_recv, mp_send, mp_recv,
    table_send, table_recv,
):
    seqs, length, word_length, heads = sizes
    width = stream.shape[1]
    me_dp, me_mp = lax.axis_index("dp"), lax.axis_index("mp")
    units = w_up.shape[1]
    one = Quarters(part1, r11, s21, r21, first_low, send1, recv1)
    two = Quarters(part2, r12, s22, r22, center2, send2, recv2)
    barrier = pltpu.get_barrier_semaphore()
    greet(barrier, "dp", n)
    greet(barrier, "mp", n_mp)
    word_copies = [
        pltpu.make_async_copy(
            words.at[s], stream.at[pl.ds(s * length, word_length)], word_sem.at[s]
        )
        for s in range(seqs)
    ]
    for copy in word_copies:
        copy.start()
    asks = Spread("dp", n, lambda peer: requests.at[peer], received, dp_send.at[0], dp_recv.at[0])
    backs = Spread("dp", n, lambda peer: answers.at[peer], answered, dp_send.at[1], dp_recv.at[1])
    projs = Spread("mp", n_mp, lambda peer: ent_proj, proj_all, mp_send.at[0], mp_recv.at[0])
    vecs = Spread(
        "mp", n_mp, lambda peer: vec_all.at[me_mp], vec_all, mp_send.at[1], mp_recv.at[1]
    )
    ent_count = length - word_length
    ents = seqs * ent_count

    pieces = table_send.shape[1]
    cols_dev = table.shape[0]
    piece_rows = cols_dev // pieces

    def table_copy(kind, owner, piece):
        place_all = table_all.at[span(owner * cols_dev + piece * piece_rows, piece_rows)]
        source = place_all if kind == 2 else table.at[span(piece * piece_rows, piece_rows)]
        return remote(
            source, place_all, table_send.at[kind, piece], table_recv.at[kind, piece], "mp",
            one.p2 if kind == 1 else one.p1,
        )

    own_table = pltpu.make_async_copy(
        table, table_all.at[span(me_mp * cols_dev, cols_dev)], word_sem.at[seqs]
    )

    def table_begin(kind, first_piece, last_piece):
        for piece in range(first_piece, last_piece):
            table_copy(kind, me_mp, piece).start()

    def table_forward(first_piece, last_piece):
        for piece in range(first_piece, last_piece):
            table_copy(1, one.p2, piece).wait_recv()
            table_copy(2, one.p2, piece).start()

    def table_end():
        own_table.wait()
        for piece in range(pieces):
            table_copy(0, one.p1, piece).wait_recv()
            table_copy(2, lax.rem(one.p1 + 2, n_mp), piece).wait_recv()
            table_copy(0, me_mp, piece).wait_send()
            table_copy(1, me_mp, piece).wait_send()
            table_copy(2, one.p2, piece).wait_send()

    def rows_joined(ref):
        return jnp.concatenate([ref[s : s + 1] for s in range(seqs)], axis=1)

    def prepare():
        owner = rows_joined(shard).astype(F32)
        owner_of = jnp.transpose(jnp.broadcast_to(owner, (ents, ents)))
        earlier = lax.broadcasted_iota(jnp.int32, (ents, ents), 0) < lax.broadcasted_iota(
            jnp.int32, (ents, ents), 1
        )
        rank = jnp.sum(jnp.where(earlier & (owner_of == owner), 1.0, 0.0), axis=0, keepdims=True)
        spot = owner * LANES + rank
        place[...] = spot.astype(jnp.int32)
        spot_of = jnp.transpose(jnp.broadcast_to(spot, (LANES, ents)))
        row_of = jnp.transpose(jnp.broadcast_to(rows_joined(wanted).astype(F32) + 1.0, (LANES, ents)))
        lane = lax.broadcasted_iota(jnp.int32, (ents, LANES), 1).astype(F32)

        def ask_of(peer, carry):
            first_spot = (peer * LANES).astype(F32)
            asked = jnp.where(spot_of == lane + first_spot, row_of, 0.0)
            asked = jnp.sum(asked, axis=0, keepdims=True) - 1.0
            requests[peer] = jnp.broadcast_to(asked.astype(jnp.int32), (8, LANES))
            return carry

        lax.fori_loop(0, n, ask_of, 0)

    def prepare_spans():
        for row, source in enumerate((gain_attn, bias_attn, gain_ffn, bias_ffn)):
            norms[row : row + 1] = source[...].reshape(1, width)
        for s in range(seqs):
            count = word_length // 8 + word_extra[s]
            position = lax.broadcasted_iota(jnp.int32, (word_length, LANES), 0)
            mask[s] = jnp.where(position < count, 0.0, MASKED_SCORE)
            many = span_len[s : s + 1]
            start = lax.shift_right_logical(
                span_pos[s : s + 1] * (count - SPANW), word_length.bit_length() - 1
            )
            position = lax.broadcasted_iota(jnp.int32, (word_length, ent_count), 0)
            within = (position >= start) & (position < start + many)
            inside[s] = jnp.where(within, 1.0, 0.0).astype(BF)
            spans[s * ent_count : (s + 1) * ent_count] = jnp.transpose(
                jnp.broadcast_to(many.astype(F32), (LANES, ent_count))
            )

    def answer():
        ids = jnp.concatenate([received[source, 0:1, 0:capacity] for source in range(n)], axis=1)

        def body(row):
            index = lax.broadcasted_iota(jnp.int32, (80, n * capacity), 0) + row
            onehot[span(row, 80)] = jnp.where(index == ids, 1.0, 0.0).astype(BF)

        each(table.shape[1], 80, body)
        found = matmul(table[...], onehot[...]).astype(BF)
        for source in range(n):
            answers[source, :, 0:capacity] = found[:, source * capacity : (source + 1) * capacity]

    def collect():
        slot = lax.broadcasted_iota(jnp.int32, (capacity, seqs * ent_count), 0)

        def add(owner, total):
            placed = jnp.where(slot + owner * LANES == place[...], 1.0, 0.0).astype(BF)
            return total + matmul(answered[owner, :, 0:capacity], placed)

        total = lax.fori_loop(0, n, add, jnp.zeros(vec_rows.shape, F32))
        vec_rows[...] = total.astype(BF)
        vec_all[me_mp] = total.astype(BF)

    def span_means():
        for s in range(seqs):
            at = slice(s * ent_count, (s + 1) * ent_count)
            start = s * length
            spanned[at] = (
                contract(inside[s], stream[start : start + word_length], 0, 0) / spans[at, 0:1]
            )

    def entity_rows():
        vectors = vec_all[...].reshape(n_mp * vec_rows.shape[0], seqs * ent_count)
        projection = proj_all[...].reshape(n_mp * vec_rows.shape[0], width)
        value = (contract(vectors, projection, 0, 0) + spanned[...]).astype(BF)
        for s in range(seqs):
            at = s * length + word_length
            stream[at : at + ent_count] = value[s * ent_count : (s + 1) * ent_count]

    prepare()
    pl.semaphore_wait(barrier, n + n_mp - 2)
    received[me_dp] = requests[me_dp]
    asks.start()
    proj_all[me_mp] = ent_proj[...]
    projs.start()
    own_table.start()
    table_begin(1, 0, pieces // 2)
    table_begin(0, 0, pieces)
    prepare_spans()

    for target, first_query in ((wt_words, 0), (wt_ents, 2)):
        sources = (query_weight[first_query], query_weight[first_query + 1], w_key[...], w_value[...])
        for g, source in enumerate(sources):
            for h in range(heads):
                target[h, g * DH : (g + 1) * DH] = source[h * DH : (h + 1) * DH]

    def project(s, weight, start, count):
        base = s * length + start
        for h in range(heads):
            value = contract(weight[h], stream[base : base + count], 1, 1)
            qkv[h, 0:128, base : base + count] = (value[0:128] * 0.125).astype(BF)
            qkv[h, 128:256, base : base + count] = value[128:256].astype(BF)

    def attend(s, h):
        cols = pl.ds(s * length, length)
        scores_of(qkv, sT, h, cols, word_length)

        def body(col):
            here = pl.ds(col, LANES)
            words = sT[0:word_length, here] + mask[s]
            ents = sT[word_length:, here]
            top = jnp.maximum(
                jnp.max(words, axis=0, keepdims=True), jnp.max(ents, axis=0, keepdims=True)
            )
            words = jnp.exp(words - top)
            ents = jnp.exp(ents - top)
            total = jnp.sum(words, axis=0, keepdims=True) + jnp.sum(ents, axis=0, keepdims=True)
            pT[0:word_length, here] = words.astype(BF)
            pT[word_length:, here] = ents.astype(BF)
            lse[h, 0:1, pl.ds(pl.multiple_of(s * length + col, LANES), LANES)] = top + jnp.log(total)
            lse[h, 1:2, pl.ds(pl.multiple_of(s * length + col, LANES), LANES)] = 1.0 / total

        each(length, LANES, body)
        value = matmul(qkv[h, 192:256, cols], pT[...]) * lse[h, 1:2, cols]
        ctx[h * DH : (h + 1) * DH, cols] = value.astype(BF)

    def attention_part(s):
        value = contract(ctx[:, s * length : (s + 1) * length], w_out[...], 0, 0)
        part1[s] = value.astype(BF)

    def first_rows(s):
        def body(row):
            at = one.own_row(s, row)
            value = stream[span(at, 16)].astype(F32) + one.total(s, row)
            center = value - jnp.mean(value, axis=-1, keepdims=True)
            mine = span(s * one.quarter + row, 16)
            center1[mine] = center
            normed = center * scaled(center) * norms[0:1] + norms[1:2]
            first[mine] = normed
            first_low[span(at, 16)] = normed.astype(BF)

        each(one.quarter, 16, body, 5)

    def second_rows(s):
        def body(row):
            at = two.own_row(s, row)
            value = first[span(s * two.quarter + row, 16)] + two.total(s, row)
            center = value - jnp.mean(value, axis=-1, keepdims=True)
            center2[span(at, 16)] = center.astype(BF)

        each(two.quarter, 16, body, 5)

    def feed(s):
        rows = slice(s * length, (s + 1) * length)
        tile = 256
        for j in range(units // tile):
            cols = slice(j * tile, (j + 1) * tile)
            pre[...] = matmul(first_low[rows], w_up[:, cols])

            def body(row):
                value = pre[pl.ds(row, 32)]
                bell = lax.erf(value * 0.7071067811865476) * 0.5 + 0.5
                at = span(s * length + row, 32)
                hidden[at, cols] = (value * bell).astype(BF)
                slope[at, cols] = (
                    bell + value * jnp.exp(value * value * -0.5) * 0.3989422804014327
                ).astype(BF)

            each(length, 32, body, 4)
        for j in range(width // tile):
            cols = slice(j * tile, (j + 1) * tile)
            part2[s, :, cols] = matmul(hidden[rows], w_down[:, cols]).astype(BF)

    def output_rows(s):
        def rows_of(row):
            center = center2[span(s * length + row, 16)].astype(F32)
            return (center * scaled(center) * norms[2:3] + norms[3:4]).astype(BF)

        def word_rows(row):
            out_words[s, span(row, 16)] = rows_of(row)

        def ent_rows(row):
            out_ents[s, span(row, 16)] = rows_of(row + word_length)

        each(word_length, 16, word_rows, 4)
        each(ent_count, 16, ent_rows, 4)
        scored = head_in.shape[0] // seqs
        head_in[s * scored : (s + 1) * scored] = out_ents[s, 0:scored]

    for copy in word_copies:
        copy.wait()
    project(0, wt_words, 0, word_length)
    asks.wait()
    answer()
    answered[me_dp] = answers[me_dp]
    backs.start()
    span_means()
    project(1, wt_words, 0, word_length)
    backs.wait()
    collect()
    vecs.start()
    projs.wait()
    vecs.wait()
    table_begin(1, pieces // 2, pieces)
    entity_rows()
    project(0, wt_ents, word_length, ent_count)
    for h in range(heads):
        attend(0, h)
    attention_part(0)
    one.begin(0)
    table_forward(0, pieces // 2)
    project(1, wt_ents, word_length, ent_count)
    attend(1, 0)
    one.pass_on(0)
    for h in range(1, heads):
        attend(1, h)
    attention_part(1)
    one.begin(1)
    table_forward(pieces // 2, pieces)
    one.wait_sum(0)
    first_rows(0)
    one.spread(0)
    one.pass_on(1)
    one.forward(0)
    one.wait_full(0)
    feed(0)
    two.begin(0)
    one.wait_sum(1)
    first_rows(1)
    one.spread(1)
    two.pass_on(0)
    one.forward(1)
    one.wait_full(1)
    feed(1)
    two.begin(1)
    two.wait_sum(0)
    second_rows(0)
    two.spread(0)
    two.pass_on(1)
    two.forward(0)
    two.wait_full(0)
    output_rows(0)
    two.wait_sum(1)
    second_rows(1)
    two.spread(1)
    two.forward(1)
    two.wait_full(1)
    output_rows(1)
    for s in range(seqs):
        one.drain(s)
        two.drain(s)
    table_end()


def quarter_scratch(seqs, length, width):
    return [
        pltpu.VMEM((seqs, length, width), BF),
        pltpu.VMEM((seqs, length // 2, width), BF),
        pltpu.VMEM((seqs, length // 4, width), BF),
        pltpu.VMEM((seqs, length // 4, width), BF),
    ]


def forward_layer(sizes, scored, capacity, words, arrays):
    seqs, length, word_length, heads = sizes
    n, n_mp = lax.axis_size("dp"), lax.axis_size("mp")
    width = words.shape[2]
    tokens = seqs * length
    local, ents = heads * DH, seqs * (length - word_length)
    table, w_up = arrays[5], arrays[11]
    cols_dev, rows_dev = table.shape
    units = w_up.shape[1]

    def like(*shape, dtype=BF):
        return jax.ShapeDtypeStruct(shape, dtype)

    outs = [
        like(n, 8, LANES, dtype=jnp.int32), like(1, ents, dtype=jnp.int32),
        like(seqs, word_length, length - word_length), like(ents, LANES, dtype=F32),
        like(seqs, word_length, LANES, dtype=F32), like(4, width, dtype=F32),
        like(cols_dev, ents), like(tokens, width),
        like(heads, 4 * DH, tokens), like(heads, 8, tokens, dtype=F32), like(local, tokens),
        like(heads, 4 * DH, width), like(heads, 4 * DH, width), like(tokens // 4, width, dtype=F32),
        like(tokens, width), like(tokens, units), like(tokens, units), like(tokens, width),
        like(seqs, word_length, width), like(seqs, length - word_length, width),
        like(seqs * scored, width), like(n_mp * cols_dev, rows_dev),
    ]
    return pl.pallas_call(
        functools.partial(forward_kernel, sizes, n, n_mp, capacity),
        out_shape=outs,
        in_specs=[pl.BlockSpec(memory_space=pl.ANY), pl.BlockSpec(memory_space=pltpu.SMEM)]
        + [VM] * (len(arrays) - 1),
        out_specs=[VM] * (len(outs) - 1) + [pl.BlockSpec(memory_space=pl.ANY)],
        scratch_shapes=[
            pltpu.VMEM((length, length), F32),
            pltpu.VMEM((length, length), BF),
            pltpu.VMEM((length, 256), F32),
            pltpu.VMEM((tokens // 4, width), F32),
            *quarter_scratch(seqs, length, width),
            *quarter_scratch(seqs, length, width),
            pltpu.VMEM((rows_dev, n * capacity), BF),
            pltpu.VMEM((n, cols_dev, LANES), BF), pltpu.VMEM((n, cols_dev, LANES), BF),
            pltpu.VMEM((n_mp, cols_dev, ents), BF), pltpu.VMEM((n_mp, cols_dev, width), BF),
            pltpu.VMEM((ents, width), F32), pltpu.VMEM((n, 8, LANES), jnp.int32),
            pltpu.SemaphoreType.DMA((seqs, 5)), pltpu.SemaphoreType.DMA((seqs, 5)),
            pltpu.SemaphoreType.DMA((seqs, 5)), pltpu.SemaphoreType.DMA((seqs, 5)),
            pltpu.SemaphoreType.DMA((seqs + 1,)),
            pltpu.SemaphoreType.DMA((2, n - 1)), pltpu.SemaphoreType.DMA((2, n - 1)),
            pltpu.SemaphoreType.DMA((2, n_mp - 1)), pltpu.SemaphoreType.DMA((2, n_mp - 1)),
            pltpu.SemaphoreType.DMA((3, cols_dev // 16)), pltpu.SemaphoreType.DMA((3, cols_dev // 16)),
        ],
        compiler_params=pltpu.CompilerParams(
            collective_id=3, has_side_effects=True, vmem_limit_bytes=60 * 2**20
        ),
    )(words, *arrays)


class Job:
    def __init__(self, rows, buf, out, arrivals, send, recv, n, first=(0, 1, 2)):
        self.buf, self.out, self.arrivals, self.send, self.recv = buf, out, arrivals, send, recv
        self.rows = rows
        self.me = lax.axis_index("dp")
        self.bits, self.halvings = job_plan(rows, n)
        self.order = list(range(self.bits))
        if self.bits >= len(first):
            self.order[: len(first)] = first

    def bit(self, k):
        return lax.rem(self.me // 2 ** self.order[k], 2)

    def peer(self, k):
        return self.me + (1 - 2 * self.bit(k)) * 2 ** self.order[k]

    def offset(self, k):
        start = 0
        for i in range(k):
            start = start + self.bit(i) * (self.rows >> (i + 1))
        return start

    def copy(self, index, k, src, dst):
        return remote(src, dst, self.send.at[index], self.recv.at[index], "dp", self.peer(k))

    def steps(self):
        size = self.rows
        for k in range(self.bits):
            keep = self.offset(min(k, self.halvings))
            away = keep
            if k < self.halvings:
                size //= 2
                away = keep + (1 - self.bit(k)) * size
                keep = keep + self.bit(k) * size
            arrived = self.arrivals[k]
            copy = self.copy(k, k, self.buf.at[span(away, size)], arrived)
            copy.start()
            yield
            copy.wait()
            last = k == self.bits - 1

            def body(row, keep=keep, arrived=arrived, last=last):
                at = span(keep + row, 16)
                value = self.buf[at].astype(F32) + arrived[span(row, 16)].astype(F32)
                (self.out if last else self.buf)[at] = value.astype(BF)

            each(size, 16, body, 4)
        for k in reversed(range(self.halvings)):
            done = self.out.at[span(self.offset(k + 1), size)]
            copy = self.copy(self.bits + k, k, done, done)
            copy.start()
            yield
            copy.wait()
            size *= 2


def job_plan(rows, n):
    bits, halvings, size = n.bit_length() - 1, 0, rows
    while halvings < bits - 1 and (size // 2) % 16 == 0:
        size, halvings = size // 2, halvings + 1
    return bits, halvings


def job_cuts(units, width, head_rows, proj_rows, heads):
    orders = [
        ((1, 0, 2), (0, 1, 2), (1, 0, 2)),
        ((0, 1, 2), (0, 1, 2), (0, 1, 2)),
        ((0, 1, 2),),
        ((0, 1, 2),),
        ((0, 1, 2), (1, 0, 2)),
        ((0, 1, 2), (1, 0, 2)),
        ((0, 1, 2), (1, 0, 2)),
    ]
    cuts = [(units, [units // 3] * 3), (width, [width // 3] * 3)]
    cuts += [(head_rows, [head_rows]), (proj_rows, [proj_rows])]
    cuts += [(7 * DH, [4 * DH, 3 * DH])] * heads
    return [(rows, pieces, order) for (rows, pieces), order in zip(cuts, orders)]


def job_scratch(rows, width, n):
    bits, halvings = job_plan(rows, n)
    return [
        pltpu.VMEM((rows >> min(k + 1, halvings), width), BF) for k in range(bits)
    ]


def backward_kernel(sizes, n, n_mp, *refs):
    seqs, length, word_length, heads = sizes
    refs = list(refs)

    def take(count):
        taken = refs[:count]
        del refs[:count]
        return taken

    cot_words, cot_ents = take(2)
    (
        d_head, head_grad, center2, slope, hidden, first_low, center1, w_up, w_down, norms,
        small_in, ent_proj, vec_rows, place, received, inside, spans,
    ) = take(17)
    late_in = take(8)
    down_out, up_out, head_all, proj_out, heads_out = take(5)
    per_head_out = [heads_out.at[h] for h in range(heads)]
    word_grads, table_hits, small = take(3)
    ctx, qkv, lse, wt_words, wt_ents, stream, mask, w_out = late = take(8)
    sums, d_ffn, d_pre, d_attn, d_first, dctx, sT, dpT, pT, dsT, dcat = take(11)
    head_out, small_mp, small_dp, outbox, gw, inbox, onehot = take(7)
    part, r1, s2, r2 = take(4)
    (
        send1, recv1, send2, recv2, job_send, job_recv, late_sem, cot_sem,
        mp_send, mp_recv, dp_send, dp_recv, out_sem,
    ) = take(13)
    width = stream.shape[1]
    units = w_up.shape[1]
    me_mp, me_dp = lax.axis_index("mp"), lax.axis_index("dp")
    bits = n.bit_length() - 1
    jobs = []
    groups = [[], [], [], []] + [[] for h in range(heads)]
    buffers = take(len(groups))
    for group, buf, out, (rows, cuts, orders) in zip(
        groups, buffers, [down_out, up_out, head_out, proj_out, *per_head_out],
        job_cuts(units, width, head_out.shape[0], proj_out.shape[0], heads),
    ):
        start = 0
        for count, order in zip(cuts, orders):
            at = pl.ds(start, count)
            start += count
            index = len(jobs)
            jobs.append(
                Job(
                    count, buf.at[at], out.at[at], take(bits), job_send.at[index],
                    job_recv.at[index], n, order,
                )
            )
            group.append(jobs[-1])
    down_jobs, up_jobs, (head_job,), (proj_job,), *heads_jobs = groups
    down_buf, up_buf, head_buf, proj_buf, *heads_buf = buffers
    one = Quarters(part, r1, s2, r2, d_attn, send1, recv1)
    two = Quarters(part, r1, s2, r2, gw, send2, recv2)
    barrier = pltpu.get_barrier_semaphore()
    greet(barrier, "mp", n_mp)
    greet(barrier, "dp", n)
    cots = []
    for s in range(seqs):
        for k, (source, start, count) in enumerate(
            ((cot_words, 0, word_length), (cot_ents, word_length, length - word_length))
        ):
            target = d_attn.at[pl.ds(s * length + start, count)]
            cots.append(pltpu.make_async_copy(source.at[s], target, cot_sem.at[s, k]))
            cots[-1].start()
    late_copies = [
        pltpu.make_async_copy(source, target, late_sem.at[i])
        for i, (source, target) in enumerate(zip(late_in, late))
    ]
    for copy in late_copies:
        copy.start()
    running = {}

    def launch(job):
        running[id(job)] = job.steps()
        next(running[id(job)])

    def step(*which):
        for job in which:
            next(running[id(job)], 0)

    def finish(job):
        for _ in running[id(job)]:
            pass

    sums[...] = jnp.zeros_like(sums)

    spare = d_first.shape[0] - 16

    def second_back(s):
        start = one.own_row(0, 0)

        def rows_of(row, extra=None):
            at = span(s * length + row, 16)
            cot = d_attn[at].astype(F32)
            if extra is not None:
                cot = cot + extra
            center = center2[at].astype(F32)
            inv = scaled(center)
            normed = center * inv
            sums[0] += cot * normed
            sums[1] += cot
            grad = cot * norms[2:3]
            value = inv * (
                grad
                - jnp.mean(grad, axis=-1, keepdims=True)
                - normed * jnp.mean(grad * normed, axis=-1, keepdims=True)
            )
            d_ffn[at] = value.astype(BF)

            own = (row >= start) & (row < start + one.quarter)
            d_first[span(jnp.where(own, s * one.quarter + row - start, spare), 16)] = value

        scored = d_head.shape[1]
        each(word_length, 16, rows_of, 4)
        each(scored, 16, lambda row: rows_of(row + word_length, d_head[s, span(row, 16)]))
        each(length - word_length - scored, 16, lambda row: rows_of(row + word_length + scored), 7)

    def feed_back(s):
        rows = slice(s * length, (s + 1) * length)
        tile = 256
        for j in range(units // tile):
            cols = slice(j * tile, (j + 1) * tile)
            sT[:, 0:tile] = contract(d_ffn[rows], w_down[cols], 1, 1)

            def body(row):
                at = span(s * length + row, 32)
                d_pre[at, cols] = (
                    sT[pl.ds(row, 32), 0:tile] * slope[at, cols].astype(F32)
                ).astype(BF)

            each(length, 32, body, 4)
        for j in range(width // tile):
            cols = slice(j * tile, (j + 1) * tile)
            part[s, :, cols] = contract(d_pre[rows], w_up[cols], 1, 1).astype(BF)

    def first_back(s):
        def body(row):
            at = one.own_row(s, row)
            mine = span(s * one.quarter + row, 16)
            value = d_first[mine] + one.total(s, row)
            center = center1[mine]
            inv = scaled(center)
            normed = center * inv
            sums[2] += value * normed
            sums[3] += value
            grad = value * norms[0:1]
            value = inv * (
                grad
                - jnp.mean(grad, axis=-1, keepdims=True)
                - normed * jnp.mean(grad * normed, axis=-1, keepdims=True)
            )
            d_first[mine] = value
            d_attn[span(at, 16)] = value.astype(BF)

        each(one.quarter, 16, body, 5)

    def context_back(s):
        cols = slice(s * length, (s + 1) * length)
        dctx[:, cols] = contract(w_out[...], d_attn[cols], 1, 1).astype(BF)

    def attend_back(s, h):
        cols = pl.ds(s * length, length)
        w_cols = pl.ds(s * length, word_length)
        e_cols = pl.ds(s * length + word_length, length - word_length)
        mine = slice(h * DH, (h + 1) * DH)
        scores_of(qkv, sT, h, cols, word_length)
        dpT[...] = contract(qkv[h, 192:256, cols], dctx[mine, cols], 0, 0)

        def body(col):
            here = pl.ds(col, LANES)
            at = pl.ds(pl.multiple_of(s * length + col, LANES), LANES)
            delta = jnp.sum(
                ctx[mine, at].astype(F32) * dctx[mine, at].astype(F32), axis=0, keepdims=True
            )
            log_total = lse[h, 0:1, at]
            probs = jnp.exp(sT[0:word_length, here] + mask[s] - log_total)
            pT[0:word_length, here] = probs.astype(BF)
            dsT[0:word_length, here] = (probs * (dpT[0:word_length, here] - delta)).astype(BF)
            probs = jnp.exp(sT[word_length:, here] - log_total)
            pT[word_length:, here] = probs.astype(BF)
            dsT[word_length:, here] = (probs * (dpT[word_length:, here] - delta)).astype(BF)

        each(length, LANES, body)
        d_words, d_ents = dsT[0:word_length], dsT[word_length:]
        dcat[h, 0:64, cols] = (contract(qkv[h, 128:192, w_cols], d_words, 1, 0) * 0.125).astype(BF)
        dcat[h, 64:128, cols] = (contract(qkv[h, 128:192, e_cols], d_ents, 1, 0) * 0.125).astype(BF)
        dcat[h, 128:192, w_cols] = contract(qkv[h, 0:64, cols], d_words, 1, 1).astype(BF)
        dcat[h, 128:192, e_cols] = contract(qkv[h, 64:128, cols], d_ents, 1, 1).astype(BF)
        dcat[h, 192:256, cols] = contract(dctx[mine, cols], pT[...], 1, 1).astype(BF)

    def head_grads(h):
        buf = heads_buf[h]
        from_words, from_ents = None, None
        for s in range(seqs):
            middle, start, end = s * length + word_length, s * length, (s + 1) * length
            words = matmul(dcat[h, :, start:middle], stream[start:middle])
            ents = matmul(dcat[h, :, middle:end], stream[middle:end])
            from_words = words if s == 0 else from_words + words
            from_ents = ents if s == 0 else from_ents + ents
        buf[0:128] = from_words[0:128].astype(BF)
        buf[128:256] = from_ents[0:128].astype(BF)
        buf[256:384] = (from_words[128:256] + from_ents[128:256]).astype(BF)
        buf[384:448] = matmul(ctx[h * DH : (h + 1) * DH], d_attn[...]).astype(BF)

    def stream_part(s):
        for start in range(0, length, LANES):
            weight = wt_words if start < word_length else wt_ents
            cols = slice(s * length + start, s * length + start + LANES)
            value = contract(dcat[0, :, cols], weight[0], 0, 0)
            for h in range(1, heads):
                value = value + contract(dcat[h, :, cols], weight[h], 0, 0)
            part[s, start : start + LANES] = value.astype(BF)

    def last_rows(s):
        def body(row):
            at = two.own_row(s, row)
            value = d_first[span(s * two.quarter + row, 16)] + two.total(s, row)
            gw[span(at, 16)] = value.astype(BF)

        each(two.quarter, 16, body, 5)

    def down_tile(j):
        cols = slice(j * 256, (j + 1) * 256)
        down_buf[cols] = contract(hidden[:, cols], d_ffn[...], 0, 0).astype(BF)

    def up_tile(j):
        cols = slice(j * 256, (j + 1) * 256)
        up_buf[cols] = contract(first_low[:, cols], d_pre[...], 0, 0).astype(BF)

    def wait_cots(s):
        for copy in cots[2 * s : 2 * s + 2]:
            copy.wait()

    def wait_late():
        for copy in late_copies:
            copy.wait()

    small_over_mp = Spread(
        "mp", n_mp, lambda peer: small_mp.at[me_mp], small_mp, mp_send.at[0], mp_recv.at[0]
    )
    small_over_dp = Spread(
        "dp", n, lambda peer: small_dp.at[me_dp], small_dp, dp_send.at[0], dp_recv.at[0]
    )
    boxes = Spread("dp", n, lambda peer: outbox.at[peer], inbox, dp_send.at[1], dp_recv.at[1])
    head_rows = head_out.shape[0]
    head_place = span(me_mp * head_rows, head_rows)

    def head_copy(distance, peer, owner):
        return remote(
            head_out, head_all.at[span(owner * head_rows, head_rows)], mp_send.at[1, distance - 1],
            mp_recv.at[1, distance - 1], "mp", peer,
        )

    def small_first():
        mine = small_in[...]
        mine = mine + jnp.concatenate(
            [jnp.sum(sums[row], axis=0, keepdims=True) for row in range(4)]
            + [jnp.zeros((4, width), F32)]
        )
        small_mp[me_mp] = mine
        small_over_mp.start()

    def small_second():
        small_over_mp.wait()
        total = small_mp[0]
        for device in range(1, n_mp):
            total = total + small_mp[device]
        row = lax.broadcasted_iota(jnp.int32, total.shape, 0)
        small_dp[me_dp] = jnp.where((row == 2) | (row == 3), total, small_mp[me_mp])
        small_over_dp.start()

    def small_last():
        small_over_dp.wait()

        def add(device, total):
            return total + small_dp[device]

        small[...] = lax.fori_loop(1, n, add, small_dp[0])

    def head_first():
        head_all[head_place] = head_out[...]
        for distance in range(1, n_mp):
            head_copy(distance, lax.rem(me_mp + distance, n_mp), me_mp).start()

    def head_last():
        for distance in range(1, n_mp):
            source = lax.rem(me_mp + n_mp - distance, n_mp)
            head_copy(distance, source, source).wait()

    def entities():
        grads, rows = None, []
        count = length - word_length
        for s in range(seqs):
            d_ent = gw[s * length + word_length : (s + 1) * length]
            value = matmul(vec_rows[:, s * count : (s + 1) * count], d_ent)
            grads = value if s == 0 else grads + value
            rows.append(contract(ent_proj[...], d_ent, 1, 1).astype(BF))
        proj_buf[...] = grads.astype(BF)
        launch(proj_job)
        rows = jnp.concatenate(rows, axis=1)
        slot = lax.broadcasted_iota(jnp.int32, (LANES, seqs * count), 0)

        def fill(owner, carry):
            placed = jnp.where(slot + owner * LANES == place[...], 1.0, 0.0).astype(BF)
            outbox[owner] = contract(rows, placed, 1, 1).astype(BF)
            return carry

        lax.fori_loop(0, n, fill, 0)
        inbox[me_dp] = outbox[me_dp]
        boxes.start()

    out_copies = []

    def words_out(s):
        width_part = width // 2
        rows = slice(s * length, s * length + word_length)
        at = slice(s * (length - word_length), (s + 1) * (length - word_length))
        shared = gw[s * length + word_length : (s + 1) * length].astype(F32) / spans[at, 0:1]
        for half, source in enumerate((sT, dpT)):
            if s > 0:
                out_copies[2 * (s - 1) + half].wait()
            cols = slice(half * width_part, (half + 1) * width_part)
            source[0:word_length, 0:width_part] = gw[rows, cols].astype(F32) + matmul(
                inside[s], shared[:, cols].astype(BF)
            )
            out_copies.append(
                pltpu.make_async_copy(
                    source.at[pl.ds(0, word_length), pl.ds(0, width_part)],
                    word_grads.at[s, :, pl.ds(half * width_part, width_part)], out_sem.at[s, half],
                )
            )
            out_copies[-1].start()

    pieces = chunks_of(table_hits.shape[1], onehot.shape[0])
    parts = (len(pieces) + 3) // 4

    def table_part(part):
        capacity = onehot.shape[1] // n
        ids = jnp.concatenate([received[source, 0:1, 0:capacity] for source in range(n)], axis=1)
        rows = jnp.concatenate([inbox[source, :, 0:capacity] for source in range(n)], axis=1)
        for start, count in pieces[part * parts : (part + 1) * parts]:

            def body(row, start=start):
                index = lax.broadcasted_iota(jnp.int32, (32, n * capacity), 0) + (row + start)
                onehot[span(row, 32)] = jnp.where(index == ids, 1.0, 0.0).astype(BF)

            each(count, 32, body, 2)
            table_hits[:, start : start + count] = contract(rows, onehot[0:count], 1, 1)

    head_buf[...] = head_grad[head_place]
    wait_cots(0)
    second_back(0)
    feed_back(0)
    pl.semaphore_wait(barrier, n_mp - 1 + n - 1)
    one.begin(0)
    launch(head_job)
    wait_cots(1)
    second_back(1)
    one.pass_on(0)
    feed_back(1)
    one.begin(1)
    step(head_job)
    down_tile(0)
    launch(down_jobs[0])
    down_tile(1)
    launch(down_jobs[1])
    down_tile(2)
    launch(down_jobs[2])
    up_tile(0)
    launch(up_jobs[0])
    up_tile(1)
    launch(up_jobs[1])
    up_tile(2)
    launch(up_jobs[2])
    one.pass_on(1)
    step(head_job)
    one.wait_sum(0)
    first_back(0)
    one.spread(0)
    step(down_jobs[0], head_job, down_jobs[1])
    one.wait_sum(1)
    first_back(1)
    one.spread(1)
    small_first()
    step(down_jobs[2], head_job, up_jobs[0], down_jobs[1])
    one.forward(0)
    step(up_jobs[1], up_jobs[0])
    one.wait_full(0)
    small_second()
    wait_late()
    context_back(0)
    attend_back(0, 0)
    step(up_jobs[2])
    attend_back(0, 1)
    step(down_jobs[1], up_jobs[1], down_jobs[0])
    attend_back(0, 2)
    step(down_jobs[2], head_job)
    finish(head_job)
    head_first()
    step(up_jobs[0], up_jobs[2])
    one.first(0).wait_send()
    stream_part(0)
    two.begin(0)
    one.forward(1)
    step(down_jobs[1], up_jobs[1])
    one.wait_full(1)
    one.drain(0, True)
    one.drain(1)
    context_back(1)
    step(up_jobs[0])
    attend_back(1, 0)
    two.pass_on(0)
    head_grads(0)
    launch(heads_jobs[0][0])
    launch(heads_jobs[0][1])
    step(down_jobs[0], down_jobs[1], up_jobs[1])
    attend_back(1, 1)
    head_grads(1)
    launch(heads_jobs[1][0])
    launch(heads_jobs[1][1])
    step(down_jobs[2], up_jobs[0])
    attend_back(1, 2)
    step(heads_jobs[0][1])
    stream_part(1)
    two.begin(1)
    step(up_jobs[2], heads_jobs[0][0])
    head_grads(2)
    launch(heads_jobs[2][0])
    launch(heads_jobs[2][1])
    step(heads_jobs[1][1], down_jobs[0])
    two.pass_on(1)
    two.wait_sum(0)
    last_rows(0)
    two.spread(0)
    small_last()
    step(up_jobs[2], up_jobs[1], heads_jobs[0][0])
    two.wait_sum(1)
    last_rows(1)
    two.spread(1)
    step(heads_jobs[2][1], heads_jobs[1][0], down_jobs[2], heads_jobs[0][1])
    step(down_jobs[0], heads_jobs[0][0])
    two.forward(0)
    step(heads_jobs[1][0], heads_jobs[2][0], heads_jobs[1][1])
    two.forward(1)
    two.wait_full(0)
    step(heads_jobs[0][1], down_jobs[2])
    two.wait_full(1)
    entities()
    step(heads_jobs[0][0], up_jobs[2])
    words_out(0)
    step(heads_jobs[1][0], heads_jobs[2][0], heads_jobs[2][1])
    words_out(1)
    step(heads_jobs[0][1], heads_jobs[1][1], proj_job)
    boxes.wait()
    table_part(0)
    step(heads_jobs[1][0])
    table_part(1)
    step(heads_jobs[0][0])
    table_part(2)
    step(heads_jobs[2][0], heads_jobs[0][1], heads_jobs[1][1], proj_job)
    table_part(3)
    step(heads_jobs[2][1], heads_jobs[1][0], proj_job, heads_jobs[2][0])
    step(heads_jobs[2][1], heads_jobs[1][1], proj_job, heads_jobs[2][0])
    step(heads_jobs[2][1], proj_job)
    head_last()
    for s in range(seqs):
        two.drain(s)
    for copy in out_copies[-2:]:
        copy.wait()
    for job in jobs:
        finish(job)


def backward_layer(sizes, n, capacity, rows_dev, cots, now, late):
    seqs, length, word_length, heads = sizes
    stream, w_up, ent_proj = late[5], now[7], now[11]
    n_mp = lax.axis_size("mp")
    tokens, width = stream.shape
    units, local = w_up.shape[1], heads * DH
    head_rows, head_width = now[1].shape[0] // n_mp, now[1].shape[1]
    bits = n.bit_length() - 1
    outs = [(units, width), (width, units), (n_mp * head_rows, head_width), ent_proj.shape]
    outs += [(heads, 7 * DH, width)]
    outs = [jax.ShapeDtypeStruct(shape, BF) for shape in outs]
    outs += [
        jax.ShapeDtypeStruct((seqs, word_length, width), F32),
        jax.ShapeDtypeStruct((ent_proj.shape[0], rows_dev), F32),
        jax.ShapeDtypeStruct((8, width), F32),
    ]
    cuts = job_cuts(units, width, head_rows, ent_proj.shape[0], heads)
    widths = [width, units, head_width] + [width] * (1 + heads)
    job_count = sum(len(sizes) for _, sizes, _ in cuts)
    scratch = [pltpu.VMEM(value.shape, value.dtype) for value in late]
    scratch += [
        pltpu.VMEM((4, 16, width), F32), pltpu.VMEM((tokens, width), BF),
        pltpu.VMEM((tokens, units), BF), pltpu.VMEM((tokens, width), BF),
        pltpu.VMEM((tokens // 4 + 16, width), F32), pltpu.VMEM((local, tokens), BF),
        pltpu.VMEM((length, length), F32), pltpu.VMEM((length, length), F32),
        pltpu.VMEM((length, length), BF), pltpu.VMEM((length, length), BF),
        pltpu.VMEM((heads, 4 * DH, tokens), BF),
        pltpu.VMEM((head_rows, head_width), BF), pltpu.VMEM((n_mp, 8, width), F32),
        pltpu.VMEM((n, 8, width), F32), pltpu.VMEM((n, ent_proj.shape[0], LANES), BF),
        pltpu.VMEM((tokens, width), BF), pltpu.VMEM((n, ent_proj.shape[0], LANES), BF),
        pltpu.VMEM((256, n * capacity), BF),
        *quarter_scratch(seqs, length, width),
        pltpu.SemaphoreType.DMA((seqs, 5)), pltpu.SemaphoreType.DMA((seqs, 5)),
        pltpu.SemaphoreType.DMA((seqs, 5)), pltpu.SemaphoreType.DMA((seqs, 5)),
        pltpu.SemaphoreType.DMA((job_count, 2 * bits)),
        pltpu.SemaphoreType.DMA((job_count, 2 * bits)),
        pltpu.SemaphoreType.DMA((len(late),)), pltpu.SemaphoreType.DMA((seqs, 2)),
        pltpu.SemaphoreType.DMA((2, n_mp - 1)), pltpu.SemaphoreType.DMA((2, n_mp - 1)),
        pltpu.SemaphoreType.DMA((2, n - 1)), pltpu.SemaphoreType.DMA((2, n - 1)),
        pltpu.SemaphoreType.DMA((seqs, 2)),
    ]
    scratch += [pltpu.VMEM((rows, columns), BF) for (rows, _, _), columns in zip(cuts, widths)]
    for (_, counts, _), columns in zip(cuts, widths):
        for count in counts:
            scratch += job_scratch(count, columns, n)
    hbm = pl.BlockSpec(memory_space=pl.ANY)
    return pl.pallas_call(
        functools.partial(backward_kernel, sizes, n, n_mp),
        out_shape=outs,
        in_specs=[hbm] * len(cots) + [VM] * len(now) + [hbm] * len(late),
        out_specs=[VM] * (len(outs) - 3) + [hbm, VM, VM],
        scratch_shapes=scratch,
        compiler_params=pltpu.CompilerParams(
            collective_id=7, has_side_effects=True, vmem_limit_bytes=62 * 2**20
        ),
    )(*cots, *now, *late)


def head_kernel(
    n, head_in, w_head, gain, table, target, d_head, grad_head, small, loss, table_grad,
    all_head, logits, probs, onehot, turned, tops, parts_out, parts_in, rows_out, rows_in,
    stats_out, stats_in, send, recv,
):
    me_dp, me_mp = lax.axis_index("dp"), lax.axis_index("mp")
    mine, vec_width = all_head.shape[1:]
    total = n * mine
    rows_dev = table.shape[1]
    cols_dev = table_grad.shape[0]
    block = logits.shape[0]
    blocks = total // block
    owners = block // mine
    barrier = pltpu.get_barrier_semaphore()
    greet(barrier, "dp", n)

    pre = matmul(head_in[...], w_head[...])
    bell = lax.erf(pre * 0.7071067811865476) * 0.5 + 0.5
    value = pre * bell
    center = value - jnp.mean(value, axis=-1, keepdims=True)
    inv = scaled(center)
    normed = center * inv
    all_head[me_dp] = (normed * gain[...]).astype(BF)
    pl.semaphore_wait(barrier, n - 1)
    heads = Spread("dp", n, lambda peer: all_head.at[me_dp], all_head, send.at[0], recv.at[0])
    heads.start()

    def fill_onehot(b):
        count = block // target.shape[1]
        rows = target[pl.ds(pl.multiple_of(b * count, count), count)]
        wanted = jnp.concatenate([rows[i : i + 1] for i in range(count)], axis=1) - me_dp * rows_dev

        def body(row):
            index = lax.broadcasted_iota(jnp.int32, (80, block), 0) + row
            onehot[span(row, 80)] = jnp.where(index == wanted, 1.0, 0.0).astype(BF)

        each(rows_dev, 80, body)

    def slots_of(b):
        return all_head[pl.ds(b * owners, owners)].reshape(block, vec_width)

    def fill_probs(b):
        slots = slots_of(b)
        for start, count in chunks_of(rows_dev, 1024):
            logits[:, start : start + count] = matmul(slots, table[:, start : start + count])

        def body(row):
            x = logits[span(row, 16)]
            top = jnp.max(x, axis=-1, keepdims=True)
            x = jnp.exp(x - top)
            lane = lax.broadcasted_iota(jnp.int32, (16, LANES), 1)
            amount = jnp.sum(x, axis=-1, keepdims=True)
            tops[span(row, 16)] = jnp.where(lane == 0, top, jnp.where(lane == 1, amount, 0.0))
            probs[span(row, 16)] = x.astype(BF)

        each(block, 16, body, 2)

    def over_blocks(body):
        if blocks == 1:
            body(0)
        else:
            lax.fori_loop(0, blocks, lambda b, carry: (body(b), carry)[1], 0)

    def target_part(b):
        fill_onehot(b)
        found = matmul(table[...], onehot[...])
        turned[...] = found
        rows = jnp.transpose(found).astype(BF).reshape(owners, mine, vec_width)
        rows_out[pl.ds(b * owners, owners)] = rows

    def block_part(b):
        if blocks > 1:
            target_part(b)
        slots = jnp.transpose(slots_of(b).astype(F32))
        own = jnp.sum(slots * turned[...], axis=0, keepdims=True)
        fill_probs(b)
        part = contract(probs[...], table[...], 1, 1)
        at = pl.ds(b * owners, owners)
        parts_out[at] = part.astype(BF).reshape(owners, mine, vec_width)
        columns = pl.ds(pl.multiple_of(b * block, LANES), block)
        stats_out[0:2, columns] = jnp.transpose(tops[...])[0:2]
        stats_out[2:3, columns] = own

    row_exchange = Spread("dp", n, lambda peer: rows_out.at[peer], rows_in, send.at[2], recv.at[2])
    if blocks == 1:
        target_part(0)
        row_exchange.start()
    heads.wait()
    stats_out[...] = jnp.zeros_like(stats_out)
    over_blocks(block_part)
    exchanges = [
        Spread("dp", n, lambda peer: parts_out.at[peer], parts_in, send.at[1], recv.at[1]),
        Spread("dp", n, lambda peer: stats_out, stats_in, send.at[3], recv.at[3]),
    ]
    for exchange_one in exchanges:
        exchange_one.start()
    if blocks > 1:
        row_exchange.start()
    parts_in[me_dp] = parts_out[me_dp]
    rows_in[me_dp] = rows_out[me_dp]
    stats_in[me_dp] = stats_out[...]
    row_exchange.wait()
    for exchange_one in exchanges:
        exchange_one.wait()
    chosen = lax.broadcasted_iota(jnp.int32, (mine, total), 0) + me_dp * mine
    chosen = jnp.where(lax.broadcasted_iota(jnp.int32, (mine, total), 1) == chosen, 1.0, 0.0)

    def columns_of(source):
        return lax.dot_general(
            chosen, stats_in[source], (((1,), (1,)), ((), ())), precision=lax.Precision.HIGHEST,
            preferred_element_type=F32,
        )

    def combine(source, state):
        top, amount, sums, targets = state
        columns = columns_of(source)
        other = columns[:, 0:1]
        new_top = jnp.maximum(top, other)
        old, new = jnp.exp(top - new_top), jnp.exp(other - new_top)
        amount = amount * old + columns[:, 1:2] * new
        sums = sums * old + parts_in[source].astype(F32) * new
        return new_top, amount, sums, targets + rows_in[source].astype(F32)

    columns = columns_of(0)
    state = (columns[:, 0:1], columns[:, 1:2], parts_in[0].astype(F32), rows_in[0].astype(F32))
    _, amount, sums, targets = lax.fori_loop(1, n, combine, state)
    d_vec = sums / amount - targets
    small[...] = jnp.zeros_like(small)
    small[4:5, 0:vec_width] = jnp.sum(d_vec * normed, axis=0, keepdims=True)
    grad = d_vec * gain[...]
    d_value = inv * (
        grad
        - jnp.mean(grad, axis=-1, keepdims=True)
        - normed * jnp.mean(grad * normed, axis=-1, keepdims=True)
    )
    d_pre = d_value * (bell + pre * jnp.exp(pre * pre * -0.5) * 0.3989422804014327)
    d_low = d_pre.astype(BF)
    d_head[...] = contract(d_low, w_head[...], 1, 1)
    grad_head[...] = contract(head_in[...], d_low, 0, 0).astype(BF)

    def stat(row):
        def top_of(source, top):
            return jnp.maximum(top, stats_in[source, 0:1])

        top = lax.fori_loop(1, n, top_of, stats_in[0, 0:1])

        def add(source, state):
            amount, targets = state
            amount = amount + stats_in[source, 1:2] * jnp.exp(stats_in[source, 0:1] - top)
            return amount, targets + stats_in[source, 2:3]

        zero = jnp.zeros_like(top)
        amount, targets = lax.fori_loop(0, n, add, (zero, zero))
        return top + jnp.log(amount), targets

    log_total, targets = stat(0)
    loss[...] = jnp.broadcast_to(log_total - targets, loss.shape)
    stats_out[3:4] = jnp.exp(stats_out[0:1] - log_total)

    def table_part(b):
        if blocks > 1:
            fill_onehot(b)
            fill_probs(b)
        columns = pl.ds(pl.multiple_of(b * block, LANES), block)
        turned[...] = jnp.transpose(slots_of(b).astype(F32))
        own = turned[span(me_mp * cols_dev, cols_dev)]
        scaled_own = (own * stats_out[3:4, columns]).astype(BF)
        own = own.astype(BF)
        for start, count in chunks_of(rows_dev, 1024):
            at = slice(start, start + count)
            value = matmul(scaled_own, probs[:, at]) - contract(own, onehot[at], 1, 1)
            if blocks == 1:
                table_grad[:, at] = value
            else:
                table_grad[:, at] += value

    if blocks > 1:
        table_grad[...] = jnp.zeros_like(table_grad)
    over_blocks(table_part)


def head_layer(n, head_in, w_head, gain, table, target, cols_dev):
    mine, width = head_in.shape
    vec_width = w_head.shape[1]
    total = n * mine
    rows_dev = table.shape[1]
    block = math.gcd(total, 256)
    shapes = [
        ((mine, width), F32), ((width, vec_width), BF), ((8, width), F32), ((8, total), F32),
        ((cols_dev, rows_dev), F32),
    ]
    return pl.pallas_call(
        functools.partial(head_kernel, n),
        out_shape=[jax.ShapeDtypeStruct(*shape) for shape in shapes],
        in_specs=[VM] * 5,
        out_specs=[VM] * 5,
        scratch_shapes=[
            pltpu.VMEM((n, mine, vec_width), BF), pltpu.VMEM((block, rows_dev), F32),
            pltpu.VMEM((block, rows_dev), BF), pltpu.VMEM((rows_dev, block), BF),
            pltpu.VMEM((vec_width, block), F32), pltpu.VMEM((block, LANES), F32),
            pltpu.VMEM((n, mine, vec_width), BF), pltpu.VMEM((n, mine, vec_width), BF),
            pltpu.VMEM((n, mine, vec_width), BF), pltpu.VMEM((n, mine, vec_width), BF),
            pltpu.VMEM((8, total), F32), pltpu.VMEM((n, 8, total), F32),
            pltpu.SemaphoreType.DMA((4, n - 1)), pltpu.SemaphoreType.DMA((4, n - 1)),
        ],
        compiler_params=pltpu.CompilerParams(
            collective_id=5, has_side_effects=True, vmem_limit_bytes=56 * 2**20
        ),
    )(head_in, w_head, gain, table, target)


def shards(
    words, word_extra, span_pos, span_len, entity_shard, entity_row, targets, table, ent_proj,
    query_weight, w_key, w_value, w_out, gain_attn, bias_attn, w_up, w_down, gain_ffn, bias_ffn,
    w_head, gain_head, cot_words, cot_ents,
):
    n_dp = lax.axis_size("dp")
    n_mp = lax.axis_size("mp")
    seq_count, word_length, model_width = words.shape
    ent_len = span_pos.shape[1]
    masked_len = targets.shape[1]
    tokens_len = word_length + ent_len
    rows_dev, cols_dev = table.shape
    local_width = w_key.shape[1]
    heads_local = local_width // DH
    ent_total = seq_count * ent_len

    capacity = max(16, 2 * ent_total // n_dp)
    sizes = (seq_count, tokens_len, word_length, heads_local)
    (
        received, place, inside, spans, mask, norms, vec_rows, stream, qkv, lse, ctx, wt_words, wt_ents,
        center1, first_low, hidden, slope, center2, out_words, out_ents, head_in, table_rows,
    ) = forward_layer(
        sizes, masked_len, capacity, words,
        (
            word_extra, span_pos, span_len, entity_shard.reshape(seq_count, ent_len), entity_row,
            table.T, ent_proj, query_weight.transpose(0, 2, 1), w_key.T, w_value.T, w_out, w_up, w_down,
            gain_attn, bias_attn, gain_ffn, bias_ffn,
        ),
    )
    d_head, grad_head, small, loss, table_grad = head_layer(
        n_dp, head_in, w_head, gain_head[None], table_rows, targets, cols_dev
    )
    loss = loss[0]
    *sums, grad_words, table_hits, small = backward_layer(
        sizes, n_dp, capacity, rows_dev,
        (cot_words, cot_ents),
        (
            d_head.reshape(seq_count, masked_len, model_width), grad_head, center2, slope, hidden,
            first_low, center1, w_up, w_down, norms, small, ent_proj, vec_rows, place,
            received, inside, spans,
        ),
        (
            ctx, qkv, lse, wt_words, wt_ents, stream, mask, w_out,
        ),
    )
    grad_down, grad_up, grad_head, grad_ent_proj, per_head = (a.astype(F32) for a in sums)
    per_head = per_head.reshape(heads_local, 7, DH, model_width).transpose(1, 0, 2, 3)
    per_head = per_head.reshape(7, local_width, model_width)
    grad_query = per_head[:4].transpose(0, 2, 1)
    grad_key, grad_value, grad_out = per_head[4].T, per_head[5].T, per_head[6]
    table_grad = (table_grad + table_hits).T
    grad_gain_ffn, grad_bias_ffn, grad_gain_attn, grad_bias_attn = (small[i] for i in range(4))
    grad_gain_head = small[4, : w_head.shape[1]]
    return (
        out_words, out_ents, loss, grad_words, table_grad, grad_ent_proj, grad_query, grad_key,
        grad_value, grad_out, grad_gain_attn, grad_bias_attn, grad_up, grad_down, grad_gain_ffn,
        grad_bias_ffn, grad_head, grad_gain_head,
    )


def solution(mesh):
    return jax.shard_map(
        shards,
        mesh=mesh,
        in_specs=(
            P("dp", None, None), P("dp"), P("dp", None), P("dp", None), P("dp", None, None),
            P("dp", None), P(), P("dp", "mp"), P("mp", None), P(None, None, "mp"), P(None, "mp"),
            P(None, "mp"), P("mp", None), P(), P(), P(None, "mp"), P("mp", None), P(), P(), P(),
            P(), P("dp", None, None), P("dp", None, None),
        ),
        out_specs=(
            P("dp", None, None), P("dp", None, None), P(), P("dp", None, None), P("dp", "mp"),
            P("mp", None), P(None, None, "mp"), P(None, "mp"), P(None, "mp"), P("mp", None), P(),
            P(), P(None, "mp"), P("mp", None), P(), P(), P(), P(),
        ),
        check_vma=False,
    )
```
